32 devices in a mesh: ka: 8 (over y, x, core), hist: 4 (over z).
Axes of the slice: x: 2, y: 2, z: 4, core: 2. Of those that a mesh axis runs over, the one named last changes fastest.
Arguments:
- green_row: float32 [256, 576, 128], P('hist', 'ka'), may hold values from -6 to 6
- screened: float32 [256, 576, 128], P('hist', 'ka'), may hold values from -0.2 to 0.2
- hamilton: float32 [576, 128], P('ka'), may hold values from -6 to 6
- equal_time: float32 [576, 128], P('ka'), may hold values from -0.5 to 2.5, as said below
- quad_class: int32 [256], P('hist'), may hold values from 0 to 3
- live_count: int32 [4], P('hist'), may hold values from 1 to 64
Outputs:
- green_next: float32 [256, 576, 128], P('hist', 'ka')
The draws below stay inside these ranges and needn't reach their ends.
Inputs may be any that keep to these rules, and one draw needn't show every extreme that they name: `quad_class`: class c selects the weight q[c] of q = (0.375, 1.1666666, 0.9583333, 1.0). Stored times at positions live_count[j] or later inside block j carry no weight. `equal_time`: the imaginary diagonal entries are positive.
All inputs are finite; a program needn't handle non-finite values.
Results may differ from the reference program's by a relative error of at most 0.00005.
Values sent between devices are 32-bit elements; how exact they have to be, the bound alone decides.
No kernel may reach another device: no remote copies, remote signals or barrier semaphores. Data moves between devices by JAX's collectives and lax.ppermute only.
A program may use at most 64 MiB of HBM per device.

```python
import math
import jax
import jax.numpy as jnp
from jax import lax

SIDE = 24
BANDS = 8
TB = 64
NT = 256
NK = 576
N_HIST = 4


def draw_equal_time(key, part):
    points = SIDE * SIDE
    width = 2 * BANDS * BANDS
    first_key = jax.random.fold_in(key, 11)
    second_key = jax.random.fold_in(key, 23)
    base = jnp.clip(0.1 * jax.random.normal(first_key, (points, width), jnp.float32), -0.5, 0.5)
    ramp = 1.0 + 2.0 * jnp.arange(points, dtype=jnp.float32) / (points - 1)
    occupied = jax.random.uniform(second_key, (points, BANDS), jnp.float32, 0.1, 0.6)
    occupied = occupied * ramp[:, None]
    spots = BANDS * BANDS + jnp.arange(BANDS, dtype=jnp.int32) * (BANDS + 1)
    placing = (jnp.arange(width, dtype=jnp.int32)[None, :] == spots[:, None]).astype(jnp.float32)
    return base * (1.0 - jnp.sum(placing, axis=0))[None, :] + jnp.dot(occupied, placing)


def with_ends(result, stream_key, least, high):
    dims = result.shape
    spot = [jax.random.randint(jax.random.fold_in(stream_key, axis), (), 0, dims[axis]) for axis in range(len(dims))]
    result = result.at[tuple(spot)].set(least)
    longest = dims.index(max(dims))
    spot[longest] = (spot[longest] + 1) % dims[longest]
    return result.at[tuple(spot)].set(high)


def shard_levels(rng, extent, cuts, least, largest):
    factor_of, own = 1.0, jax.random.fold_in(rng, 6)
    for dim, parts in cuts:
        steps = jnp.exp(jax.random.uniform(jax.random.fold_in(own, dim), (parts,), jnp.float32, least / len(cuts), largest / len(cuts)))
        factor_of = factor_of * jnp.repeat(steps, extent[dim] // parts).reshape([-1 if axis == dim else 1 for axis in range(len(extent))])
    return factor_of


def gaussian(rng, shape, deviation, most, shards=(), kind=jnp.bfloat16):
    drawn = deviation * jax.random.normal(rng, shape, jnp.float32)
    if shards:
        drawn = drawn * shard_levels(rng, shape, shards, -0.22, 0.18)
    return jnp.clip(drawn, -most, most).astype(kind)


def setup_inputs(seed: int = 0) -> dict:
    splits = jax.random.split(jax.random.key(seed), 7)
    green_row = gaussian(splits[0], (NT, NK, 2 * BANDS * BANDS), 1.0, 6.0, ((0, 4), (1, 8)), jnp.float32)
    screened = gaussian(splits[1], (NT, NK, 2 * BANDS * BANDS), 0.03, 0.2, ((0, 4), (1, 8)), jnp.float32)
    hamilton = gaussian(splits[2], (NK, 2 * BANDS * BANDS), 1.0, 6.0, ((0, 8),), jnp.float32)
    equal_time = draw_equal_time(jax.random.fold_in(splits[6], 71), 0)
    quad_class = with_ends(jax.random.randint(splits[4], (NT,), 0, 4), jax.random.fold_in(splits[4], 1), 0, 3).astype(jnp.int32)
    live_count = with_ends(jax.random.randint(splits[5], (N_HIST,), 1, TB + 1), jax.random.fold_in(splits[5], 1), 1, TB).astype(jnp.int32)
    return {"green_row": green_row, "screened": screened, "hamilton": hamilton, "equal_time": equal_time, "quad_class": quad_class, "live_count": live_count}


time_step = 0.1
hubbard = 1.0
quadrature = (0.375, 1.1666666, 0.9583333, 1.0)


def phase_tables(side):
    points = jnp.arange(side * side, dtype=jnp.int32)
    first_axis = points // side
    second = points % side
    winding = (first_axis[:, None] * first_axis[None, :] + second[:, None] * second[None, :]) % side
    angles = winding.astype(jnp.float32) * (2.0 * math.pi / side)
    return jnp.cos(angles) / side, jnp.sin(angles) / side


def transform(phases, values):
    return jnp.einsum("rk,tke->tre", phases, values, precision=lax.Precision.HIGHEST)


def self_energy(greens, screen, cosine_table, sine_table):
    entries = greens.shape[-1] // 2
    green_real, green_imag = greens[..., :entries], greens[..., entries:]
    lattice_real = transform(cosine_table, green_real) + transform(sine_table, green_imag)
    lattice_imag = transform(cosine_table, green_imag) - transform(sine_table, green_real)
    screen_real, screen_imag = screen[..., :entries], screen[..., entries:]
    sigma_real = -(lattice_real * screen_imag + lattice_imag * screen_real)
    sigma_imag = lattice_real * screen_real - lattice_imag * screen_imag
    back_real = transform(cosine_table, sigma_real) - transform(sine_table, sigma_imag)
    back_imag = transform(cosine_table, sigma_imag) + transform(sine_table, sigma_real)
    return back_real, back_imag


def contract(self_real, self_imag, greens, weights):
    history, points, width = greens.shape
    entries = width // 2
    matrix_shape = (history, points, BANDS, BANDS)
    weighted_real = (self_real * weights[:, None, None]).reshape(matrix_shape)
    weighted_imag = (self_imag * weights[:, None, None]).reshape(matrix_shape)
    green_real = greens[..., :entries].reshape(matrix_shape)
    green_imag = greens[..., entries:].reshape(matrix_shape)
    highest = lax.Precision.HIGHEST
    out_real = -(jnp.einsum("tkab,tkcb->kac", weighted_real, green_real, precision=highest)
                 + jnp.einsum("tkab,tkcb->kac", weighted_imag, green_imag, precision=highest))
    out_imag = (jnp.einsum("tkab,tkcb->kac", weighted_real, green_imag, precision=highest)
                - jnp.einsum("tkab,tkcb->kac", weighted_imag, green_real, precision=highest))
    return jnp.concatenate([out_real.reshape(points, entries), out_imag.reshape(points, entries)], axis=1)


def propagate(greens, effective):
    history, points, width = greens.shape
    entries = width // 2
    matrix_shape = (history, points, BANDS, BANDS)
    green_real = greens[..., :entries].reshape(matrix_shape)
    green_imag = greens[..., entries:].reshape(matrix_shape)
    hamil_real = effective[:, :entries].reshape(points, BANDS, BANDS)
    hamil_imag = effective[:, entries:].reshape(points, BANDS, BANDS)
    highest = lax.Precision.HIGHEST
    prod_real = (jnp.einsum("kab,tkbc->tkac", hamil_real, green_real, precision=highest)
                 - jnp.einsum("kab,tkbc->tkac", hamil_imag, green_imag, precision=highest))
    prod_imag = (jnp.einsum("kab,tkbc->tkac", hamil_real, green_imag, precision=highest)
                 + jnp.einsum("kab,tkbc->tkac", hamil_imag, green_real, precision=highest))
    new_real = greens[..., :entries] + time_step * prod_imag.reshape(history, points, entries)
    new_imag = greens[..., entries:] - time_step * prod_real.reshape(history, points, entries)
    return jnp.concatenate([new_real, new_imag], axis=2)


def class_weights(quad_class):
    table = jnp.array(quadrature, jnp.float32)
    match = quad_class[:, None] == jnp.arange(4, dtype=jnp.int32)[None, :]
    return jnp.sum(jnp.where(match, table[None, :], jnp.float32(0.0)), axis=1)


def diagonal_mask(offset):
    width = 2 * BANDS * BANDS
    spots = offset + jnp.arange(BANDS, dtype=jnp.int32) * (BANDS + 1)
    return jnp.any(jnp.arange(width, dtype=jnp.int32)[:, None] == spots[None, :], axis=1).astype(jnp.float32)


def reference(green_row, screened, hamilton, equal_time, quad_class, live_count):
    points = SIDE * SIDE
    width = 2 * BANDS * BANDS
    cosine_table, sine_table = phase_tables(SIDE)
    position = jnp.arange(NT, dtype=jnp.int32)
    limits = live_count[position // TB]
    weights = jnp.where(position % TB < limits, time_step * class_weights(quad_class), jnp.float32(0.0))

    def collide(pieces):
        greens, screen, weight = pieces
        self_real, self_imag = self_energy(greens, screen, cosine_table, sine_table)
        return contract(self_real, self_imag, greens, weight)

    blocks = (green_row.reshape(N_HIST, TB, points, width), screened.reshape(N_HIST, TB, points, width),
              weights.reshape(N_HIST, TB))
    collision = jnp.sum(lax.map(collide, blocks), axis=0)
    density = jnp.sum(equal_time * diagonal_mask(BANDS * BANDS)[None, :]) / points
    effective = hamilton + collision + hubbard * density * diagonal_mask(0)[None, :]

    def advance(greens):
        return propagate(greens, effective)

    stepped = lax.map(advance, green_row.reshape(N_HIST, TB, points, width))
    return stepped.reshape(NT, points, width)
```

```python
import functools
import math

import jax
import jax.numpy as jnp
import ml_dtypes
import numpy as np
from jax import lax
from jax.experimental import pallas as pl
from jax.experimental.pallas import tpu as pltpu
from jax.sharding import PartitionSpec as P

SIDE = 24
BANDS = 8
ENTRIES = BANDS * BANDS
WIDTH = 2 * ENTRIES
TILE = 8

time_step = 0.1
hubbard = 1.0
quadrature = (0.375, 1.1666666, 0.9583333, 1.0)

VMEM_LIMIT = 48 * 1024 * 1024


def lane_sign(shape):
    lane = lax.broadcasted_iota(jnp.int32, shape, len(shape) - 1)
    return lane < ENTRIES


def swap(x):
    return pltpu.roll(x, ENTRIES, 1)


def dft24(x, sign, low):
    root3 = jnp.where(low, -1.0, 1.0) * (sign * math.sqrt(3.0) / 2)
    turn = jnp.where(low, -1.0, 1.0) * float(sign)
    half = math.sqrt(0.5)
    turn_half = turn * half
    columns = [[None] * 8 for _ in range(3)]
    for n2 in range(8):
        x0, x1, x2 = (x[(8 * n1 + 3 * n2) % 24] for n1 in range(3))
        total = x1 + x2
        base = x0 - 0.5 * total
        spin = swap(x1 - x2) * root3
        columns[0][n2] = x0 + total
        columns[1][n2] = base + spin
        columns[2][n2] = base - spin
    out = [None] * 24
    for k1 in range(3):
        c = columns[k1]
        a0, a1 = c[0] + c[4], c[0] - c[4]
        a2, a3 = c[2] + c[6], c[2] - c[6]
        a4, a5 = c[1] + c[5], c[1] - c[5]
        a6, a7 = c[3] + c[7], c[3] - c[7]
        b0, b1 = a0 + a2, a0 - a2
        b2, b3 = a4 + a6, a4 - a6
        i_a3 = swap(a3) * turn
        i_b3 = swap(b3) * turn
        c0, c1 = a1 + i_a3, a1 - i_a3
        p = (a5 - a7) * half
        m = swap(a5 + a7) * turn_half
        e, f = p + m, p - m
        values = [b0 + b2, c0 + e, b1 + i_b3, c1 - f, b0 - b2, c0 - e, b1 - i_b3, c1 + f]
        for k2 in range(8):
            out[(16 * k1 + 9 * k2) % 24] = values[k2]
    return out


def first_row(line, block):
    point = line * SIDE
    return (point // block) * (TILE * block) + point % block


def forward_kernel(block, green_ref, lattice_ref, work_ref):
    low = lane_sign((TILE, WIDTH))

    def along_second(k1, carry):
        start = first_row(k1, block)
        rows = [green_ref[pl.ds(start + k2, TILE, stride=block), :] for k2 in range(SIDE)]
        for r2, value in enumerate(dft24(rows, -1, low)):
            work_ref[k1 * SIDE + r2] = value
        return carry

    lax.fori_loop(0, SIDE, along_second, 0)

    def along_first(r2, carry):
        rows = [work_ref[k1 * SIDE + r2] for k1 in range(SIDE)]
        for r1, value in enumerate(dft24(rows, -1, low)):
            lattice_ref[r1 * SIDE + r2] = value
        return carry

    lax.fori_loop(0, SIDE, along_first, 0)


def backward_kernel(
    block, share, lattice_ref, screen_ref, green_ref, weight_ref, equal_ref, gather_ref,
    partial_ref, work_ref, sigma_ref, sums_ref,
):
    points = SIDE * SIDE
    low = lane_sign((TILE, WIDTH))
    turn = jnp.where(low, -1.0, 1.0)
    weights = weight_ref[...]

    def along_second(r1, carry):
        start = first_row(r1, block)
        rows = []
        for r2 in range(SIDE):
            screen = screen_ref[pl.ds(start + r2, TILE, stride=block), :] * weights
            other = swap(screen)
            lattice = lattice_ref[r1 * SIDE + r2]
            rows.append(
                swap(lattice) * turn * jnp.where(low, screen, other)
                - lattice * jnp.where(low, other, screen)
            )
        for k2, value in enumerate(dft24(rows, 1, low)):
            work_ref[r1 * SIDE + k2] = value
        return carry

    lax.fori_loop(0, SIDE, along_second, 0)

    def along_first(k2, carry):
        rows = [work_ref[r1 * SIDE + k2] for r1 in range(SIDE)]
        for k1, value in enumerate(dft24(rows, 1, low)):
            sigma_ref[pl.ds(k1 * SIDE + k2, TILE, stride=points), :] = value
        return carry

    lax.fori_loop(0, SIDE, along_first, 0)

    tiles = block // TILE

    def contract(tile, carry):
        base = (tile // tiles) * (TILE * block) + (tile % tiles) * TILE
        sums = [None] * (2 * BANDS)
        for s in range(TILE):
            sigma = sigma_ref[pl.ds(pl.multiple_of(s * points + tile * TILE, TILE), TILE), :]
            green = green_ref[pl.ds(pl.multiple_of(base + s * block, TILE), TILE), :]
            other = swap(green)
            parts = (jnp.where(low, green, other), jnp.where(low, other, green))
            for d in range(BANDS):
                for h in range(2):
                    part = parts[h] if d == 0 else pltpu.roll(parts[h], WIDTH - BANDS * d, 1)
                    term = sigma * part
                    spot = 2 * d + h
                    sums[spot] = term if s == 0 else sums[spot] + term
        row = pl.ds(pl.multiple_of(tile * TILE, TILE), TILE)
        for spot, value in enumerate(sums):
            sums_ref[row, spot * WIDTH : (spot + 1) * WIDTH] = value
        return carry

    lax.fori_loop(0, points // TILE, contract, 0)

    lane = lax.broadcasted_iota(jnp.int32, equal_ref.shape, 1)
    inner = lane - ENTRIES
    occupied = jnp.sum(jnp.where((inner >= 0) & (inner % (BANDS + 1) == 0), equal_ref[...], 0.0))
    spots = lax.broadcasted_iota(jnp.int32, (points, WIDTH), 1)
    on_diagonal = (spots < ENTRIES) & (spots % (BANDS + 1) == 0)
    sums = sums_ref[...]
    coarse = sums.astype(jnp.bfloat16)
    fine = (sums - coarse.astype(jnp.float32)).astype(jnp.bfloat16)
    gather = gather_ref[...]
    total = jnp.dot(coarse, gather, preferred_element_type=jnp.float32)
    total = total + jnp.dot(fine, gather, preferred_element_type=jnp.float32)
    partial_ref[...] = total + jnp.where(on_diagonal, occupied * share, 0.0)


def propagate_kernel(green_ref, effective_ref, spread_ref, out_ref, factor_ref):
    history, points, _ = green_ref.shape

    @pl.when(pl.program_id(0) == 0)
    def _():
        rest = effective_ref[...] * time_step
        total = None
        for _ in range(3):
            piece = rest.astype(jnp.bfloat16)
            rest = rest - piece.astype(jnp.float32)
            term = jnp.dot(piece, spread_ref[...], preferred_element_type=jnp.float32)
            total = term if total is None else total + term
        factor_ref[...] = total

    for start in range(0, points, TILE):
        stop = min(start + TILE, points)
        low = lane_sign((stop - start, WIDTH))
        factors = [
            factor_ref[start:stop, spot * WIDTH : (spot + 1) * WIDTH] for spot in range(2 * BANDS)
        ]

        def step(s, carry):
            green = green_ref[s, start:stop, :]
            other = swap(green)
            parts = (jnp.where(low, green, other), jnp.where(low, other, green))
            total = green
            for d in range(BANDS):
                for h in range(2):
                    part = parts[h] if d == 0 else pltpu.roll(parts[h], WIDTH - BANDS * d, 1)
                    total = total + factors[2 * d + h] * part
            out_ref[s, start:stop, :] = total
            return carry

        lax.fori_loop(0, history, step, 0, unroll=True)


def gather_table():
    table = np.zeros((2 * BANDS, 2, BANDS, BANDS, 2, BANDS, BANDS), np.float32)
    for d in range(BANDS):
        for a in range(BANDS):
            c = (a + d) % BANDS
            table[2 * d, 0, a, :, 0, a, c] = -1
            table[2 * d, 1, a, :, 1, a, c] = -1
            table[2 * d + 1, 0, a, :, 1, a, c] = 1
            table[2 * d + 1, 1, a, :, 0, a, c] = -1
    return table.reshape(2 * BANDS * WIDTH, WIDTH).astype(ml_dtypes.bfloat16)


def spread_table():
    table = np.zeros((2, BANDS, BANDS, 2 * BANDS, 2, BANDS, BANDS), np.float32)
    for d in range(BANDS):
        for a in range(BANDS):
            b = (a + d) % BANDS
            table[1, a, b, 2 * d, 0, a, :] = 1
            table[0, a, b, 2 * d, 1, a, :] = -1
            table[0, a, b, 2 * d + 1, 0, a, :] = 1
            table[1, a, b, 2 * d + 1, 1, a, :] = 1
    return table.reshape(WIDTH, 2 * BANDS * WIDTH).astype(ml_dtypes.bfloat16)


def forward(green, block):
    points = SIDE * SIDE
    return pl.pallas_call(
        functools.partial(forward_kernel, block),
        out_shape=jax.ShapeDtypeStruct((points, TILE, WIDTH), jnp.float32),
        scratch_shapes=[pltpu.VMEM((points, TILE, WIDTH), jnp.float32)],
        compiler_params=pltpu.CompilerParams(vmem_limit_bytes=VMEM_LIMIT),
        cost_estimate=pl.CostEstimate(
            flops=400 * points * TILE * WIDTH, bytes_accessed=8 * points * TILE * WIDTH, transcendentals=0
        ),
        name="forward",
    )(green)


def backward(lattice, screen, green, weights, equal_time, block, share):
    points = SIDE * SIDE
    return pl.pallas_call(
        functools.partial(backward_kernel, block, share),
        out_shape=jax.ShapeDtypeStruct((points, WIDTH), jnp.float32),
        scratch_shapes=[
            pltpu.VMEM((points, TILE, WIDTH), jnp.float32),
            pltpu.VMEM((TILE * points, WIDTH), jnp.float32),
            pltpu.VMEM((points, 2 * BANDS * WIDTH), jnp.float32),
        ],
        compiler_params=pltpu.CompilerParams(vmem_limit_bytes=VMEM_LIMIT),
        cost_estimate=pl.CostEstimate(
            flops=800 * points * TILE * WIDTH, bytes_accessed=12 * points * TILE * WIDTH, transcendentals=0
        ),
        name="backward",
    )(lattice, screen, green, weights, equal_time, jnp.asarray(gather_table()))


def propagate(greens, effective):
    history, points, width = greens.shape
    step = math.gcd(history, TILE)
    chunk = pl.BlockSpec((step, points, width), lambda i: (i, 0, 0))
    spread = spread_table()
    return pl.pallas_call(
        propagate_kernel,
        grid=(history // step,),
        out_shape=jax.ShapeDtypeStruct(greens.shape, jnp.float32),
        in_specs=[
            chunk,
            pl.BlockSpec((points, width), lambda i: (0, 0)),
            pl.BlockSpec(spread.shape, lambda i: (0, 0)),
        ],
        out_specs=chunk,
        scratch_shapes=[pltpu.VMEM((points, spread.shape[1]), jnp.float32)],
        compiler_params=pltpu.CompilerParams(vmem_limit_bytes=VMEM_LIMIT),
        cost_estimate=pl.CostEstimate(
            flops=32 * greens.size, bytes_accessed=8 * greens.size, transcendentals=0
        ),
        name="propagate",
    )(greens, effective, jnp.asarray(spread))


def class_weights(quad_class):
    table = jnp.array(quadrature, jnp.float32)
    match = quad_class[:, None] == jnp.arange(4, dtype=jnp.int32)[None, :]
    return jnp.sum(jnp.where(match, table[None, :], jnp.float32(0.0)), axis=1)


def per_device(parts, blocks, green_row, screened, hamilton, equal_time, quad_class, live_count):
    history, local, width = green_row.shape
    points = local * parts
    times = history // parts
    moved = [
        lax.all_to_all(x, "ka", split_axis=0, concat_axis=0, tiled=True)
        for x in (green_row, screened)
    ]
    position = jnp.arange(history, dtype=jnp.int32)
    weights = jnp.where(
        position < live_count[0], time_step * class_weights(quad_class), jnp.float32(0.0)
    ) * jnp.float32(1.0 / points)
    weights = lax.dynamic_slice_in_dim(weights, lax.axis_index("ka") * times, times)

    groups = -(-times // TILE)
    if times == TILE and local % SIDE == 0:
        block = local
        moved = [[x.reshape(-1, width)] for x in moved]
    else:
        block = points
        padding = groups * TILE - times
        moved = [
            jnp.pad(
                x.reshape(parts, times, local, width).transpose(1, 0, 2, 3).reshape(times, points, width),
                ((0, padding), (0, 0), (0, 0)),
            ).reshape(groups, TILE * points, width)
            for x in moved
        ]
        weights = jnp.pad(weights, (0, padding))
    weights = jnp.broadcast_to(weights.reshape(groups, TILE, 1), (groups, TILE, width))

    partial_value = None
    for group in range(groups):
        green, screen = moved[0][group], moved[1][group]
        lattice = forward(green, block)
        share = hubbard / (points * blocks) if group == 0 else 0.0
        term = backward(lattice, screen, green, weights[group], equal_time, block, share)
        partial_value = term if partial_value is None else partial_value + term

    collision = lax.psum_scatter(partial_value, "ka", scatter_dimension=0, tiled=True)
    collision = lax.psum(collision, "hist")
    return propagate(green_row, hamilton + collision)


def solution(mesh):
    in_specs = (
        P("hist", "ka", None),
        P("hist", "ka", None),
        P("ka", None),
        P("ka", None),
        P("hist"),
        P("hist"),
    )
    out_specs = P("hist", "ka", None)
    return jax.shard_map(
        functools.partial(per_device, mesh.shape["ka"], mesh.shape["hist"]),
        mesh=mesh,
        in_specs=in_specs,
        out_specs=out_specs,
        check_vma=False,
    )
```

```python
import functools
import math

import jax
import jax.numpy as jnp
import ml_dtypes
import numpy as np
from jax import lax
from jax.experimental import pallas as pl
from jax.experimental.pallas import tpu as pltpu
from jax.sharding import PartitionSpec as P

SIDE = 24
BANDS = 8
ENTRIES = BANDS * BANDS
WIDTH = 2 * ENTRIES
TILE = 8

time_step = 0.1
hubbard = 1.0
quadrature = (0.375, 1.1666666, 0.9583333, 1.0)

VMEM_LIMIT = 48 * 1024 * 1024


def lane_sign(shape):
    lane = lax.broadcasted_iota(jnp.int32, shape, len(shape) - 1)
    return lane < ENTRIES


def swap(x):
    return pltpu.roll(x, ENTRIES, 1)


def tree_sum(terms):
    while len(terms) > 1:
        terms = [sum(terms[i : i + 2][1:], terms[i]) for i in range(0, len(terms), 2)]
    return terms[0]


def dft24(x, sign, low):
    root3 = jnp.where(low, -1.0, 1.0) * (sign * math.sqrt(3.0) / 2)
    turn = jnp.where(low, -1.0, 1.0) * float(sign)
    half = math.sqrt(0.5)
    turn_half = turn * half
    columns = [[None] * 8 for _ in range(3)]
    for n2 in range(8):
        x0, x1, x2 = (x[(8 * n1 + 3 * n2) % 24] for n1 in range(3))
        total = x1 + x2
        base = x0 - 0.5 * total
        spin = swap(x1 - x2) * root3
        columns[0][n2] = x0 + total
        columns[1][n2] = base + spin
        columns[2][n2] = base - spin
    out = [None] * 24
    for k1 in range(3):
        c = columns[k1]
        a0, a1 = c[0] + c[4], c[0] - c[4]
        a2, a3 = c[2] + c[6], c[2] - c[6]
        a4, a5 = c[1] + c[5], c[1] - c[5]
        a6, a7 = c[3] + c[7], c[3] - c[7]
        b0, b1 = a0 + a2, a0 - a2
        b2, b3 = a4 + a6, a4 - a6
        i_a3 = swap(a3) * turn
        i_b3 = swap(b3) * turn
        c0, c1 = a1 + i_a3, a1 - i_a3
        p = (a5 - a7) * half
        m = swap(a5 + a7) * turn_half
        e, f = p + m, p - m
        values = [b0 + b2, c0 + e, b1 + i_b3, c1 - f, b0 - b2, c0 - e, b1 - i_b3, c1 + f]
        for k2 in range(8):
            out[(16 * k1 + 9 * k2) % 24] = values[k2]
    return out


def first_row(line, block):
    point = line * SIDE
    return (point // block) * (TILE * block) + point % block


def forward_kernel(block, green_ref, lattice_ref, work_ref):
    low = lane_sign((TILE, WIDTH))

    def along_second(k1, carry):
        start = first_row(k1, block)
        rows = [green_ref[pl.ds(start + k2, TILE, stride=block), :] for k2 in range(SIDE)]
        for r2, value in enumerate(dft24(rows, -1, low)):
            work_ref[k1 * SIDE + r2] = value
        return carry

    lax.fori_loop(0, SIDE, along_second, 0)

    def along_first(r2, carry):
        rows = [work_ref[k1 * SIDE + r2] for k1 in range(SIDE)]
        for r1, value in enumerate(dft24(rows, -1, low)):
            lattice_ref[r1 * SIDE + r2] = value
        return carry

    lax.fori_loop(0, SIDE, along_first, 0)


def backward_kernel(
    block, share, place_ref, lattice_ref, screen_ref, green_ref, weight_ref, equal_ref, gather_ref, *rest
):
    *partial_refs, work_ref, sigma_ref, sums_ref = rest
    points = SIDE * SIDE
    low = lane_sign((TILE, WIDTH))
    turn = jnp.where(low, -1.0, 1.0)
    weights = weight_ref[...]

    def along_second(r1, carry):
        start = first_row(r1, block)
        rows = []
        for r2 in range(SIDE):
            screen = screen_ref[pl.ds(start + r2, TILE, stride=block), :] * weights
            other = swap(screen)
            lattice = lattice_ref[r1 * SIDE + r2]
            rows.append(
                swap(lattice) * turn * jnp.where(low, screen, other)
                - lattice * jnp.where(low, other, screen)
            )
        for k2, value in enumerate(dft24(rows, 1, low)):
            work_ref[r1 * SIDE + k2] = value
        return carry

    lax.fori_loop(0, SIDE, along_second, 0)

    def along_first(k2, carry):
        rows = [work_ref[r1 * SIDE + k2] for r1 in range(SIDE)]
        for k1, value in enumerate(dft24(rows, 1, low)):
            sigma_ref[pl.ds(k1 * SIDE + k2, TILE, stride=points), :] = value
        return carry

    lax.fori_loop(0, SIDE, along_first, 0)

    tiles = block // TILE

    def contract(tile, carry):
        base = (tile // tiles) * (TILE * block) + (tile % tiles) * TILE
        sigma, parts = [], []
        for s in range(TILE):
            sigma.append(sigma_ref[pl.ds(pl.multiple_of(s * points + tile * TILE, TILE), TILE), :])
            green = green_ref[pl.ds(pl.multiple_of(base + s * block, TILE), TILE), :]
            other = swap(green)
            parts.append((jnp.where(low, green, other), jnp.where(low, other, green)))
        row = pl.ds(pl.multiple_of(tile * TILE, TILE), TILE)
        for d in range(BANDS):
            for h in range(2):
                terms = [
                    sigma[s] * (parts[s][h] if d == 0 else pltpu.roll(parts[s][h], WIDTH - BANDS * d, 1))
                    for s in range(TILE)
                ]
                spot = 2 * d + h
                sums_ref[row, spot * WIDTH : (spot + 1) * WIDTH] = tree_sum(terms)
        return carry

    lax.fori_loop(0, points // TILE, contract, 0)

    lane = lax.broadcasted_iota(jnp.int32, equal_ref.shape, 1)
    inner = lane - ENTRIES
    occupied = jnp.sum(jnp.where((inner >= 0) & (inner % (BANDS + 1) == 0), equal_ref[...], 0.0))
    spots = lax.broadcasted_iota(jnp.int32, (points, WIDTH), 1)
    on_diagonal = (spots < ENTRIES) & (spots % (BANDS + 1) == 0)
    sums = sums_ref[...]
    coarse = sums.astype(jnp.bfloat16)
    fine = (sums - coarse.astype(jnp.float32)).astype(jnp.bfloat16)
    gather = gather_ref[...]
    total = jnp.dot(coarse, gather, preferred_element_type=jnp.float32)
    total = total + jnp.dot(fine, gather, preferred_element_type=jnp.float32)
    sigma_ref[:points, :] = total + jnp.where(on_diagonal, occupied * share, 0.0)
    local = partial_refs[0].shape[0]
    for step, partial_ref in enumerate(partial_refs):
        owner = partner_of(place_ref[0], step, len(partial_refs))
        partial_ref[...] = sigma_ref[pl.ds(owner * local, local), :]


def propagate_kernel(green_ref, effective_ref, spread_ref, out_ref, factor_ref):
    history, points, _ = green_ref.shape

    @pl.when(pl.program_id(0) == 0)
    def _():
        rest = effective_ref[...] * time_step
        total = None
        for _ in range(3):
            piece = rest.astype(jnp.bfloat16)
            rest = rest - piece.astype(jnp.float32)
            term = jnp.dot(piece, spread_ref[...], preferred_element_type=jnp.float32)
            total = term if total is None else total + term
        factor_ref[...] = total

    def advance(start, stop):
        low = lane_sign((history, stop - start, WIDTH))
        green = green_ref[:, start:stop, :]
        other = pltpu.roll(green, ENTRIES, 2)
        parts = (jnp.where(low, green, other), jnp.where(low, other, green))
        terms = [green]
        for d in range(BANDS):
            for h in range(2):
                spot = 2 * d + h
                factor = factor_ref[start:stop, spot * WIDTH : (spot + 1) * WIDTH]
                part = parts[h] if d == 0 else pltpu.roll(parts[h], WIDTH - BANDS * d, 2)
                terms.append(factor[None] * part)
                if len(terms) == 4:
                    terms = [tree_sum(terms)]
        out_ref[:, start:stop, :] = tree_sum(terms)

    for start in range(0, points, 2 * TILE):
        advance(start, min(start + 2 * TILE, points))


def gather_table():
    table = np.zeros((2 * BANDS, 2, BANDS, BANDS, 2, BANDS, BANDS), np.float32)
    for d in range(BANDS):
        for a in range(BANDS):
            c = (a + d) % BANDS
            table[2 * d, 0, a, :, 0, a, c] = -1
            table[2 * d, 1, a, :, 1, a, c] = -1
            table[2 * d + 1, 0, a, :, 1, a, c] = 1
            table[2 * d + 1, 1, a, :, 0, a, c] = -1
    return table.reshape(2 * BANDS * WIDTH, WIDTH).astype(ml_dtypes.bfloat16)


def spread_table():
    table = np.zeros((2, BANDS, BANDS, 2 * BANDS, 2, BANDS, BANDS), np.float32)
    for d in range(BANDS):
        for a in range(BANDS):
            b = (a + d) % BANDS
            table[1, a, b, 2 * d, 0, a, :] = 1
            table[0, a, b, 2 * d, 1, a, :] = -1
            table[0, a, b, 2 * d + 1, 0, a, :] = 1
            table[1, a, b, 2 * d + 1, 1, a, :] = 1
    return table.reshape(WIDTH, 2 * BANDS * WIDTH).astype(ml_dtypes.bfloat16)


def forward(green, block):
    points = SIDE * SIDE
    return pl.pallas_call(
        functools.partial(forward_kernel, block),
        out_shape=jax.ShapeDtypeStruct((points, TILE, WIDTH), jnp.float32),
        scratch_shapes=[pltpu.VMEM((points, TILE, WIDTH), jnp.float32)],
        compiler_params=pltpu.CompilerParams(vmem_limit_bytes=VMEM_LIMIT),
        cost_estimate=pl.CostEstimate(
            flops=400 * points * TILE * WIDTH, bytes_accessed=8 * points * TILE * WIDTH, transcendentals=0
        ),
        name="forward",
    )(green)


def backward(place, lattice, screen, green, weights, equal_time, block, share, parts):
    points = SIDE * SIDE
    whole = pl.BlockSpec(memory_space=pltpu.VMEM)
    return pl.pallas_call(
        functools.partial(backward_kernel, block, share),
        out_shape=[jax.ShapeDtypeStruct((points // parts, WIDTH), jnp.float32)] * parts,
        in_specs=[pl.BlockSpec(memory_space=pltpu.SMEM)] + [whole] * 6,
        out_specs=[whole] * parts,
        scratch_shapes=[
            pltpu.VMEM((points, TILE, WIDTH), jnp.float32),
            pltpu.VMEM((TILE * points, WIDTH), jnp.float32),
            pltpu.VMEM((points, 2 * BANDS * WIDTH), jnp.float32),
        ],
        compiler_params=pltpu.CompilerParams(vmem_limit_bytes=VMEM_LIMIT),
        cost_estimate=pl.CostEstimate(
            flops=800 * points * TILE * WIDTH, bytes_accessed=12 * points * TILE * WIDTH, transcendentals=0
        ),
        name="backward",
    )(place, lattice, screen, green, weights, equal_time, jnp.asarray(gather_table()))


def propagate(greens, effective):
    history, points, width = greens.shape
    step = math.gcd(history, TILE)
    chunk = pl.BlockSpec((step, points, width), lambda i: (i, 0, 0))
    spread = spread_table()
    return pl.pallas_call(
        propagate_kernel,
        grid=(history // step,),
        out_shape=jax.ShapeDtypeStruct(greens.shape, jnp.float32),
        in_specs=[
            chunk,
            pl.BlockSpec((points, width), lambda i: (0, 0)),
            pl.BlockSpec(spread.shape, lambda i: (0, 0)),
        ],
        out_specs=chunk,
        scratch_shapes=[pltpu.VMEM((points, spread.shape[1]), jnp.float32)],
        compiler_params=pltpu.CompilerParams(vmem_limit_bytes=VMEM_LIMIT),
        cost_estimate=pl.CostEstimate(
            flops=32 * greens.size, bytes_accessed=8 * greens.size, transcendentals=0
        ),
        name="propagate",
    )(greens, effective, jnp.asarray(spread))


def partner_of(place, step, count):
    if count & (count - 1) == 0:
        return place ^ step
    return (place + step) % count


def exchange(value, axis, step, count):
    pairs = [(place, partner_of(place, step, count)) for place in range(count)]
    return lax.ppermute(value, axis, pairs)


def class_weights(quad_class):
    table = jnp.array(quadrature, jnp.float32)
    match = quad_class[:, None] == jnp.arange(4, dtype=jnp.int32)[None, :]
    return jnp.sum(jnp.where(match, table[None, :], jnp.float32(0.0)), axis=1)


def per_device(parts, blocks, green_row, screened, hamilton, equal_time, quad_class, live_count):
    history, local, width = green_row.shape
    points = local * parts
    times = history // parts
    moved = [
        lax.all_to_all(x, "ka", split_axis=0, concat_axis=0, tiled=True)
        for x in (green_row, screened)
    ]
    position = jnp.arange(history, dtype=jnp.int32)
    weights = jnp.where(
        position < live_count[0], time_step * class_weights(quad_class), jnp.float32(0.0)
    ) * jnp.float32(1.0 / points)
    weights = lax.dynamic_slice_in_dim(weights, lax.axis_index("ka") * times, times)

    groups = -(-times // TILE)
    if times == TILE and local % SIDE == 0:
        block = local
        moved = [[x.reshape(-1, width)] for x in moved]
    else:
        block = points
        padding = groups * TILE - times
        moved = [
            jnp.pad(
                x.reshape(parts, times, local, width).transpose(1, 0, 2, 3).reshape(times, points, width),
                ((0, padding), (0, 0), (0, 0)),
            ).reshape(groups, TILE * points, width)
            for x in moved
        ]
        weights = jnp.pad(weights, (0, padding))
    weights = jnp.broadcast_to(weights.reshape(groups, TILE, 1), (groups, TILE, width))

    place = lax.axis_index("ka")
    pieces = None
    for group in range(groups):
        green, screen = moved[0][group], moved[1][group]
        lattice = forward(green, block)
        share = hubbard / (points * blocks) if group == 0 else 0.0
        terms = backward(
            place.reshape(1), lattice, screen, green, weights[group], equal_time, block, share, parts
        )
        pieces = list(terms) if pieces is None else [a + b for a, b in zip(pieces, terms)]

    partial_value = tree_sum(
        pieces[:1] + [exchange(pieces[step], "ka", step, parts) for step in range(1, parts)]
    )
    collision = tree_sum(
        [partial_value] + [exchange(partial_value, "hist", step, blocks) for step in range(1, blocks)]
    )
    return propagate(green_row, hamilton + collision)


def solution(mesh):
    in_specs = (
        P("hist", "ka", None),
        P("hist", "ka", None),
        P("ka", None),
        P("ka", None),
        P("hist"),
        P("hist"),
    )
    out_specs = P("hist", "ka", None)
    return jax.shard_map(
        functools.partial(per_device, mesh.shape["ka"], mesh.shape["hist"]),
        mesh=mesh,
        in_specs=in_specs,
        out_specs=out_specs,
        check_vma=False,
    )
```

```python
import functools
import math

import jax
import jax.numpy as jnp
import ml_dtypes
import numpy as np
from jax import lax
from jax.experimental import pallas as pl
from jax.experimental.pallas import tpu as pltpu
from jax.sharding import PartitionSpec as P

SIDE = 24
BANDS = 8
ENTRIES = BANDS * BANDS
WIDTH = 2 * ENTRIES
TILE = 8
STEPS = 4

time_step = 0.1
hubbard = 1.0
quadrature = (0.375, 1.1666666, 0.9583333, 1.0)

VMEM_LIMIT = 48 * 1024 * 1024


def lane_sign(shape):
    lane = lax.broadcasted_iota(jnp.int32, shape, len(shape) - 1)
    return lane < ENTRIES


def swap(x):
    return pltpu.roll(x, ENTRIES, 1)


def roll_blocks(x, blocks):
    return x if blocks == 0 else pltpu.roll(x, WIDTH - BANDS * blocks, x.ndim - 1)


def tree_sum(terms):
    while len(terms) > 1:
        terms = [sum(terms[i : i + 2][1:], terms[i]) for i in range(0, len(terms), 2)]
    return terms[0]


def dft24(x, sign, low):
    root3 = jnp.where(low, -1.0, 1.0) * (sign * math.sqrt(3.0) / 2)
    turn = jnp.where(low, -1.0, 1.0) * float(sign)
    half = math.sqrt(0.5)
    turn_half = turn * half
    columns = [[None] * 8 for _ in range(3)]
    for n2 in range(8):
        x0, x1, x2 = (x[(8 * n1 + 3 * n2) % 24] for n1 in range(3))
        total = x1 + x2
        base = x0 - 0.5 * total
        spin = swap(x1 - x2) * root3
        columns[0][n2] = x0 + total
        columns[1][n2] = base + spin
        columns[2][n2] = base - spin
    out = [None] * 24
    for k1 in range(3):
        c = columns[k1]
        a0, a1 = c[0] + c[4], c[0] - c[4]
        a2, a3 = c[2] + c[6], c[2] - c[6]
        a4, a5 = c[1] + c[5], c[1] - c[5]
        a6, a7 = c[3] + c[7], c[3] - c[7]
        b0, b1 = a0 + a2, a0 - a2
        b2, b3 = a4 + a6, a4 - a6
        i_a3 = swap(a3) * turn
        i_b3 = swap(b3) * turn
        c0, c1 = a1 + i_a3, a1 - i_a3
        p = (a5 - a7) * half
        m = swap(a5 + a7) * turn_half
        e, f = p + m, p - m
        values = [b0 + b2, c0 + e, b1 + i_b3, c1 - f, b0 - b2, c0 - e, b1 - i_b3, c1 + f]
        for k2 in range(8):
            out[(16 * k1 + 9 * k2) % 24] = values[k2]
    return out


def line_of(place, step, ref, count):
    lines = ref.shape[0] // (TILE * SIDE)
    return partner_of(place, step, count) * lines if count > 1 else 0


def load_line(ref, line):
    stride = ref.shape[0] // TILE
    return [ref[pl.ds(line * SIDE + k2, TILE, stride=stride), :] for k2 in range(SIDE)]


def along_first(work_ref, sign, low, out_ref):
    def columns(pair, carry):
        for column in (2 * pair, 2 * pair + 1):
            rows = [work_ref[k1 * SIDE + column] for k1 in range(SIDE)]
            for r1, value in enumerate(dft24(rows, sign, low)):
                out_ref[r1 * SIDE + column] = value
        return carry

    lax.fori_loop(0, SIDE // 2, columns, 0)


def forward_kernel(count, place_ref, *refs):
    green_refs, (lattice_ref, work_ref) = refs[:count], refs[count:]
    low = lane_sign((TILE, WIDTH))
    place = place_ref[0]
    for step, green_ref in enumerate(green_refs):
        first = line_of(place, step, green_ref, count)
        lines = green_ref.shape[0] // (TILE * SIDE)

        def along_second(i, carry):
            for r2, value in enumerate(dft24(load_line(green_ref, i), -1, low)):
                work_ref[(first + i) * SIDE + r2] = value
            return carry

        lax.fori_loop(0, lines, along_second, 0, unroll=lines <= 4)
    along_first(work_ref, -1, low, lattice_ref)


def backward_kernel(count, share, place_ref, lattice_ref, weight_ref, equal_ref, gather_ref, *refs):
    screen_refs, green_refs, partial_refs = refs[:count], refs[count : 2 * count], refs[2 * count : -3]
    work_ref, sigma_ref, sums_ref = refs[-3:]
    points = SIDE * SIDE
    low = lane_sign((TILE, WIDTH))
    turn = jnp.where(low, -1.0, 1.0)
    weights = weight_ref[...]
    place = place_ref[0]

    for step, screen_ref in enumerate(screen_refs):
        first = line_of(place, step, screen_ref, count)
        lines = screen_ref.shape[0] // (TILE * SIDE)

        def along_second(i, carry):
            rows = []
            for r2, value in enumerate(load_line(screen_ref, i)):
                screen = value * weights
                other = swap(screen)
                lattice = lattice_ref[(first + i) * SIDE + r2]
                rows.append(
                    swap(lattice) * turn * jnp.where(low, screen, other)
                    - lattice * jnp.where(low, other, screen)
                )
            for k2, value in enumerate(dft24(rows, 1, low)):
                work_ref[(first + i) * SIDE + k2] = value
            return carry

        lax.fori_loop(0, lines, along_second, 0, unroll=lines <= 4)
    sigma_at = sigma_ref.reshape(points, TILE, WIDTH)
    along_first(work_ref, 1, low, sigma_at)

    for step, green_ref in enumerate(green_refs):
        first = line_of(place, step, green_ref, count) * SIDE
        block = green_ref.shape[0] // TILE

        def contract(tile, carry):
            start = (first + tile * TILE) * TILE
            sums = [None] * (STEPS * STEPS)
            for s in range(TILE):
                sigma = sigma_ref[pl.ds(start + s, TILE, stride=TILE), :]
                green = green_ref[pl.ds(pl.multiple_of(s * block + tile * TILE, TILE), TILE), :]
                sigmas = [roll_blocks(sigma, STEPS * i) for i in range(STEPS)]
                greens = [roll_blocks(green, j) for j in range(STEPS)]
                for i in range(STEPS):
                    for j in range(STEPS):
                        term = sigmas[i] * greens[j]
                        spot = STEPS * i + j
                        sums[spot] = term if s == 0 else sums[spot] + term
            row = pl.ds(pl.multiple_of(step * block + tile * TILE, TILE), TILE)
            for spot, value in enumerate(sums):
                sums_ref[row, spot * WIDTH : (spot + 1) * WIDTH] = value
            return carry

        lax.fori_loop(0, block // TILE, contract, 0)

    lane = lax.broadcasted_iota(jnp.int32, equal_ref.shape, 1)
    inner = lane - ENTRIES
    occupied = jnp.sum(jnp.where((inner >= 0) & (inner % (BANDS + 1) == 0), equal_ref[...], 0.0))
    spots = lax.broadcasted_iota(jnp.int32, (points, WIDTH), 1)
    on_diagonal = (spots < ENTRIES) & (spots % (BANDS + 1) == 0)
    sums = sums_ref[...]
    coarse = sums.astype(jnp.bfloat16)
    fine = (sums - coarse.astype(jnp.float32)).astype(jnp.bfloat16)
    gather = gather_ref[...]
    total = jnp.dot(coarse, gather, preferred_element_type=jnp.float32)
    total = total + jnp.dot(fine, gather, preferred_element_type=jnp.float32)
    total = total + jnp.where(on_diagonal, occupied * share, 0.0)
    parts = len(partial_refs)
    local = points // parts
    if count == parts:
        for step, partial_ref in enumerate(partial_refs):
            partial_ref[...] = total[step * local : (step + 1) * local]
    else:
        sigma_ref[:points, :] = total
        for step, partial_ref in enumerate(partial_refs):
            owner = partner_of(place, step, parts)
            partial_ref[...] = sigma_ref[pl.ds(owner * local, local), :]


def propagate_kernel(green_ref, effective_ref, spread_ref, out_ref, factor_ref):
    history, points, _ = green_ref.shape

    @pl.when(pl.program_id(0) == 0)
    def _():
        rest = effective_ref[...] * time_step
        total = None
        for _ in range(3):
            piece = rest.astype(jnp.bfloat16)
            rest = rest - piece.astype(jnp.float32)
            term = jnp.dot(piece, spread_ref[...], preferred_element_type=jnp.float32)
            total = term if total is None else total + term
        factor_ref[...] = total

    def advance(start, stop):
        green = green_ref[:, start:stop, :]
        greens = [roll_blocks(green, j) for j in range(STEPS)]
        terms = [green]
        for i in range(STEPS):
            total = None
            for j in range(STEPS):
                spot = STEPS * i + j
                factor = factor_ref[start:stop, spot * WIDTH : (spot + 1) * WIDTH]
                term = factor[None] * greens[j]
                total = term if total is None else total + term
            terms.append(roll_blocks(total, STEPS * i))
        out_ref[:, start:stop, :] = tree_sum(terms)

    for start in range(0, points, 2 * TILE):
        advance(start, min(start + 2 * TILE, points))


def gather_table():
    blocks = 2 * BANDS
    table = np.zeros((STEPS, STEPS, blocks, BANDS, 2, BANDS, BANDS), np.float32)
    for i in range(STEPS):
        for j in range(STEPS):
            for p in range(blocks):
                h, a = divmod((p + STEPS * i) % blocks, BANDS)
                g, c = divmod((p + j) % blocks, BANDS)
                table[i, j, p, :, h ^ g, a, c] = 1 if (h, g) == (0, 1) else -1
    return table.reshape(-1, WIDTH).astype(ml_dtypes.bfloat16)


def spread_table():
    blocks = 2 * BANDS
    table = np.zeros((2, BANDS, BANDS, STEPS, STEPS, blocks, BANDS), np.float32)
    for i in range(STEPS):
        for j in range(STEPS):
            for p in range(blocks):
                h, a = divmod((p - STEPS * i) % blocks, BANDS)
                g, b = divmod((p + j) % blocks, BANDS)
                table[1 if h == g else 0, a, b, i, j, p, :] = -1 if (h, g) == (1, 0) else 1
    return table.reshape(WIDTH, -1).astype(ml_dtypes.bfloat16)


def forward(place, greens):
    points = SIDE * SIDE
    whole = pl.BlockSpec(memory_space=pltpu.VMEM)
    return pl.pallas_call(
        functools.partial(forward_kernel, len(greens)),
        out_shape=jax.ShapeDtypeStruct((points, TILE, WIDTH), jnp.float32),
        in_specs=[pl.BlockSpec(memory_space=pltpu.SMEM)] + [whole] * len(greens),
        out_specs=whole,
        scratch_shapes=[pltpu.VMEM((points, TILE, WIDTH), jnp.float32)],
        compiler_params=pltpu.CompilerParams(vmem_limit_bytes=VMEM_LIMIT),
        cost_estimate=pl.CostEstimate(
            flops=400 * points * TILE * WIDTH, bytes_accessed=8 * points * TILE * WIDTH, transcendentals=0
        ),
        name="forward",
    )(place, *greens)


def backward(place, lattice, screens, greens, weights, equal_time, share, parts):
    points = SIDE * SIDE
    whole = pl.BlockSpec(memory_space=pltpu.VMEM)
    return pl.pallas_call(
        functools.partial(backward_kernel, len(greens), share),
        out_shape=[jax.ShapeDtypeStruct((points // parts, WIDTH), jnp.float32)] * parts,
        in_specs=[pl.BlockSpec(memory_space=pltpu.SMEM)] + [whole] * (4 + 2 * len(greens)),
        out_specs=[whole] * parts,
        scratch_shapes=[
            pltpu.VMEM((points, TILE, WIDTH), jnp.float32),
            pltpu.VMEM((TILE * points, WIDTH), jnp.float32),
            pltpu.VMEM((points, STEPS * STEPS * WIDTH), jnp.float32),
        ],
        compiler_params=pltpu.CompilerParams(vmem_limit_bytes=VMEM_LIMIT),
        cost_estimate=pl.CostEstimate(
            flops=800 * points * TILE * WIDTH, bytes_accessed=12 * points * TILE * WIDTH, transcendentals=0
        ),
        name="backward",
    )(place, lattice, weights, equal_time, jnp.asarray(gather_table()), *screens, *greens)


def propagate(greens, effective):
    history, points, width = greens.shape
    step = math.gcd(history, TILE)
    chunk = pl.BlockSpec((step, points, width), lambda i: (i, 0, 0))
    spread = spread_table()
    return pl.pallas_call(
        propagate_kernel,
        grid=(history // step,),
        out_shape=jax.ShapeDtypeStruct(greens.shape, jnp.float32),
        in_specs=[
            chunk,
            pl.BlockSpec((points, width), lambda i: (0, 0)),
            pl.BlockSpec(spread.shape, lambda i: (0, 0)),
        ],
        out_specs=chunk,
        scratch_shapes=[pltpu.VMEM((points, spread.shape[1]), jnp.float32)],
        compiler_params=pltpu.CompilerParams(vmem_limit_bytes=VMEM_LIMIT),
        cost_estimate=pl.CostEstimate(
            flops=32 * greens.size, bytes_accessed=8 * greens.size, transcendentals=0
        ),
        name="propagate",
    )(greens, effective, jnp.asarray(spread))


def partner_of(place, step, count):
    if count & (count - 1) == 0:
        return place ^ step
    return (place + step) % count


def exchange(value, axis, step, count):
    pairs = [(place, partner_of(place, step, count)) for place in range(count)]
    return lax.ppermute(value, axis, pairs)


def class_weights(quad_class):
    table = jnp.array(quadrature, jnp.float32)
    match = quad_class[:, None] == jnp.arange(4, dtype=jnp.int32)[None, :]
    return jnp.sum(jnp.where(match, table[None, :], jnp.float32(0.0)), axis=1)


def per_device(parts, blocks, green_row, screened, hamilton, equal_time, quad_class, live_count):
    history, local, width = green_row.shape
    points = local * parts
    times = history // parts
    place = lax.axis_index("ka")
    position = jnp.arange(history, dtype=jnp.int32)
    weights = jnp.where(
        position < live_count[0], time_step * class_weights(quad_class), jnp.float32(0.0)
    ) * jnp.float32(1.0 / points)
    weights = lax.dynamic_slice_in_dim(weights, place * times, times)

    if times == TILE and local % SIDE == 0:
        groups = 1
        moved = []
        for x in (green_row, screened):
            blocks_of = x.reshape(parts, TILE * local, width)
            moved.append([[]])
            for step in range(parts):
                block = lax.dynamic_index_in_dim(blocks_of, partner_of(place, step, parts), 0, keepdims=False)
                moved[-1][0].append(block if step == 0 else exchange(block, "ka", step, parts))
    else:
        groups = -(-times // TILE)
        padding = groups * TILE - times
        moved = []
        for x in (green_row, screened):
            x = lax.all_to_all(x, "ka", split_axis=0, concat_axis=0, tiled=True)
            x = x.reshape(parts, times, local, width).transpose(1, 0, 2, 3).reshape(times, points, width)
            x = jnp.pad(x, ((0, padding), (0, 0), (0, 0))).reshape(groups, TILE * points, width)
            moved.append([[x[group]] for group in range(groups)])
        weights = jnp.pad(weights, (0, padding))
    weights = jnp.broadcast_to(weights.reshape(groups, TILE, 1), (groups, TILE, width))

    pieces = None
    for group in range(groups):
        green, screen = moved[0][group], moved[1][group]
        lattice = forward(place.reshape(1), green)
        share = hubbard / (points * blocks) if group == 0 else 0.0
        terms = backward(
            place.reshape(1), lattice, screen, green, weights[group], equal_time, share, parts
        )
        pieces = list(terms) if pieces is None else [a + b for a, b in zip(pieces, terms)]

    partial_value = tree_sum(
        pieces[:1] + [exchange(pieces[step], "ka", step, parts) for step in range(1, parts)]
    )
    collision = tree_sum(
        [partial_value] + [exchange(partial_value, "hist", step, blocks) for step in range(1, blocks)]
    )
    return propagate(green_row, hamilton + collision)


def solution(mesh):
    in_specs = (
        P("hist", "ka", None),
        P("hist", "ka", None),
        P("ka", None),
        P("ka", None),
        P("hist"),
        P("hist"),
    )
    out_specs = P("hist", "ka", None)
    return jax.shard_map(
        functools.partial(per_device, mesh.shape["ka"], mesh.shape["hist"]),
        mesh=mesh,
        in_specs=in_specs,
        out_specs=out_specs,
        check_vma=False,
    )
```

```python
import functools
import math

import jax
import jax.numpy as jnp
import ml_dtypes
import numpy as np
from jax import lax
from jax.experimental import pallas as pl
from jax.experimental.pallas import tpu as pltpu
from jax.sharding import PartitionSpec as P

SIDE = 24
BANDS = 8
ENTRIES = BANDS * BANDS
WIDTH = 2 * ENTRIES
TILE = 8
STEPS = 4

time_step = 0.1
hubbard = 1.0
quadrature = (0.375, 1.1666666, 0.9583333, 1.0)

IN_FLIGHT = 5

VMEM_LIMIT = 48 * 1024 * 1024


def lane_sign(shape):
    lane = lax.broadcasted_iota(jnp.int32, shape, len(shape) - 1)
    return lane < ENTRIES


def swap(x):
    return pltpu.roll(x, ENTRIES, 1)


def roll_blocks(x, blocks):
    return x if blocks == 0 else pltpu.roll(x, WIDTH - BANDS * blocks, x.ndim - 1)


def tree_sum(terms):
    while len(terms) > 1:
        terms = [sum(terms[i : i + 2][1:], terms[i]) for i in range(0, len(terms), 2)]
    return terms[0]


def dft24(x, sign, low):
    root3 = jnp.where(low, -1.0, 1.0) * (sign * math.sqrt(3.0) / 2)
    turn = jnp.where(low, -1.0, 1.0) * float(sign)
    half = math.sqrt(0.5)
    turn_half = turn * half
    columns = [[None] * 8 for _ in range(3)]
    for n2 in range(8):
        x0, x1, x2 = (x[(8 * n1 + 3 * n2) % 24] for n1 in range(3))
        total = x1 + x2
        base = x0 - 0.5 * total
        spin = swap(x1 - x2) * root3
        columns[0][n2] = x0 + total
        columns[1][n2] = base + spin
        columns[2][n2] = base - spin
    out = [None] * 24
    for k1 in range(3):
        c = columns[k1]
        a0, a1 = c[0] + c[4], c[0] - c[4]
        a2, a3 = c[2] + c[6], c[2] - c[6]
        a4, a5 = c[1] + c[5], c[1] - c[5]
        a6, a7 = c[3] + c[7], c[3] - c[7]
        b0, b1 = a0 + a2, a0 - a2
        b2, b3 = a4 + a6, a4 - a6
        i_a3 = swap(a3) * turn
        i_b3 = swap(b3) * turn
        c0, c1 = a1 + i_a3, a1 - i_a3
        p = (a5 - a7) * half
        m = swap(a5 + a7) * turn_half
        e, f = p + m, p - m
        values = [b0 + b2, c0 + e, b1 + i_b3, c1 - f, b0 - b2, c0 - e, b1 - i_b3, c1 + f]
        for k2 in range(8):
            out[(16 * k1 + 9 * k2) % 24] = values[k2]
    return out


def line_of(place, step, ref, count):
    lines = ref.shape[0] // (TILE * SIDE)
    return partner_of(place, step, count) * lines if count > 1 else 0


def load_line(ref, line):
    stride = ref.shape[0] // TILE
    return [ref[pl.ds(line * SIDE + k2, TILE, stride=stride), :] for k2 in range(SIDE)]


def fetch(place, order, block_refs, held_ref, sems):
    copies = [None] * len(block_refs)
    for step in order:
        source = block_refs[step]
        rows = held_ref.shape[1]
        if step == 0 and len(order) > 1:
            source = source.at[pl.ds(pl.multiple_of(place * rows, TILE), rows)]
        copies[step] = pltpu.make_async_copy(source, held_ref.at[step], sems.at[step])
        copies[step].start()
    return copies


def along_first(work_ref, sign, low, out_ref):
    def columns(pair, carry):
        for column in (2 * pair, 2 * pair + 1):
            rows = [work_ref[k1 * SIDE + column] for k1 in range(SIDE)]
            for r1, value in enumerate(dft24(rows, sign, low)):
                out_ref[r1 * SIDE + column] = value
        return carry

    lax.fori_loop(0, SIDE // 2, columns, 0)


def forward_kernel(order, place_ref, *refs):
    count = len(order)
    block_refs, (lattice_ref, work_ref, held_ref, sems) = refs[:count], refs[count:]
    low = lane_sign((TILE, WIDTH))
    place = place_ref[0]
    copies = fetch(place, order, block_refs, held_ref, sems)
    for step in order:
        copies[step].wait()
        green_ref = held_ref.at[step]
        first = line_of(place, step, green_ref, count)
        lines = green_ref.shape[0] // (TILE * SIDE)

        def along_second(i, carry):
            for r2, value in enumerate(dft24(load_line(green_ref, i), -1, low)):
                work_ref[(first + i) * SIDE + r2] = value
            return carry

        lax.fori_loop(0, lines, along_second, 0, unroll=lines <= 4)
    along_first(work_ref, -1, low, lattice_ref)


def backward_kernel(order, share, place_ref, lattice_ref, weight_ref, equal_ref, sign_ref, gather_ref, *refs):
    count = len(order)
    screen_refs, green_refs, partial_refs = refs[:count], refs[count : 2 * count], refs[2 * count : -7]
    work_ref, sigma_ref, sums_ref, screen_held, green_held, screen_sems, green_sems = refs[-7:]
    points = SIDE * SIDE
    low = lane_sign((TILE, WIDTH))
    turn = jnp.where(low, -1.0, 1.0)
    weights = weight_ref[...]
    place = place_ref[0]
    screen_copies = fetch(place, order, screen_refs, screen_held, screen_sems)
    green_copies = fetch(place, order, green_refs, green_held, green_sems)

    for step in order:
        screen_copies[step].wait()
        screen_ref = screen_held.at[step]
        first = line_of(place, step, screen_ref, count)
        lines = screen_ref.shape[0] // (TILE * SIDE)

        def along_second(i, carry):
            rows = []
            for r2, value in enumerate(load_line(screen_ref, i)):
                screen = value * weights
                other = swap(screen)
                lattice = lattice_ref[(first + i) * SIDE + r2]
                rows.append(
                    swap(lattice) * turn * jnp.where(low, screen, other)
                    - lattice * jnp.where(low, other, screen)
                )
            for k2, value in enumerate(dft24(rows, 1, low)):
                work_ref[(first + i) * SIDE + k2] = value
            return carry

        lax.fori_loop(0, lines, along_second, 0, unroll=lines <= 4)
    sigma_at = sigma_ref.reshape(points, TILE, WIDTH)
    along_first(work_ref, 1, low, sigma_at)

    for step in order:
        green_copies[step].wait()
        green_ref = green_held.at[step]
        first = line_of(place, step, green_ref, count) * SIDE
        block = green_ref.shape[0] // TILE
        tiles = block // TILE
        batch = max(n for n in (1, 2, 3) if tiles % n == 0)

        def contract(group, carry):
            values = []
            for tile in range(batch):
                tile = group * batch + tile
                start = (first + tile * TILE) * TILE
                sums = [None] * (STEPS * STEPS)
                for s in range(TILE):
                    sigma = sigma_ref[pl.ds(start + s, TILE, stride=TILE), :]
                    green = green_ref[pl.ds(pl.multiple_of(s * block + tile * TILE, TILE), TILE), :]
                    sigmas = [roll_blocks(sigma, STEPS * i) for i in range(STEPS)]
                    greens = [roll_blocks(green, j) for j in range(STEPS)]
                    for i in range(STEPS):
                        for j in range(STEPS):
                            term = sigmas[i] * greens[j]
                            spot = STEPS * i + j
                            sums[spot] = term if s == 0 else sums[spot] + term
                values.append((pl.ds(pl.multiple_of(step * block + tile * TILE, TILE), TILE), sums))
            for row, sums in values:
                for spot, value in enumerate(sums):
                    sums_ref[row, spot * WIDTH : (spot + 1) * WIDTH] = value
            return carry

        lax.fori_loop(0, tiles // batch, contract, 0)

    lane = lax.broadcasted_iota(jnp.int32, equal_ref.shape, 1)
    inner = lane - ENTRIES
    occupied = jnp.sum(jnp.where((inner >= 0) & (inner % (BANDS + 1) == 0), equal_ref[...], 0.0))
    spots = lax.broadcasted_iota(jnp.int32, (points, WIDTH), 1)
    on_diagonal = (spots < ENTRIES) & (spots % (BANDS + 1) == 0)
    total = jnp.where(on_diagonal, occupied * share, 0.0)
    lower = spots < ENTRIES
    for pair in range(STEPS * STEPS // 2):
        first_part = sums_ref[:, 2 * pair * WIDTH : (2 * pair + 1) * WIDTH]
        second_part = sums_ref[:, (2 * pair + 1) * WIDTH : (2 * pair + 2) * WIDTH]
        folded = jnp.where(lower, first_part, second_part) + sign_ref[pair : pair + 1, :] * swap(
            jnp.where(lower, second_part, first_part)
        )
        coarse = folded.astype(jnp.bfloat16)
        fine = (folded - coarse.astype(jnp.float32)).astype(jnp.bfloat16)
        gather = gather_ref[2 * pair * WIDTH : (2 * pair + 2) * WIDTH, :]
        both = jnp.concatenate([coarse, fine], axis=1)
        total = total + jnp.dot(both, gather, preferred_element_type=jnp.float32)
    parts = len(partial_refs)
    local = points // parts
    if count == parts:
        for step, partial_ref in enumerate(partial_refs):
            partial_ref[...] = total[step * local : (step + 1) * local]
    else:
        sigma_ref[:points, :] = total
        for step, partial_ref in enumerate(partial_refs):
            owner = partner_of(place, step, parts)
            partial_ref[...] = sigma_ref[pl.ds(owner * local, local), :]


def propagate_kernel(green_ref, effective_ref, spread_ref, out_ref, factor_ref):
    history, points, _ = green_ref.shape

    @pl.when(pl.program_id(0) == 0)
    def _():
        rest = effective_ref[...] * time_step
        pieces = []
        for _ in range(3):
            pieces.append(rest.astype(jnp.bfloat16).astype(jnp.float32))
            rest = rest - pieces[-1]
        stacked = jnp.concatenate(pieces, axis=0).astype(jnp.bfloat16)
        spread = jnp.dot(stacked, spread_ref[...], preferred_element_type=jnp.float32)
        factor_ref[...] = tree_sum([spread[n * points : (n + 1) * points] for n in range(3)])

    def advance(start, stop):
        green = green_ref[:, start:stop, :]
        greens = [roll_blocks(green, j) for j in range(STEPS)]
        terms = [green]
        for i in range(STEPS):
            total = None
            for j in range(STEPS):
                spot = STEPS * i + j
                factor = factor_ref[start:stop, spot * WIDTH : (spot + 1) * WIDTH]
                term = factor[None] * greens[j]
                total = term if total is None else total + term
            terms.append(roll_blocks(total, STEPS * i))
        out_ref[:, start:stop, :] = tree_sum(terms)

    for start in range(0, points, 2 * TILE):
        advance(start, min(start + 2 * TILE, points))


def gather_tables():
    blocks = 2 * BANDS
    pairs = STEPS * STEPS // 2
    table = np.zeros((pairs, 2, blocks, BANDS, 2, BANDS, BANDS), np.float32)
    signs = np.zeros((pairs, blocks, BANDS), np.float32)
    for pair in range(pairs):
        for p in range(blocks):
            i, j = divmod(2 * pair + p // BANDS, STEPS)
            h, a = divmod((p + STEPS * i) % blocks, BANDS)
            g, c = divmod((p + j) % blocks, BANDS)
            table[pair, :, p, :, h ^ g, a, c] = 1 if (h, g) == (0, 1) else -1
            signs[pair, p] = 1 if h == g else -1
    return signs.reshape(pairs, WIDTH), table.reshape(-1, WIDTH).astype(ml_dtypes.bfloat16)


def spread_table():
    blocks = 2 * BANDS
    table = np.zeros((2, BANDS, BANDS, STEPS, STEPS, blocks, BANDS), np.float32)
    for i in range(STEPS):
        for j in range(STEPS):
            for p in range(blocks):
                h, a = divmod((p - STEPS * i) % blocks, BANDS)
                g, b = divmod((p + j) % blocks, BANDS)
                table[1 if h == g else 0, a, b, i, j, p, :] = -1 if (h, g) == (1, 0) else 1
    return table.reshape(WIDTH, -1).astype(ml_dtypes.bfloat16)


def forward(place, greens, order):
    points = SIDE * SIDE
    count = len(greens)
    whole = pl.BlockSpec(memory_space=pltpu.VMEM)
    return pl.pallas_call(
        functools.partial(forward_kernel, order),
        out_shape=jax.ShapeDtypeStruct((points, TILE, WIDTH), jnp.float32),
        in_specs=[pl.BlockSpec(memory_space=pltpu.SMEM)] + [pl.BlockSpec(memory_space=pl.ANY)] * count,
        out_specs=whole,
        scratch_shapes=[
            pltpu.VMEM((points, TILE, WIDTH), jnp.float32),
            pltpu.VMEM((count, TILE * points // count, WIDTH), jnp.float32),
            pltpu.SemaphoreType.DMA((count,)),
        ],
        compiler_params=pltpu.CompilerParams(vmem_limit_bytes=VMEM_LIMIT),
        cost_estimate=pl.CostEstimate(
            flops=400 * points * TILE * WIDTH, bytes_accessed=8 * points * TILE * WIDTH, transcendentals=0
        ),
        name="forward",
    )(place, *greens)


def backward(place, lattice, screens, greens, weights, equal_time, order, share, parts):
    points = SIDE * SIDE
    count = len(greens)
    whole = pl.BlockSpec(memory_space=pltpu.VMEM)
    signs, gather = gather_tables()
    held = pltpu.VMEM((count, TILE * points // count, WIDTH), jnp.float32)
    return pl.pallas_call(
        functools.partial(backward_kernel, order, share),
        out_shape=[jax.ShapeDtypeStruct((points // parts, WIDTH), jnp.float32)] * parts,
        in_specs=[pl.BlockSpec(memory_space=pltpu.SMEM)]
        + [whole] * 5
        + [pl.BlockSpec(memory_space=pl.ANY)] * (2 * count),
        out_specs=[whole] * parts,
        scratch_shapes=[
            pltpu.VMEM((points, TILE, WIDTH), jnp.float32),
            pltpu.VMEM((TILE * points, WIDTH), jnp.float32),
            pltpu.VMEM((points, STEPS * STEPS * WIDTH), jnp.float32),
            held,
            held,
            pltpu.SemaphoreType.DMA((count,)),
            pltpu.SemaphoreType.DMA((count,)),
        ],
        compiler_params=pltpu.CompilerParams(vmem_limit_bytes=VMEM_LIMIT),
        cost_estimate=pl.CostEstimate(
            flops=800 * points * TILE * WIDTH, bytes_accessed=12 * points * TILE * WIDTH, transcendentals=0
        ),
        name="backward",
    )(place, lattice, weights, equal_time, jnp.asarray(signs), jnp.asarray(gather), *screens, *greens)


def propagate(greens, effective):
    history, points, width = greens.shape
    step = math.gcd(history, TILE)
    chunk = pl.BlockSpec((step, points, width), lambda i: (i, 0, 0))
    spread = spread_table()
    return pl.pallas_call(
        propagate_kernel,
        grid=(history // step,),
        out_shape=jax.ShapeDtypeStruct(greens.shape, jnp.float32),
        in_specs=[
            chunk,
            pl.BlockSpec((points, width), lambda i: (0, 0)),
            pl.BlockSpec(spread.shape, lambda i: (0, 0)),
        ],
        out_specs=chunk,
        scratch_shapes=[pltpu.VMEM((points, spread.shape[1]), jnp.float32)],
        compiler_params=pltpu.CompilerParams(vmem_limit_bytes=VMEM_LIMIT),
        cost_estimate=pl.CostEstimate(
            flops=32 * greens.size, bytes_accessed=8 * greens.size, transcendentals=0
        ),
        name="propagate",
    )(greens, effective, jnp.asarray(spread))


def partner_of(place, step, count):
    if count & (count - 1) == 0:
        return place ^ step
    return (place + step) % count


def exchange(value, axis, step, count):
    pairs = [(place, partner_of(place, step, count)) for place in range(count)]
    return lax.ppermute(value, axis, pairs)


def exchange_order(count):
    along = {}
    for step in range(1, count):
        along.setdefault(step // 2, []).append(step)
    single = [along[n] for n in along if n and n & (n - 1) == 0]
    mixed = [along[n] for n in along if n & (n - 1)]
    order = [step for steps in zip(*single) for step in steps]
    order += [step for steps in mixed for step in steps]
    return order + along[0]


def class_weights(quad_class):
    table = jnp.array(quadrature, jnp.float32)
    match = quad_class[:, None] == jnp.arange(4, dtype=jnp.int32)[None, :]
    return jnp.sum(jnp.where(match, table[None, :], jnp.float32(0.0)), axis=1)


def per_device(parts, blocks, green_row, screened, hamilton, equal_time, quad_class, live_count):
    history, local, width = green_row.shape
    points = local * parts
    times = history // parts
    place = lax.axis_index("ka")
    position = jnp.arange(history, dtype=jnp.int32)
    weights = jnp.where(
        position < live_count[0], time_step * class_weights(quad_class), jnp.float32(0.0)
    ) * jnp.float32(1.0 / points)
    weights = lax.dynamic_slice_in_dim(weights, place * times, times)

    if times == TILE and local % SIDE == 0:
        groups = 1
        order = exchange_order(parts)
        wholes = [x.reshape(parts * TILE * local, width) for x in (green_row, screened)]
        received = []
        for whole in wholes:
            for step in order:
                start = partner_of(place, step, parts) * (TILE * local)
                block = lax.dynamic_slice_in_dim(whole, start, TILE * local)
                if len(received) >= IN_FLIGHT:
                    block, _ = lax.optimization_barrier((block, received[-IN_FLIGHT]))
                received.append(exchange(block, "ka", step, parts))
        moved = []
        for n, whole in enumerate(wholes):
            found = dict(zip(order, received[n * (parts - 1) :]))
            moved.append([[whole] + [found[step] for step in range(1, parts)]])
        order = order + [0]
    else:
        groups = -(-times // TILE)
        order = [0]
        padding = groups * TILE - times
        moved = []
        for x in (green_row, screened):
            x = lax.all_to_all(x, "ka", split_axis=0, concat_axis=0, tiled=True)
            x = x.reshape(parts, times, local, width).transpose(1, 0, 2, 3).reshape(times, points, width)
            x = jnp.pad(x, ((0, padding), (0, 0), (0, 0))).reshape(groups, TILE * points, width)
            moved.append([[x[group]] for group in range(groups)])
        weights = jnp.pad(weights, (0, padding))
    weights = jnp.broadcast_to(weights.reshape(groups, TILE, 1), (groups, TILE, width))

    pieces = None
    for group in range(groups):
        green, screen = moved[0][group], moved[1][group]
        lattice = forward(place.reshape(1), green, order)
        share = hubbard / (points * blocks) if group == 0 else 0.0
        terms = backward(
            place.reshape(1), lattice, screen, green, weights[group], equal_time, order, share, parts
        )
        pieces = list(terms) if pieces is None else [a + b for a, b in zip(pieces, terms)]

    if parts % 2 == 0 and parts & (parts - 1) == 0:
        pairs = jnp.concatenate([pieces[step] for step in range(1, parts, 2)], axis=0)
        pairs = exchange(pairs, "ka", 1, parts)
        mine = jnp.concatenate([pieces[step] for step in range(0, parts, 2)], axis=0) + pairs
        pieces = [mine[n * local : (n + 1) * local] for n in range(parts // 2)]
        partial_value = tree_sum(
            pieces[:1] + [exchange(pieces[n], "ka", 2 * n, parts) for n in range(1, parts // 2)]
        )
    else:
        partial_value = tree_sum(
            pieces[:1] + [exchange(pieces[step], "ka", step, parts) for step in range(1, parts)]
        )
    collision = tree_sum(
        [partial_value] + [exchange(partial_value, "hist", step, blocks) for step in range(1, blocks)]
    )
    return propagate(green_row, hamilton + collision)


def solution(mesh):
    in_specs = (
        P("hist", "ka", None),
        P("hist", "ka", None),
        P("ka", None),
        P("ka", None),
        P("hist"),
        P("hist"),
    )
    out_specs = P("hist", "ka", None)
    return jax.shard_map(
        functools.partial(per_device, mesh.shape["ka"], mesh.shape["hist"]),
        mesh=mesh,
        in_specs=in_specs,
        out_specs=out_specs,
        check_vma=False,
    )
```

```python
import functools
import math

import jax
import jax.numpy as jnp
import ml_dtypes
import numpy as np
from jax import lax
from jax.experimental import pallas as pl
from jax.experimental.pallas import tpu as pltpu
from jax.sharding import PartitionSpec as P

SIDE = 24
BANDS = 8
ENTRIES = BANDS * BANDS
WIDTH = 2 * ENTRIES
TILE = 8
STEPS = 4

time_step = 0.1
hubbard = 1.0
quadrature = (0.375, 1.1666666, 0.9583333, 1.0)

IN_FLIGHT = 5

AHEAD = 3

VMEM_LIMIT = 48 * 1024 * 1024


def lane_sign(shape):
    lane = lax.broadcasted_iota(jnp.int32, shape, len(shape) - 1)
    return lane < ENTRIES


def swap(x):
    return pltpu.roll(x, ENTRIES, 1)


def roll_blocks(x, blocks):
    return x if blocks == 0 else pltpu.roll(x, WIDTH - BANDS * blocks, x.ndim - 1)


def tree_sum(terms):
    while len(terms) > 1:
        terms = [sum(terms[i : i + 2][1:], terms[i]) for i in range(0, len(terms), 2)]
    return terms[0]


def dft24(x, sign, low):
    root3 = jnp.where(low, -1.0, 1.0) * (sign * math.sqrt(3.0) / 2)
    turn = jnp.where(low, -1.0, 1.0) * float(sign)
    half = math.sqrt(0.5)
    turn_half = turn * half
    columns = [[None] * 8 for _ in range(3)]
    for n2 in range(8):
        x0, x1, x2 = (x[(8 * n1 + 3 * n2) % 24] for n1 in range(3))
        total = x1 + x2
        base = x0 - 0.5 * total
        spin = swap(x1 - x2) * root3
        columns[0][n2] = x0 + total
        columns[1][n2] = base + spin
        columns[2][n2] = base - spin
    out = [None] * 24
    for k1 in range(3):
        c = columns[k1]
        a0, a1 = c[0] + c[4], c[0] - c[4]
        a2, a3 = c[2] + c[6], c[2] - c[6]
        a4, a5 = c[1] + c[5], c[1] - c[5]
        a6, a7 = c[3] + c[7], c[3] - c[7]
        b0, b1 = a0 + a2, a0 - a2
        b2, b3 = a4 + a6, a4 - a6
        i_a3 = swap(a3) * turn
        i_b3 = swap(b3) * turn
        c0, c1 = a1 + i_a3, a1 - i_a3
        p = (a5 - a7) * half
        m = swap(a5 + a7) * turn_half
        e, f = p + m, p - m
        values = [b0 + b2, c0 + e, b1 + i_b3, c1 - f, b0 - b2, c0 - e, b1 - i_b3, c1 + f]
        for k2 in range(8):
            out[(16 * k1 + 9 * k2) % 24] = values[k2]
    return out


def load_line(ref, line):
    stride = ref.shape[0] // TILE
    return [ref[pl.ds(line * SIDE + k2, TILE, stride=stride), :] for k2 in range(SIDE)]


def fetch(place, order, block_refs, held_ref, sems):
    copies = [None] * len(block_refs)
    for step in order:
        source = block_refs[step]
        rows = held_ref.shape[1]
        if step == 0 and len(order) > 1:
            source = source.at[pl.ds(pl.multiple_of(place * rows, TILE), rows)]
        slot = partner_of(place, step, len(order))
        copies[step] = pltpu.make_async_copy(source, held_ref.at[slot], sems.at[step])
        copies[step].start()
    return copies


def along_first(work_ref, sign, low, out_ref):
    def columns(pair, carry):
        both = (2 * pair, 2 * pair + 1)
        rows = [[work_ref[k1 * SIDE + column] for k1 in range(SIDE)] for column in both]
        values = [dft24(row, sign, low) for row in rows]
        for column, value in zip(both, values):
            for r1 in range(SIDE):
                out_ref[r1 * SIDE + column] = value[r1]
        return carry

    lax.fori_loop(0, SIDE // 2, columns, 0)


def forward_kernel(order, place_ref, *refs):
    count = len(order)
    block_refs, (lattice_ref, work_ref, held_ref, sems) = refs[:count], refs[count:]
    low = lane_sign((TILE, WIDTH))
    place = place_ref[0]
    copies = fetch(place, order, block_refs, held_ref, sems)
    for step in order:
        copies[step].wait()
        slot = partner_of(place, step, count)
        green_ref = held_ref.at[slot]
        lines = green_ref.shape[0] // (TILE * SIDE)
        first = slot * lines

        def along_second(i, carry):
            for r2, value in enumerate(dft24(load_line(green_ref, i), -1, low)):
                work_ref[(first + i) * SIDE + r2] = value
            return carry

        lax.fori_loop(0, lines, along_second, 0, unroll=lines <= 4)
    along_first(work_ref, -1, low, lattice_ref)


def backward_kernel(order, share, place_ref, lattice_ref, weight_ref, equal_ref, sign_ref, gather_ref, *refs):
    count = len(order)
    screen_refs, green_refs, partial_ref = refs[:count], refs[count : 2 * count], refs[2 * count]
    work_ref, sigma_ref, sums_ref, pieces_ref, screen_held, green_held, screen_sems, green_sems = refs[2 * count + 1 :]
    points = SIDE * SIDE
    low = lane_sign((TILE, WIDTH))
    turn = jnp.where(low, -1.0, 1.0)
    weights = weight_ref[...]
    place = place_ref[0]
    screen_copies = fetch(place, order, screen_refs, screen_held, screen_sems)
    green_copies = fetch(place, order, green_refs, green_held, green_sems)

    for step in order:
        screen_copies[step].wait()
        slot = partner_of(place, step, count)
        screen_ref = screen_held.at[slot]
        lines = screen_ref.shape[0] // (TILE * SIDE)
        first = slot * lines

        def along_second(i, carry):
            rows = []
            for r2, value in enumerate(load_line(screen_ref, i)):
                screen = value * weights
                other = swap(screen)
                lattice = lattice_ref[(first + i) * SIDE + r2]
                rows.append(
                    swap(lattice) * turn * jnp.where(low, screen, other)
                    - lattice * jnp.where(low, other, screen)
                )
            for k2, value in enumerate(dft24(rows, 1, low)):
                work_ref[(first + i) * SIDE + k2] = value
            return carry

        lax.fori_loop(0, lines, along_second, 0, unroll=lines <= 4)
    sigma_at = sigma_ref.reshape(points, TILE, WIDTH)
    along_first(work_ref, 1, low, sigma_at)

    for step in order:
        green_copies[step].wait()
    block = green_held.shape[1] // TILE
    tiles = block // TILE
    batch = max(n for n in range(1, 10) if tiles % n == 0)

    def contract(group, carry):
        first = group * batch
        green_row = (first // tiles) * TILE * block + (first % tiles) * TILE
        units = [(tile, s) for tile in range(batch) for s in range(TILE)]

        def prepare(tile, s):
            sigma = sigma_ref[pl.ds((first + tile) * TILE * TILE + s, TILE, stride=TILE), :]
            row = pl.multiple_of(green_row + s * block + tile * TILE, TILE)
            green = greens_ref[pl.ds(row, TILE), :]
            return (
                [roll_blocks(sigma, STEPS * i) for i in range(STEPS)],
                [roll_blocks(green, j) for j in range(STEPS)],
            )

        ready = [prepare(*unit) for unit in units[:AHEAD]]
        for n, (tile, s) in enumerate(units):
            if n + AHEAD < len(units):
                ready.append(prepare(*units[n + AHEAD]))
            sigmas, greens = ready.pop(0)
            terms = [sigma * green for sigma in sigmas for green in greens]
            sums = terms if s == 0 else [a + b for a, b in zip(sums, terms)]
            if s == TILE - 1:
                row = pl.ds(pl.multiple_of((first + tile) * TILE, TILE), TILE)
                for spot, value in enumerate(sums):
                    sums_ref[row, spot * WIDTH : (spot + 1) * WIDTH] = value
        return carry

    greens_ref = green_held.reshape(TILE * points, WIDTH)
    lax.fori_loop(0, points // (TILE * batch), contract, 0)

    lane = lax.broadcasted_iota(jnp.int32, equal_ref.shape, 1)
    inner = lane - ENTRIES
    occupied = jnp.sum(jnp.where((inner >= 0) & (inner % (BANDS + 1) == 0), equal_ref[...], 0.0))
    spots = lax.broadcasted_iota(jnp.int32, (points, WIDTH), 1)
    on_diagonal = (spots < ENTRIES) & (spots % (BANDS + 1) == 0)
    lower = spots < ENTRIES
    for pair in range(STEPS * STEPS // 2):
        first_part = sums_ref[:, 2 * pair * WIDTH : (2 * pair + 1) * WIDTH]
        second_part = sums_ref[:, (2 * pair + 1) * WIDTH : (2 * pair + 2) * WIDTH]
        folded = jnp.where(lower, first_part, second_part) + sign_ref[pair : pair + 1, :] * swap(
            jnp.where(lower, second_part, first_part)
        )
        coarse = folded.astype(jnp.bfloat16)
        fine = (folded - coarse.astype(jnp.float32)).astype(jnp.bfloat16)
        pieces_ref[:, 2 * pair * WIDTH : (2 * pair + 1) * WIDTH] = coarse
        pieces_ref[:, (2 * pair + 1) * WIDTH : (2 * pair + 2) * WIDTH] = fine
    total = jnp.dot(pieces_ref[...], gather_ref[...], preferred_element_type=jnp.float32)
    partial_ref[...] = total + jnp.where(on_diagonal, occupied * share, 0.0)


def propagate_kernel(green_ref, effective_ref, spread_ref, out_ref, factor_ref):
    history, points, _ = green_ref.shape

    @pl.when(pl.program_id(0) == 0)
    def _():
        rest = effective_ref[...] * time_step
        pieces = []
        for _ in range(3):
            pieces.append(rest.astype(jnp.bfloat16).astype(jnp.float32))
            rest = rest - pieces[-1]
        stacked = jnp.concatenate(pieces, axis=0).astype(jnp.bfloat16)
        spread = jnp.dot(stacked, spread_ref[...], preferred_element_type=jnp.float32)
        factor_ref[...] = tree_sum([spread[n * points : (n + 1) * points] for n in range(3)])

    starts = list(range(0, points, TILE))

    def prepare(start):
        green = green_ref[:, start : min(start + TILE, points), :]
        return [roll_blocks(green, j) for j in range(STEPS)]

    ready = prepare(starts[0])
    for n, start in enumerate(starts):
        greens = ready
        if n + 1 < len(starts):
            ready = prepare(starts[n + 1])
        stop = min(start + TILE, points)
        terms = [greens[0]]
        for i in range(STEPS):
            total = None
            for j in range(STEPS):
                spot = STEPS * i + j
                factor = factor_ref[start:stop, spot * WIDTH : (spot + 1) * WIDTH]
                term = factor[None] * greens[j]
                total = term if total is None else total + term
            terms.append(roll_blocks(total, STEPS * i))
        out_ref[:, start:stop, :] = tree_sum(terms)


def gather_tables():
    blocks = 2 * BANDS
    pairs = STEPS * STEPS // 2
    table = np.zeros((pairs, 2, blocks, BANDS, 2, BANDS, BANDS), np.float32)
    signs = np.zeros((pairs, blocks, BANDS), np.float32)
    for pair in range(pairs):
        for p in range(blocks):
            i, j = divmod(2 * pair + p // BANDS, STEPS)
            h, a = divmod((p + STEPS * i) % blocks, BANDS)
            g, c = divmod((p + j) % blocks, BANDS)
            table[pair, :, p, :, h ^ g, a, c] = 1 if (h, g) == (0, 1) else -1
            signs[pair, p] = 1 if h == g else -1
    return signs.reshape(pairs, WIDTH), table.reshape(-1, WIDTH).astype(ml_dtypes.bfloat16)


def spread_table():
    blocks = 2 * BANDS
    table = np.zeros((2, BANDS, BANDS, STEPS, STEPS, blocks, BANDS), np.float32)
    for i in range(STEPS):
        for j in range(STEPS):
            for p in range(blocks):
                h, a = divmod((p - STEPS * i) % blocks, BANDS)
                g, b = divmod((p + j) % blocks, BANDS)
                table[1 if h == g else 0, a, b, i, j, p, :] = -1 if (h, g) == (1, 0) else 1
    return table.reshape(WIDTH, -1).astype(ml_dtypes.bfloat16)


def forward(place, greens, order):
    points = SIDE * SIDE
    count = len(greens)
    whole = pl.BlockSpec(memory_space=pltpu.VMEM)
    return pl.pallas_call(
        functools.partial(forward_kernel, order),
        out_shape=jax.ShapeDtypeStruct((points, TILE, WIDTH), jnp.float32),
        in_specs=[pl.BlockSpec(memory_space=pltpu.SMEM)] + [pl.BlockSpec(memory_space=pl.ANY)] * count,
        out_specs=whole,
        scratch_shapes=[
            pltpu.VMEM((points, TILE, WIDTH), jnp.float32),
            pltpu.VMEM((count, TILE * points // count, WIDTH), jnp.float32),
            pltpu.SemaphoreType.DMA((count,)),
        ],
        compiler_params=pltpu.CompilerParams(vmem_limit_bytes=VMEM_LIMIT),
        cost_estimate=pl.CostEstimate(
            flops=400 * points * TILE * WIDTH, bytes_accessed=8 * points * TILE * WIDTH, transcendentals=0
        ),
        name="forward",
    )(place, *greens)


def backward(place, lattice, screens, greens, weights, equal_time, order, share):
    points = SIDE * SIDE
    count = len(greens)
    whole = pl.BlockSpec(memory_space=pltpu.VMEM)
    signs, gather = gather_tables()
    held = pltpu.VMEM((count, TILE * points // count, WIDTH), jnp.float32)
    return pl.pallas_call(
        functools.partial(backward_kernel, order, share),
        out_shape=jax.ShapeDtypeStruct((points, WIDTH), jnp.float32),
        in_specs=[pl.BlockSpec(memory_space=pltpu.SMEM)]
        + [whole] * 5
        + [pl.BlockSpec(memory_space=pl.ANY)] * (2 * count),
        out_specs=whole,
        scratch_shapes=[
            pltpu.VMEM((points, TILE, WIDTH), jnp.float32),
            pltpu.VMEM((TILE * points, WIDTH), jnp.float32),
            pltpu.VMEM((points, STEPS * STEPS * WIDTH), jnp.float32),
            pltpu.VMEM((points, STEPS * STEPS * WIDTH), jnp.bfloat16),
            held,
            held,
            pltpu.SemaphoreType.DMA((count,)),
            pltpu.SemaphoreType.DMA((count,)),
        ],
        compiler_params=pltpu.CompilerParams(vmem_limit_bytes=VMEM_LIMIT),
        cost_estimate=pl.CostEstimate(
            flops=800 * points * TILE * WIDTH, bytes_accessed=12 * points * TILE * WIDTH, transcendentals=0
        ),
        name="backward",
    )(place, lattice, weights, equal_time, jnp.asarray(signs), jnp.asarray(gather), *screens, *greens)


def propagate(greens, effective):
    history, points, width = greens.shape
    step = math.gcd(history, TILE)
    chunk = pl.BlockSpec((step, points, width), lambda i: (i, 0, 0))
    spread = spread_table()
    return pl.pallas_call(
        propagate_kernel,
        grid=(history // step,),
        out_shape=jax.ShapeDtypeStruct(greens.shape, jnp.float32),
        in_specs=[
            chunk,
            pl.BlockSpec((points, width), lambda i: (0, 0)),
            pl.BlockSpec(spread.shape, lambda i: (0, 0)),
        ],
        out_specs=chunk,
        scratch_shapes=[pltpu.VMEM((points, spread.shape[1]), jnp.float32)],
        compiler_params=pltpu.CompilerParams(vmem_limit_bytes=VMEM_LIMIT),
        cost_estimate=pl.CostEstimate(
            flops=32 * greens.size, bytes_accessed=8 * greens.size, transcendentals=0
        ),
        name="propagate",
    )(greens, effective, jnp.asarray(spread))


def partner_of(place, step, count):
    if count == 1:
        return 0
    if count & (count - 1) == 0:
        return place ^ step
    return (place + step) % count


def exchange(value, axis, step, count):
    pairs = [(place, partner_of(place, step, count)) for place in range(count)]
    return lax.ppermute(value, axis, pairs)


def exchange_order(count):
    along = {}
    for step in range(1, count):
        along.setdefault(step // 2, []).append(step)
    single = [along[n] for n in along if n and n & (n - 1) == 0]
    mixed = [along[n] for n in along if n & (n - 1)]
    order = [step for steps in zip(*single) for step in steps]
    order += [step for steps in mixed for step in steps]
    return order + along[0]


def class_weights(quad_class):
    table = jnp.array(quadrature, jnp.float32)
    match = quad_class[:, None] == jnp.arange(4, dtype=jnp.int32)[None, :]
    return jnp.sum(jnp.where(match, table[None, :], jnp.float32(0.0)), axis=1)


def per_device(parts, blocks, green_row, screened, hamilton, equal_time, quad_class, live_count):
    history, local, width = green_row.shape
    points = local * parts
    times = history // parts
    place = lax.axis_index("ka")
    position = jnp.arange(history, dtype=jnp.int32)
    weights = jnp.where(
        position < live_count[0], time_step * class_weights(quad_class), jnp.float32(0.0)
    ) * jnp.float32(1.0 / points)
    weights = lax.dynamic_slice_in_dim(weights, place * times, times)

    if times == TILE and local % SIDE == 0:
        groups = 1
        order = exchange_order(parts)
        wholes = [x.reshape(parts * TILE * local, width) for x in (green_row, screened)]
        received = []
        for whole in wholes:
            for step in order:
                start = partner_of(place, step, parts) * (TILE * local)
                block = lax.dynamic_slice_in_dim(whole, start, TILE * local)
                if len(received) >= IN_FLIGHT:
                    block, _ = lax.optimization_barrier((block, received[-IN_FLIGHT]))
                received.append(exchange(block, "ka", step, parts))
        moved = []
        for n, whole in enumerate(wholes):
            found = dict(zip(order, received[n * (parts - 1) :]))
            moved.append([[whole] + [found[step] for step in range(1, parts)]])
        order = order + [0]
    else:
        groups = -(-times // TILE)
        order = [0]
        padding = groups * TILE - times
        moved = []
        for x in (green_row, screened):
            x = lax.all_to_all(x, "ka", split_axis=0, concat_axis=0, tiled=True)
            x = x.reshape(parts, times, local, width).transpose(1, 0, 2, 3).reshape(times, points, width)
            x = jnp.pad(x, ((0, padding), (0, 0), (0, 0))).reshape(groups, TILE * points, width)
            moved.append([[x[group]] for group in range(groups)])
        weights = jnp.pad(weights, (0, padding))
    weights = jnp.broadcast_to(weights.reshape(groups, TILE, 1), (groups, TILE, width))

    partial_value = None
    for group in range(groups):
        green, screen = moved[0][group], moved[1][group]
        lattice = forward(place.reshape(1), green, order)
        share = hubbard / (points * blocks) if group == 0 else 0.0
        term = backward(
            place.reshape(1), lattice, screen, green, weights[group], equal_time, order, share
        )
        partial_value = term if partial_value is None else partial_value + term

    shares = lax.all_to_all(
        partial_value.reshape(parts, local, width), "ka", split_axis=0, concat_axis=0, tiled=True
    )
    collision = jnp.sum(shares, axis=0)
    if blocks & (blocks - 1) == 0:
        for bit in range(blocks.bit_length() - 1):
            collision = collision + exchange(collision, "hist", 1 << bit, blocks)
    else:
        collision = tree_sum(
            [collision] + [exchange(collision, "hist", step, blocks) for step in range(1, blocks)]
        )
    return propagate(green_row, hamilton + collision)


def solution(mesh):
    in_specs = (
        P("hist", "ka", None),
        P("hist", "ka", None),
        P("ka", None),
        P("ka", None),
        P("hist"),
        P("hist"),
    )
    out_specs = P("hist", "ka", None)
    return jax.shard_map(
        functools.partial(per_device, mesh.shape["ka"], mesh.shape["hist"]),
        mesh=mesh,
        in_specs=in_specs,
        out_specs=out_specs,
        check_vma=False,
    )
```

```python
import functools
import math

import jax
import jax.numpy as jnp
import ml_dtypes
import numpy as np
from jax import lax
from jax.experimental import pallas as pl
from jax.experimental.pallas import tpu as pltpu
from jax.sharding import PartitionSpec as P

SIDE = 24
BANDS = 8
ENTRIES = BANDS * BANDS
WIDTH = 2 * ENTRIES
TILE = 8
STEPS = 4

time_step = 0.1
hubbard = 1.0
quadrature = (0.375, 1.1666666, 0.9583333, 1.0)

LATE = 3
AHEAD = 3


def lane_sign(shape):
    lane = lax.broadcasted_iota(jnp.int32, shape, len(shape) - 1)
    return lane < ENTRIES


def swap(x):
    return pltpu.roll(x, ENTRIES, 1)


def roll_blocks(x, blocks):
    return x if blocks == 0 else pltpu.roll(x, WIDTH - BANDS * blocks, x.ndim - 1)


def tree_sum(terms):
    while len(terms) > 1:
        terms = [sum(terms[i : i + 2][1:], terms[i]) for i in range(0, len(terms), 2)]
    return terms[0]


def dft24(x, sign, low):
    root3 = jnp.where(low, -1.0, 1.0) * (sign * math.sqrt(3.0) / 2)
    turn = jnp.where(low, -1.0, 1.0) * float(sign)
    half = math.sqrt(0.5)
    turn_half = turn * half
    columns = [[None] * 8 for _ in range(3)]
    for n2 in range(8):
        x0, x1, x2 = (x[(8 * n1 + 3 * n2) % 24] for n1 in range(3))
        total = x1 + x2
        base = x0 - 0.5 * total
        spin = swap(x1 - x2) * root3
        columns[0][n2] = x0 + total
        columns[1][n2] = base + spin
        columns[2][n2] = base - spin
    out = [None] * 24
    for k1 in range(3):
        c = columns[k1]
        a0, a1 = c[0] + c[4], c[0] - c[4]
        a2, a3 = c[2] + c[6], c[2] - c[6]
        a4, a5 = c[1] + c[5], c[1] - c[5]
        a6, a7 = c[3] + c[7], c[3] - c[7]
        b0, b1 = a0 + a2, a0 - a2
        b2, b3 = a4 + a6, a4 - a6
        i_a3 = swap(a3) * turn
        i_b3 = swap(b3) * turn
        c0, c1 = a1 + i_a3, a1 - i_a3
        p = (a5 - a7) * half
        m = swap(a5 + a7) * turn_half
        e, f = p + m, p - m
        values = [b0 + b2, c0 + e, b1 + i_b3, c1 - f, b0 - b2, c0 - e, b1 - i_b3, c1 + f]
        for k2 in range(8):
            out[(16 * k1 + 9 * k2) % 24] = values[k2]
    return out


def load_line(ref, line):
    stride = ref.shape[0] // TILE
    return [ref[pl.ds(line * SIDE + k2, TILE, stride=stride), :] for k2 in range(SIDE)]


def fetch(place, steps, block_refs, held_ref, sems):
    copies = []
    for slot, (step, source) in enumerate(zip(steps, block_refs)):
        rows = held_ref.shape[1]
        if step == 0 and source.shape[0] != rows:
            source = source.at[pl.ds(pl.multiple_of(place * rows, TILE), rows)]
        copies.append(pltpu.make_async_copy(source, held_ref.at[slot], sems.at[slot]))
        copies[-1].start()
    return copies


def along_first(work_ref, sign, low, out_ref):
    def columns(pair, carry):
        both = (2 * pair, 2 * pair + 1)
        rows = [[work_ref[k1 * SIDE + column] for k1 in range(SIDE)] for column in both]
        values = [dft24(row, sign, low) for row in rows]
        for column, value in zip(both, values):
            for r1 in range(SIDE):
                out_ref[r1 * SIDE + column] = value[r1]
        return carry

    lax.fori_loop(0, SIDE // 2, columns, 0)


def roll_kernel(green_ref, greens_ref):
    def rolls(s, carry):
        green = green_ref[s]
        for j in range(STEPS):
            greens_ref[j, s] = roll_blocks(green, j)
        return carry

    lax.fori_loop(0, green_ref.shape[0], rolls, 0)


def forward_kernel(steps, parts, place_ref, *refs):
    block_refs, (lattice_ref, greens_ref, work_ref, held_ref, sems) = refs[: len(steps)], refs[len(steps) :]
    low = lane_sign((TILE, WIDTH))
    place = place_ref[0]
    copies = fetch(place, steps, block_refs, held_ref, sems)
    rows = held_ref.shape[1]
    lines = rows // (TILE * SIDE)
    for slot, step in enumerate(steps):
        copies[slot].wait()
        green_ref = held_ref.at[slot]
        owner = partner_of(place, step, parts)

        def along_second(i, carry):
            for r2, value in enumerate(dft24(load_line(green_ref, i), -1, low)):
                work_ref[(owner * lines + i) * SIDE + r2] = value
            return carry

        lax.fori_loop(0, lines, along_second, 0, unroll=lines <= 4)
        green = green_ref[...]
        spot = pl.ds(pl.multiple_of(owner * rows, TILE), rows)
        for j in range(STEPS):
            greens_ref[j, spot, :] = roll_blocks(green, j)
    along_first(work_ref, -1, low, lattice_ref)


def product_lines(steps, parts, place, lattice_ref, weights, screen_refs, held_ref, sems, work_ref):
    low = lane_sign((TILE, WIDTH))
    turn = jnp.where(low, -1.0, 1.0)
    copies = fetch(place, steps, screen_refs, held_ref, sems)
    lines = held_ref.shape[1] // (TILE * SIDE)
    for slot, step in enumerate(steps):
        copies[slot].wait()
        screen_ref = held_ref.at[slot]
        first = partner_of(place, step, parts) * lines

        def along_second(i, carry):
            rows = []
            for r2, value in enumerate(load_line(screen_ref, i)):
                screen = value * weights
                other = swap(screen)
                lattice = lattice_ref[(first + i) * SIDE + r2]
                rows.append(
                    swap(lattice) * turn * jnp.where(low, screen, other)
                    - lattice * jnp.where(low, other, screen)
                )
            for k2, value in enumerate(dft24(rows, 1, low)):
                work_ref[(first + i) * SIDE + k2] = value
            return carry

        lax.fori_loop(0, lines, along_second, 0, unroll=lines <= 4)


def early_kernel(steps, parts, place_ref, lattice_ref, weight_ref, *refs):
    screen_refs, (work_ref, held_ref, sems) = refs[: len(steps)], refs[len(steps) :]
    product_lines(
        steps, parts, place_ref[0], lattice_ref, weight_ref[...], screen_refs, held_ref, sems, work_ref
    )


def backward_kernel(
    steps, parts, share, place_ref, lattice_ref, weight_ref, equal_ref, sign_ref, gather_ref, greens_ref, *refs
):
    screen_refs, refs = refs[: len(steps)], refs[len(steps) :]
    _, partial_ref, work_ref, sigma_ref, sums_ref, pieces_ref, *late = refs
    points = SIDE * SIDE
    low = lane_sign((TILE, WIDTH))
    if steps:
        held_ref, sems = late
        product_lines(
            steps, parts, place_ref[0], lattice_ref, weight_ref[...], screen_refs, held_ref, sems, work_ref
        )
    sigma_at = sigma_ref.reshape(points, TILE, WIDTH)
    along_first(work_ref, 1, low, sigma_at)

    block = points // parts
    tiles = block // TILE
    batch = max(n for n in range(1, 10) if tiles % n == 0)

    def contract(group, carry):
        first = group * batch
        green_row = (first // tiles) * TILE * block + (first % tiles) * TILE
        units = [(tile, s) for tile in range(batch) for s in range(TILE)]

        def prepare(tile, s):
            sigma = sigma_ref[pl.ds((first + tile) * TILE * TILE + s, TILE, stride=TILE), :]
            row = pl.multiple_of(green_row + s * block + tile * TILE, TILE)
            return (
                [roll_blocks(sigma, STEPS * i) for i in range(STEPS)],
                [greens_ref[j, pl.ds(row, TILE), :] for j in range(STEPS)],
            )

        ready = [prepare(*unit) for unit in units[:AHEAD]]
        for n, (tile, s) in enumerate(units):
            if n + AHEAD < len(units):
                ready.append(prepare(*units[n + AHEAD]))
            sigmas, greens = ready.pop(0)
            terms = [sigma * green for sigma in sigmas for green in greens]
            sums = terms if s == 0 else [a + b for a, b in zip(sums, terms)]
            if s == TILE - 1:
                row = pl.ds(pl.multiple_of((first + tile) * TILE, TILE), TILE)
                for spot, value in enumerate(sums):
                    sums_ref[row, spot * WIDTH : (spot + 1) * WIDTH] = value
        return carry

    lax.fori_loop(0, points // (TILE * batch), contract, 0)

    lane = lax.broadcasted_iota(jnp.int32, equal_ref.shape, 1)
    inner = lane - ENTRIES
    occupied = jnp.sum(jnp.where((inner >= 0) & (inner % (BANDS + 1) == 0), equal_ref[...], 0.0))
    spots = lax.broadcasted_iota(jnp.int32, (points, WIDTH), 1)
    on_diagonal = (spots < ENTRIES) & (spots % (BANDS + 1) == 0)
    lower = spots < ENTRIES
    for pair in range(STEPS * STEPS // 2):
        first_part = sums_ref[:, 2 * pair * WIDTH : (2 * pair + 1) * WIDTH]
        second_part = sums_ref[:, (2 * pair + 1) * WIDTH : (2 * pair + 2) * WIDTH]
        folded = jnp.where(lower, first_part, second_part) + sign_ref[pair : pair + 1, :] * swap(
            jnp.where(lower, second_part, first_part)
        )
        coarse = folded.astype(jnp.bfloat16)
        fine = (folded - coarse.astype(jnp.float32)).astype(jnp.bfloat16)
        pieces_ref[:, 2 * pair * WIDTH : (2 * pair + 1) * WIDTH] = coarse
        pieces_ref[:, (2 * pair + 1) * WIDTH : (2 * pair + 2) * WIDTH] = fine
    total = jnp.dot(pieces_ref[...], gather_ref[...], preferred_element_type=jnp.float32)
    partial_ref[...] = total + jnp.where(on_diagonal, occupied * share, 0.0)


def propagate_kernel(greens_ref, effective_ref, spread_ref, out_ref, factor_ref, held_ref, sems):
    _, history, points, _ = greens_ref.shape
    rest = effective_ref[...] * time_step
    pieces = []
    for _ in range(3):
        pieces.append(rest.astype(jnp.bfloat16).astype(jnp.float32))
        rest = rest - pieces[-1]
    stacked = jnp.concatenate(pieces, axis=0).astype(jnp.bfloat16)
    spread = jnp.dot(stacked, spread_ref[...], preferred_element_type=jnp.float32)
    factor_ref[...] = tree_sum([spread[n * points : (n + 1) * points] for n in range(3)])

    slots, chunk = held_ref.shape[:2]

    def copy(number, slot):
        return pltpu.make_async_copy(
            held_ref.at[slot], out_ref.at[pl.ds(number * chunk, chunk)], sems.at[slot]
        )

    def advance(group, carry):
        for slot in range(slots):
            number = group * slots + slot

            @pl.when(group > 0)
            def _():
                copy(number - slots, slot).wait()

            times = pl.ds(number * chunk, chunk)
            for start in range(0, points, TILE):
                stop = min(start + TILE, points)
                greens = [greens_ref[j, times, start:stop, :] for j in range(STEPS)]
                terms = [greens[0]]
                for i in range(STEPS):
                    total = None
                    for j in range(STEPS):
                        spot = STEPS * i + j
                        factor = factor_ref[start:stop, spot * WIDTH : (spot + 1) * WIDTH]
                        term = factor[None] * greens[j]
                        total = term if total is None else total + term
                    terms.append(roll_blocks(total, STEPS * i))
                held_ref[slot, :, start:stop, :] = tree_sum(terms)
            copy(number, slot).start()
        return carry

    groups = history // (chunk * slots)
    lax.fori_loop(0, groups, advance, 0)
    for slot in range(slots):
        copy((groups - 1) * slots + slot, slot).wait()


def gather_tables():
    blocks = 2 * BANDS
    pairs = STEPS * STEPS // 2
    table = np.zeros((pairs, 2, blocks, BANDS, 2, BANDS, BANDS), np.float32)
    signs = np.zeros((pairs, blocks, BANDS), np.float32)
    for pair in range(pairs):
        for p in range(blocks):
            i, j = divmod(2 * pair + p // BANDS, STEPS)
            h, a = divmod((p + STEPS * i) % blocks, BANDS)
            g, c = divmod((p + j) % blocks, BANDS)
            table[pair, :, p, :, h ^ g, a, c] = 1 if (h, g) == (0, 1) else -1
            signs[pair, p] = 1 if h == g else -1
    return signs.reshape(pairs, WIDTH), table.reshape(-1, WIDTH).astype(ml_dtypes.bfloat16)


def spread_table():
    blocks = 2 * BANDS
    table = np.zeros((2, BANDS, BANDS, STEPS, STEPS, blocks, BANDS), np.float32)
    for i in range(STEPS):
        for j in range(STEPS):
            for p in range(blocks):
                h, a = divmod((p - STEPS * i) % blocks, BANDS)
                g, b = divmod((p + j) % blocks, BANDS)
                table[1 if h == g else 0, a, b, i, j, p, :] = -1 if (h, g) == (1, 0) else 1
    return table.reshape(WIDTH, -1).astype(ml_dtypes.bfloat16)


def in_vmem():
    return pl.BlockSpec(memory_space=pltpu.VMEM)


def in_smem():
    return pl.BlockSpec(memory_space=pltpu.SMEM)


def anywhere():
    return pl.BlockSpec(memory_space=pl.ANY)


def params(megabytes):
    return pltpu.CompilerParams(vmem_limit_bytes=megabytes * 1024 * 1024)


def cost(per_element, arrays):
    size = SIDE * SIDE * TILE * WIDTH
    return pl.CostEstimate(flops=per_element * size, bytes_accessed=4 * arrays * size, transcendentals=0)


def held_blocks(count, parts):
    return [
        pltpu.VMEM((count, TILE * SIDE * SIDE // parts, WIDTH), jnp.float32),
        pltpu.SemaphoreType.DMA((count,)),
    ]


def forward(place, greens, steps, parts):
    points = SIDE * SIDE
    return pl.pallas_call(
        functools.partial(forward_kernel, steps, parts),
        out_shape=[
            jax.ShapeDtypeStruct((points, TILE, WIDTH), jnp.float32),
            jax.ShapeDtypeStruct((STEPS, TILE * points, WIDTH), jnp.float32),
        ],
        in_specs=[in_smem()] + [anywhere()] * len(steps),
        out_specs=[in_vmem()] * 2,
        scratch_shapes=[pltpu.VMEM((points, TILE, WIDTH), jnp.float32)] + held_blocks(len(steps), parts),
        compiler_params=params(24),
        cost_estimate=cost(400, 6),
        name="forward",
    )(place, *greens)


def early_lines(place, lattice, weights, screens, steps, parts):
    points = SIDE * SIDE
    return pl.pallas_call(
        functools.partial(early_kernel, steps, parts),
        out_shape=jax.ShapeDtypeStruct((points, TILE, WIDTH), jnp.float32),
        in_specs=[in_smem(), in_vmem(), in_vmem()] + [anywhere()] * len(steps),
        out_specs=in_vmem(),
        scratch_shapes=held_blocks(len(steps), parts),
        compiler_params=params(16),
        cost_estimate=cost(150, 3),
        name="early",
    )(place, lattice, weights, *screens)


def backward(place, lattice, weights, equal_time, greens, screens, work, steps, parts, share):
    points = SIDE * SIDE
    signs, gather = gather_tables()
    inputs = (place, lattice, weights, equal_time, jnp.asarray(signs), jnp.asarray(gather), greens, *screens, work)
    partial_value, _ = pl.pallas_call(
        functools.partial(backward_kernel, steps, parts, share),
        out_shape=[
            jax.ShapeDtypeStruct((points, WIDTH), jnp.float32),
            jax.ShapeDtypeStruct((points, TILE, WIDTH), jnp.float32),
        ],
        in_specs=[in_smem()] + [in_vmem()] * 6 + [anywhere()] * len(steps) + [in_vmem()],
        out_specs=[in_vmem()] * 2,
        input_output_aliases={len(inputs) - 1: 1},
        scratch_shapes=[
            pltpu.VMEM((TILE * points, WIDTH), jnp.float32),
            pltpu.VMEM((points, STEPS * STEPS * WIDTH), jnp.float32),
            pltpu.VMEM((points, STEPS * STEPS * WIDTH), jnp.bfloat16),
        ]
        + (held_blocks(len(steps), parts) if steps else []),
        compiler_params=params(36),
        cost_estimate=cost(800, 6),
        name="backward",
    )(*inputs)
    return partial_value


def roll_own(greens):
    return pl.pallas_call(
        roll_kernel,
        out_shape=jax.ShapeDtypeStruct((STEPS, *greens.shape), jnp.float32),
        in_specs=[in_vmem()],
        out_specs=in_vmem(),
        compiler_params=params(24),
        cost_estimate=cost(3, 5),
        name="roll_own",
    )(greens)


def propagate(greens, effective):
    _, history, points, width = greens.shape
    chunk = math.gcd(history // 2, TILE)
    spread = spread_table()
    return pl.pallas_call(
        propagate_kernel,
        out_shape=jax.ShapeDtypeStruct(greens.shape[1:], jnp.float32),
        in_specs=[in_vmem()] * 3,
        out_specs=anywhere(),
        scratch_shapes=[
            pltpu.VMEM((points, spread.shape[1]), jnp.float32),
            pltpu.VMEM((2, chunk, points, width), jnp.float32),
            pltpu.SemaphoreType.DMA((2,)),
        ],
        compiler_params=params(24),
        cost_estimate=cost(32, 5),
        name="propagate",
    )(greens, effective, jnp.asarray(spread))


def partner_of(place, step, count):
    if count == 1:
        return 0
    if count & (count - 1) == 0:
        return place ^ step
    return (place + step) % count


def exchange(value, axis, step, count):
    pairs = [(place, partner_of(place, step, count)) for place in range(count)]
    return lax.ppermute(value, axis, pairs)


def exchange_order(count):
    along = {}
    for step in range(1, count):
        along.setdefault(step // 2, []).append(step)
    single = [along[n] for n in along if n and n & (n - 1) == 0]
    mixed = [along[n] for n in along if n & (n - 1)]
    order = along[0] + [step for steps in zip(*single) for step in steps]
    return order + [step for steps in mixed for step in steps]


def class_weights(quad_class):
    table = jnp.array(quadrature, jnp.float32)
    match = quad_class[:, None] == jnp.arange(4, dtype=jnp.int32)[None, :]
    return jnp.sum(jnp.where(match, table[None, :], jnp.float32(0.0)), axis=1)


def per_device(parts, blocks, green_row, screened, hamilton, equal_time, quad_class, live_count):
    history, local, width = green_row.shape
    points = local * parts
    times = history // parts
    place = lax.axis_index("ka")
    position = jnp.arange(history, dtype=jnp.int32)
    weights = jnp.where(
        position < live_count[0], time_step * class_weights(quad_class), jnp.float32(0.0)
    ) * jnp.float32(1.0 / points)
    weights = lax.dynamic_slice_in_dim(weights, place * times, times)

    if times == TILE and local % SIDE == 0:
        groups, sources = 1, parts
        order = exchange_order(parts)
        moved = []
        for x in (green_row, screened):
            whole = x.reshape(parts * TILE * local, width)
            found = {0: whole}
            for step in order:
                start = partner_of(place, step, parts) * (TILE * local)
                block = lax.dynamic_slice_in_dim(whole, start, TILE * local)
                found[step] = exchange(block, "ka", step, parts)
            moved.append([found])
        order = [0] + order
    else:
        groups, sources = -(-times // TILE), 1
        order = [0]
        padding = groups * TILE - times
        moved = []
        for x in (green_row, screened):
            x = lax.all_to_all(x, "ka", split_axis=0, concat_axis=0, tiled=True)
            x = x.reshape(parts, times, local, width).transpose(1, 0, 2, 3).reshape(times, points, width)
            x = jnp.pad(x, ((0, padding), (0, 0), (0, 0))).reshape(groups, TILE * points, width)
            moved.append([{0: x[group]} for group in range(groups)])
        weights = jnp.pad(weights, (0, padding))
    weights = jnp.broadcast_to(weights.reshape(groups, TILE, 1), (groups, TILE, width))

    early = order[: max(1, len(order) - LATE)]
    late = order[len(early) :]
    seat = place.reshape(1)
    partial_value = None
    for group in range(groups):
        green, screen = moved[0][group], moved[1][group]
        lattice, greens = forward(seat, [green[step] for step in order], order, sources)
        work = early_lines(seat, lattice, weights[group], [screen[step] for step in early], early, sources)
        share = hubbard / (points * blocks) if group == 0 else 0.0
        term = backward(
            seat, lattice, weights[group], equal_time, greens, [screen[step] for step in late], work,
            late, sources, share,
        )
        partial_value = term if partial_value is None else partial_value + term
    own_greens = roll_own(green_row)

    owners = [partner_of(place, step, parts) for step in range(parts)]
    pieces = [lax.dynamic_slice_in_dim(partial_value, owner * local, local) for owner in owners]
    if parts % 2 == 0 and parts & (parts - 1) == 0:
        pairs = jnp.concatenate([pieces[step] for step in range(1, parts, 2)], axis=0)
        pairs = exchange(pairs, "ka", 1, parts)
        mine = jnp.concatenate([pieces[step] for step in range(0, parts, 2)], axis=0) + pairs
        pieces = [mine[n * local : (n + 1) * local] for n in range(parts // 2)]
        collision = tree_sum(
            pieces[:1] + [exchange(pieces[n], "ka", 2 * n, parts) for n in range(1, parts // 2)]
        )
    else:
        collision = tree_sum(
            pieces[:1] + [exchange(pieces[step], "ka", step, parts) for step in range(1, parts)]
        )
    collision = tree_sum(
        [collision] + [exchange(collision, "hist", step, blocks) for step in range(1, blocks)]
    )
    return propagate(own_greens, hamilton + collision)


def solution(mesh):
    in_specs = (
        P("hist", "ka", None),
        P("hist", "ka", None),
        P("ka", None),
        P("ka", None),
        P("hist"),
        P("hist"),
    )
    out_specs = P("hist", "ka", None)
    return jax.shard_map(
        functools.partial(per_device, mesh.shape["ka"], mesh.shape["hist"]),
        mesh=mesh,
        in_specs=in_specs,
        out_specs=out_specs,
        check_vma=False,
    )
```

```python
import functools
import math

import jax
import jax.numpy as jnp
import ml_dtypes
import numpy as np
from jax import lax
from jax.experimental import pallas as pl
from jax.experimental.pallas import tpu as pltpu
from jax.sharding import PartitionSpec as P

SIDE = 24
BANDS = 8
ENTRIES = BANDS * BANDS
WIDTH = 2 * ENTRIES
TILE = 8
STEPS = 4

time_step = 0.1
hubbard = 1.0
quadrature = (0.375, 1.1666666, 0.9583333, 1.0)

PITCH = 9
LATE = 3
AHEAD = 3


def lane_sign(shape):
    lane = lax.broadcasted_iota(jnp.int32, shape, len(shape) - 1)
    return lane < ENTRIES


def swap(x):
    return pltpu.roll(x, ENTRIES, 1)


def roll_blocks(x, blocks):
    return x if blocks == 0 else pltpu.roll(x, WIDTH - BANDS * blocks, x.ndim - 1)


def tree_sum(terms):
    while len(terms) > 1:
        terms = [sum(terms[i : i + 2][1:], terms[i]) for i in range(0, len(terms), 2)]
    return terms[0]


def dft24(x, sign, low):
    root3 = jnp.where(low, -1.0, 1.0) * (sign * math.sqrt(3.0) / 2)
    turn = jnp.where(low, -1.0, 1.0) * float(sign)
    half = math.sqrt(0.5)
    turn_half = turn * half
    columns = [[None] * 8 for _ in range(3)]
    for n2 in range(8):
        x0, x1, x2 = (x[(8 * n1 + 3 * n2) % 24] for n1 in range(3))
        total = x1 + x2
        base = x0 - 0.5 * total
        spin = swap(x1 - x2) * root3
        columns[0][n2] = x0 + total
        columns[1][n2] = base + spin
        columns[2][n2] = base - spin
    out = [None] * 24
    for k1 in range(3):
        c = columns[k1]
        a0, a1 = c[0] + c[4], c[0] - c[4]
        a2, a3 = c[2] + c[6], c[2] - c[6]
        a4, a5 = c[1] + c[5], c[1] - c[5]
        a6, a7 = c[3] + c[7], c[3] - c[7]
        b0, b1 = a0 + a2, a0 - a2
        b2, b3 = a4 + a6, a4 - a6
        i_a3 = swap(a3) * turn
        i_b3 = swap(b3) * turn
        c0, c1 = a1 + i_a3, a1 - i_a3
        p = (a5 - a7) * half
        m = swap(a5 + a7) * turn_half
        e, f = p + m, p - m
        values = [b0 + b2, c0 + e, b1 + i_b3, c1 - f, b0 - b2, c0 - e, b1 - i_b3, c1 + f]
        for k2 in range(8):
            out[(16 * k1 + 9 * k2) % 24] = values[k2]
    return out


def load_line(ref, line):
    stride = ref.shape[0] // TILE
    return [ref[pl.ds(line * SIDE + k2, TILE, stride=stride), :] for k2 in range(SIDE)]


def fetch(place, steps, block_refs, held_ref, sems):
    copies = []
    for slot, (step, source) in enumerate(zip(steps, block_refs)):
        rows = held_ref.shape[1]
        if step == 0 and source.shape[0] != rows:
            source = source.at[pl.ds(pl.multiple_of(place * rows, TILE), rows)]
        copies.append(pltpu.make_async_copy(source, held_ref.at[slot], sems.at[slot]))
        copies[-1].start()
    return copies


def along_first(work_ref, sign, low, store):
    def columns(pair, carry):
        both = (2 * pair, 2 * pair + 1)
        rows = [[work_ref[k1 * SIDE + column] for k1 in range(SIDE)] for column in both]
        values = [dft24(row, sign, low) for row in rows]
        for column, value in zip(both, values):
            for r1 in range(SIDE):
                store(r1 * SIDE + column, value[r1])
        return carry

    lax.fori_loop(0, SIDE // 2, columns, 0)


def pick_kernel(steps, parts, place_ref, whole_ref, *refs):
    block_refs, sems = refs[:-1], refs[-1]
    copies = []
    for n, (step, block_ref) in enumerate(zip(steps, block_refs)):
        rows = block_ref.shape[0]
        start = pl.multiple_of(partner_of(place_ref[0], step, parts) * rows, TILE)
        copies.append(pltpu.make_async_copy(whole_ref.at[pl.ds(start, rows)], block_ref, sems.at[n]))
        copies[-1].start()
    for copy in copies:
        copy.wait()


def roll_kernel(green_ref, greens_ref):
    batch = math.gcd(green_ref.shape[0], STEPS)

    def rolls(n, carry):
        times = pl.ds(n * batch, batch)
        green = green_ref[times]
        rolled = [roll_blocks(green, j) for j in range(STEPS)]
        for j in range(STEPS):
            greens_ref[j, times] = rolled[j]
        return carry

    lax.fori_loop(0, green_ref.shape[0] // batch, rolls, 0)


def forward_kernel(steps, parts, place_ref, *refs):
    block_refs, (lattice_ref, greens_ref, work_ref, held_ref, sems) = refs[: len(steps)], refs[len(steps) :]
    low = lane_sign((TILE, WIDTH))
    place = place_ref[0]
    copies = fetch(place, steps, block_refs, held_ref, sems)
    rows = held_ref.shape[1]
    lines = rows // (TILE * SIDE)
    for slot, step in enumerate(steps):
        copies[slot].wait()
        green_ref = held_ref.at[slot]
        owner = partner_of(place, step, parts)

        def along_second(i, carry):
            for r2, value in enumerate(dft24(load_line(green_ref, i), -1, low)):
                work_ref[(owner * lines + i) * SIDE + r2] = value
            return carry

        lax.fori_loop(0, lines, along_second, 0, unroll=lines <= 4)
        green = green_ref[...]
        spot = pl.ds(pl.multiple_of(owner * rows, TILE), rows)
        for j in range(STEPS):
            greens_ref[j, spot, :] = roll_blocks(green, j)

    def store(point, value):
        lattice_ref[point] = value

    along_first(work_ref, -1, low, store)


def product_lines(steps, parts, place, lattice_ref, weights, screen_refs, held_ref, sems, work_ref):
    low = lane_sign((TILE, WIDTH))
    turn = jnp.where(low, -1.0, 1.0)
    copies = fetch(place, steps, screen_refs, held_ref, sems)
    lines = held_ref.shape[1] // (TILE * SIDE)
    for slot, step in enumerate(steps):
        copies[slot].wait()
        screen_ref = held_ref.at[slot]
        first = partner_of(place, step, parts) * lines

        def along_second(i, carry):
            rows = []
            for r2, value in enumerate(load_line(screen_ref, i)):
                screen = value * weights
                other = swap(screen)
                lattice = lattice_ref[(first + i) * SIDE + r2]
                rows.append(
                    swap(lattice) * turn * jnp.where(low, screen, other)
                    - lattice * jnp.where(low, other, screen)
                )
            for k2, value in enumerate(dft24(rows, 1, low)):
                work_ref[(first + i) * SIDE + k2] = value
            return carry

        lax.fori_loop(0, lines, along_second, 0, unroll=lines <= 4)


def early_kernel(steps, parts, place_ref, lattice_ref, weight_ref, _, *refs):
    screen_refs, (work_ref, held_ref, sems) = refs[: len(steps)], refs[len(steps) :]
    product_lines(
        steps, parts, place_ref[0], lattice_ref, weight_ref[...], screen_refs, held_ref, sems, work_ref
    )


def backward_kernel(
    steps, parts, share, place_ref, lattice_ref, weight_ref, equal_ref, sign_ref, gather_ref, greens_ref, *refs
):
    screen_refs, refs = refs[: len(steps)], refs[len(steps) :]
    _, partial_ref, work_ref, sigma_ref, sums_ref, pieces_ref, *late = refs
    points = SIDE * SIDE
    low = lane_sign((TILE, WIDTH))
    if steps:
        held_ref, sems = late
        product_lines(
            steps, parts, place_ref[0], lattice_ref, weight_ref[...], screen_refs, held_ref, sems, work_ref
        )

    def store(point, value):
        sigma_ref[pl.ds(point * PITCH, TILE), :] = value

    along_first(work_ref, 1, low, store)

    block = points // parts
    tiles = block // TILE
    batch = max(n for n in range(1, 10) if tiles % n == 0)

    def contract(group, carry):
        first = group * batch
        green_row = (first // tiles) * TILE * block + (first % tiles) * TILE
        units = [(tile, s) for tile in range(batch) for s in range(TILE)]

        def prepare(tile, s):
            sigma = sigma_ref[pl.ds((first + tile) * TILE * PITCH + s, TILE, stride=PITCH), :]
            row = pl.multiple_of(green_row + s * block + tile * TILE, TILE)
            return (
                [roll_blocks(sigma, STEPS * i) for i in range(STEPS)],
                [greens_ref[j, pl.ds(row, TILE), :] for j in range(STEPS)],
            )

        ready = [prepare(*unit) for unit in units[:AHEAD]]
        for n, (tile, s) in enumerate(units):
            if n + AHEAD < len(units):
                ready.append(prepare(*units[n + AHEAD]))
            sigmas, greens = ready.pop(0)
            terms = [sigma * green for sigma in sigmas for green in greens]
            sums = terms if s == 0 else [a + b for a, b in zip(sums, terms)]
            if s == TILE - 1:
                row = pl.ds(pl.multiple_of((first + tile) * TILE, TILE), TILE)
                for spot, value in enumerate(sums):
                    sums_ref[row, spot * WIDTH : (spot + 1) * WIDTH] = value
        return carry

    lax.fori_loop(0, points // (TILE * batch), contract, 0)

    lane = lax.broadcasted_iota(jnp.int32, equal_ref.shape, 1)
    inner = lane - ENTRIES
    occupied = jnp.sum(jnp.where((inner >= 0) & (inner % (BANDS + 1) == 0), equal_ref[...], 0.0))
    spots = lax.broadcasted_iota(jnp.int32, (points, WIDTH), 1)
    on_diagonal = (spots < ENTRIES) & (spots % (BANDS + 1) == 0)
    lower = spots < ENTRIES
    for pair in range(STEPS * STEPS // 2):
        first_part = sums_ref[:, 2 * pair * WIDTH : (2 * pair + 1) * WIDTH]
        second_part = sums_ref[:, (2 * pair + 1) * WIDTH : (2 * pair + 2) * WIDTH]
        folded = jnp.where(lower, first_part, second_part) + sign_ref[pair : pair + 1, :] * swap(
            jnp.where(lower, second_part, first_part)
        )
        coarse = folded.astype(jnp.bfloat16)
        fine = (folded - coarse.astype(jnp.float32)).astype(jnp.bfloat16)
        pieces_ref[:, 2 * pair * WIDTH : (2 * pair + 1) * WIDTH] = coarse
        pieces_ref[:, (2 * pair + 1) * WIDTH : (2 * pair + 2) * WIDTH] = fine
    total = jnp.dot(pieces_ref[...], gather_ref[...], preferred_element_type=jnp.float32)
    partial_ref[...] = total + jnp.where(on_diagonal, occupied * share, 0.0)


def propagate_kernel(greens_ref, effective_ref, spread_ref, out_ref, factor_ref, held_ref, sems):
    _, history, points, _ = greens_ref.shape
    rest = effective_ref[...] * time_step
    pieces = []
    for _ in range(3):
        pieces.append(rest.astype(jnp.bfloat16).astype(jnp.float32))
        rest = rest - pieces[-1]
    stacked = jnp.concatenate(pieces, axis=0).astype(jnp.bfloat16)
    spread = jnp.dot(stacked, spread_ref[...], preferred_element_type=jnp.float32)
    factor_ref[...] = tree_sum([spread[n * points : (n + 1) * points] for n in range(3)])

    slots, chunk = held_ref.shape[:2]

    def copy(number, slot):
        return pltpu.make_async_copy(
            held_ref.at[slot], out_ref.at[pl.ds(number * chunk, chunk)], sems.at[slot]
        )

    def advance(group, carry):
        for slot in range(slots):
            number = group * slots + slot

            @pl.when(group > 0)
            def _():
                copy(number - slots, slot).wait()

            times = pl.ds(number * chunk, chunk)
            for start in range(0, points, TILE):
                stop = min(start + TILE, points)
                greens = [greens_ref[j, times, start:stop, :] for j in range(STEPS)]
                terms = [greens[0]]
                for i in range(STEPS):
                    total = None
                    for j in range(STEPS):
                        spot = STEPS * i + j
                        factor = factor_ref[start:stop, spot * WIDTH : (spot + 1) * WIDTH]
                        term = factor[None] * greens[j]
                        total = term if total is None else total + term
                    terms.append(roll_blocks(total, STEPS * i))
                held_ref[slot, :, start:stop, :] = tree_sum(terms)
            copy(number, slot).start()
        return carry

    groups = history // (chunk * slots)
    lax.fori_loop(0, groups, advance, 0)
    for slot in range(slots):
        copy((groups - 1) * slots + slot, slot).wait()


def gather_tables():
    blocks = 2 * BANDS
    pairs = STEPS * STEPS // 2
    table = np.zeros((pairs, 2, blocks, BANDS, 2, BANDS, BANDS), np.float32)
    signs = np.zeros((pairs, blocks, BANDS), np.float32)
    for pair in range(pairs):
        for p in range(blocks):
            i, j = divmod(2 * pair + p // BANDS, STEPS)
            h, a = divmod((p + STEPS * i) % blocks, BANDS)
            g, c = divmod((p + j) % blocks, BANDS)
            table[pair, :, p, :, h ^ g, a, c] = 1 if (h, g) == (0, 1) else -1
            signs[pair, p] = 1 if h == g else -1
    return signs.reshape(pairs, WIDTH), table.reshape(-1, WIDTH).astype(ml_dtypes.bfloat16)


def spread_table():
    blocks = 2 * BANDS
    table = np.zeros((2, BANDS, BANDS, STEPS, STEPS, blocks, BANDS), np.float32)
    for i in range(STEPS):
        for j in range(STEPS):
            for p in range(blocks):
                h, a = divmod((p - STEPS * i) % blocks, BANDS)
                g, b = divmod((p + j) % blocks, BANDS)
                table[1 if h == g else 0, a, b, i, j, p, :] = -1 if (h, g) == (1, 0) else 1
    return table.reshape(WIDTH, -1).astype(ml_dtypes.bfloat16)


def in_vmem():
    return pl.BlockSpec(memory_space=pltpu.VMEM)


def in_smem():
    return pl.BlockSpec(memory_space=pltpu.SMEM)


def anywhere():
    return pl.BlockSpec(memory_space=pl.ANY)


def params(megabytes):
    return pltpu.CompilerParams(vmem_limit_bytes=megabytes * 1024 * 1024)


def cost(per_element, arrays):
    size = SIDE * SIDE * TILE * WIDTH
    return pl.CostEstimate(flops=per_element * size, bytes_accessed=4 * arrays * size, transcendentals=0)


def held_blocks(count, parts):
    return [
        pltpu.VMEM((count, TILE * SIDE * SIDE // parts, WIDTH), jnp.float32),
        pltpu.SemaphoreType.DMA((count,)),
    ]


def forward(place, greens, steps, parts):
    points = SIDE * SIDE
    return pl.pallas_call(
        functools.partial(forward_kernel, steps, parts),
        out_shape=[
            jax.ShapeDtypeStruct((points, TILE, WIDTH), jnp.float32),
            jax.ShapeDtypeStruct((STEPS, TILE * points, WIDTH), jnp.float32),
        ],
        in_specs=[in_smem()] + [anywhere()] * len(steps),
        out_specs=[in_vmem()] * 2,
        scratch_shapes=[pltpu.VMEM((points, TILE, WIDTH), jnp.float32)] + held_blocks(len(steps), parts),
        compiler_params=params(24),
        cost_estimate=cost(400, 6),
        name="forward",
    )(place, *greens)


def early_lines(place, lattice, weights, before, screens, steps, parts):
    points = SIDE * SIDE
    return pl.pallas_call(
        functools.partial(early_kernel, steps, parts),
        out_shape=jax.ShapeDtypeStruct((points, TILE, WIDTH), jnp.float32),
        in_specs=[in_smem(), in_vmem(), in_vmem(), anywhere()] + [anywhere()] * len(steps),
        out_specs=in_vmem(),
        scratch_shapes=held_blocks(len(steps), parts),
        compiler_params=params(16),
        cost_estimate=cost(150, 3),
        name="early",
    )(place, lattice, weights, before, *screens)


def backward(place, lattice, weights, equal_time, greens, screens, work, steps, parts, share):
    points = SIDE * SIDE
    signs, gather = gather_tables()
    inputs = (place, lattice, weights, equal_time, jnp.asarray(signs), jnp.asarray(gather), greens, *screens, work)
    partial_value, _ = pl.pallas_call(
        functools.partial(backward_kernel, steps, parts, share),
        out_shape=[
            jax.ShapeDtypeStruct((points, WIDTH), jnp.float32),
            jax.ShapeDtypeStruct((points, TILE, WIDTH), jnp.float32),
        ],
        in_specs=[in_smem()] + [in_vmem()] * 6 + [anywhere()] * len(steps) + [in_vmem()],
        out_specs=[in_vmem()] * 2,
        input_output_aliases={len(inputs) - 1: 1},
        scratch_shapes=[
            pltpu.VMEM((PITCH * points, WIDTH), jnp.float32),
            pltpu.VMEM((points, STEPS * STEPS * WIDTH), jnp.float32),
            pltpu.VMEM((points, STEPS * STEPS * WIDTH), jnp.bfloat16),
        ]
        + (held_blocks(len(steps), parts) if steps else []),
        compiler_params=params(36),
        cost_estimate=cost(800, 6),
        name="backward",
    )(*inputs)
    return partial_value


def pick(place, whole, steps, parts):
    rows = whole.shape[0] // parts
    return pl.pallas_call(
        functools.partial(pick_kernel, steps, parts),
        out_shape=[jax.ShapeDtypeStruct((rows, whole.shape[1]), whole.dtype)] * len(steps),
        in_specs=[in_smem(), anywhere()],
        out_specs=[anywhere()] * len(steps),
        scratch_shapes=[pltpu.SemaphoreType.DMA((len(steps),))],
        cost_estimate=pl.CostEstimate(
            flops=0, bytes_accessed=8 * len(steps) * rows * whole.shape[1], transcendentals=0
        ),
        name="pick",
    )(place, whole)


def roll_own(greens):
    return pl.pallas_call(
        roll_kernel,
        out_shape=jax.ShapeDtypeStruct((STEPS, *greens.shape), jnp.float32),
        in_specs=[in_vmem()],
        out_specs=in_vmem(),
        compiler_params=params(24),
        cost_estimate=cost(3, 5),
        name="roll_own",
    )(greens)


def propagate(greens, effective):
    _, history, points, width = greens.shape
    chunk = math.gcd(history // 2, TILE)
    spread = spread_table()
    return pl.pallas_call(
        propagate_kernel,
        out_shape=jax.ShapeDtypeStruct(greens.shape[1:], jnp.float32),
        in_specs=[in_vmem()] * 3,
        out_specs=anywhere(),
        scratch_shapes=[
            pltpu.VMEM((points, spread.shape[1]), jnp.float32),
            pltpu.VMEM((2, chunk, points, width), jnp.float32),
            pltpu.SemaphoreType.DMA((2,)),
        ],
        compiler_params=params(24),
        cost_estimate=cost(32, 5),
        name="propagate",
    )(greens, effective, jnp.asarray(spread))


def partner_of(place, step, count):
    if count == 1:
        return 0
    if count & (count - 1) == 0:
        return place ^ step
    return (place + step) % count


def exchange(value, axis, step, count):
    pairs = [(place, partner_of(place, step, count)) for place in range(count)]
    return lax.ppermute(value, axis, pairs)


def exchange_order(count):
    along = {}
    for step in range(1, count):
        along.setdefault(step // 2, []).append(step)
    single = [along[n] for n in along if n and n & (n - 1) == 0]
    mixed = [along[n] for n in along if n & (n - 1)]
    order = [step for steps in zip(*single[::-1]) for step in steps]
    return order + [step for steps in mixed for step in steps] + along[0]


def class_weights(quad_class):
    table = jnp.array(quadrature, jnp.float32)
    match = quad_class[:, None] == jnp.arange(4, dtype=jnp.int32)[None, :]
    return jnp.sum(jnp.where(match, table[None, :], jnp.float32(0.0)), axis=1)


def per_device(parts, blocks, green_row, screened, hamilton, equal_time, quad_class, live_count):
    history, local, width = green_row.shape
    points = local * parts
    times = history // parts
    place = lax.axis_index("ka")
    seat = place.reshape(1)
    position = jnp.arange(history, dtype=jnp.int32)
    weights = jnp.where(
        position < live_count[0], time_step * class_weights(quad_class), jnp.float32(0.0)
    ) * jnp.float32(1.0 / points)
    weights = lax.dynamic_slice_in_dim(weights, place * times, times)

    if times == TILE and local % SIDE == 0:
        groups, sources = 1, parts
        order = exchange_order(parts)
        moved = []
        for x in (green_row, screened):
            whole = x.reshape(parts * TILE * local, width)
            picked = pick(seat, whole, order[:2], parts) if x is green_row else []
            found = {0: whole}
            for n, step in enumerate(order):
                start = partner_of(place, step, parts) * (TILE * local)
                block = picked[n] if n < len(picked) else lax.dynamic_slice_in_dim(whole, start, TILE * local)
                found[step] = exchange(block, "ka", step, parts)
            moved.append([found])
        order = [0] + order
    else:
        groups, sources = -(-times // TILE), 1
        order = [0]
        padding = groups * TILE - times
        moved = []
        for x in (green_row, screened):
            x = lax.all_to_all(x, "ka", split_axis=0, concat_axis=0, tiled=True)
            x = x.reshape(parts, times, local, width).transpose(1, 0, 2, 3).reshape(times, points, width)
            x = jnp.pad(x, ((0, padding), (0, 0), (0, 0))).reshape(groups, TILE * points, width)
            moved.append([{0: x[group]} for group in range(groups)])
        weights = jnp.pad(weights, (0, padding))
    weights = jnp.broadcast_to(weights.reshape(groups, TILE, 1), (groups, TILE, width))

    early = order[: max(1, len(order) - LATE)]
    late = order[len(early) :]
    own_greens = roll_own(green_row)
    partial_value = None
    for group in range(groups):
        green, screen = moved[0][group], moved[1][group]
        lattice, greens = forward(seat, [green[step] for step in order], order, sources)
        work = early_lines(
            seat, lattice, weights[group], own_greens, [screen[step] for step in early], early, sources
        )
        share = hubbard / (points * blocks) if group == 0 else 0.0
        term = backward(
            seat, lattice, weights[group], equal_time, greens, [screen[step] for step in late], work,
            late, sources, share,
        )
        partial_value = term if partial_value is None else partial_value + term

    owners = [partner_of(place, step, parts) for step in range(parts)]
    pieces = [lax.dynamic_slice_in_dim(partial_value, owner * local, local) for owner in owners]
    if parts % 2 == 0 and parts & (parts - 1) == 0:
        pairs = jnp.concatenate([pieces[step] for step in range(1, parts, 2)], axis=0)
        pairs = exchange(pairs, "ka", 1, parts)
        mine = jnp.concatenate([pieces[step] for step in range(0, parts, 2)], axis=0) + pairs
        pieces = [mine[n * local : (n + 1) * local] for n in range(parts // 2)]
        collision = tree_sum(
            pieces[:1] + [exchange(pieces[n], "ka", 2 * n, parts) for n in range(1, parts // 2)]
        )
    else:
        collision = tree_sum(
            pieces[:1] + [exchange(pieces[step], "ka", step, parts) for step in range(1, parts)]
        )
    collision = tree_sum(
        [collision] + [exchange(collision, "hist", step, blocks) for step in range(1, blocks)]
    )
    return propagate(own_greens, hamilton + collision)


def solution(mesh):
    in_specs = (
        P("hist", "ka", None),
        P("hist", "ka", None),
        P("ka", None),
        P("ka", None),
        P("hist"),
        P("hist"),
    )
    out_specs = P("hist", "ka", None)
    return jax.shard_map(
        functools.partial(per_device, mesh.shape["ka"], mesh.shape["hist"]),
        mesh=mesh,
        in_specs=in_specs,
        out_specs=out_specs,
        check_vma=False,
    )
```

```python
import functools
import math

import jax
import jax.numpy as jnp
import ml_dtypes
import numpy as np
from jax import lax
from jax.experimental import pallas as pl
from jax.experimental.pallas import tpu as pltpu
from jax.sharding import PartitionSpec as P

SIDE = 24
BANDS = 8
ENTRIES = BANDS * BANDS
WIDTH = 2 * ENTRIES
TILE = 8
STEPS = 4

time_step = 0.1
hubbard = 1.0
quadrature = (0.375, 1.1666666, 0.9583333, 1.0)

LATE = 3
AHEAD = 3


def lane_sign(shape):
    lane = lax.broadcasted_iota(jnp.int32, shape, len(shape) - 1)
    return lane < ENTRIES


def swap(x):
    return pltpu.roll(x, ENTRIES, 1)


def roll_blocks(x, blocks):
    return x if blocks == 0 else pltpu.roll(x, WIDTH - BANDS * blocks, x.ndim - 1)


def tree_sum(terms):
    while len(terms) > 1:
        terms = [sum(terms[i : i + 2][1:], terms[i]) for i in range(0, len(terms), 2)]
    return terms[0]


def dft24(x, sign, low):
    root3 = jnp.where(low, -1.0, 1.0) * (sign * math.sqrt(3.0) / 2)
    turn = jnp.where(low, -1.0, 1.0) * float(sign)
    half = math.sqrt(0.5)
    turn_half = turn * half
    columns = [[None] * 8 for _ in range(3)]
    for n2 in range(8):
        x0, x1, x2 = (x[(8 * n1 + 3 * n2) % 24] for n1 in range(3))
        total = x1 + x2
        base = x0 - 0.5 * total
        spin = swap(x1 - x2) * root3
        columns[0][n2] = x0 + total
        columns[1][n2] = base + spin
        columns[2][n2] = base - spin
    out = [None] * 24
    for k1 in range(3):
        c = columns[k1]
        a0, a1 = c[0] + c[4], c[0] - c[4]
        a2, a3 = c[2] + c[6], c[2] - c[6]
        a4, a5 = c[1] + c[5], c[1] - c[5]
        a6, a7 = c[3] + c[7], c[3] - c[7]
        b0, b1 = a0 + a2, a0 - a2
        b2, b3 = a4 + a6, a4 - a6
        i_a3 = swap(a3) * turn
        i_b3 = swap(b3) * turn
        c0, c1 = a1 + i_a3, a1 - i_a3
        p = (a5 - a7) * half
        m = swap(a5 + a7) * turn_half
        e, f = p + m, p - m
        values = [b0 + b2, c0 + e, b1 + i_b3, c1 - f, b0 - b2, c0 - e, b1 - i_b3, c1 + f]
        for k2 in range(8):
            out[(16 * k1 + 9 * k2) % 24] = values[k2]
    return out


def load_line(ref, line):
    stride = ref.shape[0] // TILE
    return [ref[pl.ds(line * SIDE + k2, TILE, stride=stride), :] for k2 in range(SIDE)]


def fetch(place, steps, block_refs, held_ref, sems):
    copies = []
    for slot, (step, source) in enumerate(zip(steps, block_refs)):
        rows = held_ref.shape[1]
        if step == 0 and source.shape[0] != rows:
            source = source.at[pl.ds(pl.multiple_of(place * rows, TILE), rows)]
        copies.append(pltpu.make_async_copy(source, held_ref.at[slot], sems.at[slot]))
        copies[-1].start()
    return copies


def along_first(work_ref, sign, low, store):
    def load(column):
        return [work_ref[k1 * SIDE + column] for k1 in range(SIDE)]

    rows = load(0)
    for column in range(SIDE):
        following = load(column + 1) if column + 1 < SIDE else None
        for r1, value in enumerate(dft24(rows, sign, low)):
            store(r1 * SIDE + column, value)
        rows = following


def roll_kernel(green_ref, greens_ref):
    batch = math.gcd(green_ref.shape[0], STEPS)

    def rolls(n, carry):
        times = pl.ds(n * batch, batch)
        green = green_ref[times]
        rolled = [roll_blocks(green, j) for j in range(STEPS)]
        for j in range(STEPS):
            greens_ref[j, times] = rolled[j]
        return carry

    lax.fori_loop(0, green_ref.shape[0] // batch, rolls, 0)


def forward_kernel(steps, parts, place_ref, *refs):
    block_refs, (lattice_ref, greens_ref, work_ref, held_ref, sems) = refs[: len(steps)], refs[len(steps) :]
    low = lane_sign((TILE, WIDTH))
    place = place_ref[0]
    copies = fetch(place, steps, block_refs, held_ref, sems)
    rows = held_ref.shape[1]
    lines = rows // (TILE * SIDE)
    for slot, step in enumerate(steps):
        copies[slot].wait()
        green_ref = held_ref.at[slot]
        owner = partner_of(place, step, parts)

        def along_second(i, carry):
            for r2, value in enumerate(dft24(load_line(green_ref, i), -1, low)):
                work_ref[(owner * lines + i) * SIDE + r2] = value
            return carry

        lax.fori_loop(0, lines, along_second, 0, unroll=lines <= 4)
        green = green_ref[...]
        spot = pl.ds(pl.multiple_of(owner * rows, TILE), rows)
        for j in range(STEPS):
            greens_ref[j, spot, :] = roll_blocks(green, j)

    def store(point, value):
        lattice_ref[point] = value

    along_first(work_ref, -1, low, store)


def product_lines(steps, parts, place, lattice_ref, weights, screen_refs, held_ref, sems, work_ref):
    low = lane_sign((TILE, WIDTH))
    turn = jnp.where(low, -1.0, 1.0)
    copies = fetch(place, steps, screen_refs, held_ref, sems)
    lines = held_ref.shape[1] // (TILE * SIDE)
    for copy in copies:
        copy.wait()

    def load(slot, step, i):
        line = partner_of(place, step, parts) * lines + i
        rows = []
        for r2, value in enumerate(load_line(held_ref.at[slot], i)):
            screen = value * weights
            other = swap(screen)
            lattice = lattice_ref[line * SIDE + r2]
            rows.append(
                swap(lattice) * turn * jnp.where(low, screen, other)
                - lattice * jnp.where(low, other, screen)
            )
        return line, rows

    def store(line, rows):
        for k2, value in enumerate(dft24(rows, 1, low)):
            work_ref[line * SIDE + k2] = value

    if lines > 4:
        for slot, step in enumerate(steps):
            lax.fori_loop(0, lines, lambda i, carry: store(*load(slot, step, i)), None)
        return
    each = [(slot, step, i) for slot, step in enumerate(steps) for i in range(lines)]
    ready = load(*each[0])
    for n in range(len(each)):
        present = ready
        ready = load(*each[n + 1]) if n + 1 < len(each) else None
        store(*present)


def early_kernel(steps, parts, place_ref, lattice_ref, weight_ref, _, *refs):
    screen_refs, (work_ref, held_ref, sems) = refs[: len(steps)], refs[len(steps) :]
    product_lines(
        steps, parts, place_ref[0], lattice_ref, weight_ref[...], screen_refs, held_ref, sems, work_ref
    )


def backward_kernel(
    steps, parts, share, place_ref, lattice_ref, weight_ref, equal_ref, sign_ref, gather_ref, greens_ref, *refs
):
    screen_refs, refs = refs[: len(steps)], refs[len(steps) :]
    _, partial_ref, work_ref, sigma_ref, sums_ref, pieces_ref, *late = refs
    points = SIDE * SIDE
    low = lane_sign((TILE, WIDTH))
    if steps:
        held_ref, sems = late
        product_lines(
            steps, parts, place_ref[0], lattice_ref, weight_ref[...], screen_refs, held_ref, sems, work_ref
        )

    def store(point, value):
        sigma_ref[pl.ds(point * TILE, TILE), :] = value

    along_first(work_ref, 1, low, store)

    block = points // parts
    tiles = block // TILE
    batch = max(n for n in range(1, 10) if tiles % n == 0)

    def contract(group, carry):
        first = group * batch
        green_row = (first // tiles) * TILE * block + (first % tiles) * TILE
        units = [(tile, s) for tile in range(batch) for s in range(TILE)]

        def prepare(tile, s):
            sigma = sigma_ref[pl.ds((first + tile) * TILE * TILE + s, TILE, stride=TILE), :]
            row = pl.multiple_of(green_row + s * block + tile * TILE, TILE)
            return (
                [roll_blocks(sigma, STEPS * i) for i in range(STEPS)],
                [greens_ref[j, pl.ds(row, TILE), :] for j in range(STEPS)],
            )

        ready = [prepare(*unit) for unit in units[:AHEAD]]
        for n, (tile, s) in enumerate(units):
            if n + AHEAD < len(units):
                ready.append(prepare(*units[n + AHEAD]))
            sigmas, greens = ready.pop(0)
            terms = [sigma * green for sigma in sigmas for green in greens]
            sums = terms if s == 0 else [a + b for a, b in zip(sums, terms)]
            if s == TILE - 1:
                row = pl.ds(pl.multiple_of((first + tile) * TILE, TILE), TILE)
                for spot, value in enumerate(sums):
                    sums_ref[row, spot * WIDTH : (spot + 1) * WIDTH] = value
        return carry

    lax.fori_loop(0, points // (TILE * batch), contract, 0)

    lane = lax.broadcasted_iota(jnp.int32, equal_ref.shape, 1)
    inner = lane - ENTRIES
    occupied = jnp.sum(jnp.where((inner >= 0) & (inner % (BANDS + 1) == 0), equal_ref[...], 0.0))
    spots = lax.broadcasted_iota(jnp.int32, (points, WIDTH), 1)
    on_diagonal = (spots < ENTRIES) & (spots % (BANDS + 1) == 0)
    lower = spots < ENTRIES
    for pair in range(STEPS * STEPS // 2):
        first_part = sums_ref[:, 2 * pair * WIDTH : (2 * pair + 1) * WIDTH]
        second_part = sums_ref[:, (2 * pair + 1) * WIDTH : (2 * pair + 2) * WIDTH]
        folded = jnp.where(lower, first_part, second_part) + sign_ref[pair : pair + 1, :] * swap(
            jnp.where(lower, second_part, first_part)
        )
        coarse = folded.astype(jnp.bfloat16)
        fine = (folded - coarse.astype(jnp.float32)).astype(jnp.bfloat16)
        pieces_ref[:, 2 * pair * WIDTH : (2 * pair + 1) * WIDTH] = coarse
        pieces_ref[:, (2 * pair + 1) * WIDTH : (2 * pair + 2) * WIDTH] = fine
    total = jnp.dot(pieces_ref[...], gather_ref[...], preferred_element_type=jnp.float32)
    partial_ref[...] = total + jnp.where(on_diagonal, occupied * share, 0.0)


def propagate_kernel(greens_ref, effective_ref, spread_ref, out_ref, factor_ref, held_ref, sems):
    _, history, points, _ = greens_ref.shape
    rest = effective_ref[...] * time_step
    pieces = []
    for _ in range(3):
        pieces.append(rest.astype(jnp.bfloat16).astype(jnp.float32))
        rest = rest - pieces[-1]
    stacked = jnp.concatenate(pieces, axis=0).astype(jnp.bfloat16)
    spread = jnp.dot(stacked, spread_ref[...], preferred_element_type=jnp.float32)
    factor_ref[...] = tree_sum([spread[n * points : (n + 1) * points] for n in range(3)])

    slots, chunk = held_ref.shape[:2]

    def copy(number, slot):
        return pltpu.make_async_copy(
            held_ref.at[slot], out_ref.at[pl.ds(number * chunk, chunk)], sems.at[slot]
        )

    def advance(group, carry):
        for slot in range(slots):
            number = group * slots + slot

            @pl.when(group > 0)
            def _():
                copy(number - slots, slot).wait()

            batch = math.gcd(chunk, 4)
            pending = None
            for start in range(0, points, TILE):
                stop = min(start + TILE, points)
                for first in range(0, chunk, batch):
                    times = pl.ds(number * chunk + first, batch)
                    greens = [greens_ref[j, times, start:stop, :] for j in range(STEPS)]
                    terms = [greens[0]]
                    for i in range(STEPS):
                        total = None
                        for j in range(STEPS):
                            spot = STEPS * i + j
                            factor = factor_ref[start:stop, spot * WIDTH : (spot + 1) * WIDTH]
                            term = factor[None] * greens[j]
                            total = term if total is None else total + term
                        terms.append(roll_blocks(total, STEPS * i))
                    if pending is not None:
                        held_ref[pending[0]] = tree_sum(pending[1])
                    pending = ((slot, slice(first, first + batch), slice(start, stop)), terms)
            held_ref[pending[0]] = tree_sum(pending[1])
            copy(number, slot).start()
        return carry

    groups = history // (chunk * slots)
    lax.fori_loop(0, groups, advance, 0)
    for slot in range(slots):
        copy((groups - 1) * slots + slot, slot).wait()


def gather_tables():
    blocks = 2 * BANDS
    pairs = STEPS * STEPS // 2
    table = np.zeros((pairs, 2, blocks, BANDS, 2, BANDS, BANDS), np.float32)
    signs = np.zeros((pairs, blocks, BANDS), np.float32)
    for pair in range(pairs):
        for p in range(blocks):
            i, j = divmod(2 * pair + p // BANDS, STEPS)
            h, a = divmod((p + STEPS * i) % blocks, BANDS)
            g, c = divmod((p + j) % blocks, BANDS)
            table[pair, :, p, :, h ^ g, a, c] = 1 if (h, g) == (0, 1) else -1
            signs[pair, p] = 1 if h == g else -1
    return signs.reshape(pairs, WIDTH), table.reshape(-1, WIDTH).astype(ml_dtypes.bfloat16)


def spread_table():
    blocks = 2 * BANDS
    table = np.zeros((2, BANDS, BANDS, STEPS, STEPS, blocks, BANDS), np.float32)
    for i in range(STEPS):
        for j in range(STEPS):
            for p in range(blocks):
                h, a = divmod((p - STEPS * i) % blocks, BANDS)
                g, b = divmod((p + j) % blocks, BANDS)
                table[1 if h == g else 0, a, b, i, j, p, :] = -1 if (h, g) == (1, 0) else 1
    return table.reshape(WIDTH, -1).astype(ml_dtypes.bfloat16)


def in_vmem():
    return pl.BlockSpec(memory_space=pltpu.VMEM)


def in_smem():
    return pl.BlockSpec(memory_space=pltpu.SMEM)


def anywhere():
    return pl.BlockSpec(memory_space=pl.ANY)


def params(megabytes):
    return pltpu.CompilerParams(vmem_limit_bytes=megabytes * 1024 * 1024)


def cost(per_element, arrays):
    size = SIDE * SIDE * TILE * WIDTH
    return pl.CostEstimate(flops=per_element * size, bytes_accessed=4 * arrays * size, transcendentals=0)


def held_blocks(count, parts):
    return [
        pltpu.VMEM((count, TILE * SIDE * SIDE // parts, WIDTH), jnp.float32),
        pltpu.SemaphoreType.DMA((count,)),
    ]


def forward(place, greens, steps, parts):
    points = SIDE * SIDE
    return pl.pallas_call(
        functools.partial(forward_kernel, steps, parts),
        out_shape=[
            jax.ShapeDtypeStruct((points, TILE, WIDTH), jnp.float32),
            jax.ShapeDtypeStruct((STEPS, TILE * points, WIDTH), jnp.float32),
        ],
        in_specs=[in_smem()] + [anywhere()] * len(steps),
        out_specs=[in_vmem()] * 2,
        scratch_shapes=[pltpu.VMEM((points, TILE, WIDTH), jnp.float32)] + held_blocks(len(steps), parts),
        compiler_params=params(8),
        cost_estimate=cost(400, 6),
        name="forward",
    )(place, *greens)


def early_lines(place, lattice, weights, before, screens, steps, parts):
    points = SIDE * SIDE
    return pl.pallas_call(
        functools.partial(early_kernel, steps, parts),
        out_shape=jax.ShapeDtypeStruct((points, TILE, WIDTH), jnp.float32),
        in_specs=[in_smem(), in_vmem(), in_vmem(), anywhere()] + [anywhere()] * len(steps),
        out_specs=in_vmem(),
        scratch_shapes=held_blocks(len(steps), parts),
        compiler_params=params(4),
        cost_estimate=cost(150, 3),
        name="early",
    )(place, lattice, weights, before, *screens)


def backward(place, lattice, weights, equal_time, greens, screens, work, steps, parts, share):
    points = SIDE * SIDE
    signs, gather = gather_tables()
    inputs = (place, lattice, weights, equal_time, jnp.asarray(signs), jnp.asarray(gather), greens, *screens, work)
    partial_value, _ = pl.pallas_call(
        functools.partial(backward_kernel, steps, parts, share),
        out_shape=[
            jax.ShapeDtypeStruct((points, WIDTH), jnp.float32),
            jax.ShapeDtypeStruct((points, TILE, WIDTH), jnp.float32),
        ],
        in_specs=[in_smem()] + [in_vmem()] * 6 + [anywhere()] * len(steps) + [in_vmem()],
        out_specs=[in_vmem()] * 2,
        input_output_aliases={len(inputs) - 1: 1},
        scratch_shapes=[
            pltpu.VMEM((TILE * points, WIDTH), jnp.float32),
            pltpu.VMEM((points, STEPS * STEPS * WIDTH), jnp.float32),
            pltpu.VMEM((points, STEPS * STEPS * WIDTH), jnp.bfloat16),
        ]
        + (held_blocks(len(steps), parts) if steps else []),
        compiler_params=params(16),
        cost_estimate=cost(800, 6),
        name="backward",
    )(*inputs)
    return partial_value


def roll_own(greens):
    return pl.pallas_call(
        roll_kernel,
        out_shape=jax.ShapeDtypeStruct((STEPS, *greens.shape), jnp.float32),
        in_specs=[in_vmem()],
        out_specs=in_vmem(),
        compiler_params=params(4),
        cost_estimate=cost(3, 5),
        name="roll_own",
    )(greens)


def propagate(greens, effective):
    _, history, points, width = greens.shape
    chunk = math.gcd(history // 2, TILE)
    spread = spread_table()
    return pl.pallas_call(
        propagate_kernel,
        out_shape=jax.ShapeDtypeStruct(greens.shape[1:], jnp.float32),
        in_specs=[in_vmem()] * 3,
        out_specs=anywhere(),
        scratch_shapes=[
            pltpu.VMEM((points, spread.shape[1]), jnp.float32),
            pltpu.VMEM((2, chunk, points, width), jnp.float32),
            pltpu.SemaphoreType.DMA((2,)),
        ],
        compiler_params=params(6),
        cost_estimate=cost(32, 5),
        name="propagate",
    )(greens, effective, jnp.asarray(spread))


def partner_of(place, step, count):
    if count == 1:
        return 0
    if count & (count - 1) == 0:
        return place ^ step
    return (place + step) % count


def exchange(value, axis, step, count):
    pairs = [(place, partner_of(place, step, count)) for place in range(count)]
    return lax.ppermute(value, axis, pairs)


def exchange_order(count):
    along = {}
    for step in range(1, count):
        along.setdefault(step // 2, []).append(step)
    single = [along[n] for n in along if n and n & (n - 1) == 0]
    mixed = [along[n] for n in along if n & (n - 1)]
    order = [step for steps in zip(*single[::-1]) for step in steps]
    return order + [step for steps in mixed for step in steps] + along[0]


def class_weights(quad_class):
    table = jnp.array(quadrature, jnp.float32)
    match = quad_class[:, None] == jnp.arange(4, dtype=jnp.int32)[None, :]
    return jnp.sum(jnp.where(match, table[None, :], jnp.float32(0.0)), axis=1)


def per_device(parts, blocks, green_row, screened, hamilton, equal_time, quad_class, live_count):
    history, local, width = green_row.shape
    points = local * parts
    times = history // parts
    place = lax.axis_index("ka")
    seat = place.reshape(1)
    position = jnp.arange(history, dtype=jnp.int32)
    weights = jnp.where(
        position < live_count[0], time_step * class_weights(quad_class), jnp.float32(0.0)
    ) * jnp.float32(1.0 / points)
    weights = lax.dynamic_slice_in_dim(weights, place * times, times)

    if times == TILE and local % SIDE == 0:
        groups, sources = 1, parts
        order = exchange_order(parts)
        moved = []
        for x in (green_row, screened):
            whole = x.reshape(parts * TILE * local, width)
            found = {0: whole}
            for step in order:
                start = partner_of(place, step, parts) * (TILE * local)
                block = lax.dynamic_slice_in_dim(whole, start, TILE * local)
                found[step] = exchange(block, "ka", step, parts)
            moved.append([found])
        order = [0] + order
    else:
        groups, sources = -(-times // TILE), 1
        order = [0]
        padding = groups * TILE - times
        moved = []
        for x in (green_row, screened):
            x = lax.all_to_all(x, "ka", split_axis=0, concat_axis=0, tiled=True)
            x = x.reshape(parts, times, local, width).transpose(1, 0, 2, 3).reshape(times, points, width)
            x = jnp.pad(x, ((0, padding), (0, 0), (0, 0))).reshape(groups, TILE * points, width)
            moved.append([{0: x[group]} for group in range(groups)])
        weights = jnp.pad(weights, (0, padding))
    weights = jnp.broadcast_to(weights.reshape(groups, TILE, 1), (groups, TILE, width))

    early = order[: max(1, len(order) - LATE)]
    late = order[len(early) :]
    own_greens = roll_own(green_row)
    partial_value = None
    for group in range(groups):
        green, screen = moved[0][group], moved[1][group]
        lattice, greens = forward(seat, [green[step] for step in order], order, sources)
        work = early_lines(
            seat, lattice, weights[group], own_greens, [screen[step] for step in early], early, sources
        )
        share = hubbard / (points * blocks) if group == 0 else 0.0
        term = backward(
            seat, lattice, weights[group], equal_time, greens, [screen[step] for step in late], work,
            late, sources, share,
        )
        partial_value = term if partial_value is None else partial_value + term

    owners = [partner_of(place, step, parts) for step in range(parts)]
    pieces = [lax.dynamic_slice_in_dim(partial_value, owner * local, local) for owner in owners]
    if parts % 2 == 0 and parts & (parts - 1) == 0:
        pairs = jnp.concatenate([pieces[step] for step in range(1, parts, 2)], axis=0)
        pairs = exchange(pairs, "ka", 1, parts)
        mine = jnp.concatenate([pieces[step] for step in range(0, parts, 2)], axis=0) + pairs
        pieces = [mine[n * local : (n + 1) * local] for n in range(parts // 2)]
        collision = tree_sum(
            pieces[:1] + [exchange(pieces[n], "ka", 2 * n, parts) for n in range(parts // 2 - 1, 0, -1)]
        )
    else:
        collision = tree_sum(
            pieces[:1] + [exchange(pieces[step], "ka", step, parts) for step in range(1, parts)]
        )
    collision = tree_sum(
        [collision] + [exchange(collision, "hist", step, blocks) for step in range(blocks - 1, 0, -1)]
    )
    return propagate(own_greens, hamilton + collision)


def solution(mesh):
    in_specs = (
        P("hist", "ka", None),
        P("hist", "ka", None),
        P("ka", None),
        P("ka", None),
        P("hist"),
        P("hist"),
    )
    out_specs = P("hist", "ka", None)
    return jax.shard_map(
        functools.partial(per_device, mesh.shape["ka"], mesh.shape["hist"]),
        mesh=mesh,
        in_specs=in_specs,
        out_specs=out_specs,
        check_vma=False,
    )
```

```python
import functools
import math

import jax
import jax.numpy as jnp
import ml_dtypes
import numpy as np
from jax import lax
from jax.experimental import pallas as pl
from jax.experimental.pallas import tpu as pltpu
from jax.sharding import PartitionSpec as P

SIDE = 24
BANDS = 8
ENTRIES = BANDS * BANDS
WIDTH = 2 * ENTRIES
TILE = 8
STEPS = 4

time_step = 0.1
hubbard = 1.0
quadrature = (0.375, 1.1666666, 0.9583333, 1.0)

LATE = 3
AHEAD = 3


def lane_sign(shape):
    lane = lax.broadcasted_iota(jnp.int32, shape, len(shape) - 1)
    return lane < ENTRIES


def swap(x):
    return pltpu.roll(x, ENTRIES, 1)


def roll_blocks(x, blocks):
    return x if blocks == 0 else pltpu.roll(x, WIDTH - BANDS * blocks, x.ndim - 1)


def tree_sum(terms):
    while len(terms) > 1:
        terms = [sum(terms[i : i + 2][1:], terms[i]) for i in range(0, len(terms), 2)]
    return terms[0]


def merge_lanes(values):
    lane = lax.broadcasted_iota(jnp.int32, values[0].shape, 1)
    while len(values) > 1:
        half = len(values) // 2
        lower = lane & half == 0
        merged = []
        for x, y in zip(values[:half], values[half:]):
            rest = jnp.where(lower, y, x)
            other = jnp.where(lower, pltpu.roll(rest, WIDTH - half, 1), pltpu.roll(rest, half, 1))
            merged.append(jnp.where(lower, x, y) + other)
        values = merged
    return values[0]


def split(x):
    high = x.astype(jnp.bfloat16)
    return jnp.concatenate([high, (x - high.astype(jnp.float32)).astype(jnp.bfloat16)], axis=1)


def dft24(x, sign, low):
    root3 = jnp.where(low, -1.0, 1.0) * (sign * math.sqrt(3.0) / 2)
    turn = jnp.where(low, -1.0, 1.0) * float(sign)
    half = math.sqrt(0.5)
    turn_half = turn * half
    columns = [[None] * 8 for _ in range(3)]
    for n2 in range(8):
        x0, x1, x2 = (x[(8 * n1 + 3 * n2) % 24] for n1 in range(3))
        total = x1 + x2
        base = x0 - 0.5 * total
        spin = swap(x1 - x2) * root3
        columns[0][n2] = x0 + total
        columns[1][n2] = base + spin
        columns[2][n2] = base - spin
    out = [None] * 24
    for k1 in range(3):
        c = columns[k1]
        a0, a1 = c[0] + c[4], c[0] - c[4]
        a2, a3 = c[2] + c[6], c[2] - c[6]
        a4, a5 = c[1] + c[5], c[1] - c[5]
        a6, a7 = c[3] + c[7], c[3] - c[7]
        b0, b1 = a0 + a2, a0 - a2
        b2, b3 = a4 + a6, a4 - a6
        i_a3 = swap(a3) * turn
        i_b3 = swap(b3) * turn
        c0, c1 = a1 + i_a3, a1 - i_a3
        p = (a5 - a7) * half
        m = swap(a5 + a7) * turn_half
        e, f = p + m, p - m
        values = [b0 + b2, c0 + e, b1 + i_b3, c1 - f, b0 - b2, c0 - e, b1 - i_b3, c1 + f]
        for k2 in range(8):
            out[(16 * k1 + 9 * k2) % 24] = values[k2]
    return out


def load_line(ref, line):
    stride = ref.shape[0] // TILE
    return [ref[pl.ds(line * SIDE + k2, TILE, stride=stride), :] for k2 in range(SIDE)]


def along_first(work_ref, sign, low, store):
    def load(column):
        return [work_ref[k1 * SIDE + column] for k1 in range(SIDE)]

    rows = load(0)
    for column in range(SIDE):
        following = load(column + 1) if column + 1 < SIDE else None
        for r1, value in enumerate(dft24(rows, sign, low)):
            store(r1 * SIDE + column, value)
        rows = following


def roll_kernel(green_ref, greens_ref):
    batch = math.gcd(green_ref.shape[0], STEPS)

    def rolls(n, carry):
        times = pl.ds(n * batch, batch)
        green = green_ref[times]
        rolled = [roll_blocks(green, j) for j in range(STEPS)]
        for j in range(STEPS):
            greens_ref[j, times] = rolled[j]
        return carry

    lax.fori_loop(0, green_ref.shape[0] // batch, rolls, 0)


def forward_kernel(steps, parts, place_ref, *refs):
    block_refs, (lattice_ref, greens_ref, work_ref) = refs[: len(steps)], refs[len(steps) :]
    low = lane_sign((TILE, WIDTH))
    place = place_ref[0]
    rows = block_refs[0].shape[0]
    lines = rows // (TILE * SIDE)
    for step, green_ref in zip(steps, block_refs):
        owner = partner_of(place, step, parts)

        def along_second(i, carry):
            for r2, value in enumerate(dft24(load_line(green_ref, i), -1, low)):
                work_ref[(owner * lines + i) * SIDE + r2] = value
            return carry

        lax.fori_loop(0, lines, along_second, 0, unroll=lines <= 4)
        green = green_ref[...]
        spot = pl.ds(pl.multiple_of(owner * rows, TILE), rows)
        for j in range(STEPS):
            greens_ref[j, spot, :] = roll_blocks(green, j)

    def store(point, value):
        lattice_ref[point] = value

    along_first(work_ref, -1, low, store)


def product_lines(steps, parts, place, lattice_ref, weights, screen_refs, work_ref):
    low = lane_sign((TILE, WIDTH))
    turn = jnp.where(low, -1.0, 1.0)
    lines = screen_refs[0].shape[0] // (TILE * SIDE)

    def load(screen_ref, step, i):
        line = partner_of(place, step, parts) * lines + i
        rows = []
        for r2, value in enumerate(load_line(screen_ref, i)):
            screen = value * weights
            other = swap(screen)
            lattice = lattice_ref[line * SIDE + r2]
            rows.append(
                swap(lattice) * turn * jnp.where(low, screen, other)
                - lattice * jnp.where(low, other, screen)
            )
        return line, rows

    def store(line, rows):
        for k2, value in enumerate(dft24(rows, 1, low)):
            work_ref[line * SIDE + k2] = value

    if lines > 4:
        for screen_ref, step in zip(screen_refs, steps):
            lax.fori_loop(0, lines, lambda i, carry: store(*load(screen_ref, step, i)), None)
        return
    for screen_ref, step in zip(screen_refs, steps):
        for i in range(lines):
            store(*load(screen_ref, step, i))


def early_kernel(steps, parts, place_ref, lattice_ref, weight_ref, _, *refs):
    *screen_refs, work_ref = refs
    product_lines(steps, parts, place_ref[0], lattice_ref, weight_ref[...], screen_refs, work_ref)


def backward_kernel(
    steps, parts, share, place_ref, lattice_ref, weight_ref, equal_ref, sign_ref, gather_ref, greens_ref, *refs
):
    screen_refs, refs = refs[: len(steps)], refs[len(steps) :]
    _, partial_ref, work_ref, sigma_ref, sums_ref = refs
    points = SIDE * SIDE
    low = lane_sign((TILE, WIDTH))
    if steps:
        product_lines(steps, parts, place_ref[0], lattice_ref, weight_ref[...], screen_refs, work_ref)

    def store(point, value):
        sigma_ref[pl.ds(point * TILE, TILE), :] = value

    along_first(work_ref, 1, low, store)

    block = points // parts
    tiles = block // TILE
    batch = max(n for n in range(1, 10) if tiles % n == 0)

    def contract(group, carry):
        first = group * batch
        green_row = (first // tiles) * TILE * block + (first % tiles) * TILE
        units = [(tile, s) for tile in range(batch) for s in range(TILE)]

        def prepare(tile, s):
            sigma = sigma_ref[pl.ds((first + tile) * TILE * TILE + s, TILE, stride=TILE), :]
            row = pl.multiple_of(green_row + s * block + tile * TILE, TILE)
            return (
                [roll_blocks(sigma, STEPS * i) for i in range(STEPS)],
                [greens_ref[j, pl.ds(row, TILE), :] for j in range(STEPS)],
            )

        ready = [prepare(*unit) for unit in units[:AHEAD]]
        for n, (tile, s) in enumerate(units):
            if n + AHEAD < len(units):
                ready.append(prepare(*units[n + AHEAD]))
            sigmas, greens = ready.pop(0)
            terms = [sigma * green for sigma in sigmas for green in greens]
            sums = terms if s == 0 else [a + b for a, b in zip(sums, terms)]
            if s == TILE - 1:
                folded = [
                    jnp.where(low, sums[2 * q], sums[2 * q + 1])
                    + sign_ref[q] * swap(jnp.where(low, sums[2 * q + 1], sums[2 * q]))
                    for q in range(BANDS)
                ]
                row = pl.ds(pl.multiple_of((first + tile) * TILE, TILE), TILE)
                sums_ref[row, :] = merge_lanes(folded)
        return carry

    lax.fori_loop(0, points // (TILE * batch), contract, 0)

    lane = lax.broadcasted_iota(jnp.int32, equal_ref.shape, 1)
    inner = lane - ENTRIES
    occupied = jnp.sum(jnp.where((inner >= 0) & (inner % (BANDS + 1) == 0), equal_ref[...], 0.0))
    spots = lax.broadcasted_iota(jnp.int32, (points, WIDTH), 1)
    on_diagonal = (spots < ENTRIES) & (spots % (BANDS + 1) == 0)
    total = jnp.dot(split(sums_ref[...]), gather_ref[...], preferred_element_type=jnp.float32)
    partial_ref[...] = total + jnp.where(on_diagonal, occupied * share, 0.0)


def propagate_kernel(greens_ref, effective_ref, spread_ref, out_ref, factor_ref, held_ref, sems):
    _, history, points, _ = greens_ref.shape
    factor_ref[...] = jnp.dot(
        split(effective_ref[...] * time_step), spread_ref[...], preferred_element_type=jnp.float32
    )

    slots, chunk = held_ref.shape[:2]

    def copy(number, slot):
        return pltpu.make_async_copy(
            held_ref.at[slot], out_ref.at[pl.ds(number * chunk, chunk)], sems.at[slot]
        )

    def advance(group, carry):
        for slot in range(slots):
            number = group * slots + slot

            @pl.when(group > 0)
            def _():
                copy(number - slots, slot).wait()

            batch = math.gcd(chunk, 4)
            pending = None
            for start in range(0, points, TILE):
                stop = min(start + TILE, points)
                for first in range(0, chunk, batch):
                    times = pl.ds(number * chunk + first, batch)
                    greens = [greens_ref[j, times, start:stop, :] for j in range(STEPS)]
                    terms = [greens[0]]
                    for i in range(STEPS):
                        total = None
                        for j in range(STEPS):
                            spot = STEPS * i + j
                            factor = factor_ref[start:stop, spot * WIDTH : (spot + 1) * WIDTH]
                            term = factor[None] * greens[j]
                            total = term if total is None else total + term
                        terms.append(roll_blocks(total, STEPS * i))
                    if pending is not None:
                        held_ref[pending[0]] = tree_sum(pending[1])
                    pending = ((slot, slice(first, first + batch), slice(start, stop)), terms)
            held_ref[pending[0]] = tree_sum(pending[1])
            copy(number, slot).start()
        return carry

    groups = history // (chunk * slots)
    lax.fori_loop(0, groups, advance, 0)
    for slot in range(slots):
        copy((groups - 1) * slots + slot, slot).wait()


def gather_tables():
    blocks = 2 * BANDS
    table = np.zeros((2, blocks, BANDS, 2, BANDS, BANDS), np.float32)
    signs = np.zeros((BANDS, TILE, blocks, BANDS), np.float32)
    for pair in range(BANDS):
        for p in range(blocks):
            i, j = divmod(2 * pair + p // BANDS, STEPS)
            h, a = divmod((p + STEPS * i) % blocks, BANDS)
            g, c = divmod((p + j) % blocks, BANDS)
            table[:, p, pair, h ^ g, a, c] = 1 if (h, g) == (0, 1) else -1
            signs[pair, :, p] = 1 if h == g else -1
    return signs.reshape(BANDS, TILE, WIDTH), table.reshape(2 * WIDTH, WIDTH).astype(ml_dtypes.bfloat16)


def spread_table():
    blocks = 2 * BANDS
    table = np.zeros((2, BANDS, BANDS, STEPS, STEPS, blocks, BANDS), np.float32)
    for i in range(STEPS):
        for j in range(STEPS):
            for p in range(blocks):
                h, a = divmod((p - STEPS * i) % blocks, BANDS)
                g, b = divmod((p + j) % blocks, BANDS)
                table[1 if h == g else 0, a, b, i, j, p, :] = -1 if (h, g) == (1, 0) else 1
    return np.tile(table.reshape(WIDTH, -1), (2, 1)).astype(ml_dtypes.bfloat16)


def in_vmem():
    return pl.BlockSpec(memory_space=pltpu.VMEM)


def in_smem():
    return pl.BlockSpec(memory_space=pltpu.SMEM)


def anywhere():
    return pl.BlockSpec(memory_space=pl.ANY)


def params(megabytes):
    return pltpu.CompilerParams(vmem_limit_bytes=megabytes * 1024 * 1024)


def cost(per_element, arrays):
    size = SIDE * SIDE * TILE * WIDTH
    return pl.CostEstimate(flops=per_element * size, bytes_accessed=4 * arrays * size, transcendentals=0)


def forward(place, greens, steps, parts):
    points = SIDE * SIDE
    return pl.pallas_call(
        functools.partial(forward_kernel, steps, parts),
        out_shape=[
            jax.ShapeDtypeStruct((points, TILE, WIDTH), jnp.float32),
            jax.ShapeDtypeStruct((STEPS, TILE * points, WIDTH), jnp.float32),
        ],
        in_specs=[in_smem()] + [in_vmem()] * len(steps),
        out_specs=[in_vmem()] * 2,
        scratch_shapes=[pltpu.VMEM((points, TILE, WIDTH), jnp.float32)],
        compiler_params=params(6),
        cost_estimate=cost(400, 6),
        name="forward",
    )(place, *greens)


def early_lines(place, lattice, weights, before, screens, steps, parts):
    points = SIDE * SIDE
    return pl.pallas_call(
        functools.partial(early_kernel, steps, parts),
        out_shape=jax.ShapeDtypeStruct((points, TILE, WIDTH), jnp.float32),
        in_specs=[in_smem(), in_vmem(), in_vmem(), anywhere()] + [in_vmem()] * len(steps),
        out_specs=in_vmem(),
        compiler_params=params(4),
        cost_estimate=cost(150, 3),
        name="early",
    )(place, lattice, weights, before, *screens)


def backward(place, lattice, weights, equal_time, greens, screens, work, steps, parts, share):
    points = SIDE * SIDE
    signs, gather = gather_tables()
    inputs = (place, lattice, weights, equal_time, jnp.asarray(signs), jnp.asarray(gather), greens, *screens, work)
    partial_value, _ = pl.pallas_call(
        functools.partial(backward_kernel, steps, parts, share),
        out_shape=[
            jax.ShapeDtypeStruct((points, WIDTH), jnp.float32),
            jax.ShapeDtypeStruct((points, TILE, WIDTH), jnp.float32),
        ],
        in_specs=[in_smem()] + [in_vmem()] * (7 + len(steps)),
        out_specs=[in_vmem()] * 2,
        input_output_aliases={len(inputs) - 1: 1},
        scratch_shapes=[
            pltpu.VMEM((TILE * points, WIDTH), jnp.float32),
            pltpu.VMEM((points, WIDTH), jnp.float32),
        ],
        compiler_params=params(8),
        cost_estimate=cost(800, 6),
        name="backward",
    )(*inputs)
    return partial_value


def roll_own(greens):
    return pl.pallas_call(
        roll_kernel,
        out_shape=jax.ShapeDtypeStruct((STEPS, *greens.shape), jnp.float32),
        in_specs=[in_vmem()],
        out_specs=in_vmem(),
        compiler_params=params(4),
        cost_estimate=cost(3, 5),
        name="roll_own",
    )(greens)


def propagate(greens, effective):
    _, history, points, width = greens.shape
    chunk = math.gcd(history // 2, TILE)
    spread = spread_table()
    return pl.pallas_call(
        propagate_kernel,
        out_shape=jax.ShapeDtypeStruct(greens.shape[1:], jnp.float32),
        in_specs=[in_vmem()] * 3,
        out_specs=anywhere(),
        scratch_shapes=[
            pltpu.VMEM((points, spread.shape[1]), jnp.float32),
            pltpu.VMEM((2, chunk, points, width), jnp.float32),
            pltpu.SemaphoreType.DMA((2,)),
        ],
        compiler_params=params(6),
        cost_estimate=cost(32, 5),
        name="propagate",
    )(greens, effective, jnp.asarray(spread))


def partner_of(place, step, count):
    if count == 1:
        return 0
    if count & (count - 1) == 0:
        return place ^ step
    return (place + step) % count


def exchange(value, axis, step, count):
    pairs = [(place, partner_of(place, step, count)) for place in range(count)]
    return lax.ppermute(value, axis, pairs)


def exchange_order(count):
    along = {}
    for step in range(1, count):
        along.setdefault(step // 2, []).append(step)
    single = [along[n] for n in along if n and n & (n - 1) == 0]
    mixed = [along[n] for n in along if n & (n - 1)]
    order = [step for steps in zip(*single[::-1]) for step in steps]
    return order + [step for steps in mixed for step in steps] + along[0]


def class_weights(quad_class):
    table = jnp.array(quadrature, jnp.float32)
    match = quad_class[:, None] == jnp.arange(4, dtype=jnp.int32)[None, :]
    return jnp.sum(jnp.where(match, table[None, :], jnp.float32(0.0)), axis=1)


def per_device(parts, blocks, green_row, screened, hamilton, equal_time, quad_class, live_count):
    history, local, width = green_row.shape
    points = local * parts
    times = history // parts
    place = lax.axis_index("ka")
    seat = place.reshape(1)
    position = jnp.arange(history, dtype=jnp.int32)
    weights = jnp.where(
        position < live_count[0], time_step * class_weights(quad_class), jnp.float32(0.0)
    ) * jnp.float32(1.0 / points)
    weights = lax.dynamic_slice_in_dim(weights, place * times, times)

    if times == TILE and local % SIDE == 0:
        groups, sources = 1, parts
        order = exchange_order(parts)
        moved = []
        for x in (green_row, screened):
            whole = x.reshape(parts * TILE * local, width)
            found = {}
            for step in [0] + order:
                start = partner_of(place, step, parts) * (TILE * local)
                block = lax.dynamic_slice_in_dim(whole, start, TILE * local)
                found[step] = exchange(block, "ka", step, parts) if step else block
            moved.append([found])
        order = [0] + order
    else:
        groups, sources = -(-times // TILE), 1
        order = [0]
        padding = groups * TILE - times
        moved = []
        for x in (green_row, screened):
            x = lax.all_to_all(x, "ka", split_axis=0, concat_axis=0, tiled=True)
            x = x.reshape(parts, times, local, width).transpose(1, 0, 2, 3).reshape(times, points, width)
            x = jnp.pad(x, ((0, padding), (0, 0), (0, 0))).reshape(groups, TILE * points, width)
            moved.append([{0: x[group]} for group in range(groups)])
        weights = jnp.pad(weights, (0, padding))
    weights = jnp.broadcast_to(weights.reshape(groups, TILE, 1), (groups, TILE, width))

    early = order[: max(1, len(order) - LATE)]
    late = order[len(early) :]
    own_greens = roll_own(green_row)
    partial_value = None
    for group in range(groups):
        green, screen = moved[0][group], moved[1][group]
        lattice, greens = forward(seat, [green[step] for step in order], order, sources)
        work = early_lines(
            seat, lattice, weights[group], own_greens, [screen[step] for step in early], early, sources
        )
        share = hubbard / (points * blocks) if group == 0 else 0.0
        term = backward(
            seat, lattice, weights[group], equal_time, greens, [screen[step] for step in late], work,
            late, sources, share,
        )
        partial_value = term if partial_value is None else partial_value + term

    owners = [partner_of(place, step, parts) for step in range(parts)]
    pieces = [lax.dynamic_slice_in_dim(partial_value, owner * local, local) for owner in owners]
    if parts % 2 == 0 and parts & (parts - 1) == 0:
        pairs = jnp.concatenate([pieces[step] for step in range(1, parts, 2)], axis=0)
        pairs = exchange(pairs, "ka", 1, parts)
        mine = jnp.concatenate([pieces[step] for step in range(0, parts, 2)], axis=0) + pairs
        pieces = [mine[n * local : (n + 1) * local] for n in range(parts // 2)]
        collision = tree_sum(
            pieces[:1] + [exchange(pieces[n], "ka", 2 * n, parts) for n in range(parts // 2 - 1, 0, -1)]
        )
    else:
        collision = tree_sum(
            pieces[:1] + [exchange(pieces[step], "ka", step, parts) for step in range(1, parts)]
        )
    collision = tree_sum(
        [collision] + [exchange(collision, "hist", step, blocks) for step in range(blocks - 1, 0, -1)]
    )
    return propagate(own_greens, hamilton + collision)


def solution(mesh):
    in_specs = (
        P("hist", "ka", None),
        P("hist", "ka", None),
        P("ka", None),
        P("ka", None),
        P("hist"),
        P("hist"),
    )
    out_specs = P("hist", "ka", None)
    return jax.shard_map(
        functools.partial(per_device, mesh.shape["ka"], mesh.shape["hist"]),
        mesh=mesh,
        in_specs=in_specs,
        out_specs=out_specs,
        check_vma=False,
    )
```

```python
import functools
import math

import jax
import jax.numpy as jnp
import ml_dtypes
import numpy as np
from jax import lax
from jax.experimental import pallas as pl
from jax.experimental.pallas import tpu as pltpu
from jax.sharding import PartitionSpec as P

SIDE = 24
BANDS = 8
ENTRIES = BANDS * BANDS
WIDTH = 2 * ENTRIES
TILE = 8
BABY, GIANT = 8, 2

time_step = 0.1
hubbard = 1.0
quadrature = (0.375, 1.1666666, 0.9583333, 1.0)

ROLLED = 192
HANDED = 2
LATE = 2


def lane_sign(shape):
    lane = lax.broadcasted_iota(jnp.int32, shape, len(shape) - 1)
    return lane < ENTRIES


def swap(x):
    return pltpu.roll(x, ENTRIES, 1)


def roll_blocks(x, blocks):
    return x if blocks == 0 else pltpu.roll(x, WIDTH - BANDS * blocks, x.ndim - 1)


def tree_sum(terms):
    while len(terms) > 1:
        terms = [sum(terms[i : i + 2][1:], terms[i]) for i in range(0, len(terms), 2)]
    return terms[0]


def split(x):
    high = x.astype(jnp.bfloat16)
    return jnp.concatenate([high, (x - high.astype(jnp.float32)).astype(jnp.bfloat16)], axis=1)


def dft24(x, sign, low):
    root3 = jnp.where(low, -1.0, 1.0) * (sign * math.sqrt(3.0) / 2)
    turn = jnp.where(low, -1.0, 1.0) * float(sign)
    half = math.sqrt(0.5)
    turn_half = turn * half
    columns = [[None] * 8 for _ in range(3)]
    for n2 in range(8):
        x0, x1, x2 = (x[(8 * n1 + 3 * n2) % 24] for n1 in range(3))
        total = x1 + x2
        base = x0 - 0.5 * total
        spin = swap(x1 - x2) * root3
        columns[0][n2] = x0 + total
        columns[1][n2] = base + spin
        columns[2][n2] = base - spin
    out = [None] * 24
    for k1 in range(3):
        c = columns[k1]
        a0, a1 = c[0] + c[4], c[0] - c[4]
        a2, a3 = c[2] + c[6], c[2] - c[6]
        a4, a5 = c[1] + c[5], c[1] - c[5]
        a6, a7 = c[3] + c[7], c[3] - c[7]
        b0, b1 = a0 + a2, a0 - a2
        b2, b3 = a4 + a6, a4 - a6
        i_a3 = swap(a3) * turn
        i_b3 = swap(b3) * turn
        c0, c1 = a1 + i_a3, a1 - i_a3
        p = (a5 - a7) * half
        m = swap(a5 + a7) * turn_half
        e, f = p + m, p - m
        values = [b0 + b2, c0 + e, b1 + i_b3, c1 - f, b0 - b2, c0 - e, b1 - i_b3, c1 + f]
        for k2 in range(8):
            out[(16 * k1 + 9 * k2) % 24] = values[k2]
    return out


def fenced(place):
    return pl.when(place >= 0)


def load_line(ref, line):
    stride = ref.shape[0] // TILE
    return [ref[pl.ds(line * SIDE + k2, TILE, stride=stride), :] for k2 in range(SIDE)]


def along_first(work_ref, sign, low, store):
    def columns(pair, carry):
        both = (2 * pair, 2 * pair + 1)
        rows = [[work_ref[k1 * SIDE + column] for k1 in range(SIDE)] for column in both]
        values = [dft24(row, sign, low) for row in rows]
        for column, value in zip(both, values):
            for r1 in range(SIDE):
                store(r1 * SIDE + column, value[r1])
        return carry

    lax.fori_loop(0, SIDE // 2, columns, 0)


def roll_kernel(place_ref, green_ref, whole_ref, greens_ref, block_ref, *, step, parts):
    rows = block_ref.shape[0]
    block_ref[...] = whole_ref[pl.ds(pl.multiple_of(partner_of(place_ref[0], step, parts) * rows, TILE), rows), :]
    batch = math.gcd(green_ref.shape[0], 4)

    def rolls(n, carry):
        times = pl.ds(n * batch, batch)
        green = green_ref[times]
        rolled = [roll_blocks(green, j) for j in range(BABY)]
        for j in range(BABY):
            greens_ref[j, times] = rolled[j]
        return carry

    lax.fori_loop(0, green_ref.shape[0] // batch, rolls, 0)


def forward_kernel(steps, parts, place_ref, *refs):
    block_refs, (lattice_ref, greens_ref, work_ref) = refs[: len(steps)], refs[len(steps) :]
    low = lane_sign((TILE, WIDTH))
    place = place_ref[0]
    rows = block_refs[0].shape[0]
    lines = rows // (TILE * SIDE)
    for step, green_ref in zip(steps, block_refs):
        owner = partner_of(place, step, parts)

        def along_second(i, carry):
            for r2, value in enumerate(dft24(load_line(green_ref, i), -1, low)):
                work_ref[(owner * lines + i) * SIDE + r2] = value
            return carry

        @fenced(place)
        def _():
            lax.fori_loop(0, lines, along_second, 0, unroll=lines <= 4)

    def store(point, value):
        lattice_ref[point] = value

    along_first(work_ref, -1, low, store)

    for step, green_ref in zip(steps, block_refs):

        def rolls(n, carry):
            green = green_ref[pl.ds(n * ROLLED, ROLLED), :]
            start = partner_of(place, step, parts) * rows + n * ROLLED
            spot = pl.ds(pl.multiple_of(start, TILE), ROLLED)
            for j in range(BABY):
                greens_ref[j, spot, :] = roll_blocks(green, j)
            return carry

        lax.fori_loop(0, rows // ROLLED, rolls, 0)


def product_lines(steps, parts, place, lattice_ref, weights, screen_refs, work_ref):
    low = lane_sign((TILE, WIDTH))
    turn = jnp.where(low, -1.0, 1.0)
    lines = screen_refs[0].shape[0] // (TILE * SIDE)

    def load(screen_ref, step, i):
        line = partner_of(place, step, parts) * lines + i
        rows = []
        for r2, value in enumerate(load_line(screen_ref, i)):
            screen = value * weights
            other = swap(screen)
            lattice = lattice_ref[line * SIDE + r2]
            rows.append(
                swap(lattice) * turn * jnp.where(low, screen, other)
                - lattice * jnp.where(low, other, screen)
            )
        return line, rows

    def store(line, rows):
        for k2, value in enumerate(dft24(rows, 1, low)):
            work_ref[line * SIDE + k2] = value

    for screen_ref, step in zip(screen_refs, steps):

        @fenced(place)
        def _():
            lax.fori_loop(
                0, lines, lambda i, carry: store(*load(screen_ref, step, i)), None, unroll=lines <= 4
            )


def early_kernel(steps, parts, place_ref, lattice_ref, weight_ref, *refs):
    *screen_refs, work_ref = refs
    product_lines(steps, parts, place_ref[0], lattice_ref, weight_ref[...], screen_refs, work_ref)


def backward_kernel(
    steps, parts, share, place_ref, lattice_ref, weight_ref, equal_ref, sign_ref, gather_ref, greens_ref, *refs
):
    screen_refs, refs = refs[: len(steps)], refs[len(steps) :]
    _, partial_ref, work_ref, sigma_ref, sums_ref, pieces_ref = refs
    points = SIDE * SIDE
    low = lane_sign((TILE, WIDTH))
    if steps:
        product_lines(steps, parts, place_ref[0], lattice_ref, weight_ref[...], screen_refs, work_ref)

    def store(point, value):
        sigma_ref[pl.ds(point * TILE, TILE), :] = value

    along_first(work_ref, 1, low, store)

    block = points // parts
    tiles = block // TILE
    batch = max(n for n in (1, 2, 3) if tiles % n == 0)

    def contract(group, carry):
        first = group * batch
        green_row = (first // tiles) * TILE * block + (first % tiles) * TILE
        values = []
        for tile in range(batch):
            sums = None
            for s in range(TILE):
                sigma = sigma_ref[pl.ds((first + tile) * TILE * TILE + s, TILE, stride=TILE), :]
                row = pl.ds(pl.multiple_of(green_row + s * block + tile * TILE, TILE), TILE)
                greens = [greens_ref[j, row, :] for j in range(BABY)]
                terms = [part * green for part in (sigma, swap(sigma)) for green in greens]
                sums = terms if s == 0 else [a + b for a, b in zip(sums, terms)]
            row = pl.ds(pl.multiple_of((first + tile) * TILE, TILE), TILE)
            for spot, value in enumerate(sums):
                sums_ref[row, spot * WIDTH : (spot + 1) * WIDTH] = value
        return carry

    lax.fori_loop(0, points // (TILE * batch), contract, 0)

    lane = lax.broadcasted_iota(jnp.int32, equal_ref.shape, 1)
    inner = lane - ENTRIES
    occupied = jnp.sum(jnp.where((inner >= 0) & (inner % (BANDS + 1) == 0), equal_ref[...], 0.0))
    spots = lax.broadcasted_iota(jnp.int32, (points, WIDTH), 1)
    on_diagonal = (spots < ENTRIES) & (spots % (BANDS + 1) == 0)
    lower = spots < ENTRIES
    for pair in range(BABY * GIANT // 2):
        first_part = sums_ref[:, 2 * pair * WIDTH : (2 * pair + 1) * WIDTH]
        second_part = sums_ref[:, (2 * pair + 1) * WIDTH : (2 * pair + 2) * WIDTH]
        folded = jnp.where(lower, first_part, second_part) + sign_ref[pair : pair + 1, :] * swap(
            jnp.where(lower, second_part, first_part)
        )
        coarse = folded.astype(jnp.bfloat16)
        fine = (folded - coarse.astype(jnp.float32)).astype(jnp.bfloat16)
        pieces_ref[:, 2 * pair * WIDTH : (2 * pair + 1) * WIDTH] = coarse
        pieces_ref[:, (2 * pair + 1) * WIDTH : (2 * pair + 2) * WIDTH] = fine
    total = jnp.dot(pieces_ref[...], gather_ref[...], preferred_element_type=jnp.float32)
    partial_ref[...] = total + jnp.where(on_diagonal, occupied * share, 0.0)


def propagate_kernel(greens_ref, effective_ref, spread_ref, out_ref, factor_ref, held_ref, sems):
    _, history, points, _ = greens_ref.shape
    factor_ref[...] = jnp.dot(
        split(effective_ref[...] * time_step), spread_ref[...], preferred_element_type=jnp.float32
    )

    slots, chunk = held_ref.shape[:2]

    def copy(number, slot):
        return pltpu.make_async_copy(
            held_ref.at[slot], out_ref.at[pl.ds(number * chunk, chunk)], sems.at[slot]
        )

    def advance(group, carry):
        for slot in range(slots):
            number = group * slots + slot

            @pl.when(group > 0)
            def _():
                copy(number - slots, slot).wait()

            for start in range(0, points, TILE):
                stop = min(start + TILE, points)
                greens = [greens_ref[j, pl.ds(number * chunk, chunk), start:stop, :] for j in range(BABY)]
                terms = [greens[0]]
                for i in range(GIANT):
                    total = None
                    for j in range(BABY):
                        spot = BABY * i + j
                        factor = factor_ref[start:stop, spot * WIDTH : (spot + 1) * WIDTH]
                        term = factor[None] * greens[j]
                        total = term if total is None else total + term
                    terms.append(roll_blocks(total, BABY * i))
                held_ref[slot, :, start:stop, :] = tree_sum(terms)
            copy(number, slot).start()
        return carry

    groups = history // (chunk * slots)
    lax.fori_loop(0, groups, advance, 0)
    for slot in range(slots):
        copy((groups - 1) * slots + slot, slot).wait()


def gather_tables():
    blocks = 2 * BANDS
    pairs = BABY * GIANT // 2
    table = np.zeros((pairs, 2, blocks, BANDS, 2, BANDS, BANDS), np.float32)
    signs = np.zeros((pairs, blocks, BANDS), np.float32)
    for pair in range(pairs):
        for p in range(blocks):
            i, j = divmod(2 * pair + p // BANDS, BABY)
            h, a = divmod((p + BABY * i) % blocks, BANDS)
            g, c = divmod((p + j) % blocks, BANDS)
            table[pair, :, p, :, h ^ g, a, c] = 1 if (h, g) == (0, 1) else -1
            signs[pair, p] = 1 if h == g else -1
    return signs.reshape(pairs, WIDTH), table.reshape(-1, WIDTH).astype(ml_dtypes.bfloat16)


def spread_table():
    blocks = 2 * BANDS
    table = np.zeros((2, BANDS, BANDS, GIANT, BABY, blocks, BANDS), np.float32)
    for i in range(GIANT):
        for j in range(BABY):
            for p in range(blocks):
                h, a = divmod((p - BABY * i) % blocks, BANDS)
                g, b = divmod((p + j) % blocks, BANDS)
                table[1 if h == g else 0, a, b, i, j, p, :] = -1 if (h, g) == (1, 0) else 1
    return np.tile(table.reshape(WIDTH, -1), (2, 1)).astype(ml_dtypes.bfloat16)


def in_vmem():
    return pl.BlockSpec(memory_space=pltpu.VMEM)


def in_smem():
    return pl.BlockSpec(memory_space=pltpu.SMEM)


def anywhere():
    return pl.BlockSpec(memory_space=pl.ANY)


def params(megabytes):
    return pltpu.CompilerParams(vmem_limit_bytes=megabytes * 1024 * 1024)


def cost(per_element, arrays):
    size = SIDE * SIDE * TILE * WIDTH
    return pl.CostEstimate(flops=per_element * size, bytes_accessed=4 * arrays * size, transcendentals=0)


def forward(place, greens, steps, parts):
    points = SIDE * SIDE
    return pl.pallas_call(
        functools.partial(forward_kernel, steps, parts),
        out_shape=[
            jax.ShapeDtypeStruct((points, TILE, WIDTH), jnp.float32),
            jax.ShapeDtypeStruct((BABY, TILE * points, WIDTH), jnp.float32),
        ],
        in_specs=[in_smem()] + [in_vmem()] * len(steps),
        out_specs=[in_vmem()] * 2,
        scratch_shapes=[pltpu.VMEM((points, TILE, WIDTH), jnp.float32)],
        compiler_params=params(6),
        cost_estimate=cost(400, 6),
        name="forward",
    )(place, *greens)


def early_lines(place, lattice, weights, screens, steps, parts):
    points = SIDE * SIDE
    return pl.pallas_call(
        functools.partial(early_kernel, steps, parts),
        out_shape=jax.ShapeDtypeStruct((points, TILE, WIDTH), jnp.float32),
        in_specs=[in_smem(), in_vmem(), in_vmem()] + [in_vmem()] * len(steps),
        out_specs=in_vmem(),
        compiler_params=params(4),
        cost_estimate=cost(150, 3),
        name="early",
    )(place, lattice, weights, *screens)


def backward(place, lattice, weights, equal_time, greens, screens, work, steps, parts, share):
    points = SIDE * SIDE
    signs, gather = gather_tables()
    inputs = (place, lattice, weights, equal_time, jnp.asarray(signs), jnp.asarray(gather), greens, *screens, work)
    partial_value, _ = pl.pallas_call(
        functools.partial(backward_kernel, steps, parts, share),
        out_shape=[
            jax.ShapeDtypeStruct((points, WIDTH), jnp.float32),
            jax.ShapeDtypeStruct((points, TILE, WIDTH), jnp.float32),
        ],
        in_specs=[in_smem()] + [in_vmem()] * (7 + len(steps)),
        out_specs=[in_vmem()] * 2,
        input_output_aliases={len(inputs) - 1: 1},
        scratch_shapes=[
            pltpu.VMEM((TILE * points, WIDTH), jnp.float32),
            pltpu.VMEM((points, BABY * GIANT * WIDTH), jnp.float32),
            pltpu.VMEM((points, BABY * GIANT * WIDTH), jnp.bfloat16),
        ],
        compiler_params=params(16),
        cost_estimate=cost(800, 6),
        name="backward",
    )(*inputs)
    return partial_value


def roll_own(place, greens, whole, step, parts):
    rows = whole.shape[0] // parts
    return pl.pallas_call(
        functools.partial(roll_kernel, step=step, parts=parts),
        out_shape=[
            jax.ShapeDtypeStruct((BABY, *greens.shape), jnp.float32),
            jax.ShapeDtypeStruct((rows, whole.shape[1]), whole.dtype),
        ],
        in_specs=[in_smem(), in_vmem(), in_vmem()],
        out_specs=[in_vmem()] * 2,
        compiler_params=params(4),
        cost_estimate=cost(8, 9),
        name="roll_own",
    )(place, greens, whole)


def propagate(greens, effective):
    _, history, points, width = greens.shape
    chunk = math.gcd(history // 2, TILE)
    spread = spread_table()
    return pl.pallas_call(
        propagate_kernel,
        out_shape=jax.ShapeDtypeStruct(greens.shape[1:], jnp.float32),
        in_specs=[in_vmem()] * 3,
        out_specs=anywhere(),
        scratch_shapes=[
            pltpu.VMEM((points, spread.shape[1]), jnp.float32),
            pltpu.VMEM((2, chunk, points, width), jnp.float32),
            pltpu.SemaphoreType.DMA((2,)),
        ],
        compiler_params=params(6),
        cost_estimate=cost(32, 5),
        name="propagate",
    )(greens, effective, jnp.asarray(spread))


def partner_of(place, step, count):
    if count == 1:
        return 0
    if count & (count - 1) == 0:
        return place ^ step
    return (place + step) % count


def exchange(value, axis, step, count):
    pairs = [(place, partner_of(place, step, count)) for place in range(count)]
    return lax.ppermute(value, axis, pairs)


def exchange_order(count):
    along = {}
    for step in range(1, count):
        along.setdefault(step // 2, []).append(step)
    single = [along[n] for n in along if n and n & (n - 1) == 0]
    mixed = [along[n] for n in along if n & (n - 1)]
    order = [step for steps in zip(*single[::-1]) for step in steps]
    return order + along[0] + [step for steps in mixed for step in steps]


def class_weights(quad_class):
    table = jnp.array(quadrature, jnp.float32)
    match = quad_class[:, None] == jnp.arange(4, dtype=jnp.int32)[None, :]
    return jnp.sum(jnp.where(match, table[None, :], jnp.float32(0.0)), axis=1)


def per_device(parts, blocks, green_row, screened, hamilton, equal_time, quad_class, live_count):
    history, local, width = green_row.shape
    points = local * parts
    times = history // parts
    place = lax.axis_index("ka")
    seat = place.reshape(1)
    position = jnp.arange(history, dtype=jnp.int32)
    weights = jnp.where(
        position < live_count[0], time_step * class_weights(quad_class), jnp.float32(0.0)
    ) * jnp.float32(1.0 / points)
    weights = lax.dynamic_slice_in_dim(weights, place * times, times)

    if times == TILE and local % SIDE == 0:
        groups, sources = 1, parts
        order = exchange_order(parts)
        wholes = [x.reshape(parts * TILE * local, width) for x in (green_row, screened)]
        waiting = order[HANDED]
        own_greens, handed = roll_own(seat, green_row, wholes[1], waiting, parts)
        moved = []
        for whole in wholes:
            found = {}
            for step in [0] + order:
                start = partner_of(place, step, parts) * (TILE * local)
                block = lax.dynamic_slice_in_dim(whole, start, TILE * local)
                if whole is wholes[1] and step == waiting:
                    block = handed
                found[step] = exchange(block, "ka", step, parts) if step else block
            moved.append([found])
        order = [0] + order
    else:
        groups, sources = -(-times // TILE), 1
        order = [0]
        padding = groups * TILE - times
        moved = []
        for x in (green_row, screened):
            x = lax.all_to_all(x, "ka", split_axis=0, concat_axis=0, tiled=True)
            x = x.reshape(parts, times, local, width).transpose(1, 0, 2, 3).reshape(times, points, width)
            x = jnp.pad(x, ((0, padding), (0, 0), (0, 0))).reshape(groups, TILE * points, width)
            moved.append([{0: x[group]} for group in range(groups)])
        weights = jnp.pad(weights, (0, padding))
        own_greens, _ = roll_own(seat, green_row, screened.reshape(-1, width), 0, 1)
    weights = jnp.broadcast_to(weights.reshape(groups, TILE, 1), (groups, TILE, width))

    early = order[: max(1, len(order) - LATE)]
    late = order[len(early) :]
    partial_value = None
    for group in range(groups):
        green, screen = moved[0][group], moved[1][group]
        lattice, greens = forward(seat, [green[step] for step in order], order, sources)
        work = early_lines(seat, lattice, weights[group], [screen[step] for step in early], early, sources)
        share = hubbard / (points * blocks) if group == 0 else 0.0
        term = backward(
            seat, lattice, weights[group], equal_time, greens, [screen[step] for step in late], work,
            late, sources, share,
        )
        partial_value = term if partial_value is None else partial_value + term

    owners = [partner_of(place, step, parts) for step in range(parts)]
    pieces = [lax.dynamic_slice_in_dim(partial_value, owner * local, local) for owner in owners]
    if parts % 2 == 0 and parts & (parts - 1) == 0:
        pairs = jnp.concatenate([pieces[step] for step in range(1, parts, 2)], axis=0)
        pairs = exchange(pairs, "ka", 1, parts)
        mine = jnp.concatenate([pieces[step] for step in range(0, parts, 2)], axis=0) + pairs
        pieces = [mine[n * local : (n + 1) * local] for n in range(parts // 2)]
        collision = tree_sum(
            pieces[:1] + [exchange(pieces[n], "ka", 2 * n, parts) for n in range(parts // 2 - 1, 0, -1)]
        )
    else:
        collision = tree_sum(
            pieces[:1] + [exchange(pieces[step], "ka", step, parts) for step in range(1, parts)]
        )
    collision = tree_sum(
        [collision] + [exchange(collision, "hist", step, blocks) for step in range(blocks - 1, 0, -1)]
    )
    return propagate(own_greens, hamilton + collision)


def solution(mesh):
    in_specs = (
        P("hist", "ka", None),
        P("hist", "ka", None),
        P("ka", None),
        P("ka", None),
        P("hist"),
        P("hist"),
    )
    out_specs = P("hist", "ka", None)
    return jax.shard_map(
        functools.partial(per_device, mesh.shape["ka"], mesh.shape["hist"]),
        mesh=mesh,
        in_specs=in_specs,
        out_specs=out_specs,
        check_vma=False,
    )
```

```python
import functools
import math

import jax
import jax.numpy as jnp
import ml_dtypes
import numpy as np
from jax import lax
from jax.experimental import pallas as pl
from jax.experimental.pallas import tpu as pltpu
from jax.sharding import PartitionSpec as P

SIDE = 24
BANDS = 8
ENTRIES = BANDS * BANDS
WIDTH = 2 * ENTRIES
TILE = 8
STEPS = 4

time_step = 0.1
hubbard = 1.0
quadrature = (0.375, 1.1666666, 0.9583333, 1.0)

LATE = 2
AHEAD = 3


def lane_sign(shape):
    lane = lax.broadcasted_iota(jnp.int32, shape, len(shape) - 1)
    return lane < ENTRIES


def swap(x):
    return pltpu.roll(x, ENTRIES, 1)


def roll_blocks(x, blocks):
    return x if blocks == 0 else pltpu.roll(x, WIDTH - BANDS * blocks, x.ndim - 1)


def tree_sum(terms):
    while len(terms) > 1:
        terms = [sum(terms[i : i + 2][1:], terms[i]) for i in range(0, len(terms), 2)]
    return terms[0]


def split(x):
    high = x.astype(jnp.bfloat16)
    return jnp.concatenate([high, (x - high.astype(jnp.float32)).astype(jnp.bfloat16)], axis=1)


def dft24(x, sign, low):
    root3 = jnp.where(low, -1.0, 1.0) * (sign * math.sqrt(3.0) / 2)
    turn = jnp.where(low, -1.0, 1.0) * float(sign)
    half = math.sqrt(0.5)
    turn_half = turn * half
    columns = [[None] * 8 for _ in range(3)]
    for n2 in range(8):
        x0, x1, x2 = (x[(8 * n1 + 3 * n2) % 24] for n1 in range(3))
        total = x1 + x2
        base = x0 - 0.5 * total
        spin = swap(x1 - x2) * root3
        columns[0][n2] = x0 + total
        columns[1][n2] = base + spin
        columns[2][n2] = base - spin
    out = [None] * 24
    for k1 in range(3):
        c = columns[k1]
        a0, a1 = c[0] + c[4], c[0] - c[4]
        a2, a3 = c[2] + c[6], c[2] - c[6]
        a4, a5 = c[1] + c[5], c[1] - c[5]
        a6, a7 = c[3] + c[7], c[3] - c[7]
        b0, b1 = a0 + a2, a0 - a2
        b2, b3 = a4 + a6, a4 - a6
        i_a3 = swap(a3) * turn
        i_b3 = swap(b3) * turn
        c0, c1 = a1 + i_a3, a1 - i_a3
        p = (a5 - a7) * half
        m = swap(a5 + a7) * turn_half
        e, f = p + m, p - m
        values = [b0 + b2, c0 + e, b1 + i_b3, c1 - f, b0 - b2, c0 - e, b1 - i_b3, c1 + f]
        for k2 in range(8):
            out[(16 * k1 + 9 * k2) % 24] = values[k2]
    return out


def load_line(ref, line):
    stride = ref.shape[0] // TILE
    return [ref[pl.ds(line * SIDE + k2, TILE, stride=stride), :] for k2 in range(SIDE)]


def fetch(place, steps, block_refs, held_ref, sems):
    copies = []
    for slot, (step, source) in enumerate(zip(steps, block_refs)):
        rows = held_ref.shape[1]
        if step == 0 and source.shape[0] != rows:
            source = source.at[pl.ds(pl.multiple_of(place * rows, TILE), rows)]
        copies.append(pltpu.make_async_copy(source, held_ref.at[slot], sems.at[slot]))
        copies[-1].start()
    return copies


def along_first(work_ref, sign, low, store):
    def columns(pair, carry):
        both = (2 * pair, 2 * pair + 1)
        rows = [[work_ref[k1 * SIDE + column] for k1 in range(SIDE)] for column in both]
        values = [dft24(row, sign, low) for row in rows]
        for column, value in zip(both, values):
            for r1 in range(SIDE):
                store(r1 * SIDE + column, value[r1])
        return carry

    lax.fori_loop(0, SIDE // 2, columns, 0)


def roll_kernel(green_ref, greens_ref):
    batch = math.gcd(green_ref.shape[0], STEPS)

    def rolls(n, carry):
        times = pl.ds(n * batch, batch)
        green = green_ref[times]
        rolled = [roll_blocks(green, j) for j in range(STEPS)]
        for j in range(STEPS):
            greens_ref[j, times] = rolled[j]
        return carry

    lax.fori_loop(0, green_ref.shape[0] // batch, rolls, 0)


def forward_kernel(steps, parts, place_ref, *refs):
    block_refs, (lattice_ref, greens_ref, work_ref, held_ref, sems) = refs[: len(steps)], refs[len(steps) :]
    low = lane_sign((TILE, WIDTH))
    place = place_ref[0]
    copies = fetch(place, steps, block_refs, held_ref, sems)
    rows = held_ref.shape[1]
    lines = rows // (TILE * SIDE)
    for slot, step in enumerate(steps):
        copies[slot].wait()
        green_ref = held_ref.at[slot]
        owner = partner_of(place, step, parts)

        def along_second(i, carry):
            for r2, value in enumerate(dft24(load_line(green_ref, i), -1, low)):
                work_ref[(owner * lines + i) * SIDE + r2] = value
            return carry

        lax.fori_loop(0, lines, along_second, 0, unroll=lines <= 4)
        green = green_ref[...]
        spot = pl.ds(pl.multiple_of(owner * rows, TILE), rows)
        for j in range(STEPS):
            greens_ref[j, spot, :] = roll_blocks(green, j)

    def store(point, value):
        lattice_ref[point] = value

    along_first(work_ref, -1, low, store)


def product_lines(steps, parts, place, lattice_ref, weights, screen_refs, held_ref, sems, work_ref):
    low = lane_sign((TILE, WIDTH))
    turn = jnp.where(low, -1.0, 1.0)
    copies = fetch(place, steps, screen_refs, held_ref, sems)
    lines = held_ref.shape[1] // (TILE * SIDE)
    for slot, step in enumerate(steps):
        copies[slot].wait()
        screen_ref = held_ref.at[slot]
        first = partner_of(place, step, parts) * lines

        def along_second(i, carry):
            rows = []
            for r2, value in enumerate(load_line(screen_ref, i)):
                screen = value * weights
                other = swap(screen)
                lattice = lattice_ref[(first + i) * SIDE + r2]
                rows.append(
                    swap(lattice) * turn * jnp.where(low, screen, other)
                    - lattice * jnp.where(low, other, screen)
                )
            for k2, value in enumerate(dft24(rows, 1, low)):
                work_ref[(first + i) * SIDE + k2] = value
            return carry

        lax.fori_loop(0, lines, along_second, 0, unroll=lines <= 4)


def early_kernel(steps, parts, place_ref, lattice_ref, weight_ref, _, *refs):
    screen_refs, (work_ref, held_ref, sems) = refs[: len(steps)], refs[len(steps) :]
    product_lines(
        steps, parts, place_ref[0], lattice_ref, weight_ref[...], screen_refs, held_ref, sems, work_ref
    )


def backward_kernel(
    steps, parts, share, place_ref, lattice_ref, weight_ref, equal_ref, sign_ref, gather_ref, greens_ref, *refs
):
    screen_refs, refs = refs[: len(steps)], refs[len(steps) :]
    _, partial_ref, work_ref, sigma_ref, sums_ref, pieces_ref, *late = refs
    points = SIDE * SIDE
    low = lane_sign((TILE, WIDTH))
    if steps:
        held_ref, sems = late
        product_lines(
            steps, parts, place_ref[0], lattice_ref, weight_ref[...], screen_refs, held_ref, sems, work_ref
        )

    def store(point, value):
        sigma_ref[pl.ds(point * TILE, TILE), :] = value

    along_first(work_ref, 1, low, store)

    block = points // parts
    tiles = block // TILE
    batch = max(n for n in range(1, 10) if tiles % n == 0)

    def contract(group, carry):
        first = group * batch
        green_row = (first // tiles) * TILE * block + (first % tiles) * TILE
        units = [(tile, s) for tile in range(batch) for s in range(TILE)]

        def prepare(tile, s):
            sigma = sigma_ref[pl.ds((first + tile) * TILE * TILE + s, TILE, stride=TILE), :]
            row = pl.multiple_of(green_row + s * block + tile * TILE, TILE)
            return (
                [roll_blocks(sigma, STEPS * i) for i in range(STEPS)],
                [greens_ref[j, pl.ds(row, TILE), :] for j in range(STEPS)],
            )

        ready = [prepare(*unit) for unit in units[:AHEAD]]
        for n, (tile, s) in enumerate(units):
            if n + AHEAD < len(units):
                ready.append(prepare(*units[n + AHEAD]))
            sigmas, greens = ready.pop(0)
            terms = [sigma * green for sigma in sigmas for green in greens]
            sums = terms if s == 0 else [a + b for a, b in zip(sums, terms)]
            if s == TILE - 1:
                row = pl.ds(pl.multiple_of((first + tile) * TILE, TILE), TILE)
                for spot, value in enumerate(sums):
                    sums_ref[row, spot * WIDTH : (spot + 1) * WIDTH] = value
        return carry

    lax.fori_loop(0, points // (TILE * batch), contract, 0)

    lane = lax.broadcasted_iota(jnp.int32, equal_ref.shape, 1)
    inner = lane - ENTRIES
    occupied = jnp.sum(jnp.where((inner >= 0) & (inner % (BANDS + 1) == 0), equal_ref[...], 0.0))
    spots = lax.broadcasted_iota(jnp.int32, (points, WIDTH), 1)
    on_diagonal = (spots < ENTRIES) & (spots % (BANDS + 1) == 0)
    lower = spots < ENTRIES
    for pair in range(STEPS * STEPS // 2):
        first_part = sums_ref[:, 2 * pair * WIDTH : (2 * pair + 1) * WIDTH]
        second_part = sums_ref[:, (2 * pair + 1) * WIDTH : (2 * pair + 2) * WIDTH]
        folded = jnp.where(lower, first_part, second_part) + sign_ref[pair : pair + 1, :] * swap(
            jnp.where(lower, second_part, first_part)
        )
        coarse = folded.astype(jnp.bfloat16)
        fine = (folded - coarse.astype(jnp.float32)).astype(jnp.bfloat16)
        pieces_ref[:, 2 * pair * WIDTH : (2 * pair + 1) * WIDTH] = coarse
        pieces_ref[:, (2 * pair + 1) * WIDTH : (2 * pair + 2) * WIDTH] = fine
    total = jnp.dot(pieces_ref[...], gather_ref[...], preferred_element_type=jnp.float32)
    partial_ref[...] = total + jnp.where(on_diagonal, occupied * share, 0.0)


def propagate_kernel(greens_ref, effective_ref, spread_ref, out_ref, factor_ref, held_ref, sems):
    _, history, points, _ = greens_ref.shape
    factor_ref[...] = jnp.dot(
        split(effective_ref[...] * time_step), spread_ref[...], preferred_element_type=jnp.float32
    )

    slots, chunk = held_ref.shape[:2]

    def copy(number, slot):
        return pltpu.make_async_copy(
            held_ref.at[slot], out_ref.at[pl.ds(number * chunk, chunk)], sems.at[slot]
        )

    def advance(group, carry):
        for slot in range(slots):
            number = group * slots + slot

            @pl.when(group > 0)
            def _():
                copy(number - slots, slot).wait()

            times = pl.ds(number * chunk, chunk)
            for start in range(0, points, TILE):
                stop = min(start + TILE, points)
                greens = [greens_ref[j, times, start:stop, :] for j in range(STEPS)]
                terms = [greens[0]]
                for i in range(STEPS):
                    total = None
                    for j in range(STEPS):
                        spot = STEPS * i + j
                        factor = factor_ref[start:stop, spot * WIDTH : (spot + 1) * WIDTH]
                        term = factor[None] * greens[j]
                        total = term if total is None else total + term
                    terms.append(roll_blocks(total, STEPS * i))
                held_ref[slot, :, start:stop, :] = tree_sum(terms)
            copy(number, slot).start()
        return carry

    groups = history // (chunk * slots)
    lax.fori_loop(0, groups, advance, 0)
    for slot in range(slots):
        copy((groups - 1) * slots + slot, slot).wait()


def gather_tables():
    blocks = 2 * BANDS
    pairs = STEPS * STEPS // 2
    table = np.zeros((pairs, 2, blocks, BANDS, 2, BANDS, BANDS), np.float32)
    signs = np.zeros((pairs, blocks, BANDS), np.float32)
    for pair in range(pairs):
        for p in range(blocks):
            i, j = divmod(2 * pair + p // BANDS, STEPS)
            h, a = divmod((p + STEPS * i) % blocks, BANDS)
            g, c = divmod((p + j) % blocks, BANDS)
            table[pair, :, p, :, h ^ g, a, c] = 1 if (h, g) == (0, 1) else -1
            signs[pair, p] = 1 if h == g else -1
    return signs.reshape(pairs, WIDTH), table.reshape(-1, WIDTH).astype(ml_dtypes.bfloat16)


def spread_table():
    blocks = 2 * BANDS
    table = np.zeros((2, BANDS, BANDS, STEPS, STEPS, blocks, BANDS), np.float32)
    for i in range(STEPS):
        for j in range(STEPS):
            for p in range(blocks):
                h, a = divmod((p - STEPS * i) % blocks, BANDS)
                g, b = divmod((p + j) % blocks, BANDS)
                table[1 if h == g else 0, a, b, i, j, p, :] = -1 if (h, g) == (1, 0) else 1
    return np.tile(table.reshape(WIDTH, -1), (2, 1)).astype(ml_dtypes.bfloat16)


def in_vmem():
    return pl.BlockSpec(memory_space=pltpu.VMEM)


def in_smem():
    return pl.BlockSpec(memory_space=pltpu.SMEM)


def anywhere():
    return pl.BlockSpec(memory_space=pl.ANY)


def params(megabytes):
    return pltpu.CompilerParams(vmem_limit_bytes=megabytes * 1024 * 1024)


def cost(per_element, arrays):
    size = SIDE * SIDE * TILE * WIDTH
    return pl.CostEstimate(flops=per_element * size, bytes_accessed=4 * arrays * size, transcendentals=0)


def held_blocks(count, parts):
    return [
        pltpu.VMEM((count, TILE * SIDE * SIDE // parts, WIDTH), jnp.float32),
        pltpu.SemaphoreType.DMA((count,)),
    ]


def forward(place, greens, steps, parts):
    points = SIDE * SIDE
    return pl.pallas_call(
        functools.partial(forward_kernel, steps, parts),
        out_shape=[
            jax.ShapeDtypeStruct((points, TILE, WIDTH), jnp.float32),
            jax.ShapeDtypeStruct((STEPS, TILE * points, WIDTH), jnp.float32),
        ],
        in_specs=[in_smem()] + [anywhere()] * len(steps),
        out_specs=[in_vmem()] * 2,
        scratch_shapes=[pltpu.VMEM((points, TILE, WIDTH), jnp.float32)] + held_blocks(len(steps), parts),
        compiler_params=params(8),
        cost_estimate=cost(400, 6),
        name="forward",
    )(place, *greens)


def early_lines(place, lattice, weights, before, screens, steps, parts):
    points = SIDE * SIDE
    return pl.pallas_call(
        functools.partial(early_kernel, steps, parts),
        out_shape=jax.ShapeDtypeStruct((points, TILE, WIDTH), jnp.float32),
        in_specs=[in_smem(), in_vmem(), in_vmem(), anywhere()] + [anywhere()] * len(steps),
        out_specs=in_vmem(),
        scratch_shapes=held_blocks(len(steps), parts),
        compiler_params=params(4),
        cost_estimate=cost(150, 3),
        name="early",
    )(place, lattice, weights, before, *screens)


def backward(place, lattice, weights, equal_time, greens, screens, work, steps, parts, share):
    points = SIDE * SIDE
    signs, gather = gather_tables()
    inputs = (place, lattice, weights, equal_time, jnp.asarray(signs), jnp.asarray(gather), greens, *screens, work)
    partial_value, _ = pl.pallas_call(
        functools.partial(backward_kernel, steps, parts, share),
        out_shape=[
            jax.ShapeDtypeStruct((points, WIDTH), jnp.float32),
            jax.ShapeDtypeStruct((points, TILE, WIDTH), jnp.float32),
        ],
        in_specs=[in_smem()] + [in_vmem()] * 6 + [anywhere()] * len(steps) + [in_vmem()],
        out_specs=[in_vmem()] * 2,
        input_output_aliases={len(inputs) - 1: 1},
        scratch_shapes=[
            pltpu.VMEM((TILE * points, WIDTH), jnp.float32),
            pltpu.VMEM((points, STEPS * STEPS * WIDTH), jnp.float32),
            pltpu.VMEM((points, STEPS * STEPS * WIDTH), jnp.bfloat16),
        ]
        + (held_blocks(len(steps), parts) if steps else []),
        compiler_params=params(16),
        cost_estimate=cost(800, 6),
        name="backward",
    )(*inputs)
    return partial_value


def roll_own(greens):
    return pl.pallas_call(
        roll_kernel,
        out_shape=jax.ShapeDtypeStruct((STEPS, *greens.shape), jnp.float32),
        in_specs=[in_vmem()],
        out_specs=in_vmem(),
        compiler_params=params(4),
        cost_estimate=cost(3, 5),
        name="roll_own",
    )(greens)


def propagate(greens, effective):
    _, history, points, width = greens.shape
    chunk = math.gcd(history // 2, TILE)
    spread = spread_table()
    return pl.pallas_call(
        propagate_kernel,
        out_shape=jax.ShapeDtypeStruct(greens.shape[1:], jnp.float32),
        in_specs=[in_vmem()] * 3,
        out_specs=anywhere(),
        scratch_shapes=[
            pltpu.VMEM((points, spread.shape[1]), jnp.float32),
            pltpu.VMEM((2, chunk, points, width), jnp.float32),
            pltpu.SemaphoreType.DMA((2,)),
        ],
        compiler_params=params(6),
        cost_estimate=cost(32, 5),
        name="propagate",
    )(greens, effective, jnp.asarray(spread))


def partner_of(place, step, count):
    if count == 1:
        return 0
    if count & (count - 1) == 0:
        return place ^ step
    return (place + step) % count


def exchange(value, axis, step, count):
    pairs = [(place, partner_of(place, step, count)) for place in range(count)]
    return lax.ppermute(value, axis, pairs)


def exchange_order(count):
    along = {}
    for step in range(1, count):
        along.setdefault(step // 2, []).append(step)
    single = [along[n] for n in along if n and n & (n - 1) == 0]
    mixed = [along[n] for n in along if n & (n - 1)]
    order = [step for steps in zip(*single[::-1]) for step in steps]
    return order + along[0] + [step for steps in mixed for step in steps]


def class_weights(quad_class):
    table = jnp.array(quadrature, jnp.float32)
    match = quad_class[:, None] == jnp.arange(4, dtype=jnp.int32)[None, :]
    return jnp.sum(jnp.where(match, table[None, :], jnp.float32(0.0)), axis=1)


def per_device(parts, blocks, green_row, screened, hamilton, equal_time, quad_class, live_count):
    history, local, width = green_row.shape
    points = local * parts
    times = history // parts
    place = lax.axis_index("ka")
    seat = place.reshape(1)
    position = jnp.arange(history, dtype=jnp.int32)
    weights = jnp.where(
        position < live_count[0], time_step * class_weights(quad_class), jnp.float32(0.0)
    ) * jnp.float32(1.0 / points)
    weights = lax.dynamic_slice_in_dim(weights, place * times, times)

    if times == TILE and local % SIDE == 0:
        groups, sources = 1, parts
        order = exchange_order(parts)
        moved = []
        wholes = [x.reshape(parts * TILE * local, width) for x in (green_row, screened)]
        for whole in wholes:
            found = {0: whole}
            for step in order:
                start = partner_of(place, step, parts) * (TILE * local)
                block = lax.dynamic_slice_in_dim(whole, start, TILE * local)
                found[step] = exchange(block, "ka", step, parts)
            moved.append([found])
        order = [0] + order
    else:
        groups, sources = -(-times // TILE), 1
        order = [0]
        padding = groups * TILE - times
        moved = []
        for x in (green_row, screened):
            x = lax.all_to_all(x, "ka", split_axis=0, concat_axis=0, tiled=True)
            x = x.reshape(parts, times, local, width).transpose(1, 0, 2, 3).reshape(times, points, width)
            x = jnp.pad(x, ((0, padding), (0, 0), (0, 0))).reshape(groups, TILE * points, width)
            moved.append([{0: x[group]} for group in range(groups)])
        weights = jnp.pad(weights, (0, padding))
    weights = jnp.broadcast_to(weights.reshape(groups, TILE, 1), (groups, TILE, width))

    early = order[: max(1, len(order) - LATE)]
    late = order[len(early) :]
    own_greens = roll_own(green_row)
    partial_value = None
    for group in range(groups):
        green, screen = moved[0][group], moved[1][group]
        lattice, greens = forward(seat, [green[step] for step in order], order, sources)
        work = early_lines(
            seat, lattice, weights[group], own_greens, [screen[step] for step in early], early, sources
        )
        share = hubbard / (points * blocks) if group == 0 else 0.0
        term = backward(
            seat, lattice, weights[group], equal_time, greens, [screen[step] for step in late], work,
            late, sources, share,
        )
        partial_value = term if partial_value is None else partial_value + term

    owners = [partner_of(place, step, parts) for step in range(parts)]
    pieces = [lax.dynamic_slice_in_dim(partial_value, owner * local, local) for owner in owners]
    if parts % 2 == 0 and parts & (parts - 1) == 0:
        pairs = jnp.concatenate([pieces[step] for step in range(1, parts, 2)], axis=0)
        pairs = exchange(pairs, "ka", 1, parts)
        mine = jnp.concatenate([pieces[step] for step in range(0, parts, 2)], axis=0) + pairs
        pieces = [mine[n * local : (n + 1) * local] for n in range(parts // 2)]
        collision = tree_sum(
            pieces[:1] + [exchange(pieces[n], "ka", 2 * n, parts) for n in range(parts // 2 - 1, 0, -1)]
        )
    else:
        collision = tree_sum(
            pieces[:1] + [exchange(pieces[step], "ka", step, parts) for step in range(1, parts)]
        )
    collision = tree_sum(
        [collision] + [exchange(collision, "hist", step, blocks) for step in range(blocks - 1, 0, -1)]
    )
    return propagate(own_greens, hamilton + collision)


def solution(mesh):
    in_specs = (
        P("hist", "ka", None),
        P("hist", "ka", None),
        P("ka", None),
        P("ka", None),
        P("hist"),
        P("hist"),
    )
    out_specs = P("hist", "ka", None)
    return jax.shard_map(
        functools.partial(per_device, mesh.shape["ka"], mesh.shape["hist"]),
        mesh=mesh,
        in_specs=in_specs,
        out_specs=out_specs,
        check_vma=False,
    )
```

```python
import functools
import math

import jax
import jax.numpy as jnp
import ml_dtypes
import numpy as np
from jax import lax
from jax.experimental import pallas as pl
from jax.experimental.pallas import tpu as pltpu
from jax.sharding import PartitionSpec as P

SIDE = 24
BANDS = 8
ENTRIES = BANDS * BANDS
WIDTH = 2 * ENTRIES
TILE = 8
STEPS = 4

time_step = 0.1
hubbard = 1.0
quadrature = (0.375, 1.1666666, 0.9583333, 1.0)

LATE = 2
AHEAD = 3


def lane_sign(shape):
    lane = lax.broadcasted_iota(jnp.int32, shape, len(shape) - 1)
    return lane < ENTRIES


def swap(x):
    return pltpu.roll(x, ENTRIES, 1)


def roll_blocks(x, blocks):
    return x if blocks == 0 else pltpu.roll(x, WIDTH - BANDS * blocks, x.ndim - 1)


def tree_sum(terms):
    while len(terms) > 1:
        terms = [sum(terms[i : i + 2][1:], terms[i]) for i in range(0, len(terms), 2)]
    return terms[0]


def split(x):
    high = x.astype(jnp.bfloat16)
    return jnp.concatenate([high, (x - high.astype(jnp.float32)).astype(jnp.bfloat16)], axis=1)


def dft24(x, sign, low):
    root3 = jnp.where(low, -1.0, 1.0) * (sign * math.sqrt(3.0) / 2)
    turn = jnp.where(low, -1.0, 1.0) * float(sign)
    half = math.sqrt(0.5)
    turn_half = turn * half
    columns = [[None] * 8 for _ in range(3)]
    for n2 in range(8):
        x0, x1, x2 = (x[(8 * n1 + 3 * n2) % 24] for n1 in range(3))
        total = x1 + x2
        base = x0 - 0.5 * total
        spin = swap(x1 - x2) * root3
        columns[0][n2] = x0 + total
        columns[1][n2] = base + spin
        columns[2][n2] = base - spin
    out = [None] * 24
    for k1 in range(3):
        c = columns[k1]
        a0, a1 = c[0] + c[4], c[0] - c[4]
        a2, a3 = c[2] + c[6], c[2] - c[6]
        a4, a5 = c[1] + c[5], c[1] - c[5]
        a6, a7 = c[3] + c[7], c[3] - c[7]
        b0, b1 = a0 + a2, a0 - a2
        b2, b3 = a4 + a6, a4 - a6
        i_a3 = swap(a3) * turn
        i_b3 = swap(b3) * turn
        c0, c1 = a1 + i_a3, a1 - i_a3
        p = (a5 - a7) * half
        m = swap(a5 + a7) * turn_half
        e, f = p + m, p - m
        values = [b0 + b2, c0 + e, b1 + i_b3, c1 - f, b0 - b2, c0 - e, b1 - i_b3, c1 + f]
        for k2 in range(8):
            out[(16 * k1 + 9 * k2) % 24] = values[k2]
    return out


def load_line(ref, line):
    stride = ref.shape[0] // TILE
    return [ref[pl.ds(line * SIDE + k2, TILE, stride=stride), :] for k2 in range(SIDE)]


def fetch(place, steps, block_refs, held_ref, sems):
    copies = []
    for slot, (step, source) in enumerate(zip(steps, block_refs)):
        rows = held_ref.shape[1]
        if step == 0 and source.shape[0] != rows:
            source = source.at[pl.ds(pl.multiple_of(place * rows, TILE), rows)]
        copies.append(pltpu.make_async_copy(source, held_ref.at[slot], sems.at[slot]))
        copies[-1].start()
    return copies


def along_first(work_ref, sign, low, store):
    def columns(pair, carry):
        both = (2 * pair, 2 * pair + 1)
        rows = [[work_ref[k1 * SIDE + column] for k1 in range(SIDE)] for column in both]
        values = [dft24(row, sign, low) for row in rows]
        for column, value in zip(both, values):
            for r1 in range(SIDE):
                store(r1 * SIDE + column, value[r1])
        return carry

    lax.fori_loop(0, SIDE // 2, columns, 0)


def roll_kernel(green_ref, greens_ref):
    batch = math.gcd(green_ref.shape[0], STEPS)

    def rolls(n, carry):
        times = pl.ds(n * batch, batch)
        green = green_ref[times]
        rolled = [roll_blocks(green, j) for j in range(STEPS)]
        for j in range(STEPS):
            greens_ref[j, times] = rolled[j]
        return carry

    lax.fori_loop(0, green_ref.shape[0] // batch, rolls, 0)


def forward_kernel(steps, parts, place_ref, *refs):
    block_refs, (lattice_ref, greens_ref, work_ref, held_ref, sems) = refs[: len(steps)], refs[len(steps) :]
    low = lane_sign((TILE, WIDTH))
    place = place_ref[0]
    copies = fetch(place, steps, block_refs, held_ref, sems)
    rows = held_ref.shape[1]
    lines = rows // (TILE * SIDE)
    for slot, step in enumerate(steps):
        copies[slot].wait()
        green_ref = held_ref.at[slot]
        owner = partner_of(place, step, parts)

        def along_second(i, carry):
            for r2, value in enumerate(dft24(load_line(green_ref, i), -1, low)):
                work_ref[(owner * lines + i) * SIDE + r2] = value
            return carry

        lax.fori_loop(0, lines, along_second, 0, unroll=lines <= 4)
        green = green_ref[...]
        spot = pl.ds(pl.multiple_of(owner * rows, TILE), rows)
        for j in range(STEPS):
            greens_ref[j, spot, :] = roll_blocks(green, j)

    def store(point, value):
        lattice_ref[point] = value

    along_first(work_ref, -1, low, store)


def product_lines(steps, parts, place, lattice_ref, weights, screen_refs, held_ref, sems, work_ref):
    low = lane_sign((TILE, WIDTH))
    turn = jnp.where(low, -1.0, 1.0)
    copies = fetch(place, steps, screen_refs, held_ref, sems)
    lines = held_ref.shape[1] // (TILE * SIDE)
    for slot, step in enumerate(steps):
        copies[slot].wait()
        screen_ref = held_ref.at[slot]
        first = partner_of(place, step, parts) * lines

        def along_second(i, carry):
            rows = []
            for r2, value in enumerate(load_line(screen_ref, i)):
                screen = value * weights
                other = swap(screen)
                lattice = lattice_ref[(first + i) * SIDE + r2]
                rows.append(
                    swap(lattice) * turn * jnp.where(low, screen, other)
                    - lattice * jnp.where(low, other, screen)
                )
            for k2, value in enumerate(dft24(rows, 1, low)):
                work_ref[(first + i) * SIDE + k2] = value
            return carry

        lax.fori_loop(0, lines, along_second, 0, unroll=lines <= 4)


def early_kernel(steps, parts, place_ref, lattice_ref, weight_ref, _, *refs):
    screen_refs, (work_ref, held_ref, sems) = refs[: len(steps)], refs[len(steps) :]
    product_lines(
        steps, parts, place_ref[0], lattice_ref, weight_ref[...], screen_refs, held_ref, sems, work_ref
    )


def sigma_kernel(steps, parts, place_ref, lattice_ref, weight_ref, *refs):
    screen_refs, refs = refs[: len(steps)], refs[len(steps) :]
    _, work_ref, sigma_ref, *late = refs
    low = lane_sign((TILE, WIDTH))
    if steps:
        held_ref, sems = late
        product_lines(
            steps, parts, place_ref[0], lattice_ref, weight_ref[...], screen_refs, held_ref, sems, work_ref
        )

    def store(point, value):
        sigma_ref[pl.ds(point * TILE, TILE), :] = value

    along_first(work_ref, 1, low, store)


def contract_kernel(share, owner_ref, sigma_ref, equal_ref, sign_ref, gather_ref, greens_ref, *refs):
    partial_ref, sums_ref, pieces_ref = refs[-3:]
    low = lane_sign((TILE, WIDTH))
    points = partial_ref.shape[0]
    block = points // owner_ref.shape[0]
    tiles = block // TILE
    batch = max(n for n in range(1, 10) if tiles % n == 0)

    def contract(group, carry):
        slot, first = group // (tiles // batch), group % (tiles // batch) * batch
        owner = owner_ref[slot]
        units = [(tile, s) for tile in range(batch) for s in range(TILE)]

        def prepare(tile, s):
            point = owner * block + (first + tile) * TILE
            sigma = sigma_ref[pl.ds(point * TILE + s, TILE, stride=TILE), :]
            row = pl.multiple_of((owner * TILE + s) * block + (first + tile) * TILE, TILE)
            return (
                [roll_blocks(sigma, STEPS * i) for i in range(STEPS)],
                [greens_ref[j, pl.ds(row, TILE), :] for j in range(STEPS)],
            )

        ready = [prepare(*unit) for unit in units[:AHEAD]]
        for n, (tile, s) in enumerate(units):
            if n + AHEAD < len(units):
                ready.append(prepare(*units[n + AHEAD]))
            sigmas, greens = ready.pop(0)
            terms = [sigma * green for sigma in sigmas for green in greens]
            sums = terms if s == 0 else [a + b for a, b in zip(sums, terms)]
            if s == TILE - 1:
                row = pl.ds(pl.multiple_of(slot * block + (first + tile) * TILE, TILE), TILE)
                for spot, value in enumerate(sums):
                    sums_ref[row, spot * WIDTH : (spot + 1) * WIDTH] = value
        return carry

    lax.fori_loop(0, points // (TILE * batch), contract, 0)

    lane = lax.broadcasted_iota(jnp.int32, equal_ref.shape, 1)
    inner = lane - ENTRIES
    occupied = jnp.sum(jnp.where((inner >= 0) & (inner % (BANDS + 1) == 0), equal_ref[...], 0.0))
    spots = lax.broadcasted_iota(jnp.int32, (points, WIDTH), 1)
    on_diagonal = (spots < ENTRIES) & (spots % (BANDS + 1) == 0)
    lower = lax.broadcasted_iota(jnp.int32, (sums_ref.shape[0], WIDTH), 1) < ENTRIES
    for pair in range(STEPS * STEPS // 2):
        first_part = sums_ref[:, 2 * pair * WIDTH : (2 * pair + 1) * WIDTH]
        second_part = sums_ref[:, (2 * pair + 1) * WIDTH : (2 * pair + 2) * WIDTH]
        folded = jnp.where(lower, first_part, second_part) + sign_ref[pair : pair + 1, :] * swap(
            jnp.where(lower, second_part, first_part)
        )
        pieces_ref[:, 2 * pair * WIDTH : (2 * pair + 2) * WIDTH] = split(folded)
    total = jnp.dot(pieces_ref[...], gather_ref[...], preferred_element_type=jnp.float32)
    partial_ref[...] = total[:points] + jnp.where(on_diagonal, occupied * share, 0.0)


def propagate_kernel(greens_ref, effective_ref, spread_ref, out_ref, factor_ref, held_ref, sems):
    _, history, points, _ = greens_ref.shape
    factor_ref[...] = jnp.dot(
        split(effective_ref[...] * time_step), spread_ref[...], preferred_element_type=jnp.float32
    )

    slots, chunk = held_ref.shape[:2]

    def copy(number, slot):
        return pltpu.make_async_copy(
            held_ref.at[slot], out_ref.at[pl.ds(number * chunk, chunk)], sems.at[slot]
        )

    def advance(group, carry):
        for slot in range(slots):
            number = group * slots + slot

            @pl.when(group > 0)
            def _():
                copy(number - slots, slot).wait()

            times = pl.ds(number * chunk, chunk)
            for start in range(0, points, TILE):
                stop = min(start + TILE, points)
                greens = [greens_ref[j, times, start:stop, :] for j in range(STEPS)]
                terms = [greens[0]]
                for i in range(STEPS):
                    total = None
                    for j in range(STEPS):
                        spot = STEPS * i + j
                        factor = factor_ref[start:stop, spot * WIDTH : (spot + 1) * WIDTH]
                        term = factor[None] * greens[j]
                        total = term if total is None else total + term
                    terms.append(roll_blocks(total, STEPS * i))
                held_ref[slot, :, start:stop, :] = tree_sum(terms)
            copy(number, slot).start()
        return carry

    groups = history // (chunk * slots)
    lax.fori_loop(0, groups, advance, 0)
    for slot in range(slots):
        copy((groups - 1) * slots + slot, slot).wait()


def gather_tables():
    blocks = 2 * BANDS
    pairs = STEPS * STEPS // 2
    table = np.zeros((pairs, 2, blocks, BANDS, 2, BANDS, BANDS), np.float32)
    signs = np.zeros((pairs, blocks, BANDS), np.float32)
    for pair in range(pairs):
        for p in range(blocks):
            i, j = divmod(2 * pair + p // BANDS, STEPS)
            h, a = divmod((p + STEPS * i) % blocks, BANDS)
            g, c = divmod((p + j) % blocks, BANDS)
            table[pair, :, p, :, h ^ g, a, c] = 1 if (h, g) == (0, 1) else -1
            signs[pair, p] = 1 if h == g else -1
    return signs.reshape(pairs, WIDTH), table.reshape(-1, WIDTH).astype(ml_dtypes.bfloat16)


def spread_table():
    blocks = 2 * BANDS
    table = np.zeros((2, BANDS, BANDS, STEPS, STEPS, blocks, BANDS), np.float32)
    for i in range(STEPS):
        for j in range(STEPS):
            for p in range(blocks):
                h, a = divmod((p - STEPS * i) % blocks, BANDS)
                g, b = divmod((p + j) % blocks, BANDS)
                table[1 if h == g else 0, a, b, i, j, p, :] = -1 if (h, g) == (1, 0) else 1
    return np.tile(table.reshape(WIDTH, -1), (2, 1)).astype(ml_dtypes.bfloat16)


def in_vmem():
    return pl.BlockSpec(memory_space=pltpu.VMEM)


def in_smem():
    return pl.BlockSpec(memory_space=pltpu.SMEM)


def anywhere():
    return pl.BlockSpec(memory_space=pl.ANY)


def params(megabytes):
    return pltpu.CompilerParams(vmem_limit_bytes=megabytes * 1024 * 1024)


def cost(per_element, arrays):
    size = SIDE * SIDE * TILE * WIDTH
    return pl.CostEstimate(flops=per_element * size, bytes_accessed=4 * arrays * size, transcendentals=0)


def held_blocks(count, parts):
    return [
        pltpu.VMEM((count, TILE * SIDE * SIDE // parts, WIDTH), jnp.float32),
        pltpu.SemaphoreType.DMA((count,)),
    ]


def forward(place, greens, steps, parts):
    points = SIDE * SIDE
    return pl.pallas_call(
        functools.partial(forward_kernel, steps, parts),
        out_shape=[
            jax.ShapeDtypeStruct((points, TILE, WIDTH), jnp.float32),
            jax.ShapeDtypeStruct((STEPS, TILE * points, WIDTH), jnp.float32),
        ],
        in_specs=[in_smem()] + [anywhere()] * len(steps),
        out_specs=[in_vmem()] * 2,
        scratch_shapes=[pltpu.VMEM((points, TILE, WIDTH), jnp.float32)] + held_blocks(len(steps), parts),
        compiler_params=params(8),
        cost_estimate=cost(400, 6),
        name="forward",
    )(place, *greens)


def early_lines(place, lattice, weights, before, screens, steps, parts):
    points = SIDE * SIDE
    return pl.pallas_call(
        functools.partial(early_kernel, steps, parts),
        out_shape=jax.ShapeDtypeStruct((points, TILE, WIDTH), jnp.float32),
        in_specs=[in_smem(), in_vmem(), in_vmem(), anywhere()] + [anywhere()] * len(steps),
        out_specs=in_vmem(),
        scratch_shapes=held_blocks(len(steps), parts),
        compiler_params=params(4),
        cost_estimate=cost(150, 3),
        name="early",
    )(place, lattice, weights, before, *screens)


def sigma_of(place, lattice, weights, screens, work, steps, parts):
    points = SIDE * SIDE
    inputs = (place, lattice, weights, *screens, work)
    work, sigma = pl.pallas_call(
        functools.partial(sigma_kernel, steps, parts),
        out_shape=[
            jax.ShapeDtypeStruct((points, TILE, WIDTH), jnp.float32),
            jax.ShapeDtypeStruct((TILE * points, WIDTH), jnp.float32),
        ],
        in_specs=[in_smem()] + [in_vmem()] * 2 + [anywhere()] * len(steps) + [in_vmem()],
        out_specs=[in_vmem()] * 2,
        input_output_aliases={len(inputs) - 1: 0},
        scratch_shapes=held_blocks(len(steps), parts) if steps else [],
        compiler_params=params(4),
        cost_estimate=cost(200, 6),
        name="sigma",
    )(*inputs)
    return sigma


def contract(owners, sigma, equal_time, greens, block, share, before=()):
    points = owners.shape[0] * block
    rows = -(-points // 16) * 16
    signs, gather = gather_tables()
    return pl.pallas_call(
        functools.partial(contract_kernel, share),
        out_shape=jax.ShapeDtypeStruct((points, WIDTH), jnp.float32),
        in_specs=[in_smem()] + [in_vmem()] * 5 + [anywhere()] * len(before),
        out_specs=in_vmem(),
        scratch_shapes=[
            pltpu.VMEM((rows, STEPS * STEPS * WIDTH), jnp.float32),
            pltpu.VMEM((rows, STEPS * STEPS * WIDTH), jnp.bfloat16),
        ],
        compiler_params=params(10),
        cost_estimate=cost(70 * owners.shape[0], 6),
        name="contract",
    )(owners, sigma, equal_time, jnp.asarray(signs), jnp.asarray(gather), greens, *before)


def roll_own(greens):
    return pl.pallas_call(
        roll_kernel,
        out_shape=jax.ShapeDtypeStruct((STEPS, *greens.shape), jnp.float32),
        in_specs=[in_vmem()],
        out_specs=in_vmem(),
        compiler_params=params(4),
        cost_estimate=cost(3, 5),
        name="roll_own",
    )(greens)


def propagate(greens, effective):
    _, history, points, width = greens.shape
    chunk = math.gcd(history // 2, TILE)
    spread = spread_table()
    return pl.pallas_call(
        propagate_kernel,
        out_shape=jax.ShapeDtypeStruct(greens.shape[1:], jnp.float32),
        in_specs=[in_vmem()] * 3,
        out_specs=anywhere(),
        scratch_shapes=[
            pltpu.VMEM((points, spread.shape[1]), jnp.float32),
            pltpu.VMEM((2, chunk, points, width), jnp.float32),
            pltpu.SemaphoreType.DMA((2,)),
        ],
        compiler_params=params(6),
        cost_estimate=cost(32, 5),
        name="propagate",
    )(greens, effective, jnp.asarray(spread))


def partner_of(place, step, count):
    if count == 1:
        return 0
    if count & (count - 1) == 0:
        return place ^ step
    return (place + step) % count


def exchange(value, axis, step, count):
    pairs = [(place, partner_of(place, step, count)) for place in range(count)]
    return lax.ppermute(value, axis, pairs)


def exchange_order(count):
    along = {}
    for step in range(1, count):
        along.setdefault(step // 2, []).append(step)
    single = [along[n] for n in along if n and n & (n - 1) == 0]
    mixed = [along[n] for n in along if n & (n - 1)]
    order = [step for steps in zip(*single[::-1]) for step in steps]
    return order + along[0] + [step for steps in mixed for step in steps]


def class_weights(quad_class):
    table = jnp.array(quadrature, jnp.float32)
    match = quad_class[:, None] == jnp.arange(4, dtype=jnp.int32)[None, :]
    return jnp.sum(jnp.where(match, table[None, :], jnp.float32(0.0)), axis=1)


def per_device(parts, blocks, green_row, screened, hamilton, equal_time, quad_class, live_count):
    history, local, width = green_row.shape
    points = local * parts
    times = history // parts
    place = lax.axis_index("ka")
    seat = place.reshape(1)
    position = jnp.arange(history, dtype=jnp.int32)
    weights = jnp.where(
        position < live_count[0], time_step * class_weights(quad_class), jnp.float32(0.0)
    ) * jnp.float32(1.0 / points)
    weights = lax.dynamic_slice_in_dim(weights, place * times, times)

    if times == TILE and local % SIDE == 0:
        groups, sources = 1, parts
        order = exchange_order(parts)
        moved = []
        wholes = [x.reshape(parts * TILE * local, width) for x in (green_row, screened)]
        for whole in wholes:
            found = {0: whole}
            for step in order:
                start = partner_of(place, step, parts) * (TILE * local)
                block = lax.dynamic_slice_in_dim(whole, start, TILE * local)
                found[step] = exchange(block, "ka", step, parts)
            moved.append([found])
        order = [0] + order
    else:
        groups, sources = -(-times // TILE), 1
        order = [0]
        padding = groups * TILE - times
        moved = []
        for x in (green_row, screened):
            x = lax.all_to_all(x, "ka", split_axis=0, concat_axis=0, tiled=True)
            x = x.reshape(parts, times, local, width).transpose(1, 0, 2, 3).reshape(times, points, width)
            x = jnp.pad(x, ((0, padding), (0, 0), (0, 0))).reshape(groups, TILE * points, width)
            moved.append([{0: x[group]} for group in range(groups)])
        weights = jnp.pad(weights, (0, padding))
    weights = jnp.broadcast_to(weights.reshape(groups, TILE, 1), (groups, TILE, width))

    early = order[: max(1, len(order) - LATE)]
    late = order[len(early) :]
    own_greens = roll_own(green_row)
    share = hubbard / (points * blocks)
    sigmas = []
    for group in range(groups):
        green, screen = moved[0][group], moved[1][group]
        lattice, greens = forward(seat, [green[step] for step in order], order, sources)
        work = early_lines(
            seat, lattice, weights[group], own_greens, [screen[step] for step in early], early, sources
        )
        sigma = sigma_of(
            seat, lattice, weights[group], [screen[step] for step in late], work, late, sources
        )
        sigmas.append((sigma, greens))

    if sources == parts and parts % 2 == 0 and parts & (parts - 1) == 0:
        (sigma, greens), = sigmas

        def blocks_of(steps, before=()):
            owners = jnp.stack([partner_of(place, step, parts) for step in steps])
            return contract(owners, sigma, equal_time, greens, local, share, before)

        others = exchange(blocks_of(list(range(3, parts, 2))), "ka", 1, parts)
        others = blocks_of(list(range(2, parts, 2))) + others
        pieces = [
            exchange(others[(n - 1) * local : n * local], "ka", 2 * n, parts)
            for n in range(parts // 2 - 1, 0, -1)
        ]
        chip = blocks_of([1, 0], (others,))
        pieces += [exchange(chip[:local], "ka", 1, parts), chip[local:]]
        collision = tree_sum(pieces)
    else:
        whole = jnp.zeros((1,), jnp.int32)
        partial_value = tree_sum(
            [
                contract(whole, sigma, equal_time, greens, points, share if group == 0 else 0.0)
                for group, (sigma, greens) in enumerate(sigmas)
            ]
        )
        owners = [partner_of(place, step, parts) for step in range(parts)]
        pieces = [lax.dynamic_slice_in_dim(partial_value, owner * local, local) for owner in owners]
        collision = tree_sum(
            pieces[:1] + [exchange(pieces[step], "ka", step, parts) for step in range(1, parts)]
        )
    collision = tree_sum(
        [collision] + [exchange(collision, "hist", step, blocks) for step in range(blocks - 1, 0, -1)]
    )
    return propagate(own_greens, hamilton + collision)


def solution(mesh):
    in_specs = (
        P("hist", "ka", None),
        P("hist", "ka", None),
        P("ka", None),
        P("ka", None),
        P("hist"),
        P("hist"),
    )
    out_specs = P("hist", "ka", None)
    return jax.shard_map(
        functools.partial(per_device, mesh.shape["ka"], mesh.shape["hist"]),
        mesh=mesh,
        in_specs=in_specs,
        out_specs=out_specs,
        check_vma=False,
    )
```

```python
import functools
import math

import jax
import jax.numpy as jnp
import ml_dtypes
import numpy as np
from jax import lax
from jax.experimental import pallas as pl
from jax.experimental.pallas import tpu as pltpu
from jax.sharding import PartitionSpec as P

SIDE = 24
BANDS = 8
ENTRIES = BANDS * BANDS
WIDTH = 2 * ENTRIES
TILE = 8
STEPS = 4

time_step = 0.1
hubbard = 1.0
quadrature = (0.375, 1.1666666, 0.9583333, 1.0)

HANDED = 2
LARGE = 1e30
LATE = 2
AHEAD = 3


def lane_sign(shape):
    lane = lax.broadcasted_iota(jnp.int32, shape, len(shape) - 1)
    return lane < ENTRIES


def swap(x):
    return pltpu.roll(x, ENTRIES, 1)


def roll_blocks(x, blocks):
    return x if blocks == 0 else pltpu.roll(x, WIDTH - BANDS * blocks, x.ndim - 1)


def tree_sum(terms):
    while len(terms) > 1:
        terms = [sum(terms[i : i + 2][1:], terms[i]) for i in range(0, len(terms), 2)]
    return terms[0]


def split(x):
    high = x.astype(jnp.bfloat16)
    return jnp.concatenate([high, (x - high.astype(jnp.float32)).astype(jnp.bfloat16)], axis=1)


def dft24(x, sign, low):
    root3 = jnp.where(low, -1.0, 1.0) * (sign * math.sqrt(3.0) / 2)
    turn = jnp.where(low, -1.0, 1.0) * float(sign)
    half = math.sqrt(0.5)
    turn_half = turn * half
    columns = [[None] * 8 for _ in range(3)]
    for n2 in range(8):
        x0, x1, x2 = (x[(8 * n1 + 3 * n2) % 24] for n1 in range(3))
        total = x1 + x2
        base = x0 - 0.5 * total
        spin = swap(x1 - x2) * root3
        columns[0][n2] = x0 + total
        columns[1][n2] = base + spin
        columns[2][n2] = base - spin
    out = [None] * 24
    for k1 in range(3):
        c = columns[k1]
        a0, a1 = c[0] + c[4], c[0] - c[4]
        a2, a3 = c[2] + c[6], c[2] - c[6]
        a4, a5 = c[1] + c[5], c[1] - c[5]
        a6, a7 = c[3] + c[7], c[3] - c[7]
        b0, b1 = a0 + a2, a0 - a2
        b2, b3 = a4 + a6, a4 - a6
        i_a3 = swap(a3) * turn
        i_b3 = swap(b3) * turn
        c0, c1 = a1 + i_a3, a1 - i_a3
        p = (a5 - a7) * half
        m = swap(a5 + a7) * turn_half
        e, f = p + m, p - m
        values = [b0 + b2, c0 + e, b1 + i_b3, c1 - f, b0 - b2, c0 - e, b1 - i_b3, c1 + f]
        for k2 in range(8):
            out[(16 * k1 + 9 * k2) % 24] = values[k2]
    return out


def load_line(ref, line):
    stride = ref.shape[0] // TILE
    return [ref[pl.ds(line * SIDE + k2, TILE, stride=stride), :] for k2 in range(SIDE)]


def fetch(place, steps, block_refs, held_ref, sems):
    copies = []
    for slot, (step, source) in enumerate(zip(steps, block_refs)):
        rows = held_ref.shape[1]
        if step == 0 and source.shape[0] != rows:
            source = source.at[pl.ds(pl.multiple_of(place * rows, TILE), rows)]
        copies.append(pltpu.make_async_copy(source, held_ref.at[slot], sems.at[slot]))
        copies[-1].start()
    return copies


def along_first(work_ref, sign, low, store):
    def columns(pair, carry):
        both = (2 * pair, 2 * pair + 1)
        rows = [[work_ref[k1 * SIDE + column] for k1 in range(SIDE)] for column in both]
        values = [dft24(row, sign, low) for row in rows]
        for column, value in zip(both, values):
            for r1 in range(SIDE):
                store(r1 * SIDE + column, value[r1])
        return carry

    lax.fori_loop(0, SIDE // 2, columns, 0)


def roll_kernel(place_ref, green_ref, whole_ref, greens_ref, block_ref, *, step, parts):
    rows = block_ref.shape[0]
    block_ref[...] = whole_ref[pl.ds(pl.multiple_of(partner_of(place_ref[0], step, parts) * rows, TILE), rows), :]
    batch = math.gcd(green_ref.shape[0], 4)

    def rolls(n, carry):
        times = pl.ds(n * batch, batch)
        green = green_ref[times]
        rolled = [roll_blocks(green, j) for j in range(STEPS)]
        for j in range(STEPS):
            greens_ref[j, times] = rolled[j]
        return carry

    lax.fori_loop(0, green_ref.shape[0] // batch, rolls, 0)


def forward_kernel(steps, parts, place_ref, *refs):
    block_refs, (lattice_ref, greens_ref, work_ref, held_ref, sems) = refs[: len(steps)], refs[len(steps) :]
    low = lane_sign((TILE, WIDTH))
    place = place_ref[0]
    copies = fetch(place, steps, block_refs, held_ref, sems)
    rows = held_ref.shape[1]
    lines = rows // (TILE * SIDE)
    for slot, step in enumerate(steps):
        copies[slot].wait()
        green_ref = held_ref.at[slot]
        owner = partner_of(place, step, parts)

        def along_second(i, carry):
            for r2, value in enumerate(dft24(load_line(green_ref, i), -1, low)):
                work_ref[(owner * lines + i) * SIDE + r2] = value
            return carry

        lax.fori_loop(0, lines, along_second, 0, unroll=lines <= 4)
        green = green_ref[...]
        spot = pl.ds(pl.multiple_of(owner * rows, TILE), rows)
        for j in range(STEPS):
            greens_ref[j, spot, :] = roll_blocks(green, j)

    def store(point, value):
        lattice_ref[point] = value

    along_first(work_ref, -1, low, store)


def product_lines(steps, parts, place, lattice_ref, weights, screen_refs, held_ref, sems, work_ref):
    low = lane_sign((TILE, WIDTH))
    turn = jnp.where(low, -1.0, 1.0)
    copies = fetch(place, steps, screen_refs, held_ref, sems)
    lines = held_ref.shape[1] // (TILE * SIDE)
    for slot, step in enumerate(steps):
        copies[slot].wait()
        screen_ref = held_ref.at[slot]
        first = partner_of(place, step, parts) * lines

        def along_second(i, carry):
            rows = []
            for r2, value in enumerate(load_line(screen_ref, i)):
                screen = value * weights
                other = swap(screen)
                lattice = lattice_ref[(first + i) * SIDE + r2]
                rows.append(
                    swap(lattice) * turn * jnp.where(low, screen, other)
                    - lattice * jnp.where(low, other, screen)
                )
            for k2, value in enumerate(dft24(rows, 1, low)):
                work_ref[(first + i) * SIDE + k2] = value
            return carry

        lax.fori_loop(0, lines, along_second, 0, unroll=lines <= 4)


def early_kernel(steps, parts, place_ref, lattice_ref, weight_ref, *refs):
    screen_refs, (*_, work_ref, held_ref, sems) = refs[: len(steps)], refs[len(steps) :]
    product_lines(
        steps, parts, place_ref[0], lattice_ref, weight_ref[...], screen_refs, held_ref, sems, work_ref
    )


def sigma_kernel(steps, parts, place_ref, lattice_ref, weight_ref, *refs):
    screen_refs, refs = refs[: len(steps)], refs[len(steps) :]
    _, work_ref, sigma_ref, *late = refs
    low = lane_sign((TILE, WIDTH))
    if steps:
        held_ref, sems = late
        product_lines(
            steps, parts, place_ref[0], lattice_ref, weight_ref[...], screen_refs, held_ref, sems, work_ref
        )

    def store(point, value):
        sigma_ref[pl.ds(point * TILE, TILE), :] = value

    along_first(work_ref, 1, low, store)


def contract_kernel(share, owner_ref, sigma_ref, equal_ref, sign_ref, gather_ref, greens_ref, *refs):
    partial_ref, sums_ref, pieces_ref = refs[-3:]
    low = lane_sign((TILE, WIDTH))
    points = partial_ref.shape[0]
    block = points // owner_ref.shape[0]
    tiles = block // TILE
    batch = max(n for n in range(1, 10) if tiles % n == 0)

    def contract(group, carry):
        slot, first = group // (tiles // batch), group % (tiles // batch) * batch
        owner = owner_ref[slot]
        units = [(tile, s) for tile in range(batch) for s in range(TILE)]

        def prepare(tile, s):
            point = owner * block + (first + tile) * TILE
            sigma = sigma_ref[pl.ds(point * TILE + s, TILE, stride=TILE), :]
            row = pl.multiple_of((owner * TILE + s) * block + (first + tile) * TILE, TILE)
            return (
                [roll_blocks(sigma, STEPS * i) for i in range(STEPS)],
                [greens_ref[j, pl.ds(row, TILE), :] for j in range(STEPS)],
            )

        ready = [prepare(*unit) for unit in units[:AHEAD]]
        for n, (tile, s) in enumerate(units):
            if n + AHEAD < len(units):
                ready.append(prepare(*units[n + AHEAD]))
            sigmas, greens = ready.pop(0)
            terms = [sigma * green for sigma in sigmas for green in greens]
            sums = terms if s == 0 else [a + b for a, b in zip(sums, terms)]
            if s == TILE - 1:
                row = pl.ds(pl.multiple_of(slot * block + (first + tile) * TILE, TILE), TILE)
                for spot, value in enumerate(sums):
                    sums_ref[row, spot * WIDTH : (spot + 1) * WIDTH] = value
        return carry

    lax.fori_loop(0, points // (TILE * batch), contract, 0)

    lane = lax.broadcasted_iota(jnp.int32, equal_ref.shape, 1)
    inner = lane - ENTRIES
    occupied = jnp.sum(jnp.where((inner >= 0) & (inner % (BANDS + 1) == 0), equal_ref[...], 0.0))
    spots = lax.broadcasted_iota(jnp.int32, (points, WIDTH), 1)
    on_diagonal = (spots < ENTRIES) & (spots % (BANDS + 1) == 0)
    lower = lax.broadcasted_iota(jnp.int32, (sums_ref.shape[0], WIDTH), 1) < ENTRIES
    for pair in range(STEPS * STEPS // 2):
        first_part = sums_ref[:, 2 * pair * WIDTH : (2 * pair + 1) * WIDTH]
        second_part = sums_ref[:, (2 * pair + 1) * WIDTH : (2 * pair + 2) * WIDTH]
        folded = jnp.where(lower, first_part, second_part) + sign_ref[pair : pair + 1, :] * swap(
            jnp.where(lower, second_part, first_part)
        )
        pieces_ref[:, 2 * pair * WIDTH : (2 * pair + 2) * WIDTH] = split(folded)
    total = jnp.dot(pieces_ref[...], gather_ref[...], preferred_element_type=jnp.float32)
    partial_ref[...] = total[:points] + jnp.where(on_diagonal, occupied * share, 0.0)


def propagate_kernel(greens_ref, effective_ref, spread_ref, out_ref, factor_ref, held_ref, sems):
    _, history, points, _ = greens_ref.shape
    factor_ref[...] = jnp.dot(
        split(effective_ref[...] * time_step), spread_ref[...], preferred_element_type=jnp.float32
    )

    slots, chunk = held_ref.shape[:2]

    def copy(number, slot):
        return pltpu.make_async_copy(
            held_ref.at[slot], out_ref.at[pl.ds(number * chunk, chunk)], sems.at[slot]
        )

    def advance(group, carry):
        for slot in range(slots):
            number = group * slots + slot

            @pl.when(group > 0)
            def _():
                copy(number - slots, slot).wait()

            times = pl.ds(number * chunk, chunk)
            for start in range(0, points, TILE):
                stop = min(start + TILE, points)
                greens = [greens_ref[j, times, start:stop, :] for j in range(STEPS)]
                terms = [greens[0]]
                for i in range(STEPS):
                    total = None
                    for j in range(STEPS):
                        spot = STEPS * i + j
                        factor = factor_ref[start:stop, spot * WIDTH : (spot + 1) * WIDTH]
                        term = factor[None] * greens[j]
                        total = term if total is None else total + term
                    terms.append(roll_blocks(total, STEPS * i))
                held_ref[slot, :, start:stop, :] = tree_sum(terms)
            copy(number, slot).start()
        return carry

    groups = history // (chunk * slots)
    lax.fori_loop(0, groups, advance, 0)
    for slot in range(slots):
        copy((groups - 1) * slots + slot, slot).wait()


def gather_tables():
    blocks = 2 * BANDS
    pairs = STEPS * STEPS // 2
    table = np.zeros((pairs, 2, blocks, BANDS, 2, BANDS, BANDS), np.float32)
    signs = np.zeros((pairs, blocks, BANDS), np.float32)
    for pair in range(pairs):
        for p in range(blocks):
            i, j = divmod(2 * pair + p // BANDS, STEPS)
            h, a = divmod((p + STEPS * i) % blocks, BANDS)
            g, c = divmod((p + j) % blocks, BANDS)
            table[pair, :, p, :, h ^ g, a, c] = 1 if (h, g) == (0, 1) else -1
            signs[pair, p] = 1 if h == g else -1
    return signs.reshape(pairs, WIDTH), table.reshape(-1, WIDTH).astype(ml_dtypes.bfloat16)


def spread_table():
    blocks = 2 * BANDS
    table = np.zeros((2, BANDS, BANDS, STEPS, STEPS, blocks, BANDS), np.float32)
    for i in range(STEPS):
        for j in range(STEPS):
            for p in range(blocks):
                h, a = divmod((p - STEPS * i) % blocks, BANDS)
                g, b = divmod((p + j) % blocks, BANDS)
                table[1 if h == g else 0, a, b, i, j, p, :] = -1 if (h, g) == (1, 0) else 1
    return np.tile(table.reshape(WIDTH, -1), (2, 1)).astype(ml_dtypes.bfloat16)


def in_vmem():
    return pl.BlockSpec(memory_space=pltpu.VMEM)


def in_smem():
    return pl.BlockSpec(memory_space=pltpu.SMEM)


def anywhere():
    return pl.BlockSpec(memory_space=pl.ANY)


def params(megabytes):
    return pltpu.CompilerParams(vmem_limit_bytes=megabytes * 1024 * 1024)


def cost(per_element, arrays):
    size = SIDE * SIDE * TILE * WIDTH
    return pl.CostEstimate(flops=per_element * size, bytes_accessed=4 * arrays * size, transcendentals=0)


def held_blocks(count, parts):
    return [
        pltpu.VMEM((count, TILE * SIDE * SIDE // parts, WIDTH), jnp.float32),
        pltpu.SemaphoreType.DMA((count,)),
    ]


def forward(place, greens, steps, parts):
    points = SIDE * SIDE
    return pl.pallas_call(
        functools.partial(forward_kernel, steps, parts),
        out_shape=[
            jax.ShapeDtypeStruct((points, TILE, WIDTH), jnp.float32),
            jax.ShapeDtypeStruct((STEPS, TILE * points, WIDTH), jnp.float32),
        ],
        in_specs=[in_smem()] + [anywhere()] * len(steps),
        out_specs=[in_vmem()] * 2,
        scratch_shapes=[pltpu.VMEM((points, TILE, WIDTH), jnp.float32)] + held_blocks(len(steps), parts),
        compiler_params=params(8),
        cost_estimate=cost(400, 6),
        name="forward",
    )(place, *greens)


def early_lines(place, lattice, weights, screens, steps, parts, work=None):
    points = SIDE * SIDE
    inputs = (place, lattice, weights, *screens) + (() if work is None else (work,))
    return pl.pallas_call(
        functools.partial(early_kernel, steps, parts),
        out_shape=jax.ShapeDtypeStruct((points, TILE, WIDTH), jnp.float32),
        in_specs=[in_smem(), in_vmem(), in_vmem()]
        + [anywhere()] * len(steps)
        + [in_vmem()] * (work is not None),
        out_specs=in_vmem(),
        input_output_aliases={} if work is None else {len(inputs) - 1: 0},
        scratch_shapes=held_blocks(len(steps), parts),
        compiler_params=params(4),
        cost_estimate=cost(25 * len(steps), 3),
        name="early",
    )(*inputs)


def sigma_of(place, lattice, weights, screens, work, steps, parts):
    points = SIDE * SIDE
    inputs = (place, lattice, weights, *screens, work)
    work, sigma = pl.pallas_call(
        functools.partial(sigma_kernel, steps, parts),
        out_shape=[
            jax.ShapeDtypeStruct((points, TILE, WIDTH), jnp.float32),
            jax.ShapeDtypeStruct((TILE * points, WIDTH), jnp.float32),
        ],
        in_specs=[in_smem()] + [in_vmem()] * 2 + [anywhere()] * len(steps) + [in_vmem()],
        out_specs=[in_vmem()] * 2,
        input_output_aliases={len(inputs) - 1: 0},
        scratch_shapes=held_blocks(len(steps), parts) if steps else [],
        compiler_params=params(4),
        cost_estimate=cost(200, 6),
        name="sigma",
    )(*inputs)
    return sigma


def contract(owners, sigma, equal_time, greens, block, share, before=()):
    points = owners.shape[0] * block
    rows = -(-points // 16) * 16
    signs, gather = gather_tables()
    return pl.pallas_call(
        functools.partial(contract_kernel, share),
        out_shape=jax.ShapeDtypeStruct((points, WIDTH), jnp.float32),
        in_specs=[in_smem()] + [in_vmem()] * 5 + [anywhere()] * len(before),
        out_specs=in_vmem(),
        scratch_shapes=[
            pltpu.VMEM((rows, STEPS * STEPS * WIDTH), jnp.float32),
            pltpu.VMEM((rows, STEPS * STEPS * WIDTH), jnp.bfloat16),
        ],
        compiler_params=params(10),
        cost_estimate=cost(70 * owners.shape[0], 6),
        name="contract",
    )(owners, sigma, equal_time, jnp.asarray(signs), jnp.asarray(gather), greens, *before)


def roll_own(place, greens, whole, step, parts):
    rows = whole.shape[0] // parts
    return pl.pallas_call(
        functools.partial(roll_kernel, step=step, parts=parts),
        out_shape=[
            jax.ShapeDtypeStruct((STEPS, *greens.shape), jnp.float32),
            jax.ShapeDtypeStruct((rows, whole.shape[1]), whole.dtype),
        ],
        in_specs=[in_smem(), in_vmem(), in_vmem()],
        out_specs=[in_vmem()] * 2,
        compiler_params=params(4),
        cost_estimate=cost(8, 9),
        name="roll_own",
    )(place, greens, whole)


def propagate(greens, effective):
    _, history, points, width = greens.shape
    chunk = math.gcd(history // 2, TILE)
    spread = spread_table()
    return pl.pallas_call(
        propagate_kernel,
        out_shape=jax.ShapeDtypeStruct(greens.shape[1:], jnp.float32),
        in_specs=[in_vmem()] * 3,
        out_specs=anywhere(),
        scratch_shapes=[
            pltpu.VMEM((points, spread.shape[1]), jnp.float32),
            pltpu.VMEM((2, chunk, points, width), jnp.float32),
            pltpu.SemaphoreType.DMA((2,)),
        ],
        compiler_params=params(6),
        cost_estimate=cost(32, 5),
        name="propagate",
    )(greens, effective, jnp.asarray(spread))


def partner_of(place, step, count):
    if count == 1:
        return 0
    if count & (count - 1) == 0:
        return place ^ step
    return (place + step) % count


def exchange(value, axis, step, count):
    pairs = [(place, partner_of(place, step, count)) for place in range(count)]
    return lax.ppermute(value, axis, pairs)


def exchange_order(count):
    along = {}
    for step in range(1, count):
        along.setdefault(step // 2, []).append(step)
    single = [along[n] for n in along if n and n & (n - 1) == 0]
    mixed = [along[n] for n in along if n & (n - 1)]
    order = [step for steps in zip(*single[::-1]) for step in steps]
    return order + along[0] + [step for steps in mixed for step in steps]


def after(index, received):
    return index + (received[0, 0] > LARGE).astype(jnp.int32)


def class_weights(quad_class):
    table = jnp.array(quadrature, jnp.float32)
    match = quad_class[:, None] == jnp.arange(4, dtype=jnp.int32)[None, :]
    return jnp.sum(jnp.where(match, table[None, :], jnp.float32(0.0)), axis=1)


def per_device(parts, blocks, green_row, screened, hamilton, equal_time, quad_class, live_count):
    history, local, width = green_row.shape
    points = local * parts
    times = history // parts
    place = lax.axis_index("ka")
    seat = place.reshape(1)
    position = jnp.arange(history, dtype=jnp.int32)
    weights = jnp.where(
        position < live_count[0], time_step * class_weights(quad_class), jnp.float32(0.0)
    ) * jnp.float32(1.0 / points)
    weights = lax.dynamic_slice_in_dim(weights, place * times, times)

    if times == TILE and local % SIDE == 0:
        groups, sources = 1, parts
        order = exchange_order(parts)
        moved = []
        wholes = [x.reshape(parts * TILE * local, width) for x in (green_row, screened)]
        first, diagonal = order[: parts - 1 - LATE], order[parts - 1 - LATE :]

        def send(whole, steps, found, received=None):
            for step in steps:
                start = partner_of(place, step, parts) * (TILE * local)
                if received is not None:
                    start = after(start, received)
                block = lax.dynamic_slice_in_dim(whole, start, TILE * local)
                if whole is wholes[1] and step == order[HANDED]:
                    block = handed
                found[step] = exchange(block, "ka", step, parts)

        own_greens, handed = roll_own(seat, green_row, wholes[1], order[HANDED], parts)
        found_green, found_screen = {0: wholes[0]}, {0: wholes[1]}
        send(wholes[0], first, found_green)
        send(wholes[0], diagonal, found_green)
        send(wholes[1], first, found_screen, found_green[first[0]])
        send(wholes[1], diagonal, found_screen, found_green[diagonal[-1]])
        moved = [[found_green], [found_screen]]
        order = [0] + order
    else:
        groups, sources = -(-times // TILE), 1
        order = [0]
        padding = groups * TILE - times
        moved = []
        for x in (green_row, screened):
            x = lax.all_to_all(x, "ka", split_axis=0, concat_axis=0, tiled=True)
            x = x.reshape(parts, times, local, width).transpose(1, 0, 2, 3).reshape(times, points, width)
            x = jnp.pad(x, ((0, padding), (0, 0), (0, 0))).reshape(groups, TILE * points, width)
            moved.append([{0: x[group]} for group in range(groups)])
        weights = jnp.pad(weights, (0, padding))
        own_greens, _ = roll_own(seat, green_row, screened.reshape(-1, width), 0, 1)
    weights = jnp.broadcast_to(weights.reshape(groups, TILE, 1), (groups, TILE, width))

    early = order[: max(1, len(order) - LATE)]
    late = order[len(early) :]
    share = hubbard / (points * blocks)
    sigmas = []
    for group in range(groups):
        green, screen = moved[0][group], moved[1][group]
        lattice, greens = forward(seat, [green[step] for step in order], order, sources)
        work = early_lines(seat, lattice, weights[group], [screen[step] for step in early], early, sources)
        for step in late[:-1]:
            work = early_lines(seat, lattice, weights[group], [screen[step]], [step], sources, work)
        last = late[-1:]
        sigma = sigma_of(
            seat, lattice, weights[group], [screen[step] for step in last], work, last, sources
        )
        sigmas.append((sigma, greens))

    if sources == parts and parts % 2 == 0 and parts & (parts - 1) == 0:
        (sigma, greens), = sigmas

        def blocks_of(steps, before=()):
            owners = jnp.stack([partner_of(place, step, parts) for step in steps])
            return contract(owners, sigma, equal_time, greens, local, share, before)

        others = exchange(blocks_of([*range(3, parts, 2), 1]), "ka", 1, parts)
        far = blocks_of(list(range(2, parts, 2))) + others[:-local]
        pieces = [
            exchange(far[(n - 1) * local : n * local], "ka", 2 * n, parts)
            for n in range(parts // 2 - 1, 0, -1)
        ]
        pieces += [blocks_of([0], pieces[:1]), others[-local:]]
        collision = tree_sum(pieces)
    else:
        whole = jnp.zeros((1,), jnp.int32)
        partial_value = tree_sum(
            [
                contract(whole, sigma, equal_time, greens, points, share if group == 0 else 0.0)
                for group, (sigma, greens) in enumerate(sigmas)
            ]
        )
        owners = [partner_of(place, step, parts) for step in range(parts)]
        pieces = [lax.dynamic_slice_in_dim(partial_value, owner * local, local) for owner in owners]
        collision = tree_sum(
            pieces[:1] + [exchange(pieces[step], "ka", step, parts) for step in range(1, parts)]
        )
    collision = tree_sum(
        [collision] + [exchange(collision, "hist", step, blocks) for step in range(blocks - 1, 0, -1)]
    )
    return propagate(own_greens, hamilton + collision)


def solution(mesh):
    in_specs = (
        P("hist", "ka", None),
        P("hist", "ka", None),
        P("ka", None),
        P("ka", None),
        P("hist"),
        P("hist"),
    )
    out_specs = P("hist", "ka", None)
    return jax.shard_map(
        functools.partial(per_device, mesh.shape["ka"], mesh.shape["hist"]),
        mesh=mesh,
        in_specs=in_specs,
        out_specs=out_specs,
        check_vma=False,
    )
```

```python
import functools
import math

import jax
import jax.numpy as jnp
import ml_dtypes
import numpy as np
from jax import lax
from jax.experimental import pallas as pl
from jax.experimental.pallas import tpu as pltpu
from jax.sharding import PartitionSpec as P

SIDE = 24
BANDS = 8
ENTRIES = BANDS * BANDS
WIDTH = 2 * ENTRIES
TILE = 8
STEPS = 4

time_step = 0.1
hubbard = 1.0
quadrature = (0.375, 1.1666666, 0.9583333, 1.0)

LATE = 2
AHEAD = 3


def lane_sign(shape):
    lane = lax.broadcasted_iota(jnp.int32, shape, len(shape) - 1)
    return lane < ENTRIES


def swap(x):
    return pltpu.roll(x, ENTRIES, 1)


def roll_blocks(x, blocks):
    return x if blocks == 0 else pltpu.roll(x, WIDTH - BANDS * blocks, x.ndim - 1)


def tree_sum(terms):
    while len(terms) > 1:
        terms = [sum(terms[i : i + 2][1:], terms[i]) for i in range(0, len(terms), 2)]
    return terms[0]


def split(x):
    high = x.astype(jnp.bfloat16)
    return jnp.concatenate([high, (x - high.astype(jnp.float32)).astype(jnp.bfloat16)], axis=1)


def dft24(x, sign, low):
    root3 = jnp.where(low, -1.0, 1.0) * (sign * math.sqrt(3.0) / 2)
    turn = jnp.where(low, -1.0, 1.0) * float(sign)
    half = math.sqrt(0.5)
    turn_half = turn * half
    columns = [[None] * 8 for _ in range(3)]
    for n2 in range(8):
        x0, x1, x2 = (x[(8 * n1 + 3 * n2) % 24] for n1 in range(3))
        total = x1 + x2
        base = x0 - 0.5 * total
        spin = swap(x1 - x2) * root3
        columns[0][n2] = x0 + total
        columns[1][n2] = base + spin
        columns[2][n2] = base - spin
    out = [None] * 24
    for k1 in range(3):
        c = columns[k1]
        a0, a1 = c[0] + c[4], c[0] - c[4]
        a2, a3 = c[2] + c[6], c[2] - c[6]
        a4, a5 = c[1] + c[5], c[1] - c[5]
        a6, a7 = c[3] + c[7], c[3] - c[7]
        b0, b1 = a0 + a2, a0 - a2
        b2, b3 = a4 + a6, a4 - a6
        i_a3 = swap(a3) * turn
        i_b3 = swap(b3) * turn
        c0, c1 = a1 + i_a3, a1 - i_a3
        p = (a5 - a7) * half
        m = swap(a5 + a7) * turn_half
        e, f = p + m, p - m
        values = [b0 + b2, c0 + e, b1 + i_b3, c1 - f, b0 - b2, c0 - e, b1 - i_b3, c1 + f]
        for k2 in range(8):
            out[(16 * k1 + 9 * k2) % 24] = values[k2]
    return out


def load_line(ref, line):
    stride = ref.shape[0] // TILE
    return [ref[pl.ds(line * SIDE + k2, TILE, stride=stride), :] for k2 in range(SIDE)]


def fetch(place, steps, block_refs, held_ref, sems):
    copies = []
    for slot, (step, source) in enumerate(zip(steps, block_refs)):
        rows = held_ref.shape[1]
        if step == 0 and source.shape[0] != rows:
            source = source.at[pl.ds(pl.multiple_of(place * rows, TILE), rows)]
        copies.append(pltpu.make_async_copy(source, held_ref.at[slot], sems.at[slot]))
        copies[-1].start()
    return copies


def along_first(work_ref, sign, low, store):
    def columns(pair, carry):
        both = (2 * pair, 2 * pair + 1)
        rows = [[work_ref[k1 * SIDE + column] for k1 in range(SIDE)] for column in both]
        values = [dft24(row, sign, low) for row in rows]
        for column, value in zip(both, values):
            for r1 in range(SIDE):
                store(r1 * SIDE + column, value[r1])
        return carry

    lax.fori_loop(0, SIDE // 2, columns, 0)


def roll_kernel(green_ref, greens_ref):
    batch = math.gcd(green_ref.shape[0], STEPS)

    def rolls(n, carry):
        times = pl.ds(n * batch, batch)
        green = green_ref[times]
        rolled = [roll_blocks(green, j) for j in range(STEPS)]
        for j in range(STEPS):
            greens_ref[j, times] = rolled[j]
        return carry

    lax.fori_loop(0, green_ref.shape[0] // batch, rolls, 0)


def forward_kernel(steps, parts, place_ref, *refs):
    block_refs, (lattice_ref, greens_ref, work_ref, held_ref, sems) = refs[: len(steps)], refs[len(steps) :]
    low = lane_sign((TILE, WIDTH))
    place = place_ref[0]
    copies = fetch(place, steps, block_refs, held_ref, sems)
    rows = held_ref.shape[1]
    lines = rows // (TILE * SIDE)
    for slot, step in enumerate(steps):
        copies[slot].wait()
        green_ref = held_ref.at[slot]
        owner = partner_of(place, step, parts)

        def along_second(i, carry):
            for r2, value in enumerate(dft24(load_line(green_ref, i), -1, low)):
                work_ref[(owner * lines + i) * SIDE + r2] = value
            return carry

        lax.fori_loop(0, lines, along_second, 0, unroll=lines <= 4)
        green = green_ref[...]
        spot = pl.ds(pl.multiple_of(owner * rows, TILE), rows)
        for j in range(STEPS):
            greens_ref[j, spot, :] = roll_blocks(green, j)

    def store(point, value):
        lattice_ref[point] = value

    along_first(work_ref, -1, low, store)


def product_lines(steps, parts, place, lattice_ref, weights, screen_refs, held_ref, sems, work_ref):
    low = lane_sign((TILE, WIDTH))
    turn = jnp.where(low, -1.0, 1.0)
    copies = fetch(place, steps, screen_refs, held_ref, sems)
    lines = held_ref.shape[1] // (TILE * SIDE)
    for slot, step in enumerate(steps):
        copies[slot].wait()
        screen_ref = held_ref.at[slot]
        first = partner_of(place, step, parts) * lines

        def along_second(i, carry):
            rows = []
            for r2, value in enumerate(load_line(screen_ref, i)):
                screen = value * weights
                other = swap(screen)
                lattice = lattice_ref[(first + i) * SIDE + r2]
                rows.append(
                    swap(lattice) * turn * jnp.where(low, screen, other)
                    - lattice * jnp.where(low, other, screen)
                )
            for k2, value in enumerate(dft24(rows, 1, low)):
                work_ref[(first + i) * SIDE + k2] = value
            return carry

        lax.fori_loop(0, lines, along_second, 0, unroll=lines <= 4)


def early_kernel(steps, parts, place_ref, lattice_ref, weight_ref, *refs):
    screen_refs, (*_, work_ref, held_ref, sems) = refs[: len(steps)], refs[len(steps) :]
    product_lines(
        steps, parts, place_ref[0], lattice_ref, weight_ref[...], screen_refs, held_ref, sems, work_ref
    )


def sigma_kernel(steps, parts, place_ref, lattice_ref, weight_ref, *refs):
    screen_refs, refs = refs[: len(steps)], refs[len(steps) :]
    _, work_ref, sigma_ref, *late = refs
    low = lane_sign((TILE, WIDTH))
    if steps:
        held_ref, sems = late
        product_lines(
            steps, parts, place_ref[0], lattice_ref, weight_ref[...], screen_refs, held_ref, sems, work_ref
        )

    def store(point, value):
        sigma_ref[pl.ds(point * TILE, TILE), :] = value

    along_first(work_ref, 1, low, store)


def contract_kernel(share, owner_ref, sigma_ref, equal_ref, sign_ref, gather_ref, greens_ref, *refs):
    partial_ref, sums_ref, pieces_ref = refs[-3:]
    low = lane_sign((TILE, WIDTH))
    points = partial_ref.shape[0]
    block = points // owner_ref.shape[0]
    tiles = block // TILE
    batch = max(n for n in range(1, 10) if tiles % n == 0)

    def contract(group, carry):
        slot, first = group // (tiles // batch), group % (tiles // batch) * batch
        owner = owner_ref[slot]
        units = [(tile, s) for tile in range(batch) for s in range(TILE)]

        def prepare(tile, s):
            point = owner * block + (first + tile) * TILE
            sigma = sigma_ref[pl.ds(point * TILE + s, TILE, stride=TILE), :]
            row = pl.multiple_of((owner * TILE + s) * block + (first + tile) * TILE, TILE)
            return (
                [roll_blocks(sigma, STEPS * i) for i in range(STEPS)],
                [greens_ref[j, pl.ds(row, TILE), :] for j in range(STEPS)],
            )

        ready = [prepare(*unit) for unit in units[:AHEAD]]
        for n, (tile, s) in enumerate(units):
            if n + AHEAD < len(units):
                ready.append(prepare(*units[n + AHEAD]))
            sigmas, greens = ready.pop(0)
            terms = [sigma * green for sigma in sigmas for green in greens]
            sums = terms if s == 0 else [a + b for a, b in zip(sums, terms)]
            if s == TILE - 1:
                row = pl.ds(pl.multiple_of(slot * block + (first + tile) * TILE, TILE), TILE)
                for spot, value in enumerate(sums):
                    sums_ref[row, spot * WIDTH : (spot + 1) * WIDTH] = value
        return carry

    lax.fori_loop(0, points // (TILE * batch), contract, 0)

    lane = lax.broadcasted_iota(jnp.int32, equal_ref.shape, 1)
    inner = lane - ENTRIES
    occupied = jnp.sum(jnp.where((inner >= 0) & (inner % (BANDS + 1) == 0), equal_ref[...], 0.0))
    spots = lax.broadcasted_iota(jnp.int32, (points, WIDTH), 1)
    on_diagonal = (spots < ENTRIES) & (spots % (BANDS + 1) == 0)
    lower = lax.broadcasted_iota(jnp.int32, (sums_ref.shape[0], WIDTH), 1) < ENTRIES
    for pair in range(STEPS * STEPS // 2):
        first_part = sums_ref[:, 2 * pair * WIDTH : (2 * pair + 1) * WIDTH]
        second_part = sums_ref[:, (2 * pair + 1) * WIDTH : (2 * pair + 2) * WIDTH]
        folded = jnp.where(lower, first_part, second_part) + sign_ref[pair : pair + 1, :] * swap(
            jnp.where(lower, second_part, first_part)
        )
        pieces_ref[:, 2 * pair * WIDTH : (2 * pair + 2) * WIDTH] = split(folded)
    total = jnp.dot(pieces_ref[...], gather_ref[...], preferred_element_type=jnp.float32)
    partial_ref[...] = total[:points] + jnp.where(on_diagonal, occupied * share, 0.0)


def propagate_kernel(greens_ref, effective_ref, spread_ref, out_ref, factor_ref, held_ref, sems):
    _, history, points, _ = greens_ref.shape
    factor_ref[...] = jnp.dot(
        split(effective_ref[...] * time_step), spread_ref[...], preferred_element_type=jnp.float32
    )

    slots, chunk = held_ref.shape[:2]

    def copy(number, slot):
        return pltpu.make_async_copy(
            held_ref.at[slot], out_ref.at[pl.ds(number * chunk, chunk)], sems.at[slot]
        )

    def advance(group, carry):
        for slot in range(slots):
            number = group * slots + slot

            @pl.when(group > 0)
            def _():
                copy(number - slots, slot).wait()

            times = pl.ds(number * chunk, chunk)
            for start in range(0, points, TILE):
                stop = min(start + TILE, points)
                greens = [greens_ref[j, times, start:stop, :] for j in range(STEPS)]
                terms = [greens[0]]
                for i in range(STEPS):
                    total = None
                    for j in range(STEPS):
                        spot = STEPS * i + j
                        factor = factor_ref[start:stop, spot * WIDTH : (spot + 1) * WIDTH]
                        term = factor[None] * greens[j]
                        total = term if total is None else total + term
                    terms.append(roll_blocks(total, STEPS * i))
                held_ref[slot, :, start:stop, :] = tree_sum(terms)
            copy(number, slot).start()
        return carry

    groups = history // (chunk * slots)
    lax.fori_loop(0, groups, advance, 0)
    for slot in range(slots):
        copy((groups - 1) * slots + slot, slot).wait()


def gather_tables():
    blocks = 2 * BANDS
    pairs = STEPS * STEPS // 2
    table = np.zeros((pairs, 2, blocks, BANDS, 2, BANDS, BANDS), np.float32)
    signs = np.zeros((pairs, blocks, BANDS), np.float32)
    for pair in range(pairs):
        for p in range(blocks):
            i, j = divmod(2 * pair + p // BANDS, STEPS)
            h, a = divmod((p + STEPS * i) % blocks, BANDS)
            g, c = divmod((p + j) % blocks, BANDS)
            table[pair, :, p, :, h ^ g, a, c] = 1 if (h, g) == (0, 1) else -1
            signs[pair, p] = 1 if h == g else -1
    return signs.reshape(pairs, WIDTH), table.reshape(-1, WIDTH).astype(ml_dtypes.bfloat16)


def spread_table():
    blocks = 2 * BANDS
    table = np.zeros((2, BANDS, BANDS, STEPS, STEPS, blocks, BANDS), np.float32)
    for i in range(STEPS):
        for j in range(STEPS):
            for p in range(blocks):
                h, a = divmod((p - STEPS * i) % blocks, BANDS)
                g, b = divmod((p + j) % blocks, BANDS)
                table[1 if h == g else 0, a, b, i, j, p, :] = -1 if (h, g) == (1, 0) else 1
    return np.tile(table.reshape(WIDTH, -1), (2, 1)).astype(ml_dtypes.bfloat16)


def in_vmem():
    return pl.BlockSpec(memory_space=pltpu.VMEM)


def in_smem():
    return pl.BlockSpec(memory_space=pltpu.SMEM)


def anywhere():
    return pl.BlockSpec(memory_space=pl.ANY)


def params(megabytes):
    return pltpu.CompilerParams(vmem_limit_bytes=megabytes * 1024 * 1024)


def cost(per_element, arrays):
    size = SIDE * SIDE * TILE * WIDTH
    return pl.CostEstimate(flops=per_element * size, bytes_accessed=4 * arrays * size, transcendentals=0)


def held_blocks(count, parts):
    return [
        pltpu.VMEM((count, TILE * SIDE * SIDE // parts, WIDTH), jnp.float32),
        pltpu.SemaphoreType.DMA((count,)),
    ]


def forward(place, greens, steps, parts):
    points = SIDE * SIDE
    return pl.pallas_call(
        functools.partial(forward_kernel, steps, parts),
        out_shape=[
            jax.ShapeDtypeStruct((points, TILE, WIDTH), jnp.float32),
            jax.ShapeDtypeStruct((STEPS, TILE * points, WIDTH), jnp.float32),
        ],
        in_specs=[in_smem()] + [anywhere()] * len(steps),
        out_specs=[in_vmem()] * 2,
        scratch_shapes=[pltpu.VMEM((points, TILE, WIDTH), jnp.float32)] + held_blocks(len(steps), parts),
        compiler_params=params(8),
        cost_estimate=cost(400, 6),
        name="forward",
    )(place, *greens)


def early_lines(place, lattice, weights, screens, steps, parts, work=None):
    points = SIDE * SIDE
    inputs = (place, lattice, weights, *screens) + (() if work is None else (work,))
    return pl.pallas_call(
        functools.partial(early_kernel, steps, parts),
        out_shape=jax.ShapeDtypeStruct((points, TILE, WIDTH), jnp.float32),
        in_specs=[in_smem(), in_vmem(), in_vmem()]
        + [anywhere()] * len(steps)
        + [in_vmem()] * (work is not None),
        out_specs=in_vmem(),
        input_output_aliases={} if work is None else {len(inputs) - 1: 0},
        scratch_shapes=held_blocks(len(steps), parts),
        compiler_params=params(4),
        cost_estimate=cost(25 * len(steps), 3),
        name="early",
    )(*inputs)


def sigma_of(place, lattice, weights, screens, work, steps, parts):
    points = SIDE * SIDE
    inputs = (place, lattice, weights, *screens, work)
    work, sigma = pl.pallas_call(
        functools.partial(sigma_kernel, steps, parts),
        out_shape=[
            jax.ShapeDtypeStruct((points, TILE, WIDTH), jnp.float32),
            jax.ShapeDtypeStruct((TILE * points, WIDTH), jnp.float32),
        ],
        in_specs=[in_smem()] + [in_vmem()] * 2 + [anywhere()] * len(steps) + [in_vmem()],
        out_specs=[in_vmem()] * 2,
        input_output_aliases={len(inputs) - 1: 0},
        scratch_shapes=held_blocks(len(steps), parts) if steps else [],
        compiler_params=params(4),
        cost_estimate=cost(200, 6),
        name="sigma",
    )(*inputs)
    return sigma


def contract(owners, sigma, equal_time, greens, block, share, before=()):
    points = owners.shape[0] * block
    rows = -(-points // 16) * 16
    signs, gather = gather_tables()
    return pl.pallas_call(
        functools.partial(contract_kernel, share),
        out_shape=jax.ShapeDtypeStruct((points, WIDTH), jnp.float32),
        in_specs=[in_smem()] + [in_vmem()] * 5 + [anywhere()] * len(before),
        out_specs=in_vmem(),
        scratch_shapes=[
            pltpu.VMEM((rows, STEPS * STEPS * WIDTH), jnp.float32),
            pltpu.VMEM((rows, STEPS * STEPS * WIDTH), jnp.bfloat16),
        ],
        compiler_params=params(10),
        cost_estimate=cost(70 * owners.shape[0], 6),
        name="contract",
    )(owners, sigma, equal_time, jnp.asarray(signs), jnp.asarray(gather), greens, *before)


def roll_own(greens):
    return pl.pallas_call(
        roll_kernel,
        out_shape=jax.ShapeDtypeStruct((STEPS, *greens.shape), jnp.float32),
        in_specs=[in_vmem()],
        out_specs=in_vmem(),
        compiler_params=params(4),
        cost_estimate=cost(3, 5),
        name="roll_own",
    )(greens)


def propagate(greens, effective):
    _, history, points, width = greens.shape
    chunk = math.gcd(history // 2, TILE)
    spread = spread_table()
    return pl.pallas_call(
        propagate_kernel,
        out_shape=jax.ShapeDtypeStruct(greens.shape[1:], jnp.float32),
        in_specs=[in_vmem()] * 3,
        out_specs=anywhere(),
        scratch_shapes=[
            pltpu.VMEM((points, spread.shape[1]), jnp.float32),
            pltpu.VMEM((2, chunk, points, width), jnp.float32),
            pltpu.SemaphoreType.DMA((2,)),
        ],
        compiler_params=params(6),
        cost_estimate=cost(32, 5),
        name="propagate",
    )(greens, effective, jnp.asarray(spread))


def partner_of(place, step, count):
    if count == 1:
        return 0
    if count & (count - 1) == 0:
        return place ^ step
    return (place + step) % count


def exchange(value, axis, step, count):
    pairs = [(place, partner_of(place, step, count)) for place in range(count)]
    return lax.ppermute(value, axis, pairs)


def exchange_order(count):
    along = {}
    for step in range(1, count):
        along.setdefault(step // 2, []).append(step)
    single = [along[n] for n in along if n and n & (n - 1) == 0]
    mixed = [along[n] for n in along if n & (n - 1)]
    order = [step for steps in zip(*single[::-1]) for step in steps]
    return order + along[0] + [step for steps in mixed for step in steps]


def class_weights(quad_class):
    table = jnp.array(quadrature, jnp.float32)
    match = quad_class[:, None] == jnp.arange(4, dtype=jnp.int32)[None, :]
    return jnp.sum(jnp.where(match, table[None, :], jnp.float32(0.0)), axis=1)


def per_device(parts, blocks, green_row, screened, hamilton, equal_time, quad_class, live_count):
    history, local, width = green_row.shape
    points = local * parts
    times = history // parts
    place = lax.axis_index("ka")
    seat = place.reshape(1)
    position = jnp.arange(history, dtype=jnp.int32)
    weights = jnp.where(
        position < live_count[0], time_step * class_weights(quad_class), jnp.float32(0.0)
    ) * jnp.float32(1.0 / points)
    weights = lax.dynamic_slice_in_dim(weights, place * times, times)

    if times == TILE and local % SIDE == 0:
        groups, sources = 1, parts
        order = exchange_order(parts)
        moved = []
        wholes = [x.reshape(parts * TILE * local, width) for x in (green_row, screened)]
        moved = []
        for whole in wholes:
            found = {0: whole}
            for step in order:
                start = partner_of(place, step, parts) * (TILE * local)
                block = lax.dynamic_slice_in_dim(whole, start, TILE * local)
                found[step] = exchange(block, "ka", step, parts)
            moved.append([found])
        order = [0] + order
    else:
        groups, sources = -(-times // TILE), 1
        order = [0]
        padding = groups * TILE - times
        moved = []
        for x in (green_row, screened):
            x = lax.all_to_all(x, "ka", split_axis=0, concat_axis=0, tiled=True)
            x = x.reshape(parts, times, local, width).transpose(1, 0, 2, 3).reshape(times, points, width)
            x = jnp.pad(x, ((0, padding), (0, 0), (0, 0))).reshape(groups, TILE * points, width)
            moved.append([{0: x[group]} for group in range(groups)])
        weights = jnp.pad(weights, (0, padding))
    weights = jnp.broadcast_to(weights.reshape(groups, TILE, 1), (groups, TILE, width))

    early = order[: max(1, len(order) - LATE)]
    late = order[len(early) :]
    own_greens = roll_own(green_row)
    share = hubbard / (points * blocks)
    sigmas = []
    for group in range(groups):
        green, screen = moved[0][group], moved[1][group]
        listed = order[::-1]
        lattice, greens = forward(seat, [green[step] for step in listed], listed, sources)
        listed = early[-2::-1] + early[-1:]
        work = early_lines(seat, lattice, weights[group], [screen[step] for step in listed], listed, sources)
        for step in late[:-1]:
            work = early_lines(seat, lattice, weights[group], [screen[step]], [step], sources, work)
        last = late[-1:]
        sigma = sigma_of(
            seat, lattice, weights[group], [screen[step] for step in last], work, last, sources
        )
        sigmas.append((sigma, greens))

    if sources == parts and parts % 2 == 0 and parts & (parts - 1) == 0:
        (sigma, greens), = sigmas

        def blocks_of(steps, before=()):
            owners = jnp.stack([partner_of(place, step, parts) for step in steps])
            return contract(owners, sigma, equal_time, greens, local, share, before)

        others = exchange(blocks_of([*range(3, parts, 2), 1]), "ka", 1, parts)
        far = blocks_of(list(range(2, parts, 2))) + others[:-local]
        pieces = [
            exchange(far[(n - 1) * local : n * local], "ka", 2 * n, parts)
            for n in range(parts // 2 - 1, 0, -1)
        ]
        pieces += [blocks_of([0], pieces[:1]), others[-local:]]
        collision = tree_sum(pieces)
    else:
        whole = jnp.zeros((1,), jnp.int32)
        partial_value = tree_sum(
            [
                contract(whole, sigma, equal_time, greens, points, share if group == 0 else 0.0)
                for group, (sigma, greens) in enumerate(sigmas)
            ]
        )
        owners = [partner_of(place, step, parts) for step in range(parts)]
        pieces = [lax.dynamic_slice_in_dim(partial_value, owner * local, local) for owner in owners]
        collision = tree_sum(
            pieces[:1] + [exchange(pieces[step], "ka", step, parts) for step in range(1, parts)]
        )
    collision = tree_sum(
        [collision] + [exchange(collision, "hist", step, blocks) for step in range(blocks - 1, 0, -1)]
    )
    return propagate(own_greens, hamilton + collision)


def solution(mesh):
    in_specs = (
        P("hist", "ka", None),
        P("hist", "ka", None),
        P("ka", None),
        P("ka", None),
        P("hist"),
        P("hist"),
    )
    out_specs = P("hist", "ka", None)
    return jax.shard_map(
        functools.partial(per_device, mesh.shape["ka"], mesh.shape["hist"]),
        mesh=mesh,
        in_specs=in_specs,
        out_specs=out_specs,
        check_vma=False,
    )
```

```python
import functools
import math

import jax
import jax.numpy as jnp
import ml_dtypes
import numpy as np
from jax import lax
from jax.experimental import pallas as pl
from jax.experimental.pallas import tpu as pltpu
from jax.sharding import PartitionSpec as P

SIDE = 24
BANDS = 8
ENTRIES = BANDS * BANDS
WIDTH = 2 * ENTRIES
TILE = 8
STEPS = 4

time_step = 0.1
hubbard = 1.0
quadrature = (0.375, 1.1666666, 0.9583333, 1.0)

LATE = 2
AHEAD = 3


def lane_sign(shape):
    lane = lax.broadcasted_iota(jnp.int32, shape, len(shape) - 1)
    return lane < ENTRIES


def swap(x):
    return pltpu.roll(x, ENTRIES, 1)


def roll_blocks(x, blocks):
    return x if blocks == 0 else pltpu.roll(x, WIDTH - BANDS * blocks, x.ndim - 1)


def tree_sum(terms):
    while len(terms) > 1:
        terms = [sum(terms[i : i + 2][1:], terms[i]) for i in range(0, len(terms), 2)]
    return terms[0]


def split(x):
    high = x.astype(jnp.bfloat16)
    return jnp.concatenate([high, (x - high.astype(jnp.float32)).astype(jnp.bfloat16)], axis=1)


def dft24(x, sign, low):
    root3 = jnp.where(low, -1.0, 1.0) * (sign * math.sqrt(3.0) / 2)
    turn = jnp.where(low, -1.0, 1.0) * float(sign)
    half = math.sqrt(0.5)
    turn_half = turn * half
    columns = [[None] * 8 for _ in range(3)]
    for n2 in range(8):
        x0, x1, x2 = (x[(8 * n1 + 3 * n2) % 24] for n1 in range(3))
        total = x1 + x2
        base = x0 - 0.5 * total
        spin = swap(x1 - x2) * root3
        columns[0][n2] = x0 + total
        columns[1][n2] = base + spin
        columns[2][n2] = base - spin
    out = [None] * 24
    for k1 in range(3):
        c = columns[k1]
        a0, a1 = c[0] + c[4], c[0] - c[4]
        a2, a3 = c[2] + c[6], c[2] - c[6]
        a4, a5 = c[1] + c[5], c[1] - c[5]
        a6, a7 = c[3] + c[7], c[3] - c[7]
        b0, b1 = a0 + a2, a0 - a2
        b2, b3 = a4 + a6, a4 - a6
        i_a3 = swap(a3) * turn
        i_b3 = swap(b3) * turn
        c0, c1 = a1 + i_a3, a1 - i_a3
        p = (a5 - a7) * half
        m = swap(a5 + a7) * turn_half
        e, f = p + m, p - m
        values = [b0 + b2, c0 + e, b1 + i_b3, c1 - f, b0 - b2, c0 - e, b1 - i_b3, c1 + f]
        for k2 in range(8):
            out[(16 * k1 + 9 * k2) % 24] = values[k2]
    return out


def load_line(ref, line):
    stride = ref.shape[0] // TILE
    return [ref[pl.ds(line * SIDE + k2, TILE, stride=stride), :] for k2 in range(SIDE)]


def fetch(place, steps, block_refs, held_ref, sems):
    copies = []
    for slot, (step, source) in enumerate(zip(steps, block_refs)):
        rows = held_ref.shape[1]
        if step == 0 and source.shape[0] != rows:
            source = source.at[pl.ds(pl.multiple_of(place * rows, TILE), rows)]
        copies.append(pltpu.make_async_copy(source, held_ref.at[slot], sems.at[slot]))
        copies[-1].start()
    return copies


def along_first(work_ref, sign, low, store):
    def columns(pair, carry):
        both = (2 * pair, 2 * pair + 1)
        rows = [[work_ref[k1 * SIDE + column] for k1 in range(SIDE)] for column in both]
        values = [dft24(row, sign, low) for row in rows]
        for column, value in zip(both, values):
            for r1 in range(SIDE):
                store(r1 * SIDE + column, value[r1])
        return carry

    lax.fori_loop(0, SIDE // 2, columns, 0)


def roll_kernel(green_ref, greens_ref):
    batch = math.gcd(green_ref.shape[0], STEPS)

    def rolls(n, carry):
        times = pl.ds(n * batch, batch)
        green = green_ref[times]
        rolled = [roll_blocks(green, j) for j in range(STEPS)]
        for j in range(STEPS):
            greens_ref[j, times] = rolled[j]
        return carry

    lax.fori_loop(0, green_ref.shape[0] // batch, rolls, 0)


def forward_kernel(steps, parts, place_ref, *refs):
    block_refs, (lattice_ref, greens_ref, work_ref, held_ref, sems) = refs[: len(steps)], refs[len(steps) :]
    low = lane_sign((TILE, WIDTH))
    place = place_ref[0]
    copies = fetch(place, steps, block_refs, held_ref, sems)
    rows = held_ref.shape[1]
    lines = rows // (TILE * SIDE)
    for slot, step in enumerate(steps):
        copies[slot].wait()
        green_ref = held_ref.at[slot]
        owner = partner_of(place, step, parts)

        def along_second(i, carry):
            for r2, value in enumerate(dft24(load_line(green_ref, i), -1, low)):
                work_ref[(owner * lines + i) * SIDE + r2] = value
            return carry

        lax.fori_loop(0, lines, along_second, 0, unroll=lines <= 4)
        green = green_ref[...]
        spot = pl.ds(pl.multiple_of(owner * rows, TILE), rows)
        for j in range(STEPS):
            greens_ref[j, spot, :] = roll_blocks(green, j)

    def store(point, value):
        lattice_ref[point] = value

    along_first(work_ref, -1, low, store)


def product_lines(steps, parts, place, lattice_ref, weights, screen_refs, held_ref, sems, work_ref):
    low = lane_sign((TILE, WIDTH))
    turn = jnp.where(low, -1.0, 1.0)
    copies = fetch(place, steps, screen_refs, held_ref, sems)
    lines = held_ref.shape[1] // (TILE * SIDE)
    for slot, step in enumerate(steps):
        copies[slot].wait()
        screen_ref = held_ref.at[slot]
        first = partner_of(place, step, parts) * lines

        def along_second(i, carry):
            rows = []
            for r2, value in enumerate(load_line(screen_ref, i)):
                screen = value * weights
                other = swap(screen)
                lattice = lattice_ref[(first + i) * SIDE + r2]
                rows.append(
                    swap(lattice) * turn * jnp.where(low, screen, other)
                    - lattice * jnp.where(low, other, screen)
                )
            for k2, value in enumerate(dft24(rows, 1, low)):
                work_ref[(first + i) * SIDE + k2] = value
            return carry

        lax.fori_loop(0, lines, along_second, 0, unroll=lines <= 4)


def early_kernel(steps, parts, place_ref, lattice_ref, weight_ref, *refs):
    screen_refs, (*_, work_ref, held_ref, sems) = refs[: len(steps)], refs[len(steps) :]
    product_lines(
        steps, parts, place_ref[0], lattice_ref, weight_ref[...], screen_refs, held_ref, sems, work_ref
    )


def sigma_kernel(steps, parts, place_ref, lattice_ref, weight_ref, *refs):
    screen_refs, refs = refs[: len(steps)], refs[len(steps) :]
    _, work_ref, sigma_ref, *late = refs
    low = lane_sign((TILE, WIDTH))
    if steps:
        held_ref, sems = late
        product_lines(
            steps, parts, place_ref[0], lattice_ref, weight_ref[...], screen_refs, held_ref, sems, work_ref
        )

    def store(point, value):
        sigma_ref[pl.ds(point * TILE, TILE), :] = value

    along_first(work_ref, 1, low, store)


def contract_kernel(share, owner_ref, sigma_ref, equal_ref, sign_ref, gather_ref, greens_ref, *refs):
    partial_ref, sums_ref, pieces_ref = refs[-3:]
    low = lane_sign((TILE, WIDTH))
    points = partial_ref.shape[0]
    block = points // owner_ref.shape[0]
    tiles = block // TILE
    batch = max(n for n in range(1, 10) if tiles % n == 0)

    def contract(group, carry):
        slot, first = group // (tiles // batch), group % (tiles // batch) * batch
        owner = owner_ref[slot]
        units = [(tile, s) for tile in range(batch) for s in range(TILE)]

        def prepare(tile, s):
            point = owner * block + (first + tile) * TILE
            sigma = sigma_ref[pl.ds(point * TILE + s, TILE, stride=TILE), :]
            row = pl.multiple_of((owner * TILE + s) * block + (first + tile) * TILE, TILE)
            return (
                [roll_blocks(sigma, STEPS * i) for i in range(STEPS)],
                [greens_ref[j, pl.ds(row, TILE), :] for j in range(STEPS)],
            )

        ready = [prepare(*unit) for unit in units[:AHEAD]]
        for n, (tile, s) in enumerate(units):
            if n + AHEAD < len(units):
                ready.append(prepare(*units[n + AHEAD]))
            sigmas, greens = ready.pop(0)
            terms = [sigma * green for sigma in sigmas for green in greens]
            sums = terms if s == 0 else [a + b for a, b in zip(sums, terms)]
            if s == TILE - 1:
                row = pl.ds(pl.multiple_of(slot * block + (first + tile) * TILE, TILE), TILE)
                for spot, value in enumerate(sums):
                    sums_ref[row, spot * WIDTH : (spot + 1) * WIDTH] = value
        return carry

    lax.fori_loop(0, points // (TILE * batch), contract, 0)

    lane = lax.broadcasted_iota(jnp.int32, equal_ref.shape, 1)
    inner = lane - ENTRIES
    occupied = jnp.sum(jnp.where((inner >= 0) & (inner % (BANDS + 1) == 0), equal_ref[...], 0.0))
    spots = lax.broadcasted_iota(jnp.int32, (points, WIDTH), 1)
    on_diagonal = (spots < ENTRIES) & (spots % (BANDS + 1) == 0)
    lower = lax.broadcasted_iota(jnp.int32, (sums_ref.shape[0], WIDTH), 1) < ENTRIES
    for pair in range(STEPS * STEPS // 2):
        first_part = sums_ref[:, 2 * pair * WIDTH : (2 * pair + 1) * WIDTH]
        second_part = sums_ref[:, (2 * pair + 1) * WIDTH : (2 * pair + 2) * WIDTH]
        folded = jnp.where(lower, first_part, second_part) + sign_ref[pair : pair + 1, :] * swap(
            jnp.where(lower, second_part, first_part)
        )
        pieces_ref[:, 2 * pair * WIDTH : (2 * pair + 2) * WIDTH] = split(folded)
    total = jnp.dot(pieces_ref[...], gather_ref[...], preferred_element_type=jnp.float32)
    partial_ref[...] = total[:points] + jnp.where(on_diagonal, occupied * share, 0.0)


def propagate_kernel(greens_ref, effective_ref, spread_ref, out_ref, factor_ref, held_ref, sems):
    _, history, points, _ = greens_ref.shape
    factor_ref[...] = jnp.dot(
        split(effective_ref[...] * time_step), spread_ref[...], preferred_element_type=jnp.float32
    )

    slots, chunk = held_ref.shape[:2]

    def copy(number, slot):
        return pltpu.make_async_copy(
            held_ref.at[slot], out_ref.at[pl.ds(number * chunk, chunk)], sems.at[slot]
        )

    def advance(group, carry):
        for slot in range(slots):
            number = group * slots + slot

            @pl.when(group > 0)
            def _():
                copy(number - slots, slot).wait()

            times = pl.ds(number * chunk, chunk)
            for start in range(0, points, TILE):
                stop = min(start + TILE, points)
                greens = [greens_ref[j, times, start:stop, :] for j in range(STEPS)]
                terms = [greens[0]]
                for i in range(STEPS):
                    total = None
                    for j in range(STEPS):
                        spot = STEPS * i + j
                        factor = factor_ref[start:stop, spot * WIDTH : (spot + 1) * WIDTH]
                        term = factor[None] * greens[j]
                        total = term if total is None else total + term
                    terms.append(roll_blocks(total, STEPS * i))
                held_ref[slot, :, start:stop, :] = tree_sum(terms)
            copy(number, slot).start()
        return carry

    groups = history // (chunk * slots)
    lax.fori_loop(0, groups, advance, 0)
    for slot in range(slots):
        copy((groups - 1) * slots + slot, slot).wait()


def gather_tables():
    blocks = 2 * BANDS
    pairs = STEPS * STEPS // 2
    table = np.zeros((pairs, 2, blocks, BANDS, 2, BANDS, BANDS), np.float32)
    signs = np.zeros((pairs, blocks, BANDS), np.float32)
    for pair in range(pairs):
        for p in range(blocks):
            i, j = divmod(2 * pair + p // BANDS, STEPS)
            h, a = divmod((p + STEPS * i) % blocks, BANDS)
            g, c = divmod((p + j) % blocks, BANDS)
            table[pair, :, p, :, h ^ g, a, c] = 1 if (h, g) == (0, 1) else -1
            signs[pair, p] = 1 if h == g else -1
    return signs.reshape(pairs, WIDTH), table.reshape(-1, WIDTH).astype(ml_dtypes.bfloat16)


def spread_table():
    blocks = 2 * BANDS
    table = np.zeros((2, BANDS, BANDS, STEPS, STEPS, blocks, BANDS), np.float32)
    for i in range(STEPS):
        for j in range(STEPS):
            for p in range(blocks):
                h, a = divmod((p - STEPS * i) % blocks, BANDS)
                g, b = divmod((p + j) % blocks, BANDS)
                table[1 if h == g else 0, a, b, i, j, p, :] = -1 if (h, g) == (1, 0) else 1
    return np.tile(table.reshape(WIDTH, -1), (2, 1)).astype(ml_dtypes.bfloat16)


def in_vmem():
    return pl.BlockSpec(memory_space=pltpu.VMEM)


def in_smem():
    return pl.BlockSpec(memory_space=pltpu.SMEM)


def anywhere():
    return pl.BlockSpec(memory_space=pl.ANY)


def params(megabytes):
    return pltpu.CompilerParams(vmem_limit_bytes=megabytes * 1024 * 1024)


def cost(per_element, arrays):
    size = SIDE * SIDE * TILE * WIDTH
    return pl.CostEstimate(flops=per_element * size, bytes_accessed=4 * arrays * size, transcendentals=0)


def held_blocks(count, parts):
    return [
        pltpu.VMEM((count, TILE * SIDE * SIDE // parts, WIDTH), jnp.float32),
        pltpu.SemaphoreType.DMA((count,)),
    ]


def forward(place, greens, steps, parts):
    points = SIDE * SIDE
    return pl.pallas_call(
        functools.partial(forward_kernel, steps, parts),
        out_shape=[
            jax.ShapeDtypeStruct((points, TILE, WIDTH), jnp.float32),
            jax.ShapeDtypeStruct((STEPS, TILE * points, WIDTH), jnp.float32),
        ],
        in_specs=[in_smem()] + [anywhere()] * len(steps),
        out_specs=[in_vmem()] * 2,
        scratch_shapes=[pltpu.VMEM((points, TILE, WIDTH), jnp.float32)] + held_blocks(len(steps), parts),
        compiler_params=params(8),
        cost_estimate=cost(400, 6),
        name="forward",
    )(place, *greens)


def early_lines(place, lattice, weights, screens, steps, parts, work=None):
    points = SIDE * SIDE
    inputs = (place, lattice, weights, *screens) + (() if work is None else (work,))
    return pl.pallas_call(
        functools.partial(early_kernel, steps, parts),
        out_shape=jax.ShapeDtypeStruct((points, TILE, WIDTH), jnp.float32),
        in_specs=[in_smem(), in_vmem(), in_vmem()]
        + [anywhere()] * len(steps)
        + [in_vmem()] * (work is not None),
        out_specs=in_vmem(),
        input_output_aliases={} if work is None else {len(inputs) - 1: 0},
        scratch_shapes=held_blocks(len(steps), parts),
        compiler_params=params(4),
        cost_estimate=cost(25 * len(steps), 3),
        name="early",
    )(*inputs)


def sigma_of(place, lattice, weights, screens, work, steps, parts):
    points = SIDE * SIDE
    inputs = (place, lattice, weights, *screens, work)
    work, sigma = pl.pallas_call(
        functools.partial(sigma_kernel, steps, parts),
        out_shape=[
            jax.ShapeDtypeStruct((points, TILE, WIDTH), jnp.float32),
            jax.ShapeDtypeStruct((TILE * points, WIDTH), jnp.float32),
        ],
        in_specs=[in_smem()] + [in_vmem()] * 2 + [anywhere()] * len(steps) + [in_vmem()],
        out_specs=[in_vmem()] * 2,
        input_output_aliases={len(inputs) - 1: 0},
        scratch_shapes=held_blocks(len(steps), parts) if steps else [],
        compiler_params=params(4),
        cost_estimate=cost(200, 6),
        name="sigma",
    )(*inputs)
    return sigma


def contract(owners, sigma, equal_time, greens, block, share, before=()):
    points = owners.shape[0] * block
    rows = -(-points // 16) * 16
    signs, gather = gather_tables()
    return pl.pallas_call(
        functools.partial(contract_kernel, share),
        out_shape=jax.ShapeDtypeStruct((points, WIDTH), jnp.float32),
        in_specs=[in_smem()] + [in_vmem()] * 5 + [anywhere()] * len(before),
        out_specs=in_vmem(),
        scratch_shapes=[
            pltpu.VMEM((rows, STEPS * STEPS * WIDTH), jnp.float32),
            pltpu.VMEM((rows, STEPS * STEPS * WIDTH), jnp.bfloat16),
        ],
        compiler_params=params(10),
        cost_estimate=cost(70 * owners.shape[0], 6),
        name="contract",
    )(owners, sigma, equal_time, jnp.asarray(signs), jnp.asarray(gather), greens, *before)


def roll_own(greens):
    return pl.pallas_call(
        roll_kernel,
        out_shape=jax.ShapeDtypeStruct((STEPS, *greens.shape), jnp.float32),
        in_specs=[in_vmem()],
        out_specs=in_vmem(),
        compiler_params=params(4),
        cost_estimate=cost(3, 5),
        name="roll_own",
    )(greens)


def propagate(greens, effective):
    _, history, points, width = greens.shape
    chunk = math.gcd(history // 2, TILE)
    spread = spread_table()
    return pl.pallas_call(
        propagate_kernel,
        out_shape=jax.ShapeDtypeStruct(greens.shape[1:], jnp.float32),
        in_specs=[in_vmem()] * 3,
        out_specs=anywhere(),
        scratch_shapes=[
            pltpu.VMEM((points, spread.shape[1]), jnp.float32),
            pltpu.VMEM((2, chunk, points, width), jnp.float32),
            pltpu.SemaphoreType.DMA((2,)),
        ],
        compiler_params=params(6),
        cost_estimate=cost(32, 5),
        name="propagate",
    )(greens, effective, jnp.asarray(spread))


def partner_of(place, step, count):
    if count == 1:
        return 0
    if count & (count - 1) == 0:
        return place ^ step
    return (place + step) % count


def exchange(value, axis, step, count):
    pairs = [(place, partner_of(place, step, count)) for place in range(count)]
    return lax.ppermute(value, axis, pairs)


def exchange_order(count):
    along = {}
    for step in range(1, count):
        along.setdefault(step // 2, []).append(step)
    single = [along[n] for n in along if n and n & (n - 1) == 0]
    mixed = [along[n] for n in along if n & (n - 1)]
    order = [step for steps in zip(*single[::-1]) for step in steps]
    return order + along[0] + [step for steps in mixed for step in steps]


def class_weights(quad_class):
    table = jnp.array(quadrature, jnp.float32)
    match = quad_class[:, None] == jnp.arange(4, dtype=jnp.int32)[None, :]
    return jnp.sum(jnp.where(match, table[None, :], jnp.float32(0.0)), axis=1)


def per_device(parts, blocks, green_row, screened, hamilton, equal_time, quad_class, live_count):
    history, local, width = green_row.shape
    points = local * parts
    times = history // parts
    place = lax.axis_index("ka")
    seat = place.reshape(1)
    position = jnp.arange(history, dtype=jnp.int32)
    weights = jnp.where(
        position < live_count[0], time_step * class_weights(quad_class), jnp.float32(0.0)
    ) * jnp.float32(1.0 / points)
    weights = lax.dynamic_slice_in_dim(weights, place * times, times)

    if times == TILE and local % SIDE == 0:
        groups, sources = 1, parts
        order = exchange_order(parts)
        moved = []
        wholes = [x.reshape(parts * TILE * local, width) for x in (green_row, screened)]
        moved = []
        for whole in wholes:
            found = {0: whole}
            for step in order:
                start = partner_of(place, step, parts) * (TILE * local)
                block = lax.dynamic_slice_in_dim(whole, start, TILE * local)
                found[step] = exchange(block, "ka", step, parts)
            moved.append([found])
        order = [0] + order
    else:
        groups, sources = -(-times // TILE), 1
        order = [0]
        padding = groups * TILE - times
        moved = []
        for x in (green_row, screened):
            x = lax.all_to_all(x, "ka", split_axis=0, concat_axis=0, tiled=True)
            x = x.reshape(parts, times, local, width).transpose(1, 0, 2, 3).reshape(times, points, width)
            x = jnp.pad(x, ((0, padding), (0, 0), (0, 0))).reshape(groups, TILE * points, width)
            moved.append([{0: x[group]} for group in range(groups)])
        weights = jnp.pad(weights, (0, padding))
    weights = jnp.broadcast_to(weights.reshape(groups, TILE, 1), (groups, TILE, width))

    early = order[: max(1, len(order) - LATE)]
    late = order[len(early) :]
    own_greens = roll_own(green_row)
    share = hubbard / (points * blocks)
    sigmas = []
    for group in range(groups):
        green, screen = moved[0][group], moved[1][group]
        listed = order
        lattice, greens = forward(seat, [green[step] for step in listed], listed, sources)
        listed = early[-1:] + early[:-1]
        work = early_lines(seat, lattice, weights[group], [screen[step] for step in listed], listed, sources)
        for step in late[:-1]:
            work = early_lines(seat, lattice, weights[group], [screen[step]], [step], sources, work)
        last = late[-1:]
        sigma = sigma_of(
            seat, lattice, weights[group], [screen[step] for step in last], work, last, sources
        )
        sigmas.append((sigma, greens))

    if sources == parts and parts % 2 == 0 and parts & (parts - 1) == 0:
        (sigma, greens), = sigmas

        def blocks_of(steps, before=()):
            owners = jnp.stack([partner_of(place, step, parts) for step in steps])
            return contract(owners, sigma, equal_time, greens, local, share, before)

        others = exchange(blocks_of([*range(3, parts, 2), 1]), "ka", 1, parts)
        far = blocks_of(list(range(2, parts, 2))) + others[:-local]
        pieces = [
            exchange(far[(n - 1) * local : n * local], "ka", 2 * n, parts)
            for n in range(parts // 2 - 1, 0, -1)
        ]
        pieces += [blocks_of([0], pieces[:1]), others[-local:]]
        collision = tree_sum(pieces)
    else:
        whole = jnp.zeros((1,), jnp.int32)
        partial_value = tree_sum(
            [
                contract(whole, sigma, equal_time, greens, points, share if group == 0 else 0.0)
                for group, (sigma, greens) in enumerate(sigmas)
            ]
        )
        owners = [partner_of(place, step, parts) for step in range(parts)]
        pieces = [lax.dynamic_slice_in_dim(partial_value, owner * local, local) for owner in owners]
        collision = tree_sum(
            pieces[:1] + [exchange(pieces[step], "ka", step, parts) for step in range(1, parts)]
        )
    collision = tree_sum(
        [collision] + [exchange(collision, "hist", step, blocks) for step in range(blocks - 1, 0, -1)]
    )
    return propagate(own_greens, hamilton + collision)


def solution(mesh):
    in_specs = (
        P("hist", "ka", None),
        P("hist", "ka", None),
        P("ka", None),
        P("ka", None),
        P("hist"),
        P("hist"),
    )
    out_specs = P("hist", "ka", None)
    return jax.shard_map(
        functools.partial(per_device, mesh.shape["ka"], mesh.shape["hist"]),
        mesh=mesh,
        in_specs=in_specs,
        out_specs=out_specs,
        check_vma=False,
    )
```

```python
import functools
import math

import jax
import jax.numpy as jnp
import ml_dtypes
import numpy as np
from jax import lax
from jax.experimental import pallas as pl
from jax.experimental.pallas import tpu as pltpu
from jax.sharding import PartitionSpec as P

SIDE = 24
BANDS = 8
ENTRIES = BANDS * BANDS
WIDTH = 2 * ENTRIES
TILE = 8
STEPS = 4

time_step = 0.1
hubbard = 1.0
quadrature = (0.375, 1.1666666, 0.9583333, 1.0)

LATE = 2
AHEAD = 3


def lane_sign(shape):
    lane = lax.broadcasted_iota(jnp.int32, shape, len(shape) - 1)
    return lane < ENTRIES


def swap(x):
    return pltpu.roll(x, ENTRIES, 1)


def roll_blocks(x, blocks):
    return x if blocks == 0 else pltpu.roll(x, WIDTH - BANDS * blocks, x.ndim - 1)


def tree_sum(terms):
    while len(terms) > 1:
        terms = [sum(terms[i : i + 2][1:], terms[i]) for i in range(0, len(terms), 2)]
    return terms[0]


def split(x):
    high = x.astype(jnp.bfloat16)
    return jnp.concatenate([high, (x - high.astype(jnp.float32)).astype(jnp.bfloat16)], axis=1)


def dft24(x, sign, low):
    root3 = jnp.where(low, -1.0, 1.0) * (sign * math.sqrt(3.0) / 2)
    turn = jnp.where(low, -1.0, 1.0) * float(sign)
    half = math.sqrt(0.5)
    turn_half = turn * half
    columns = [[None] * 8 for _ in range(3)]
    for n2 in range(8):
        x0, x1, x2 = (x[(8 * n1 + 3 * n2) % 24] for n1 in range(3))
        total = x1 + x2
        base = x0 - 0.5 * total
        spin = swap(x1 - x2) * root3
        columns[0][n2] = x0 + total
        columns[1][n2] = base + spin
        columns[2][n2] = base - spin
    out = [None] * 24
    for k1 in range(3):
        c = columns[k1]
        a0, a1 = c[0] + c[4], c[0] - c[4]
        a2, a3 = c[2] + c[6], c[2] - c[6]
        a4, a5 = c[1] + c[5], c[1] - c[5]
        a6, a7 = c[3] + c[7], c[3] - c[7]
        b0, b1 = a0 + a2, a0 - a2
        b2, b3 = a4 + a6, a4 - a6
        i_a3 = swap(a3) * turn
        i_b3 = swap(b3) * turn
        c0, c1 = a1 + i_a3, a1 - i_a3
        p = (a5 - a7) * half
        m = swap(a5 + a7) * turn_half
        e, f = p + m, p - m
        values = [b0 + b2, c0 + e, b1 + i_b3, c1 - f, b0 - b2, c0 - e, b1 - i_b3, c1 + f]
        for k2 in range(8):
            out[(16 * k1 + 9 * k2) % 24] = values[k2]
    return out


def load_line(ref, line):
    stride = ref.shape[0] // TILE
    return [ref[pl.ds(line * SIDE + k2, TILE, stride=stride), :] for k2 in range(SIDE)]


def fetch(place, steps, block_refs, held_ref, sems):
    copies = []
    for slot, (step, source) in enumerate(zip(steps, block_refs)):
        rows = held_ref.shape[1]
        if step == 0 and source.shape[0] != rows:
            source = source.at[pl.ds(pl.multiple_of(place * rows, TILE), rows)]
        copies.append(pltpu.make_async_copy(source, held_ref.at[slot], sems.at[slot]))
        copies[-1].start()
    return copies


def along_first(work_ref, sign, low, store):
    def columns(pair, carry):
        both = (2 * pair, 2 * pair + 1)
        rows = [[work_ref[k1 * SIDE + column] for k1 in range(SIDE)] for column in both]
        values = [dft24(row, sign, low) for row in rows]
        for column, value in zip(both, values):
            for r1 in range(SIDE):
                store(r1 * SIDE + column, value[r1])
        return carry

    lax.fori_loop(0, SIDE // 2, columns, 0)


def pick_kernel(steps, parts, place_ref, whole_ref, *refs):
    block_refs, sems = refs[-1 - len(steps) : -1], refs[-1]
    copies = []
    for n, (step, block_ref) in enumerate(zip(steps, block_refs)):
        rows = block_ref.shape[0]
        start = pl.multiple_of(partner_of(place_ref[0], step, parts) * rows, TILE)
        copies.append(pltpu.make_async_copy(whole_ref.at[pl.ds(start, rows)], block_ref, sems.at[n]))
        copies[-1].start()
    for copy in copies:
        copy.wait()


def roll_kernel(green_ref, greens_ref):
    batch = math.gcd(green_ref.shape[0], STEPS)

    def rolls(n, carry):
        times = pl.ds(n * batch, batch)
        green = green_ref[times]
        rolled = [roll_blocks(green, j) for j in range(STEPS)]
        for j in range(STEPS):
            greens_ref[j, times] = rolled[j]
        return carry

    lax.fori_loop(0, green_ref.shape[0] // batch, rolls, 0)


def forward_kernel(steps, parts, place_ref, *refs):
    block_refs, (lattice_ref, greens_ref, work_ref, held_ref, sems) = refs[: len(steps)], refs[len(steps) :]
    low = lane_sign((TILE, WIDTH))
    place = place_ref[0]
    copies = fetch(place, steps, block_refs, held_ref, sems)
    rows = held_ref.shape[1]
    lines = rows // (TILE * SIDE)
    for slot, step in enumerate(steps):
        copies[slot].wait()
        green_ref = held_ref.at[slot]
        owner = partner_of(place, step, parts)

        def along_second(i, carry):
            for r2, value in enumerate(dft24(load_line(green_ref, i), -1, low)):
                work_ref[(owner * lines + i) * SIDE + r2] = value
            return carry

        lax.fori_loop(0, lines, along_second, 0, unroll=lines <= 4)
        green = green_ref[...]
        spot = pl.ds(pl.multiple_of(owner * rows, TILE), rows)
        for j in range(STEPS):
            greens_ref[j, spot, :] = roll_blocks(green, j)

    def store(point, value):
        lattice_ref[point] = value

    along_first(work_ref, -1, low, store)


def product_lines(steps, parts, place, lattice_ref, weights, screen_refs, held_ref, sems, work_ref):
    low = lane_sign((TILE, WIDTH))
    turn = jnp.where(low, -1.0, 1.0)
    copies = fetch(place, steps, screen_refs, held_ref, sems)
    lines = held_ref.shape[1] // (TILE * SIDE)
    for slot, step in enumerate(steps):
        copies[slot].wait()
        screen_ref = held_ref.at[slot]
        first = partner_of(place, step, parts) * lines

        def along_second(i, carry):
            rows = []
            for r2, value in enumerate(load_line(screen_ref, i)):
                screen = value * weights
                other = swap(screen)
                lattice = lattice_ref[(first + i) * SIDE + r2]
                rows.append(
                    swap(lattice) * turn * jnp.where(low, screen, other)
                    - lattice * jnp.where(low, other, screen)
                )
            for k2, value in enumerate(dft24(rows, 1, low)):
                work_ref[(first + i) * SIDE + k2] = value
            return carry

        lax.fori_loop(0, lines, along_second, 0, unroll=lines <= 4)


def early_kernel(steps, parts, place_ref, lattice_ref, weight_ref, *refs):
    screen_refs, (*_, work_ref, held_ref, sems) = refs[: len(steps)], refs[len(steps) :]
    product_lines(
        steps, parts, place_ref[0], lattice_ref, weight_ref[...], screen_refs, held_ref, sems, work_ref
    )


def sigma_kernel(steps, parts, place_ref, lattice_ref, weight_ref, *refs):
    screen_refs, refs = refs[: len(steps)], refs[len(steps) :]
    _, work_ref, sigma_ref, *late = refs
    low = lane_sign((TILE, WIDTH))
    if steps:
        held_ref, sems = late
        product_lines(
            steps, parts, place_ref[0], lattice_ref, weight_ref[...], screen_refs, held_ref, sems, work_ref
        )

    def store(point, value):
        sigma_ref[pl.ds(point * TILE, TILE), :] = value

    along_first(work_ref, 1, low, store)


def contract_kernel(share, owner_ref, sigma_ref, equal_ref, sign_ref, gather_ref, greens_ref, *refs):
    partial_ref, sums_ref, pieces_ref = refs[-3:]
    low = lane_sign((TILE, WIDTH))
    points = partial_ref.shape[0]
    block = points // owner_ref.shape[0]
    tiles = block // TILE
    batch = max(n for n in range(1, 10) if tiles % n == 0)

    def contract(group, carry):
        slot, first = group // (tiles // batch), group % (tiles // batch) * batch
        owner = owner_ref[slot]
        units = [(tile, s) for tile in range(batch) for s in range(TILE)]

        def prepare(tile, s):
            point = owner * block + (first + tile) * TILE
            sigma = sigma_ref[pl.ds(point * TILE + s, TILE, stride=TILE), :]
            row = pl.multiple_of((owner * TILE + s) * block + (first + tile) * TILE, TILE)
            return (
                [roll_blocks(sigma, STEPS * i) for i in range(STEPS)],
                [greens_ref[j, pl.ds(row, TILE), :] for j in range(STEPS)],
            )

        ready = [prepare(*unit) for unit in units[:AHEAD]]
        for n, (tile, s) in enumerate(units):
            if n + AHEAD < len(units):
                ready.append(prepare(*units[n + AHEAD]))
            sigmas, greens = ready.pop(0)
            terms = [sigma * green for sigma in sigmas for green in greens]
            sums = terms if s == 0 else [a + b for a, b in zip(sums, terms)]
            if s == TILE - 1:
                row = pl.ds(pl.multiple_of(slot * block + (first + tile) * TILE, TILE), TILE)
                for spot, value in enumerate(sums):
                    sums_ref[row, spot * WIDTH : (spot + 1) * WIDTH] = value
        return carry

    lax.fori_loop(0, points // (TILE * batch), contract, 0)

    lane = lax.broadcasted_iota(jnp.int32, equal_ref.shape, 1)
    inner = lane - ENTRIES
    occupied = jnp.sum(jnp.where((inner >= 0) & (inner % (BANDS + 1) == 0), equal_ref[...], 0.0))
    spots = lax.broadcasted_iota(jnp.int32, (points, WIDTH), 1)
    on_diagonal = (spots < ENTRIES) & (spots % (BANDS + 1) == 0)
    lower = lax.broadcasted_iota(jnp.int32, (sums_ref.shape[0], WIDTH), 1) < ENTRIES
    for pair in range(STEPS * STEPS // 2):
        first_part = sums_ref[:, 2 * pair * WIDTH : (2 * pair + 1) * WIDTH]
        second_part = sums_ref[:, (2 * pair + 1) * WIDTH : (2 * pair + 2) * WIDTH]
        folded = jnp.where(lower, first_part, second_part) + sign_ref[pair : pair + 1, :] * swap(
            jnp.where(lower, second_part, first_part)
        )
        pieces_ref[:, 2 * pair * WIDTH : (2 * pair + 2) * WIDTH] = split(folded)
    total = jnp.dot(pieces_ref[...], gather_ref[...], preferred_element_type=jnp.float32)
    partial_ref[...] = total[:points] + jnp.where(on_diagonal, occupied * share, 0.0)


def propagate_kernel(greens_ref, effective_ref, spread_ref, out_ref, factor_ref, held_ref, sems):
    _, history, points, _ = greens_ref.shape
    factor_ref[...] = jnp.dot(
        split(effective_ref[...] * time_step), spread_ref[...], preferred_element_type=jnp.float32
    )

    slots, chunk = held_ref.shape[:2]

    def copy(number, slot):
        return pltpu.make_async_copy(
            held_ref.at[slot], out_ref.at[pl.ds(number * chunk, chunk)], sems.at[slot]
        )

    def advance(group, carry):
        for slot in range(slots):
            number = group * slots + slot

            @pl.when(group > 0)
            def _():
                copy(number - slots, slot).wait()

            times = pl.ds(number * chunk, chunk)
            for start in range(0, points, TILE):
                stop = min(start + TILE, points)
                greens = [greens_ref[j, times, start:stop, :] for j in range(STEPS)]
                terms = [greens[0]]
                for i in range(STEPS):
                    total = None
                    for j in range(STEPS):
                        spot = STEPS * i + j
                        factor = factor_ref[start:stop, spot * WIDTH : (spot + 1) * WIDTH]
                        term = factor[None] * greens[j]
                        total = term if total is None else total + term
                    terms.append(roll_blocks(total, STEPS * i))
                held_ref[slot, :, start:stop, :] = tree_sum(terms)
            copy(number, slot).start()
        return carry

    groups = history // (chunk * slots)
    lax.fori_loop(0, groups, advance, 0)
    for slot in range(slots):
        copy((groups - 1) * slots + slot, slot).wait()


def gather_tables():
    blocks = 2 * BANDS
    pairs = STEPS * STEPS // 2
    table = np.zeros((pairs, 2, blocks, BANDS, 2, BANDS, BANDS), np.float32)
    signs = np.zeros((pairs, blocks, BANDS), np.float32)
    for pair in range(pairs):
        for p in range(blocks):
            i, j = divmod(2 * pair + p // BANDS, STEPS)
            h, a = divmod((p + STEPS * i) % blocks, BANDS)
            g, c = divmod((p + j) % blocks, BANDS)
            table[pair, :, p, :, h ^ g, a, c] = 1 if (h, g) == (0, 1) else -1
            signs[pair, p] = 1 if h == g else -1
    return signs.reshape(pairs, WIDTH), table.reshape(-1, WIDTH).astype(ml_dtypes.bfloat16)


def spread_table():
    blocks = 2 * BANDS
    table = np.zeros((2, BANDS, BANDS, STEPS, STEPS, blocks, BANDS), np.float32)
    for i in range(STEPS):
        for j in range(STEPS):
            for p in range(blocks):
                h, a = divmod((p - STEPS * i) % blocks, BANDS)
                g, b = divmod((p + j) % blocks, BANDS)
                table[1 if h == g else 0, a, b, i, j, p, :] = -1 if (h, g) == (1, 0) else 1
    return np.tile(table.reshape(WIDTH, -1), (2, 1)).astype(ml_dtypes.bfloat16)


def in_vmem():
    return pl.BlockSpec(memory_space=pltpu.VMEM)


def in_smem():
    return pl.BlockSpec(memory_space=pltpu.SMEM)


def anywhere():
    return pl.BlockSpec(memory_space=pl.ANY)


def params(megabytes):
    return pltpu.CompilerParams(vmem_limit_bytes=megabytes * 1024 * 1024)


def cost(per_element, arrays):
    size = SIDE * SIDE * TILE * WIDTH
    return pl.CostEstimate(flops=per_element * size, bytes_accessed=4 * arrays * size, transcendentals=0)


def held_blocks(count, parts):
    return [
        pltpu.VMEM((count, TILE * SIDE * SIDE // parts, WIDTH), jnp.float32),
        pltpu.SemaphoreType.DMA((count,)),
    ]


def forward(place, greens, steps, parts):
    points = SIDE * SIDE
    return pl.pallas_call(
        functools.partial(forward_kernel, steps, parts),
        out_shape=[
            jax.ShapeDtypeStruct((points, TILE, WIDTH), jnp.float32),
            jax.ShapeDtypeStruct((STEPS, TILE * points, WIDTH), jnp.float32),
        ],
        in_specs=[in_smem()] + [anywhere()] * len(steps),
        out_specs=[in_vmem()] * 2,
        scratch_shapes=[pltpu.VMEM((points, TILE, WIDTH), jnp.float32)] + held_blocks(len(steps), parts),
        compiler_params=params(8),
        cost_estimate=cost(400, 6),
        name="forward",
    )(place, *greens)


def early_lines(place, lattice, weights, screens, steps, parts, work=None):
    points = SIDE * SIDE
    inputs = (place, lattice, weights, *screens) + (() if work is None else (work,))
    return pl.pallas_call(
        functools.partial(early_kernel, steps, parts),
        out_shape=jax.ShapeDtypeStruct((points, TILE, WIDTH), jnp.float32),
        in_specs=[in_smem(), in_vmem(), in_vmem()]
        + [anywhere()] * len(steps)
        + [in_vmem()] * (work is not None),
        out_specs=in_vmem(),
        input_output_aliases={} if work is None else {len(inputs) - 1: 0},
        scratch_shapes=held_blocks(len(steps), parts),
        compiler_params=params(4),
        cost_estimate=cost(25 * len(steps), 3),
        name="early",
    )(*inputs)


def sigma_of(place, lattice, weights, screens, work, steps, parts):
    points = SIDE * SIDE
    inputs = (place, lattice, weights, *screens, work)
    work, sigma = pl.pallas_call(
        functools.partial(sigma_kernel, steps, parts),
        out_shape=[
            jax.ShapeDtypeStruct((points, TILE, WIDTH), jnp.float32),
            jax.ShapeDtypeStruct((TILE * points, WIDTH), jnp.float32),
        ],
        in_specs=[in_smem()] + [in_vmem()] * 2 + [anywhere()] * len(steps) + [in_vmem()],
        out_specs=[in_vmem()] * 2,
        input_output_aliases={len(inputs) - 1: 0},
        scratch_shapes=held_blocks(len(steps), parts) if steps else [],
        compiler_params=params(4),
        cost_estimate=cost(200, 6),
        name="sigma",
    )(*inputs)
    return sigma


def contract(owners, sigma, equal_time, greens, block, share, before=()):
    points = owners.shape[0] * block
    rows = -(-points // 16) * 16
    signs, gather = gather_tables()
    return pl.pallas_call(
        functools.partial(contract_kernel, share),
        out_shape=jax.ShapeDtypeStruct((points, WIDTH), jnp.float32),
        in_specs=[in_smem()] + [in_vmem()] * 5 + [anywhere()] * len(before),
        out_specs=in_vmem(),
        scratch_shapes=[
            pltpu.VMEM((rows, STEPS * STEPS * WIDTH), jnp.float32),
            pltpu.VMEM((rows, STEPS * STEPS * WIDTH), jnp.bfloat16),
        ],
        compiler_params=params(10),
        cost_estimate=cost(70 * owners.shape[0], 6),
        name="contract",
    )(owners, sigma, equal_time, jnp.asarray(signs), jnp.asarray(gather), greens, *before)


def pick(place, whole, steps, parts, before=()):
    rows, width = whole.shape[0] // parts, whole.shape[1]
    return pl.pallas_call(
        functools.partial(pick_kernel, steps, parts),
        out_shape=[jax.ShapeDtypeStruct((rows, width), whole.dtype)] * len(steps),
        in_specs=[in_smem(), anywhere()] + [anywhere()] * len(before),
        out_specs=[in_vmem()] * len(steps),
        scratch_shapes=[pltpu.SemaphoreType.DMA((len(steps),))],
        compiler_params=params(56),
        cost_estimate=cost(0, 2),
        name="pick",
    )(place, whole, *before)


def roll_own(greens):
    return pl.pallas_call(
        roll_kernel,
        out_shape=jax.ShapeDtypeStruct((STEPS, *greens.shape), jnp.float32),
        in_specs=[in_vmem()],
        out_specs=in_vmem(),
        compiler_params=params(4),
        cost_estimate=cost(3, 5),
        name="roll_own",
    )(greens)


def propagate(greens, effective):
    _, history, points, width = greens.shape
    chunk = math.gcd(history // 2, TILE)
    spread = spread_table()
    return pl.pallas_call(
        propagate_kernel,
        out_shape=jax.ShapeDtypeStruct(greens.shape[1:], jnp.float32),
        in_specs=[in_vmem()] * 3,
        out_specs=anywhere(),
        scratch_shapes=[
            pltpu.VMEM((points, spread.shape[1]), jnp.float32),
            pltpu.VMEM((2, chunk, points, width), jnp.float32),
            pltpu.SemaphoreType.DMA((2,)),
        ],
        compiler_params=params(6),
        cost_estimate=cost(32, 5),
        name="propagate",
    )(greens, effective, jnp.asarray(spread))


def partner_of(place, step, count):
    if count == 1:
        return 0
    if count & (count - 1) == 0:
        return place ^ step
    return (place + step) % count


def exchange(value, axis, step, count):
    pairs = [(place, partner_of(place, step, count)) for place in range(count)]
    return lax.ppermute(value, axis, pairs)


def exchange_order(count):
    along = {}
    for step in range(1, count):
        along.setdefault(step // 2, []).append(step)
    single = [along[n] for n in along if n and n & (n - 1) == 0]
    mixed = [along[n] for n in along if n & (n - 1)]
    order = [step for steps in zip(*single[::-1]) for step in steps]
    return order + along[0] + [step for steps in mixed for step in steps]


def class_weights(quad_class):
    table = jnp.array(quadrature, jnp.float32)
    match = quad_class[:, None] == jnp.arange(4, dtype=jnp.int32)[None, :]
    return jnp.sum(jnp.where(match, table[None, :], jnp.float32(0.0)), axis=1)


def per_device(parts, blocks, green_row, screened, hamilton, equal_time, quad_class, live_count):
    history, local, width = green_row.shape
    points = local * parts
    times = history // parts
    place = lax.axis_index("ka")
    seat = place.reshape(1)
    position = jnp.arange(history, dtype=jnp.int32)
    weights = jnp.where(
        position < live_count[0], time_step * class_weights(quad_class), jnp.float32(0.0)
    ) * jnp.float32(1.0 / points)
    weights = lax.dynamic_slice_in_dim(weights, place * times, times)

    if times == TILE and local % SIDE == 0:
        groups, sources = 1, parts
        order = exchange_order(parts)
        moved = []
        wholes = [x.reshape(parts * TILE * local, width) for x in (green_row, screened)]
        moved, picked = [], []
        for whole in wholes:
            found = {0: whole}
            picked = pick(seat, whole, order, parts, picked[:1])
            for step, block in zip(order, picked):
                found[step] = exchange(block, "ka", step, parts)
            moved.append([found])
        order = [0] + order
    else:
        groups, sources = -(-times // TILE), 1
        order = [0]
        padding = groups * TILE - times
        moved = []
        for x in (green_row, screened):
            x = lax.all_to_all(x, "ka", split_axis=0, concat_axis=0, tiled=True)
            x = x.reshape(parts, times, local, width).transpose(1, 0, 2, 3).reshape(times, points, width)
            x = jnp.pad(x, ((0, padding), (0, 0), (0, 0))).reshape(groups, TILE * points, width)
            moved.append([{0: x[group]} for group in range(groups)])
        weights = jnp.pad(weights, (0, padding))
    weights = jnp.broadcast_to(weights.reshape(groups, TILE, 1), (groups, TILE, width))

    early = order[: max(1, len(order) - LATE)]
    late = order[len(early) :]
    own_greens = roll_own(green_row)
    share = hubbard / (points * blocks)
    sigmas = []
    for group in range(groups):
        green, screen = moved[0][group], moved[1][group]
        listed = order
        lattice, greens = forward(seat, [green[step] for step in listed], listed, sources)
        listed = early[-1:] + early[:-1]
        work = early_lines(seat, lattice, weights[group], [screen[step] for step in listed], listed, sources)
        for step in late[:-1]:
            work = early_lines(seat, lattice, weights[group], [screen[step]], [step], sources, work)
        last = late[-1:]
        sigma = sigma_of(
            seat, lattice, weights[group], [screen[step] for step in last], work, last, sources
        )
        sigmas.append((sigma, greens))

    if sources == parts and parts % 2 == 0 and parts & (parts - 1) == 0:
        (sigma, greens), = sigmas

        def blocks_of(steps, before=()):
            owners = jnp.stack([partner_of(place, step, parts) for step in steps])
            return contract(owners, sigma, equal_time, greens, local, share, before)

        others = exchange(blocks_of([*range(3, parts, 2), 1]), "ka", 1, parts)
        far = blocks_of(list(range(2, parts, 2))) + others[:-local]
        pieces = [
            exchange(far[(n - 1) * local : n * local], "ka", 2 * n, parts)
            for n in range(parts // 2 - 1, 0, -1)
        ]
        pieces += [blocks_of([0], pieces[:1]), others[-local:]]
        collision = tree_sum(pieces)
    else:
        whole = jnp.zeros((1,), jnp.int32)
        partial_value = tree_sum(
            [
                contract(whole, sigma, equal_time, greens, points, share if group == 0 else 0.0)
                for group, (sigma, greens) in enumerate(sigmas)
            ]
        )
        owners = [partner_of(place, step, parts) for step in range(parts)]
        pieces = [lax.dynamic_slice_in_dim(partial_value, owner * local, local) for owner in owners]
        collision = tree_sum(
            pieces[:1] + [exchange(pieces[step], "ka", step, parts) for step in range(1, parts)]
        )
    collision = tree_sum(
        [collision] + [exchange(collision, "hist", step, blocks) for step in range(blocks - 1, 0, -1)]
    )
    return propagate(own_greens, hamilton + collision)


def solution(mesh):
    in_specs = (
        P("hist", "ka", None),
        P("hist", "ka", None),
        P("ka", None),
        P("ka", None),
        P("hist"),
        P("hist"),
    )
    out_specs = P("hist", "ka", None)
    return jax.shard_map(
        functools.partial(per_device, mesh.shape["ka"], mesh.shape["hist"]),
        mesh=mesh,
        in_specs=in_specs,
        out_specs=out_specs,
        check_vma=False,
    )
```

```python
import functools
import math

import jax
import jax.numpy as jnp
import ml_dtypes
import numpy as np
from jax import lax
from jax.experimental import pallas as pl
from jax.experimental.pallas import tpu as pltpu
from jax.sharding import PartitionSpec as P

SIDE = 24
BANDS = 8
ENTRIES = BANDS * BANDS
WIDTH = 2 * ENTRIES
TILE = 8
STEPS = 4

time_step = 0.1
hubbard = 1.0
quadrature = (0.375, 1.1666666, 0.9583333, 1.0)

LATE = 2
AHEAD = 3


def lane_sign(shape):
    lane = lax.broadcasted_iota(jnp.int32, shape, len(shape) - 1)
    return lane < ENTRIES


def swap(x):
    return pltpu.roll(x, ENTRIES, 1)


def roll_blocks(x, blocks):
    return x if blocks == 0 else pltpu.roll(x, WIDTH - BANDS * blocks, x.ndim - 1)


def tree_sum(terms):
    while len(terms) > 1:
        terms = [sum(terms[i : i + 2][1:], terms[i]) for i in range(0, len(terms), 2)]
    return terms[0]


def split(x):
    high = x.astype(jnp.bfloat16)
    return jnp.concatenate([high, (x - high.astype(jnp.float32)).astype(jnp.bfloat16)], axis=1)


def dft24(x, sign, low):
    root3 = jnp.where(low, -1.0, 1.0) * (sign * math.sqrt(3.0) / 2)
    turn = jnp.where(low, -1.0, 1.0) * float(sign)
    half = math.sqrt(0.5)
    turn_half = turn * half
    columns = [[None] * 8 for _ in range(3)]
    for n2 in range(8):
        x0, x1, x2 = (x[(8 * n1 + 3 * n2) % 24] for n1 in range(3))
        total = x1 + x2
        base = x0 - 0.5 * total
        spin = swap(x1 - x2) * root3
        columns[0][n2] = x0 + total
        columns[1][n2] = base + spin
        columns[2][n2] = base - spin
    out = [None] * 24
    for k1 in range(3):
        c = columns[k1]
        a0, a1 = c[0] + c[4], c[0] - c[4]
        a2, a3 = c[2] + c[6], c[2] - c[6]
        a4, a5 = c[1] + c[5], c[1] - c[5]
        a6, a7 = c[3] + c[7], c[3] - c[7]
        b0, b1 = a0 + a2, a0 - a2
        b2, b3 = a4 + a6, a4 - a6
        i_a3 = swap(a3) * turn
        i_b3 = swap(b3) * turn
        c0, c1 = a1 + i_a3, a1 - i_a3
        p = (a5 - a7) * half
        m = swap(a5 + a7) * turn_half
        e, f = p + m, p - m
        values = [b0 + b2, c0 + e, b1 + i_b3, c1 - f, b0 - b2, c0 - e, b1 - i_b3, c1 + f]
        for k2 in range(8):
            out[(16 * k1 + 9 * k2) % 24] = values[k2]
    return out


def load_line(ref, line):
    stride = ref.shape[0] // TILE
    return [ref[pl.ds(line * SIDE + k2, TILE, stride=stride), :] for k2 in range(SIDE)]


def fetch(place, steps, block_refs, held_ref, sems):
    copies = []
    for slot, (step, source) in enumerate(zip(steps, block_refs)):
        rows = held_ref.shape[1]
        if step == 0 and source.shape[0] != rows:
            source = source.at[pl.ds(pl.multiple_of(place * rows, TILE), rows)]
        copies.append(pltpu.make_async_copy(source, held_ref.at[slot], sems.at[slot]))
        copies[-1].start()
    return copies


def along_first(work_ref, sign, low, store):
    def columns(pair, carry):
        both = (2 * pair, 2 * pair + 1)
        rows = [[work_ref[k1 * SIDE + column] for k1 in range(SIDE)] for column in both]
        values = [dft24(row, sign, low) for row in rows]
        for column, value in zip(both, values):
            for r1 in range(SIDE):
                store(r1 * SIDE + column, value[r1])
        return carry

    lax.fori_loop(0, SIDE // 2, columns, 0)


def times_of(ref, k):
    history, points, width = ref.shape
    if points % TILE:
        return ref[:, k, :]
    return ref.reshape(history * points, width)[pl.ds(k, history, stride=points), :]


def split_kernel(green_ref, split_ref):
    history, points, _ = green_ref.shape

    def write(k):
        green = times_of(green_ref, k)
        high = green.astype(jnp.bfloat16)
        split_ref[k, :history, :] = high
        split_ref[k, history:, :] = (green - high.astype(jnp.float32)).astype(jnp.bfloat16)

    if points % TILE:
        for k in range(points):
            write(k)
        return

    def some(n, carry):
        for k in range(4):
            write(4 * n + k)
        return carry

    lax.fori_loop(0, points // 4, some, 0)


def forward_kernel(steps, parts, place_ref, *refs):
    block_refs, (lattice_ref, greens_ref, work_ref, held_ref, sems) = refs[: len(steps)], refs[len(steps) :]
    low = lane_sign((TILE, WIDTH))
    place = place_ref[0]
    copies = fetch(place, steps, block_refs, held_ref, sems)
    rows = held_ref.shape[1]
    lines = rows // (TILE * SIDE)
    for slot, step in enumerate(steps):
        copies[slot].wait()
        green_ref = held_ref.at[slot]
        owner = partner_of(place, step, parts)

        def along_second(i, carry):
            for r2, value in enumerate(dft24(load_line(green_ref, i), -1, low)):
                work_ref[(owner * lines + i) * SIDE + r2] = value
            return carry

        lax.fori_loop(0, lines, along_second, 0, unroll=lines <= 4)
        green = green_ref[...]
        spot = pl.ds(pl.multiple_of(owner * rows, TILE), rows)
        for j in range(STEPS):
            greens_ref[j, spot, :] = roll_blocks(green, j)

    def store(point, value):
        lattice_ref[point] = value

    along_first(work_ref, -1, low, store)


def product_lines(steps, parts, place, lattice_ref, weights, screen_refs, held_ref, sems, work_ref):
    low = lane_sign((TILE, WIDTH))
    turn = jnp.where(low, -1.0, 1.0)
    copies = fetch(place, steps, screen_refs, held_ref, sems)
    lines = held_ref.shape[1] // (TILE * SIDE)
    for slot, step in enumerate(steps):
        copies[slot].wait()
        screen_ref = held_ref.at[slot]
        first = partner_of(place, step, parts) * lines

        def along_second(i, carry):
            rows = []
            for r2, value in enumerate(load_line(screen_ref, i)):
                screen = value * weights
                other = swap(screen)
                lattice = lattice_ref[(first + i) * SIDE + r2]
                rows.append(
                    swap(lattice) * turn * jnp.where(low, screen, other)
                    - lattice * jnp.where(low, other, screen)
                )
            for k2, value in enumerate(dft24(rows, 1, low)):
                work_ref[(first + i) * SIDE + k2] = value
            return carry

        lax.fori_loop(0, lines, along_second, 0, unroll=lines <= 4)


def early_kernel(steps, parts, place_ref, lattice_ref, weight_ref, *refs):
    screen_refs, (*_, work_ref, held_ref, sems) = refs[: len(steps)], refs[len(steps) :]
    product_lines(
        steps, parts, place_ref[0], lattice_ref, weight_ref[...], screen_refs, held_ref, sems, work_ref
    )


def sigma_kernel(steps, parts, place_ref, lattice_ref, weight_ref, *refs):
    screen_refs, refs = refs[: len(steps)], refs[len(steps) :]
    _, work_ref, sigma_ref, *late = refs
    low = lane_sign((TILE, WIDTH))
    if steps:
        held_ref, sems = late
        product_lines(
            steps, parts, place_ref[0], lattice_ref, weight_ref[...], screen_refs, held_ref, sems, work_ref
        )

    def store(point, value):
        sigma_ref[pl.ds(point * TILE, TILE), :] = value

    along_first(work_ref, 1, low, store)


def contract_kernel(share, owner_ref, sigma_ref, equal_ref, sign_ref, gather_ref, greens_ref, *refs):
    partial_ref, sums_ref, pieces_ref = refs[-3:]
    low = lane_sign((TILE, WIDTH))
    points = partial_ref.shape[0]
    block = points // owner_ref.shape[0]
    tiles = block // TILE
    batch = max(n for n in range(1, 10) if tiles % n == 0)

    def contract(group, carry):
        slot, first = group // (tiles // batch), group % (tiles // batch) * batch
        owner = owner_ref[slot]
        units = [(tile, s) for tile in range(batch) for s in range(TILE)]

        def prepare(tile, s):
            point = owner * block + (first + tile) * TILE
            sigma = sigma_ref[pl.ds(point * TILE + s, TILE, stride=TILE), :]
            row = pl.multiple_of((owner * TILE + s) * block + (first + tile) * TILE, TILE)
            return (
                [roll_blocks(sigma, STEPS * i) for i in range(STEPS)],
                [greens_ref[j, pl.ds(row, TILE), :] for j in range(STEPS)],
            )

        ready = [prepare(*unit) for unit in units[:AHEAD]]
        for n, (tile, s) in enumerate(units):
            if n + AHEAD < len(units):
                ready.append(prepare(*units[n + AHEAD]))
            sigmas, greens = ready.pop(0)
            terms = [sigma * green for sigma in sigmas for green in greens]
            sums = terms if s == 0 else [a + b for a, b in zip(sums, terms)]
            if s == TILE - 1:
                row = pl.ds(pl.multiple_of(slot * block + (first + tile) * TILE, TILE), TILE)
                for spot, value in enumerate(sums):
                    sums_ref[row, spot * WIDTH : (spot + 1) * WIDTH] = value
        return carry

    lax.fori_loop(0, points // (TILE * batch), contract, 0)

    lane = lax.broadcasted_iota(jnp.int32, equal_ref.shape, 1)
    inner = lane - ENTRIES
    occupied = jnp.sum(jnp.where((inner >= 0) & (inner % (BANDS + 1) == 0), equal_ref[...], 0.0))
    spots = lax.broadcasted_iota(jnp.int32, (points, WIDTH), 1)
    on_diagonal = (spots < ENTRIES) & (spots % (BANDS + 1) == 0)
    lower = lax.broadcasted_iota(jnp.int32, (sums_ref.shape[0], WIDTH), 1) < ENTRIES
    for pair in range(STEPS * STEPS // 2):
        first_part = sums_ref[:, 2 * pair * WIDTH : (2 * pair + 1) * WIDTH]
        second_part = sums_ref[:, (2 * pair + 1) * WIDTH : (2 * pair + 2) * WIDTH]
        folded = jnp.where(lower, first_part, second_part) + sign_ref[pair : pair + 1, :] * swap(
            jnp.where(lower, second_part, first_part)
        )
        pieces_ref[:, 2 * pair * WIDTH : (2 * pair + 2) * WIDTH] = split(folded)
    total = jnp.dot(pieces_ref[...], gather_ref[...], preferred_element_type=jnp.float32)
    partial_ref[...] = total[:points] + jnp.where(on_diagonal, occupied * share, 0.0)


def propagate_kernel(green_ref, split_ref, effective_ref, spread_ref, out_ref, factor_ref, held_ref, sems):
    history, points, _ = green_ref.shape
    factor_ref[...] = jnp.dot(
        split(effective_ref[...] * time_step), spread_ref[...], preferred_element_type=jnp.float32
    )
    tile = held_ref.shape[2]
    row = lax.broadcasted_iota(jnp.int32, (BANDS, WIDTH), 0)
    same = lax.broadcasted_iota(jnp.int32, (BANDS, WIDTH), 1) % BANDS == row

    def copy(number, slot):
        return pltpu.make_async_copy(
            held_ref.at[slot], out_ref.at[:, pl.ds(number * tile, tile), :], sems.at[slot]
        )

    def matrix(factors, n):
        parts = [
            jnp.where(same, jnp.broadcast_to(factor[n : n + 1], same.shape), 0.0) for factor in factors
        ]
        return split(jnp.concatenate(parts, axis=0))

    def advance(number, slot):
        start = number * tile if points == tile else pl.multiple_of(number * tile, TILE)
        factors = [
            factor_ref[pl.ds(start, tile), spot * WIDTH : (spot + 1) * WIDTH] for spot in range(2 * BANDS)
        ]
        for n in range(tile):
            k = number * tile + n
            both = jnp.dot(split_ref[k], matrix(factors, n), preferred_element_type=jnp.float32)
            added = both[:history, :WIDTH] + (both[:history, WIDTH:] + both[history:, :WIDTH])
            result = times_of(green_ref, k) + added
            if points % TILE:
                held_ref[slot, :, n, :] = result
            else:
                rows = held_ref.reshape(2 * history * tile, WIDTH)
                rows[pl.ds(slot * history * tile + n, history, stride=tile), :] = result
        copy(number, slot).start()

    tiles = points // tile
    if tiles == 1:
        advance(0, 0)
        copy(0, 0).wait()
        return

    def step(number, carry):
        slot = number % 2

        @pl.when(number > 1)
        def _():
            copy(number - 2, slot).wait()

        advance(number, slot)
        return carry

    lax.fori_loop(0, tiles, step, 0)
    for number in (tiles - 2, tiles - 1):
        copy(number, number % 2).wait()


def gather_tables():
    blocks = 2 * BANDS
    pairs = STEPS * STEPS // 2
    table = np.zeros((pairs, 2, blocks, BANDS, 2, BANDS, BANDS), np.float32)
    signs = np.zeros((pairs, blocks, BANDS), np.float32)
    for pair in range(pairs):
        for p in range(blocks):
            i, j = divmod(2 * pair + p // BANDS, STEPS)
            h, a = divmod((p + STEPS * i) % blocks, BANDS)
            g, c = divmod((p + j) % blocks, BANDS)
            table[pair, :, p, :, h ^ g, a, c] = 1 if (h, g) == (0, 1) else -1
            signs[pair, p] = 1 if h == g else -1
    return signs.reshape(pairs, WIDTH), table.reshape(-1, WIDTH).astype(ml_dtypes.bfloat16)


def spread_table():
    table = np.zeros((2, BANDS, BANDS, 2, BANDS, 2, BANDS, BANDS), np.float32)
    for h, g, a, b in np.ndindex(2, 2, BANDS, BANDS):
        table[1 if h == g else 0, a, b, g, b, h, a, :] = -1 if (h, g) == (1, 0) else 1
    return np.tile(table.reshape(WIDTH, -1), (2, 1)).astype(ml_dtypes.bfloat16)


def in_vmem():
    return pl.BlockSpec(memory_space=pltpu.VMEM)


def in_smem():
    return pl.BlockSpec(memory_space=pltpu.SMEM)


def anywhere():
    return pl.BlockSpec(memory_space=pl.ANY)


def params(megabytes):
    return pltpu.CompilerParams(vmem_limit_bytes=megabytes * 1024 * 1024)


def cost(per_element, arrays):
    size = SIDE * SIDE * TILE * WIDTH
    return pl.CostEstimate(flops=per_element * size, bytes_accessed=4 * arrays * size, transcendentals=0)


def held_blocks(count, parts):
    return [
        pltpu.VMEM((count, TILE * SIDE * SIDE // parts, WIDTH), jnp.float32),
        pltpu.SemaphoreType.DMA((count,)),
    ]


def forward(place, greens, steps, parts):
    points = SIDE * SIDE
    return pl.pallas_call(
        functools.partial(forward_kernel, steps, parts),
        out_shape=[
            jax.ShapeDtypeStruct((points, TILE, WIDTH), jnp.float32),
            jax.ShapeDtypeStruct((STEPS, TILE * points, WIDTH), jnp.float32),
        ],
        in_specs=[in_smem()] + [anywhere()] * len(steps),
        out_specs=[in_vmem()] * 2,
        scratch_shapes=[pltpu.VMEM((points, TILE, WIDTH), jnp.float32)] + held_blocks(len(steps), parts),
        compiler_params=params(8),
        cost_estimate=cost(400, 6),
        name="forward",
    )(place, *greens)


def early_lines(place, lattice, weights, screens, steps, parts, work=None):
    points = SIDE * SIDE
    inputs = (place, lattice, weights, *screens) + (() if work is None else (work,))
    return pl.pallas_call(
        functools.partial(early_kernel, steps, parts),
        out_shape=jax.ShapeDtypeStruct((points, TILE, WIDTH), jnp.float32),
        in_specs=[in_smem(), in_vmem(), in_vmem()]
        + [anywhere()] * len(steps)
        + [in_vmem()] * (work is not None),
        out_specs=in_vmem(),
        input_output_aliases={} if work is None else {len(inputs) - 1: 0},
        scratch_shapes=held_blocks(len(steps), parts),
        compiler_params=params(4),
        cost_estimate=cost(25 * len(steps), 3),
        name="early",
    )(*inputs)


def sigma_of(place, lattice, weights, screens, work, steps, parts):
    points = SIDE * SIDE
    inputs = (place, lattice, weights, *screens, work)
    work, sigma = pl.pallas_call(
        functools.partial(sigma_kernel, steps, parts),
        out_shape=[
            jax.ShapeDtypeStruct((points, TILE, WIDTH), jnp.float32),
            jax.ShapeDtypeStruct((TILE * points, WIDTH), jnp.float32),
        ],
        in_specs=[in_smem()] + [in_vmem()] * 2 + [anywhere()] * len(steps) + [in_vmem()],
        out_specs=[in_vmem()] * 2,
        input_output_aliases={len(inputs) - 1: 0},
        scratch_shapes=held_blocks(len(steps), parts) if steps else [],
        compiler_params=params(4),
        cost_estimate=cost(200, 6),
        name="sigma",
    )(*inputs)
    return sigma


def contract(owners, sigma, equal_time, greens, block, share, before=()):
    points = owners.shape[0] * block
    rows = -(-points // 16) * 16
    signs, gather = gather_tables()
    return pl.pallas_call(
        functools.partial(contract_kernel, share),
        out_shape=jax.ShapeDtypeStruct((points, WIDTH), jnp.float32),
        in_specs=[in_smem()] + [in_vmem()] * 5 + [anywhere()] * len(before),
        out_specs=in_vmem(),
        scratch_shapes=[
            pltpu.VMEM((rows, STEPS * STEPS * WIDTH), jnp.float32),
            pltpu.VMEM((rows, STEPS * STEPS * WIDTH), jnp.bfloat16),
        ],
        compiler_params=params(10),
        cost_estimate=cost(70 * owners.shape[0], 6),
        name="contract",
    )(owners, sigma, equal_time, jnp.asarray(signs), jnp.asarray(gather), greens, *before)


def split_own(greens):
    history, points, width = greens.shape
    return pl.pallas_call(
        split_kernel,
        out_shape=jax.ShapeDtypeStruct((points, 2 * history, width), jnp.bfloat16),
        in_specs=[in_vmem()],
        out_specs=in_vmem(),
        compiler_params=params(4),
        cost_estimate=cost(3, 2),
        name="split_own",
    )(greens)


def propagate(greens, pieces, effective):
    history, points, width = greens.shape
    tile = points if points % TILE else TILE
    spread = spread_table()
    return pl.pallas_call(
        propagate_kernel,
        out_shape=jax.ShapeDtypeStruct(greens.shape, jnp.float32),
        in_specs=[in_vmem()] * 4,
        out_specs=anywhere(),
        scratch_shapes=[
            pltpu.VMEM((points, spread.shape[1]), jnp.float32),
            pltpu.VMEM((2, history, tile, width), jnp.float32),
            pltpu.SemaphoreType.DMA((2,)),
        ],
        compiler_params=params(6),
        cost_estimate=cost(32, 5),
        name="propagate",
    )(greens, pieces, effective, jnp.asarray(spread))


def partner_of(place, step, count):
    if count == 1:
        return 0
    if count & (count - 1) == 0:
        return place ^ step
    return (place + step) % count


def exchange(value, axis, step, count):
    pairs = [(place, partner_of(place, step, count)) for place in range(count)]
    return lax.ppermute(value, axis, pairs)


def exchange_order(count):
    along = {}
    for step in range(1, count):
        along.setdefault(step // 2, []).append(step)
    single = [along[n] for n in along if n and n & (n - 1) == 0]
    mixed = [along[n] for n in along if n & (n - 1)]
    order = [step for steps in zip(*single[::-1]) for step in steps]
    return order + along[0] + [step for steps in mixed for step in steps]


def class_weights(quad_class):
    table = jnp.array(quadrature, jnp.float32)
    match = quad_class[:, None] == jnp.arange(4, dtype=jnp.int32)[None, :]
    return jnp.sum(jnp.where(match, table[None, :], jnp.float32(0.0)), axis=1)


def per_device(parts, blocks, green_row, screened, hamilton, equal_time, quad_class, live_count):
    history, local, width = green_row.shape
    points = local * parts
    times = history // parts
    place = lax.axis_index("ka")
    seat = place.reshape(1)
    position = jnp.arange(history, dtype=jnp.int32)
    weights = jnp.where(
        position < live_count[0], time_step * class_weights(quad_class), jnp.float32(0.0)
    ) * jnp.float32(1.0 / points)
    weights = lax.dynamic_slice_in_dim(weights, place * times, times)

    if times == TILE and local % SIDE == 0:
        groups, sources = 1, parts
        order = exchange_order(parts)
        moved = []
        wholes = [x.reshape(parts * TILE * local, width) for x in (green_row, screened)]
        moved = []
        for whole in wholes:
            found = {0: whole}
            for step in order:
                start = partner_of(place, step, parts) * (TILE * local)
                block = lax.dynamic_slice_in_dim(whole, start, TILE * local)
                found[step] = exchange(block, "ka", step, parts)
            moved.append([found])
        order = [0] + order
    else:
        groups, sources = -(-times // TILE), 1
        order = [0]
        padding = groups * TILE - times
        moved = []
        for x in (green_row, screened):
            x = lax.all_to_all(x, "ka", split_axis=0, concat_axis=0, tiled=True)
            x = x.reshape(parts, times, local, width).transpose(1, 0, 2, 3).reshape(times, points, width)
            x = jnp.pad(x, ((0, padding), (0, 0), (0, 0))).reshape(groups, TILE * points, width)
            moved.append([{0: x[group]} for group in range(groups)])
        weights = jnp.pad(weights, (0, padding))
    weights = jnp.broadcast_to(weights.reshape(groups, TILE, 1), (groups, TILE, width))

    early = order[: max(1, len(order) - LATE)]
    late = order[len(early) :]
    own_pieces = split_own(green_row)
    share = hubbard / (points * blocks)
    sigmas = []
    for group in range(groups):
        green, screen = moved[0][group], moved[1][group]
        listed = order
        lattice, greens = forward(seat, [green[step] for step in listed], listed, sources)
        listed = early[-1:] + early[:-1]
        work = early_lines(seat, lattice, weights[group], [screen[step] for step in listed], listed, sources)
        for step in late[:-1]:
            work = early_lines(seat, lattice, weights[group], [screen[step]], [step], sources, work)
        last = late[-1:]
        sigma = sigma_of(
            seat, lattice, weights[group], [screen[step] for step in last], work, last, sources
        )
        sigmas.append((sigma, greens))

    if sources == parts and parts % 2 == 0 and parts & (parts - 1) == 0:
        (sigma, greens), = sigmas

        def blocks_of(steps, before=()):
            owners = jnp.stack([partner_of(place, step, parts) for step in steps])
            return contract(owners, sigma, equal_time, greens, local, share, before)

        others = exchange(blocks_of([*range(3, parts, 2), 1]), "ka", 1, parts)
        far = blocks_of(list(range(2, parts, 2))) + others[:-local]
        pieces = [
            exchange(far[(n - 1) * local : n * local], "ka", 2 * n, parts)
            for n in range(parts // 2 - 1, 0, -1)
        ]
        pieces += [blocks_of([0], pieces[:1]), others[-local:]]
        collision = tree_sum(pieces)
    else:
        whole = jnp.zeros((1,), jnp.int32)
        partial_value = tree_sum(
            [
                contract(whole, sigma, equal_time, greens, points, share if group == 0 else 0.0)
                for group, (sigma, greens) in enumerate(sigmas)
            ]
        )
        owners = [partner_of(place, step, parts) for step in range(parts)]
        pieces = [lax.dynamic_slice_in_dim(partial_value, owner * local, local) for owner in owners]
        collision = tree_sum(
            pieces[:1] + [exchange(pieces[step], "ka", step, parts) for step in range(1, parts)]
        )
    collision = tree_sum(
        [collision] + [exchange(collision, "hist", step, blocks) for step in range(blocks - 1, 0, -1)]
    )
    return propagate(green_row, own_pieces, hamilton + collision)


def solution(mesh):
    in_specs = (
        P("hist", "ka", None),
        P("hist", "ka", None),
        P("ka", None),
        P("ka", None),
        P("hist"),
        P("hist"),
    )
    out_specs = P("hist", "ka", None)
    return jax.shard_map(
        functools.partial(per_device, mesh.shape["ka"], mesh.shape["hist"]),
        mesh=mesh,
        in_specs=in_specs,
        out_specs=out_specs,
        check_vma=False,
    )
```

```python
import functools
import math

import jax
import jax.numpy as jnp
import ml_dtypes
import numpy as np
from jax import lax
from jax.experimental import pallas as pl
from jax.experimental.pallas import tpu as pltpu
from jax.sharding import PartitionSpec as P

SIDE = 24
BANDS = 8
ENTRIES = BANDS * BANDS
WIDTH = 2 * ENTRIES
TILE = 8
STEPS = 4

time_step = 0.1
hubbard = 1.0
quadrature = (0.375, 1.1666666, 0.9583333, 1.0)

LATE = 2
AHEAD = 3


def lane_sign(shape):
    lane = lax.broadcasted_iota(jnp.int32, shape, len(shape) - 1)
    return lane < ENTRIES


def swap(x):
    return pltpu.roll(x, ENTRIES, 1)


def roll_blocks(x, blocks):
    return x if blocks == 0 else pltpu.roll(x, WIDTH - BANDS * blocks, x.ndim - 1)


def tree_sum(terms):
    while len(terms) > 1:
        terms = [sum(terms[i : i + 2][1:], terms[i]) for i in range(0, len(terms), 2)]
    return terms[0]


def split(x):
    high = x.astype(jnp.bfloat16)
    return jnp.concatenate([high, (x - high.astype(jnp.float32)).astype(jnp.bfloat16)], axis=1)


def dft24(x, sign, low):
    root3 = jnp.where(low, -1.0, 1.0) * (sign * math.sqrt(3.0) / 2)
    turn = jnp.where(low, -1.0, 1.0) * float(sign)
    half = math.sqrt(0.5)
    turn_half = turn * half
    columns = [[None] * 8 for _ in range(3)]
    for n2 in range(8):
        x0, x1, x2 = (x[(8 * n1 + 3 * n2) % 24] for n1 in range(3))
        total = x1 + x2
        base = x0 - 0.5 * total
        spin = swap(x1 - x2) * root3
        columns[0][n2] = x0 + total
        columns[1][n2] = base + spin
        columns[2][n2] = base - spin
    out = [None] * 24
    for k1 in range(3):
        c = columns[k1]
        a0, a1 = c[0] + c[4], c[0] - c[4]
        a2, a3 = c[2] + c[6], c[2] - c[6]
        a4, a5 = c[1] + c[5], c[1] - c[5]
        a6, a7 = c[3] + c[7], c[3] - c[7]
        b0, b1 = a0 + a2, a0 - a2
        b2, b3 = a4 + a6, a4 - a6
        i_a3 = swap(a3) * turn
        i_b3 = swap(b3) * turn
        c0, c1 = a1 + i_a3, a1 - i_a3
        p = (a5 - a7) * half
        m = swap(a5 + a7) * turn_half
        e, f = p + m, p - m
        values = [b0 + b2, c0 + e, b1 + i_b3, c1 - f, b0 - b2, c0 - e, b1 - i_b3, c1 + f]
        for k2 in range(8):
            out[(16 * k1 + 9 * k2) % 24] = values[k2]
    return out


def load_line(ref, line):
    stride = ref.shape[0] // TILE
    return [ref[pl.ds(line * SIDE + k2, TILE, stride=stride), :] for k2 in range(SIDE)]


def fetch(place, steps, block_refs, held_ref, sems):
    copies = []
    for slot, (step, source) in enumerate(zip(steps, block_refs)):
        rows = held_ref.shape[1]
        if step == 0 and source.shape[0] != rows:
            source = source.at[pl.ds(pl.multiple_of(place * rows, TILE), rows)]
        copies.append(pltpu.make_async_copy(source, held_ref.at[slot], sems.at[slot]))
        copies[-1].start()
    return copies


def along_first(work_ref, sign, low, store):
    def columns(pair, carry):
        both = (2 * pair, 2 * pair + 1)
        rows = [[work_ref[k1 * SIDE + column] for k1 in range(SIDE)] for column in both]
        values = [dft24(row, sign, low) for row in rows]
        for column, value in zip(both, values):
            for r1 in range(SIDE):
                store(r1 * SIDE + column, value[r1])
        return carry

    lax.fori_loop(0, SIDE // 2, columns, 0)


def times_of(ref, k):
    history, points, width = ref.shape
    if points % TILE:
        return ref[:, k, :]
    return ref.reshape(history * points, width)[pl.ds(k, history, stride=points), :]


def split_kernel(green_ref, split_ref):
    history, points, _ = green_ref.shape

    def write(k):
        green = times_of(green_ref, k)
        high = green.astype(jnp.bfloat16)
        low = (green - high.astype(jnp.float32)).astype(jnp.bfloat16)
        for n, part in enumerate((high, low, high)):
            split_ref[k, :, n * WIDTH : (n + 1) * WIDTH] = part

    if points % TILE:
        for k in range(points):
            write(k)
        return

    def some(n, carry):
        for k in range(4):
            write(4 * n + k)
        return carry

    lax.fori_loop(0, points // 4, some, 0)


def forward_kernel(steps, parts, place_ref, *refs):
    block_refs, (lattice_ref, greens_ref, work_ref, held_ref, sems) = refs[: len(steps)], refs[len(steps) :]
    low = lane_sign((TILE, WIDTH))
    place = place_ref[0]
    copies = fetch(place, steps, block_refs, held_ref, sems)
    rows = held_ref.shape[1]
    lines = rows // (TILE * SIDE)
    for slot, step in enumerate(steps):
        copies[slot].wait()
        green_ref = held_ref.at[slot]
        owner = partner_of(place, step, parts)

        def along_second(i, carry):
            for r2, value in enumerate(dft24(load_line(green_ref, i), -1, low)):
                work_ref[(owner * lines + i) * SIDE + r2] = value
            return carry

        lax.fori_loop(0, lines, along_second, 0, unroll=lines <= 4)
        green = green_ref[...]
        spot = pl.ds(pl.multiple_of(owner * rows, TILE), rows)
        for j in range(STEPS):
            greens_ref[j, spot, :] = roll_blocks(green, j)

    def store(point, value):
        lattice_ref[point] = value

    along_first(work_ref, -1, low, store)


def product_lines(steps, parts, place, lattice_ref, weights, screen_refs, held_ref, sems, work_ref):
    low = lane_sign((TILE, WIDTH))
    turn = jnp.where(low, -1.0, 1.0)
    copies = fetch(place, steps, screen_refs, held_ref, sems)
    lines = held_ref.shape[1] // (TILE * SIDE)
    for slot, step in enumerate(steps):
        copies[slot].wait()
        screen_ref = held_ref.at[slot]
        first = partner_of(place, step, parts) * lines

        def along_second(i, carry):
            rows = []
            for r2, value in enumerate(load_line(screen_ref, i)):
                screen = value * weights
                other = swap(screen)
                lattice = lattice_ref[(first + i) * SIDE + r2]
                rows.append(
                    swap(lattice) * turn * jnp.where(low, screen, other)
                    - lattice * jnp.where(low, other, screen)
                )
            for k2, value in enumerate(dft24(rows, 1, low)):
                work_ref[(first + i) * SIDE + k2] = value
            return carry

        lax.fori_loop(0, lines, along_second, 0, unroll=lines <= 4)


def early_kernel(steps, parts, place_ref, lattice_ref, weight_ref, *refs):
    screen_refs, (*_, work_ref, held_ref, sems) = refs[: len(steps)], refs[len(steps) :]
    product_lines(
        steps, parts, place_ref[0], lattice_ref, weight_ref[...], screen_refs, held_ref, sems, work_ref
    )


def sigma_kernel(steps, parts, place_ref, lattice_ref, weight_ref, *refs):
    screen_refs, refs = refs[: len(steps)], refs[len(steps) :]
    _, work_ref, sigma_ref, *late = refs
    low = lane_sign((TILE, WIDTH))
    if steps:
        held_ref, sems = late
        product_lines(
            steps, parts, place_ref[0], lattice_ref, weight_ref[...], screen_refs, held_ref, sems, work_ref
        )

    def store(point, value):
        sigma_ref[pl.ds(point * TILE, TILE), :] = value

    along_first(work_ref, 1, low, store)


def contract_kernel(share, owner_ref, sigma_ref, equal_ref, sign_ref, gather_ref, greens_ref, *refs):
    partial_ref, sums_ref, pieces_ref = refs[-3:]
    low = lane_sign((TILE, WIDTH))
    points = partial_ref.shape[0]
    block = points // owner_ref.shape[0]
    tiles = block // TILE
    batch = max(n for n in range(1, 10) if tiles % n == 0)

    def contract(group, carry):
        slot, first = group // (tiles // batch), group % (tiles // batch) * batch
        owner = owner_ref[slot]
        units = [(tile, s) for tile in range(batch) for s in range(TILE)]

        def prepare(tile, s):
            point = owner * block + (first + tile) * TILE
            sigma = sigma_ref[pl.ds(point * TILE + s, TILE, stride=TILE), :]
            row = pl.multiple_of((owner * TILE + s) * block + (first + tile) * TILE, TILE)
            return (
                [roll_blocks(sigma, STEPS * i) for i in range(STEPS)],
                [greens_ref[j, pl.ds(row, TILE), :] for j in range(STEPS)],
            )

        ready = [prepare(*unit) for unit in units[:AHEAD]]
        for n, (tile, s) in enumerate(units):
            if n + AHEAD < len(units):
                ready.append(prepare(*units[n + AHEAD]))
            sigmas, greens = ready.pop(0)
            terms = [sigma * green for sigma in sigmas for green in greens]
            sums = terms if s == 0 else [a + b for a, b in zip(sums, terms)]
            if s == TILE - 1:
                row = pl.ds(pl.multiple_of(slot * block + (first + tile) * TILE, TILE), TILE)
                for spot, value in enumerate(sums):
                    sums_ref[row, spot * WIDTH : (spot + 1) * WIDTH] = value
        return carry

    lax.fori_loop(0, points // (TILE * batch), contract, 0)

    lane = lax.broadcasted_iota(jnp.int32, equal_ref.shape, 1)
    inner = lane - ENTRIES
    occupied = jnp.sum(jnp.where((inner >= 0) & (inner % (BANDS + 1) == 0), equal_ref[...], 0.0))
    spots = lax.broadcasted_iota(jnp.int32, (points, WIDTH), 1)
    on_diagonal = (spots < ENTRIES) & (spots % (BANDS + 1) == 0)
    lower = lax.broadcasted_iota(jnp.int32, (sums_ref.shape[0], WIDTH), 1) < ENTRIES
    for pair in range(STEPS * STEPS // 2):
        first_part = sums_ref[:, 2 * pair * WIDTH : (2 * pair + 1) * WIDTH]
        second_part = sums_ref[:, (2 * pair + 1) * WIDTH : (2 * pair + 2) * WIDTH]
        folded = jnp.where(lower, first_part, second_part) + sign_ref[pair : pair + 1, :] * swap(
            jnp.where(lower, second_part, first_part)
        )
        pieces_ref[:, 2 * pair * WIDTH : (2 * pair + 2) * WIDTH] = split(folded)
    total = jnp.dot(pieces_ref[...], gather_ref[...], preferred_element_type=jnp.float32)
    partial_ref[...] = total[:points] + jnp.where(on_diagonal, occupied * share, 0.0)


def propagate_kernel(green_ref, split_ref, effective_ref, spread_ref, out_ref, factor_ref, held_ref, sems):
    history, points, _ = green_ref.shape
    factor_ref[...] = jnp.dot(
        split(effective_ref[...] * time_step), spread_ref[...], preferred_element_type=jnp.float32
    )
    tile = held_ref.shape[2]
    row = lax.broadcasted_iota(jnp.int32, (BANDS, WIDTH), 0)
    same = lax.broadcasted_iota(jnp.int32, (BANDS, WIDTH), 1) % BANDS == row

    def copy(number, slot):
        return pltpu.make_async_copy(
            held_ref.at[slot], out_ref.at[:, pl.ds(number * tile, tile), :], sems.at[slot]
        )

    def matrix(factors, n):
        parts = [
            jnp.where(same, jnp.broadcast_to(factor[n : n + 1], same.shape), 0.0) for factor in factors
        ]
        whole = jnp.concatenate(parts, axis=0)
        high = whole.astype(jnp.bfloat16)
        low = (whole - high.astype(jnp.float32)).astype(jnp.bfloat16)
        return jnp.concatenate([high, high, low], axis=0)

    def advance(number, slot):
        start = number * tile if points == tile else pl.multiple_of(number * tile, TILE)
        factors = [
            factor_ref[pl.ds(start, tile), spot * WIDTH : (spot + 1) * WIDTH] for spot in range(2 * BANDS)
        ]
        for n in range(tile):
            k = number * tile + n
            added = jnp.dot(split_ref[k], matrix(factors, n), preferred_element_type=jnp.float32)
            result = times_of(green_ref, k) + added
            if points % TILE:
                held_ref[slot, :, n, :] = result
            else:
                rows = held_ref.reshape(2 * history * tile, WIDTH)
                rows[pl.ds(slot * history * tile + n, history, stride=tile), :] = result
        copy(number, slot).start()

    tiles = points // tile
    if tiles == 1:
        advance(0, 0)
        copy(0, 0).wait()
        return

    def step(number, carry):
        slot = number % 2

        @pl.when(number > 1)
        def _():
            copy(number - 2, slot).wait()

        advance(number, slot)
        return carry

    lax.fori_loop(0, tiles, step, 0)
    for number in (tiles - 2, tiles - 1):
        copy(number, number % 2).wait()


def gather_tables():
    blocks = 2 * BANDS
    pairs = STEPS * STEPS // 2
    table = np.zeros((pairs, 2, blocks, BANDS, 2, BANDS, BANDS), np.float32)
    signs = np.zeros((pairs, blocks, BANDS), np.float32)
    for pair in range(pairs):
        for p in range(blocks):
            i, j = divmod(2 * pair + p // BANDS, STEPS)
            h, a = divmod((p + STEPS * i) % blocks, BANDS)
            g, c = divmod((p + j) % blocks, BANDS)
            table[pair, :, p, :, h ^ g, a, c] = 1 if (h, g) == (0, 1) else -1
            signs[pair, p] = 1 if h == g else -1
    return signs.reshape(pairs, WIDTH), table.reshape(-1, WIDTH).astype(ml_dtypes.bfloat16)


def spread_table():
    table = np.zeros((2, BANDS, BANDS, 2, BANDS, 2, BANDS, BANDS), np.float32)
    for h, g, a, b in np.ndindex(2, 2, BANDS, BANDS):
        table[1 if h == g else 0, a, b, g, b, h, a, :] = -1 if (h, g) == (1, 0) else 1
    return np.tile(table.reshape(WIDTH, -1), (2, 1)).astype(ml_dtypes.bfloat16)


def in_vmem():
    return pl.BlockSpec(memory_space=pltpu.VMEM)


def in_smem():
    return pl.BlockSpec(memory_space=pltpu.SMEM)


def anywhere():
    return pl.BlockSpec(memory_space=pl.ANY)


def params(megabytes):
    return pltpu.CompilerParams(vmem_limit_bytes=megabytes * 1024 * 1024)


def cost(per_element, arrays):
    size = SIDE * SIDE * TILE * WIDTH
    return pl.CostEstimate(flops=per_element * size, bytes_accessed=4 * arrays * size, transcendentals=0)


def held_blocks(count, parts):
    return [
        pltpu.VMEM((count, TILE * SIDE * SIDE // parts, WIDTH), jnp.float32),
        pltpu.SemaphoreType.DMA((count,)),
    ]


def forward(place, greens, steps, parts):
    points = SIDE * SIDE
    return pl.pallas_call(
        functools.partial(forward_kernel, steps, parts),
        out_shape=[
            jax.ShapeDtypeStruct((points, TILE, WIDTH), jnp.float32),
            jax.ShapeDtypeStruct((STEPS, TILE * points, WIDTH), jnp.float32),
        ],
        in_specs=[in_smem()] + [anywhere()] * len(steps),
        out_specs=[in_vmem()] * 2,
        scratch_shapes=[pltpu.VMEM((points, TILE, WIDTH), jnp.float32)] + held_blocks(len(steps), parts),
        compiler_params=params(8),
        cost_estimate=cost(400, 6),
        name="forward",
    )(place, *greens)


def early_lines(place, lattice, weights, screens, steps, parts, work=None):
    points = SIDE * SIDE
    inputs = (place, lattice, weights, *screens) + (() if work is None else (work,))
    return pl.pallas_call(
        functools.partial(early_kernel, steps, parts),
        out_shape=jax.ShapeDtypeStruct((points, TILE, WIDTH), jnp.float32),
        in_specs=[in_smem(), in_vmem(), in_vmem()]
        + [anywhere()] * len(steps)
        + [in_vmem()] * (work is not None),
        out_specs=in_vmem(),
        input_output_aliases={} if work is None else {len(inputs) - 1: 0},
        scratch_shapes=held_blocks(len(steps), parts),
        compiler_params=params(4),
        cost_estimate=cost(25 * len(steps), 3),
        name="early",
    )(*inputs)


def sigma_of(place, lattice, weights, screens, work, steps, parts):
    points = SIDE * SIDE
    inputs = (place, lattice, weights, *screens, work)
    work, sigma = pl.pallas_call(
        functools.partial(sigma_kernel, steps, parts),
        out_shape=[
            jax.ShapeDtypeStruct((points, TILE, WIDTH), jnp.float32),
            jax.ShapeDtypeStruct((TILE * points, WIDTH), jnp.float32),
        ],
        in_specs=[in_smem()] + [in_vmem()] * 2 + [anywhere()] * len(steps) + [in_vmem()],
        out_specs=[in_vmem()] * 2,
        input_output_aliases={len(inputs) - 1: 0},
        scratch_shapes=held_blocks(len(steps), parts) if steps else [],
        compiler_params=params(4),
        cost_estimate=cost(200, 6),
        name="sigma",
    )(*inputs)
    return sigma


def contract(owners, sigma, equal_time, greens, block, share, before=()):
    points = owners.shape[0] * block
    rows = -(-points // 16) * 16
    signs, gather = gather_tables()
    return pl.pallas_call(
        functools.partial(contract_kernel, share),
        out_shape=jax.ShapeDtypeStruct((points, WIDTH), jnp.float32),
        in_specs=[in_smem()] + [in_vmem()] * 5 + [anywhere()] * len(before),
        out_specs=in_vmem(),
        scratch_shapes=[
            pltpu.VMEM((rows, STEPS * STEPS * WIDTH), jnp.float32),
            pltpu.VMEM((rows, STEPS * STEPS * WIDTH), jnp.bfloat16),
        ],
        compiler_params=params(10),
        cost_estimate=cost(70 * owners.shape[0], 6),
        name="contract",
    )(owners, sigma, equal_time, jnp.asarray(signs), jnp.asarray(gather), greens, *before)


def split_own(greens):
    history, points, width = greens.shape
    return pl.pallas_call(
        split_kernel,
        out_shape=jax.ShapeDtypeStruct((points, history, 3 * width), jnp.bfloat16),
        in_specs=[in_vmem()],
        out_specs=in_vmem(),
        compiler_params=params(4),
        cost_estimate=cost(3, 2),
        name="split_own",
    )(greens)


def propagate(greens, pieces, effective):
    history, points, width = greens.shape
    tile = points if points % TILE else TILE
    spread = spread_table()
    return pl.pallas_call(
        propagate_kernel,
        out_shape=jax.ShapeDtypeStruct(greens.shape, jnp.float32),
        in_specs=[in_vmem()] * 4,
        out_specs=anywhere(),
        scratch_shapes=[
            pltpu.VMEM((points, spread.shape[1]), jnp.float32),
            pltpu.VMEM((2, history, tile, width), jnp.float32),
            pltpu.SemaphoreType.DMA((2,)),
        ],
        compiler_params=params(6),
        cost_estimate=cost(32, 5),
        name="propagate",
    )(greens, pieces, effective, jnp.asarray(spread))


def partner_of(place, step, count):
    if count == 1:
        return 0
    if count & (count - 1) == 0:
        return place ^ step
    return (place + step) % count


def exchange(value, axis, step, count):
    pairs = [(place, partner_of(place, step, count)) for place in range(count)]
    return lax.ppermute(value, axis, pairs)


def exchange_order(count):
    along = {}
    for step in range(1, count):
        along.setdefault(step // 2, []).append(step)
    single = [along[n] for n in along if n and n & (n - 1) == 0]
    mixed = [along[n] for n in along if n & (n - 1)]
    order = [step for steps in zip(*single[::-1]) for step in steps]
    return order + along[0] + [step for steps in mixed for step in steps]


def class_weights(quad_class):
    table = jnp.array(quadrature, jnp.float32)
    match = quad_class[:, None] == jnp.arange(4, dtype=jnp.int32)[None, :]
    return jnp.sum(jnp.where(match, table[None, :], jnp.float32(0.0)), axis=1)


def per_device(parts, blocks, green_row, screened, hamilton, equal_time, quad_class, live_count):
    history, local, width = green_row.shape
    points = local * parts
    times = history // parts
    place = lax.axis_index("ka")
    seat = place.reshape(1)
    position = jnp.arange(history, dtype=jnp.int32)
    weights = jnp.where(
        position < live_count[0], time_step * class_weights(quad_class), jnp.float32(0.0)
    ) * jnp.float32(1.0 / points)
    weights = lax.dynamic_slice_in_dim(weights, place * times, times)

    if times == TILE and local % SIDE == 0:
        groups, sources = 1, parts
        order = exchange_order(parts)
        moved = []
        wholes = [x.reshape(parts * TILE * local, width) for x in (green_row, screened)]
        moved = []
        for whole in wholes:
            found = {0: whole}
            for step in order:
                start = partner_of(place, step, parts) * (TILE * local)
                block = lax.dynamic_slice_in_dim(whole, start, TILE * local)
                found[step] = exchange(block, "ka", step, parts)
            moved.append([found])
        order = [0] + order
    else:
        groups, sources = -(-times // TILE), 1
        order = [0]
        padding = groups * TILE - times
        moved = []
        for x in (green_row, screened):
            x = lax.all_to_all(x, "ka", split_axis=0, concat_axis=0, tiled=True)
            x = x.reshape(parts, times, local, width).transpose(1, 0, 2, 3).reshape(times, points, width)
            x = jnp.pad(x, ((0, padding), (0, 0), (0, 0))).reshape(groups, TILE * points, width)
            moved.append([{0: x[group]} for group in range(groups)])
        weights = jnp.pad(weights, (0, padding))
    weights = jnp.broadcast_to(weights.reshape(groups, TILE, 1), (groups, TILE, width))

    early = order[: max(1, len(order) - LATE)]
    late = order[len(early) :]
    own_pieces = split_own(green_row)
    share = hubbard / (points * blocks)
    sigmas = []
    for group in range(groups):
        green, screen = moved[0][group], moved[1][group]
        listed = order
        lattice, greens = forward(seat, [green[step] for step in listed], listed, sources)
        listed = early[-1:] + early[:-1]
        work = early_lines(seat, lattice, weights[group], [screen[step] for step in listed], listed, sources)
        for step in late[:-1]:
            work = early_lines(seat, lattice, weights[group], [screen[step]], [step], sources, work)
        last = late[-1:]
        sigma = sigma_of(
            seat, lattice, weights[group], [screen[step] for step in last], work, last, sources
        )
        sigmas.append((sigma, greens))

    if sources == parts and parts % 2 == 0 and parts & (parts - 1) == 0:
        (sigma, greens), = sigmas

        def blocks_of(steps, before=()):
            owners = jnp.stack([partner_of(place, step, parts) for step in steps])
            return contract(owners, sigma, equal_time, greens, local, share, before)

        others = exchange(blocks_of([*range(3, parts, 2), 1]), "ka", 1, parts)
        far = blocks_of(list(range(2, parts, 2))) + others[:-local]
        pieces = [
            exchange(far[(n - 1) * local : n * local], "ka", 2 * n, parts)
            for n in range(parts // 2 - 1, 0, -1)
        ]
        pieces += [blocks_of([0], pieces[:1]), others[-local:]]
        collision = tree_sum(pieces)
    else:
        whole = jnp.zeros((1,), jnp.int32)
        partial_value = tree_sum(
            [
                contract(whole, sigma, equal_time, greens, points, share if group == 0 else 0.0)
                for group, (sigma, greens) in enumerate(sigmas)
            ]
        )
        owners = [partner_of(place, step, parts) for step in range(parts)]
        pieces = [lax.dynamic_slice_in_dim(partial_value, owner * local, local) for owner in owners]
        collision = tree_sum(
            pieces[:1] + [exchange(pieces[step], "ka", step, parts) for step in range(1, parts)]
        )
    collision = tree_sum(
        [collision] + [exchange(collision, "hist", step, blocks) for step in range(blocks - 1, 0, -1)]
    )
    return propagate(green_row, own_pieces, hamilton + collision)


def solution(mesh):
    in_specs = (
        P("hist", "ka", None),
        P("hist", "ka", None),
        P("ka", None),
        P("ka", None),
        P("hist"),
        P("hist"),
    )
    out_specs = P("hist", "ka", None)
    return jax.shard_map(
        functools.partial(per_device, mesh.shape["ka"], mesh.shape["hist"]),
        mesh=mesh,
        in_specs=in_specs,
        out_specs=out_specs,
        check_vma=False,
    )
```

```python
import functools
import math

import jax
import jax.numpy as jnp
import ml_dtypes
import numpy as np
from jax import lax
from jax.experimental import pallas as pl
from jax.experimental.pallas import tpu as pltpu
from jax.sharding import PartitionSpec as P

SIDE = 24
BANDS = 8
ENTRIES = BANDS * BANDS
WIDTH = 2 * ENTRIES
TILE = 8
STEPS = 4

time_step = 0.1
hubbard = 1.0
quadrature = (0.375, 1.1666666, 0.9583333, 1.0)

LATE = 2
AHEAD = 3


def lane_sign(shape):
    lane = lax.broadcasted_iota(jnp.int32, shape, len(shape) - 1)
    return lane < ENTRIES


def swap(x):
    return pltpu.roll(x, ENTRIES, 1)


def roll_blocks(x, blocks):
    return x if blocks == 0 else pltpu.roll(x, WIDTH - BANDS * blocks, x.ndim - 1)


def tree_sum(terms):
    while len(terms) > 1:
        terms = [sum(terms[i : i + 2][1:], terms[i]) for i in range(0, len(terms), 2)]
    return terms[0]


def split(x):
    high = x.astype(jnp.bfloat16)
    return jnp.concatenate([high, (x - high.astype(jnp.float32)).astype(jnp.bfloat16)], axis=1)


def dft24(x, sign, low):
    root3 = jnp.where(low, -1.0, 1.0) * (sign * math.sqrt(3.0) / 2)
    turn = jnp.where(low, -1.0, 1.0) * float(sign)
    half = math.sqrt(0.5)
    turn_half = turn * half
    columns = [[None] * 8 for _ in range(3)]
    for n2 in range(8):
        x0, x1, x2 = (x[(8 * n1 + 3 * n2) % 24] for n1 in range(3))
        total = x1 + x2
        base = x0 - 0.5 * total
        spin = swap(x1 - x2) * root3
        columns[0][n2] = x0 + total
        columns[1][n2] = base + spin
        columns[2][n2] = base - spin
    out = [None] * 24
    for k1 in range(3):
        c = columns[k1]
        a0, a1 = c[0] + c[4], c[0] - c[4]
        a2, a3 = c[2] + c[6], c[2] - c[6]
        a4, a5 = c[1] + c[5], c[1] - c[5]
        a6, a7 = c[3] + c[7], c[3] - c[7]
        b0, b1 = a0 + a2, a0 - a2
        b2, b3 = a4 + a6, a4 - a6
        i_a3 = swap(a3) * turn
        i_b3 = swap(b3) * turn
        c0, c1 = a1 + i_a3, a1 - i_a3
        p = (a5 - a7) * half
        m = swap(a5 + a7) * turn_half
        e, f = p + m, p - m
        values = [b0 + b2, c0 + e, b1 + i_b3, c1 - f, b0 - b2, c0 - e, b1 - i_b3, c1 + f]
        for k2 in range(8):
            out[(16 * k1 + 9 * k2) % 24] = values[k2]
    return out


def load_line(ref, line):
    stride = ref.shape[0] // TILE
    return [ref[pl.ds(line * SIDE + k2, TILE, stride=stride), :] for k2 in range(SIDE)]


def fetch(place, steps, block_refs, held_ref, sems):
    copies = []
    for slot, (step, source) in enumerate(zip(steps, block_refs)):
        rows = held_ref.shape[1]
        if step == 0 and source.shape[0] != rows:
            source = source.at[pl.ds(pl.multiple_of(place * rows, TILE), rows)]
        copies.append(pltpu.make_async_copy(source, held_ref.at[slot], sems.at[slot]))
        copies[-1].start()
    return copies


def along_first(work_ref, sign, low, store):
    def columns(pair, carry):
        both = (2 * pair, 2 * pair + 1)
        rows = [[work_ref[k1 * SIDE + column] for k1 in range(SIDE)] for column in both]
        values = [dft24(row, sign, low) for row in rows]
        for column, value in zip(both, values):
            for r1 in range(SIDE):
                store(r1 * SIDE + column, value[r1])
        return carry

    lax.fori_loop(0, SIDE // 2, columns, 0)


def pick_kernel(steps, parts, place_ref, whole_ref, *refs):
    block_refs, sems = refs[-1 - len(steps) : -1], refs[-1]
    copies = []
    for n, (step, block_ref) in enumerate(zip(steps, block_refs)):
        rows = block_ref.shape[0]
        start = pl.multiple_of(partner_of(place_ref[0], step, parts) * rows, TILE)
        copies.append(pltpu.make_async_copy(whole_ref.at[pl.ds(start, rows)], block_ref, sems.at[n]))
        copies[-1].start()
    for copy in copies:
        copy.wait()


def times_of(ref, k):
    history, points, width = ref.shape
    if points % TILE:
        return ref[:, k, :]
    return ref.reshape(history * points, width)[pl.ds(k, history, stride=points), :]


def split_kernel(green_ref, split_ref):
    history, points, _ = green_ref.shape

    def write(k):
        green = times_of(green_ref, k)
        high = green.astype(jnp.bfloat16)
        low = (green - high.astype(jnp.float32)).astype(jnp.bfloat16)
        for n, part in enumerate((high, low, high)):
            split_ref[k, :, n * WIDTH : (n + 1) * WIDTH] = part

    if points % TILE:
        for k in range(points):
            write(k)
        return

    def some(n, carry):
        for k in range(4):
            write(4 * n + k)
        return carry

    lax.fori_loop(0, points // 4, some, 0)


def forward_kernel(steps, parts, place_ref, *refs):
    block_refs, (lattice_ref, greens_ref, work_ref, held_ref, sems) = refs[: len(steps)], refs[len(steps) :]
    low = lane_sign((TILE, WIDTH))
    place = place_ref[0]
    copies = fetch(place, steps, block_refs, held_ref, sems)
    rows = held_ref.shape[1]
    lines = rows // (TILE * SIDE)
    for slot, step in enumerate(steps):
        copies[slot].wait()
        green_ref = held_ref.at[slot]
        owner = partner_of(place, step, parts)

        def along_second(i, carry):
            for r2, value in enumerate(dft24(load_line(green_ref, i), -1, low)):
                work_ref[(owner * lines + i) * SIDE + r2] = value
            return carry

        lax.fori_loop(0, lines, along_second, 0, unroll=lines <= 4)
        green = green_ref[...]
        spot = pl.ds(pl.multiple_of(owner * rows, TILE), rows)
        for j in range(STEPS):
            greens_ref[j, spot, :] = roll_blocks(green, j)

    def store(point, value):
        lattice_ref[point] = value

    along_first(work_ref, -1, low, store)


def product_lines(steps, parts, place, lattice_ref, weights, screen_refs, held_ref, sems, work_ref):
    low = lane_sign((TILE, WIDTH))
    turn = jnp.where(low, -1.0, 1.0)
    copies = fetch(place, steps, screen_refs, held_ref, sems)
    lines = held_ref.shape[1] // (TILE * SIDE)
    for slot, step in enumerate(steps):
        copies[slot].wait()
        screen_ref = held_ref.at[slot]
        first = partner_of(place, step, parts) * lines

        def along_second(i, carry):
            rows = []
            for r2, value in enumerate(load_line(screen_ref, i)):
                screen = value * weights
                other = swap(screen)
                lattice = lattice_ref[(first + i) * SIDE + r2]
                rows.append(
                    swap(lattice) * turn * jnp.where(low, screen, other)
                    - lattice * jnp.where(low, other, screen)
                )
            for k2, value in enumerate(dft24(rows, 1, low)):
                work_ref[(first + i) * SIDE + k2] = value
            return carry

        lax.fori_loop(0, lines, along_second, 0, unroll=lines <= 4)


def early_kernel(steps, parts, place_ref, lattice_ref, weight_ref, *refs):
    screen_refs, (*_, work_ref, held_ref, sems) = refs[: len(steps)], refs[len(steps) :]
    product_lines(
        steps, parts, place_ref[0], lattice_ref, weight_ref[...], screen_refs, held_ref, sems, work_ref
    )


def sigma_kernel(steps, parts, place_ref, lattice_ref, weight_ref, *refs):
    screen_refs, refs = refs[: len(steps)], refs[len(steps) :]
    _, work_ref, sigma_ref, *late = refs
    low = lane_sign((TILE, WIDTH))
    if steps:
        held_ref, sems = late
        product_lines(
            steps, parts, place_ref[0], lattice_ref, weight_ref[...], screen_refs, held_ref, sems, work_ref
        )

    def store(point, value):
        sigma_ref[pl.ds(point * TILE, TILE), :] = value

    along_first(work_ref, 1, low, store)


def contract_kernel(share, owner_ref, sigma_ref, equal_ref, sign_ref, gather_ref, greens_ref, *refs):
    partial_ref, sums_ref, pieces_ref = refs[-3:]
    low = lane_sign((TILE, WIDTH))
    points = partial_ref.shape[0]
    block = points // owner_ref.shape[0]
    tiles = block // TILE
    batch = max(n for n in range(1, 10) if tiles % n == 0)

    def contract(group, carry):
        slot, first = group // (tiles // batch), group % (tiles // batch) * batch
        owner = owner_ref[slot]
        units = [(tile, s) for tile in range(batch) for s in range(TILE)]

        def prepare(tile, s):
            point = owner * block + (first + tile) * TILE
            sigma = sigma_ref[pl.ds(point * TILE + s, TILE, stride=TILE), :]
            row = pl.multiple_of((owner * TILE + s) * block + (first + tile) * TILE, TILE)
            return (
                [roll_blocks(sigma, STEPS * i) for i in range(STEPS)],
                [greens_ref[j, pl.ds(row, TILE), :] for j in range(STEPS)],
            )

        ready = [prepare(*unit) for unit in units[:AHEAD]]
        for n, (tile, s) in enumerate(units):
            if n + AHEAD < len(units):
                ready.append(prepare(*units[n + AHEAD]))
            sigmas, greens = ready.pop(0)
            terms = [sigma * green for sigma in sigmas for green in greens]
            sums = terms if s == 0 else [a + b for a, b in zip(sums, terms)]
            if s == TILE - 1:
                row = pl.ds(pl.multiple_of(slot * block + (first + tile) * TILE, TILE), TILE)
                for spot, value in enumerate(sums):
                    sums_ref[row, spot * WIDTH : (spot + 1) * WIDTH] = value
        return carry

    lax.fori_loop(0, points // (TILE * batch), contract, 0)

    lane = lax.broadcasted_iota(jnp.int32, equal_ref.shape, 1)
    inner = lane - ENTRIES
    occupied = jnp.sum(jnp.where((inner >= 0) & (inner % (BANDS + 1) == 0), equal_ref[...], 0.0))
    spots = lax.broadcasted_iota(jnp.int32, (points, WIDTH), 1)
    on_diagonal = (spots < ENTRIES) & (spots % (BANDS + 1) == 0)
    lower = lax.broadcasted_iota(jnp.int32, (sums_ref.shape[0], WIDTH), 1) < ENTRIES
    for pair in range(STEPS * STEPS // 2):
        first_part = sums_ref[:, 2 * pair * WIDTH : (2 * pair + 1) * WIDTH]
        second_part = sums_ref[:, (2 * pair + 1) * WIDTH : (2 * pair + 2) * WIDTH]
        folded = jnp.where(lower, first_part, second_part) + sign_ref[pair : pair + 1, :] * swap(
            jnp.where(lower, second_part, first_part)
        )
        pieces_ref[:, 2 * pair * WIDTH : (2 * pair + 2) * WIDTH] = split(folded)
    total = jnp.dot(pieces_ref[...], gather_ref[...], preferred_element_type=jnp.float32)
    partial_ref[...] = total[:points] + jnp.where(on_diagonal, occupied * share, 0.0)


def propagate_kernel(green_ref, split_ref, effective_ref, spread_ref, out_ref, factor_ref, held_ref, sems):
    history, points, _ = green_ref.shape
    factor_ref[...] = jnp.dot(
        split(effective_ref[...] * time_step), spread_ref[...], preferred_element_type=jnp.float32
    )
    tile = held_ref.shape[2]
    row = lax.broadcasted_iota(jnp.int32, (BANDS, WIDTH), 0)
    same = lax.broadcasted_iota(jnp.int32, (BANDS, WIDTH), 1) % BANDS == row

    def copy(number, slot):
        return pltpu.make_async_copy(
            held_ref.at[slot], out_ref.at[:, pl.ds(number * tile, tile), :], sems.at[slot]
        )

    def matrix(factors, n):
        parts = [
            jnp.where(same, jnp.broadcast_to(factor[n : n + 1], same.shape), 0.0) for factor in factors
        ]
        whole = jnp.concatenate(parts, axis=0)
        high = whole.astype(jnp.bfloat16)
        low = (whole - high.astype(jnp.float32)).astype(jnp.bfloat16)
        return jnp.concatenate([high, high, low], axis=0)

    def advance(number, slot):
        start = number * tile if points == tile else pl.multiple_of(number * tile, TILE)
        factors = [
            factor_ref[pl.ds(start, tile), spot * WIDTH : (spot + 1) * WIDTH] for spot in range(2 * BANDS)
        ]
        for n in range(tile):
            k = number * tile + n
            added = jnp.dot(split_ref[k], matrix(factors, n), preferred_element_type=jnp.float32)
            result = times_of(green_ref, k) + added
            if points % TILE:
                held_ref[slot, :, n, :] = result
            else:
                rows = held_ref.reshape(2 * history * tile, WIDTH)
                rows[pl.ds(slot * history * tile + n, history, stride=tile), :] = result
        copy(number, slot).start()

    tiles = points // tile
    if tiles == 1:
        advance(0, 0)
        copy(0, 0).wait()
        return

    def step(number, carry):
        slot = number % 2

        @pl.when(number > 1)
        def _():
            copy(number - 2, slot).wait()

        advance(number, slot)
        return carry

    lax.fori_loop(0, tiles, step, 0)
    for number in (tiles - 2, tiles - 1):
        copy(number, number % 2).wait()


def gather_tables():
    blocks = 2 * BANDS
    pairs = STEPS * STEPS // 2
    table = np.zeros((pairs, 2, blocks, BANDS, 2, BANDS, BANDS), np.float32)
    signs = np.zeros((pairs, blocks, BANDS), np.float32)
    for pair in range(pairs):
        for p in range(blocks):
            i, j = divmod(2 * pair + p // BANDS, STEPS)
            h, a = divmod((p + STEPS * i) % blocks, BANDS)
            g, c = divmod((p + j) % blocks, BANDS)
            table[pair, :, p, :, h ^ g, a, c] = 1 if (h, g) == (0, 1) else -1
            signs[pair, p] = 1 if h == g else -1
    return signs.reshape(pairs, WIDTH), table.reshape(-1, WIDTH).astype(ml_dtypes.bfloat16)


def spread_table():
    table = np.zeros((2, BANDS, BANDS, 2, BANDS, 2, BANDS, BANDS), np.float32)
    for h, g, a, b in np.ndindex(2, 2, BANDS, BANDS):
        table[1 if h == g else 0, a, b, g, b, h, a, :] = -1 if (h, g) == (1, 0) else 1
    return np.tile(table.reshape(WIDTH, -1), (2, 1)).astype(ml_dtypes.bfloat16)


def in_vmem():
    return pl.BlockSpec(memory_space=pltpu.VMEM)


def in_smem():
    return pl.BlockSpec(memory_space=pltpu.SMEM)


def anywhere():
    return pl.BlockSpec(memory_space=pl.ANY)


def params(megabytes):
    return pltpu.CompilerParams(vmem_limit_bytes=megabytes * 1024 * 1024)


def cost(per_element, arrays):
    size = SIDE * SIDE * TILE * WIDTH
    return pl.CostEstimate(flops=per_element * size, bytes_accessed=4 * arrays * size, transcendentals=0)


def held_blocks(count, parts):
    return [
        pltpu.VMEM((count, TILE * SIDE * SIDE // parts, WIDTH), jnp.float32),
        pltpu.SemaphoreType.DMA((count,)),
    ]


def forward(place, greens, steps, parts):
    points = SIDE * SIDE
    return pl.pallas_call(
        functools.partial(forward_kernel, steps, parts),
        out_shape=[
            jax.ShapeDtypeStruct((points, TILE, WIDTH), jnp.float32),
            jax.ShapeDtypeStruct((STEPS, TILE * points, WIDTH), jnp.float32),
        ],
        in_specs=[in_smem()] + [anywhere()] * len(steps),
        out_specs=[in_vmem()] * 2,
        scratch_shapes=[pltpu.VMEM((points, TILE, WIDTH), jnp.float32)] + held_blocks(len(steps), parts),
        compiler_params=params(8),
        cost_estimate=cost(400, 6),
        name="forward",
    )(place, *greens)


def early_lines(place, lattice, weights, screens, steps, parts, work=None):
    points = SIDE * SIDE
    inputs = (place, lattice, weights, *screens) + (() if work is None else (work,))
    return pl.pallas_call(
        functools.partial(early_kernel, steps, parts),
        out_shape=jax.ShapeDtypeStruct((points, TILE, WIDTH), jnp.float32),
        in_specs=[in_smem(), in_vmem(), in_vmem()]
        + [anywhere()] * len(steps)
        + [in_vmem()] * (work is not None),
        out_specs=in_vmem(),
        input_output_aliases={} if work is None else {len(inputs) - 1: 0},
        scratch_shapes=held_blocks(len(steps), parts),
        compiler_params=params(4),
        cost_estimate=cost(25 * len(steps), 3),
        name="early",
    )(*inputs)


def sigma_of(place, lattice, weights, screens, work, steps, parts):
    points = SIDE * SIDE
    inputs = (place, lattice, weights, *screens, work)
    work, sigma = pl.pallas_call(
        functools.partial(sigma_kernel, steps, parts),
        out_shape=[
            jax.ShapeDtypeStruct((points, TILE, WIDTH), jnp.float32),
            jax.ShapeDtypeStruct((TILE * points, WIDTH), jnp.float32),
        ],
        in_specs=[in_smem()] + [in_vmem()] * 2 + [anywhere()] * len(steps) + [in_vmem()],
        out_specs=[in_vmem()] * 2,
        input_output_aliases={len(inputs) - 1: 0},
        scratch_shapes=held_blocks(len(steps), parts) if steps else [],
        compiler_params=params(4),
        cost_estimate=cost(200, 6),
        name="sigma",
    )(*inputs)
    return sigma


def contract(owners, sigma, equal_time, greens, block, share, before=()):
    points = owners.shape[0] * block
    rows = -(-points // 16) * 16
    signs, gather = gather_tables()
    return pl.pallas_call(
        functools.partial(contract_kernel, share),
        out_shape=jax.ShapeDtypeStruct((points, WIDTH), jnp.float32),
        in_specs=[in_smem()] + [in_vmem()] * 5 + [anywhere()] * len(before),
        out_specs=in_vmem(),
        scratch_shapes=[
            pltpu.VMEM((rows, STEPS * STEPS * WIDTH), jnp.float32),
            pltpu.VMEM((rows, STEPS * STEPS * WIDTH), jnp.bfloat16),
        ],
        compiler_params=params(10),
        cost_estimate=cost(70 * owners.shape[0], 6),
        name="contract",
    )(owners, sigma, equal_time, jnp.asarray(signs), jnp.asarray(gather), greens, *before)


def pick(place, whole, steps, parts, before=()):
    rows, width = whole.shape[0] // parts, whole.shape[1]
    return pl.pallas_call(
        functools.partial(pick_kernel, steps, parts),
        out_shape=[jax.ShapeDtypeStruct((rows, width), whole.dtype)] * len(steps),
        in_specs=[in_smem(), anywhere()] + [anywhere()] * len(before),
        out_specs=[in_vmem()] * len(steps),
        scratch_shapes=[pltpu.SemaphoreType.DMA((len(steps),))],
        compiler_params=params(56),
        cost_estimate=cost(0, 2),
        name="pick",
    )(place, whole, *before)


def split_own(greens):
    history, points, width = greens.shape
    return pl.pallas_call(
        split_kernel,
        out_shape=jax.ShapeDtypeStruct((points, history, 3 * width), jnp.bfloat16),
        in_specs=[in_vmem()],
        out_specs=in_vmem(),
        compiler_params=params(4),
        cost_estimate=cost(3, 2),
        name="split_own",
    )(greens)


def propagate(greens, pieces, effective):
    history, points, width = greens.shape
    tile = points if points % TILE else TILE
    spread = spread_table()
    return pl.pallas_call(
        propagate_kernel,
        out_shape=jax.ShapeDtypeStruct(greens.shape, jnp.float32),
        in_specs=[in_vmem()] * 4,
        out_specs=anywhere(),
        scratch_shapes=[
            pltpu.VMEM((points, spread.shape[1]), jnp.float32),
            pltpu.VMEM((2, history, tile, width), jnp.float32),
            pltpu.SemaphoreType.DMA((2,)),
        ],
        compiler_params=params(6),
        cost_estimate=cost(32, 5),
        name="propagate",
    )(greens, pieces, effective, jnp.asarray(spread))


def partner_of(place, step, count):
    if count == 1:
        return 0
    if count & (count - 1) == 0:
        return place ^ step
    return (place + step) % count


def exchange(value, axis, step, count):
    pairs = [(place, partner_of(place, step, count)) for place in range(count)]
    return lax.ppermute(value, axis, pairs)


def exchange_order(count):
    along = {}
    for step in range(1, count):
        along.setdefault(step // 2, []).append(step)
    single = [along[n] for n in along if n and n & (n - 1) == 0]
    mixed = [along[n] for n in along if n & (n - 1)]
    order = [step for steps in zip(*single[::-1]) for step in steps]
    return order + along[0] + [step for steps in mixed for step in steps]


def class_weights(quad_class):
    table = jnp.array(quadrature, jnp.float32)
    match = quad_class[:, None] == jnp.arange(4, dtype=jnp.int32)[None, :]
    return jnp.sum(jnp.where(match, table[None, :], jnp.float32(0.0)), axis=1)


def per_device(parts, blocks, green_row, screened, hamilton, equal_time, quad_class, live_count):
    history, local, width = green_row.shape
    points = local * parts
    times = history // parts
    place = lax.axis_index("ka")
    seat = place.reshape(1)
    position = jnp.arange(history, dtype=jnp.int32)
    weights = jnp.where(
        position < live_count[0], time_step * class_weights(quad_class), jnp.float32(0.0)
    ) * jnp.float32(1.0 / points)
    weights = lax.dynamic_slice_in_dim(weights, place * times, times)

    if times == TILE and local % SIDE == 0:
        groups, sources = 1, parts
        order = exchange_order(parts)
        moved = []
        wholes = [x.reshape(parts * TILE * local, width) for x in (green_row, screened)]
        blocks_of_green = [
            lax.dynamic_slice_in_dim(wholes[0], partner_of(place, step, parts) * (TILE * local), TILE * local)
            for step in order
        ]
        blocks_of_screen = pick(seat, wholes[1], order, parts, blocks_of_green[:1])
        moved = []
        for whole, sent in zip(wholes, (blocks_of_green, blocks_of_screen)):
            found = {step: exchange(block, "ka", step, parts) for step, block in zip(order, sent)}
            moved.append([{0: whole, **found}])
        order = [0] + order
    else:
        groups, sources = -(-times // TILE), 1
        order = [0]
        padding = groups * TILE - times
        moved = []
        for x in (green_row, screened):
            x = lax.all_to_all(x, "ka", split_axis=0, concat_axis=0, tiled=True)
            x = x.reshape(parts, times, local, width).transpose(1, 0, 2, 3).reshape(times, points, width)
            x = jnp.pad(x, ((0, padding), (0, 0), (0, 0))).reshape(groups, TILE * points, width)
            moved.append([{0: x[group]} for group in range(groups)])
        weights = jnp.pad(weights, (0, padding))
    weights = jnp.broadcast_to(weights.reshape(groups, TILE, 1), (groups, TILE, width))

    early = order[: max(1, len(order) - LATE)]
    late = order[len(early) :]
    own_pieces = split_own(green_row)
    share = hubbard / (points * blocks)
    sigmas = []
    for group in range(groups):
        green, screen = moved[0][group], moved[1][group]
        listed = order
        lattice, greens = forward(seat, [green[step] for step in listed], listed, sources)
        listed = early[-1:] + early[:-1]
        work = early_lines(seat, lattice, weights[group], [screen[step] for step in listed], listed, sources)
        for step in late[:-1]:
            work = early_lines(seat, lattice, weights[group], [screen[step]], [step], sources, work)
        last = late[-1:]
        sigma = sigma_of(
            seat, lattice, weights[group], [screen[step] for step in last], work, last, sources
        )
        sigmas.append((sigma, greens))

    if sources == parts and parts % 2 == 0 and parts & (parts - 1) == 0:
        (sigma, greens), = sigmas

        def blocks_of(steps, before=()):
            owners = jnp.stack([partner_of(place, step, parts) for step in steps])
            return contract(owners, sigma, equal_time, greens, local, share, before)

        others = exchange(blocks_of([*range(3, parts, 2), 1]), "ka", 1, parts)
        far = blocks_of(list(range(2, parts, 2))) + others[:-local]
        pieces = [
            exchange(far[(n - 1) * local : n * local], "ka", 2 * n, parts)
            for n in range(parts // 2 - 1, 0, -1)
        ]
        pieces += [blocks_of([0], pieces[:1]), others[-local:]]
        collision = tree_sum(pieces)
    else:
        whole = jnp.zeros((1,), jnp.int32)
        partial_value = tree_sum(
            [
                contract(whole, sigma, equal_time, greens, points, share if group == 0 else 0.0)
                for group, (sigma, greens) in enumerate(sigmas)
            ]
        )
        owners = [partner_of(place, step, parts) for step in range(parts)]
        pieces = [lax.dynamic_slice_in_dim(partial_value, owner * local, local) for owner in owners]
        collision = tree_sum(
            pieces[:1] + [exchange(pieces[step], "ka", step, parts) for step in range(1, parts)]
        )
    collision = tree_sum(
        [collision] + [exchange(collision, "hist", step, blocks) for step in range(blocks - 1, 0, -1)]
    )
    return propagate(green_row, own_pieces, hamilton + collision)


def solution(mesh):
    in_specs = (
        P("hist", "ka", None),
        P("hist", "ka", None),
        P("ka", None),
        P("ka", None),
        P("hist"),
        P("hist"),
    )
    out_specs = P("hist", "ka", None)
    return jax.shard_map(
        functools.partial(per_device, mesh.shape["ka"], mesh.shape["hist"]),
        mesh=mesh,
        in_specs=in_specs,
        out_specs=out_specs,
        check_vma=False,
    )
```

```python
import functools
import math

import jax
import jax.numpy as jnp
import ml_dtypes
import numpy as np
from jax import lax
from jax.experimental import pallas as pl
from jax.experimental.pallas import tpu as pltpu
from jax.sharding import PartitionSpec as P

SIDE = 24
BANDS = 8
ENTRIES = BANDS * BANDS
WIDTH = 2 * ENTRIES
TILE = 8
STEPS = 4

time_step = 0.1
hubbard = 1.0
quadrature = (0.375, 1.1666666, 0.9583333, 1.0)

AT_ONCE = 4
LATE = 2
AHEAD = 3


def lane_sign(shape):
    lane = lax.broadcasted_iota(jnp.int32, shape, len(shape) - 1)
    return lane < ENTRIES


def swap(x):
    return pltpu.roll(x, ENTRIES, 1)


def roll_blocks(x, blocks):
    return x if blocks == 0 else pltpu.roll(x, WIDTH - BANDS * blocks, x.ndim - 1)


def tree_sum(terms):
    while len(terms) > 1:
        terms = [sum(terms[i : i + 2][1:], terms[i]) for i in range(0, len(terms), 2)]
    return terms[0]


def split(x):
    high = x.astype(jnp.bfloat16)
    return jnp.concatenate([high, (x - high.astype(jnp.float32)).astype(jnp.bfloat16)], axis=1)


def dft24(x, sign, low):
    root3 = jnp.where(low, -1.0, 1.0) * (sign * math.sqrt(3.0) / 2)
    turn = jnp.where(low, -1.0, 1.0) * float(sign)
    half = math.sqrt(0.5)
    turn_half = turn * half
    columns = [[None] * 8 for _ in range(3)]
    for n2 in range(8):
        x0, x1, x2 = (x[(8 * n1 + 3 * n2) % 24] for n1 in range(3))
        total = x1 + x2
        base = x0 - 0.5 * total
        spin = swap(x1 - x2) * root3
        columns[0][n2] = x0 + total
        columns[1][n2] = base + spin
        columns[2][n2] = base - spin
    out = [None] * 24
    for k1 in range(3):
        c = columns[k1]
        a0, a1 = c[0] + c[4], c[0] - c[4]
        a2, a3 = c[2] + c[6], c[2] - c[6]
        a4, a5 = c[1] + c[5], c[1] - c[5]
        a6, a7 = c[3] + c[7], c[3] - c[7]
        b0, b1 = a0 + a2, a0 - a2
        b2, b3 = a4 + a6, a4 - a6
        i_a3 = swap(a3) * turn
        i_b3 = swap(b3) * turn
        c0, c1 = a1 + i_a3, a1 - i_a3
        p = (a5 - a7) * half
        m = swap(a5 + a7) * turn_half
        e, f = p + m, p - m
        values = [b0 + b2, c0 + e, b1 + i_b3, c1 - f, b0 - b2, c0 - e, b1 - i_b3, c1 + f]
        for k2 in range(8):
            out[(16 * k1 + 9 * k2) % 24] = values[k2]
    return out


def load_line(ref, line):
    stride = ref.shape[0] // TILE
    return [ref[pl.ds(line * SIDE + k2, TILE, stride=stride), :] for k2 in range(SIDE)]


def fetch(place, steps, block_refs, held_ref, sems):
    copies = []
    for slot, (step, source) in enumerate(zip(steps, block_refs)):
        rows = held_ref.shape[1]
        if step == 0 and source.shape[0] != rows:
            source = source.at[pl.ds(pl.multiple_of(place * rows, TILE), rows)]
        copies.append(pltpu.make_async_copy(source, held_ref.at[slot], sems.at[slot]))
        copies[-1].start()
    return copies


def along_first(work_ref, sign, low, store):
    def columns(pair, carry):
        both = (2 * pair, 2 * pair + 1)
        rows = [[work_ref[k1 * SIDE + column] for k1 in range(SIDE)] for column in both]
        values = [dft24(row, sign, low) for row in rows]
        for column, value in zip(both, values):
            for r1 in range(SIDE):
                store(r1 * SIDE + column, value[r1])
        return carry

    lax.fori_loop(0, SIDE // 2, columns, 0)


def pick_kernel(steps, parts, place_ref, whole_ref, *refs):
    block_refs, sems = refs[-1 - len(steps) : -1], refs[-1]
    copies = []
    for n, (step, block_ref) in enumerate(zip(steps, block_refs)):
        rows = block_ref.shape[0]
        start = pl.multiple_of(partner_of(place_ref[0], step, parts) * rows, TILE)
        copies.append(pltpu.make_async_copy(whole_ref.at[pl.ds(start, rows)], block_ref, sems.at[n]))
        copies[-1].start()
    for copy in copies:
        copy.wait()


def times_of(ref, k):
    history, points, width = ref.shape
    if points % TILE:
        return ref[:, k, :]
    return ref.reshape(history * points, width)[pl.ds(k, history, stride=points), :]


def split_kernel(green_ref, split_ref):
    history, points, _ = green_ref.shape

    def write(k):
        green = times_of(green_ref, k)
        high = green.astype(jnp.bfloat16)
        low = (green - high.astype(jnp.float32)).astype(jnp.bfloat16)
        for n, part in enumerate((high, low, high)):
            split_ref[k, :, n * WIDTH : (n + 1) * WIDTH] = part

    if points % TILE:
        for k in range(points):
            write(k)
        return

    def some(n, carry):
        for k in range(4):
            write(4 * n + k)
        return carry

    lax.fori_loop(0, points // 4, some, 0)


def forward_kernel(steps, parts, place_ref, *refs):
    block_refs, (lattice_ref, greens_ref, work_ref, held_ref, sems) = refs[: len(steps)], refs[len(steps) :]
    low = lane_sign((TILE, WIDTH))
    place = place_ref[0]
    copies = fetch(place, steps, block_refs, held_ref, sems)
    rows = held_ref.shape[1]
    lines = rows // (TILE * SIDE)
    for slot, step in enumerate(steps):
        copies[slot].wait()
        green_ref = held_ref.at[slot]
        owner = partner_of(place, step, parts)

        def along_second(i, carry):
            for r2, value in enumerate(dft24(load_line(green_ref, i), -1, low)):
                work_ref[(owner * lines + i) * SIDE + r2] = value
            return carry

        lax.fori_loop(0, lines, along_second, 0, unroll=lines <= 4)
        green = green_ref[...]
        spot = pl.ds(pl.multiple_of(owner * rows, TILE), rows)
        for j in range(STEPS):
            greens_ref[j, spot, :] = roll_blocks(green, j)

    def store(point, value):
        lattice_ref[point] = value

    along_first(work_ref, -1, low, store)


def product_lines(steps, parts, place, lattice_ref, weights, screen_refs, held_ref, sems, work_ref):
    low = lane_sign((TILE, WIDTH))
    turn = jnp.where(low, -1.0, 1.0)
    copies = fetch(place, steps, screen_refs, held_ref, sems)
    lines = held_ref.shape[1] // (TILE * SIDE)
    for slot, step in enumerate(steps):
        copies[slot].wait()
        screen_ref = held_ref.at[slot]
        first = partner_of(place, step, parts) * lines

        def along_second(i, carry):
            rows = []
            for r2, value in enumerate(load_line(screen_ref, i)):
                screen = value * weights
                other = swap(screen)
                lattice = lattice_ref[(first + i) * SIDE + r2]
                rows.append(
                    swap(lattice) * turn * jnp.where(low, screen, other)
                    - lattice * jnp.where(low, other, screen)
                )
            for k2, value in enumerate(dft24(rows, 1, low)):
                work_ref[(first + i) * SIDE + k2] = value
            return carry

        lax.fori_loop(0, lines, along_second, 0, unroll=lines <= 4)


def early_kernel(steps, parts, place_ref, lattice_ref, weight_ref, *refs):
    screen_refs, (*_, work_ref, held_ref, sems) = refs[: len(steps)], refs[len(steps) :]
    product_lines(
        steps, parts, place_ref[0], lattice_ref, weight_ref[...], screen_refs, held_ref, sems, work_ref
    )


def sigma_kernel(steps, parts, place_ref, lattice_ref, weight_ref, *refs):
    screen_refs, refs = refs[: len(steps)], refs[len(steps) :]
    _, work_ref, sigma_ref, *late = refs
    low = lane_sign((TILE, WIDTH))
    if steps:
        held_ref, sems = late
        product_lines(
            steps, parts, place_ref[0], lattice_ref, weight_ref[...], screen_refs, held_ref, sems, work_ref
        )

    def store(point, value):
        sigma_ref[pl.ds(point * TILE, TILE), :] = value

    along_first(work_ref, 1, low, store)


def contract_kernel(share, owner_ref, sigma_ref, equal_ref, sign_ref, gather_ref, greens_ref, *refs):
    partial_ref, sums_ref, pieces_ref = refs[-3:]
    low = lane_sign((TILE, WIDTH))
    points = partial_ref.shape[0]
    block = points // owner_ref.shape[0]
    tiles = block // TILE
    batch = max(n for n in range(1, 10) if tiles % n == 0)

    def contract(group, carry):
        slot, first = group // (tiles // batch), group % (tiles // batch) * batch
        owner = owner_ref[slot]
        units = [(tile, s) for tile in range(batch) for s in range(TILE)]

        def prepare(tile, s):
            point = owner * block + (first + tile) * TILE
            sigma = sigma_ref[pl.ds(point * TILE + s, TILE, stride=TILE), :]
            row = pl.multiple_of((owner * TILE + s) * block + (first + tile) * TILE, TILE)
            return (
                [roll_blocks(sigma, STEPS * i) for i in range(STEPS)],
                [greens_ref[j, pl.ds(row, TILE), :] for j in range(STEPS)],
            )

        ready = [prepare(*unit) for unit in units[:AHEAD]]
        for n, (tile, s) in enumerate(units):
            if n + AHEAD < len(units):
                ready.append(prepare(*units[n + AHEAD]))
            sigmas, greens = ready.pop(0)
            terms = [sigma * green for sigma in sigmas for green in greens]
            sums = terms if s == 0 else [a + b for a, b in zip(sums, terms)]
            if s == TILE - 1:
                row = pl.ds(pl.multiple_of(slot * block + (first + tile) * TILE, TILE), TILE)
                for spot, value in enumerate(sums):
                    sums_ref[row, spot * WIDTH : (spot + 1) * WIDTH] = value
        return carry

    lax.fori_loop(0, points // (TILE * batch), contract, 0)

    lane = lax.broadcasted_iota(jnp.int32, equal_ref.shape, 1)
    inner = lane - ENTRIES
    occupied = jnp.sum(jnp.where((inner >= 0) & (inner % (BANDS + 1) == 0), equal_ref[...], 0.0))
    spots = lax.broadcasted_iota(jnp.int32, (points, WIDTH), 1)
    on_diagonal = (spots < ENTRIES) & (spots % (BANDS + 1) == 0)
    lower = lax.broadcasted_iota(jnp.int32, (sums_ref.shape[0], WIDTH), 1) < ENTRIES
    for pair in range(STEPS * STEPS // 2):
        first_part = sums_ref[:, 2 * pair * WIDTH : (2 * pair + 1) * WIDTH]
        second_part = sums_ref[:, (2 * pair + 1) * WIDTH : (2 * pair + 2) * WIDTH]
        folded = jnp.where(lower, first_part, second_part) + sign_ref[pair : pair + 1, :] * swap(
            jnp.where(lower, second_part, first_part)
        )
        pieces_ref[:, 2 * pair * WIDTH : (2 * pair + 2) * WIDTH] = split(folded)
    total = jnp.dot(pieces_ref[...], gather_ref[...], preferred_element_type=jnp.float32)
    partial_ref[...] = total[:points] + jnp.where(on_diagonal, occupied * share, 0.0)


def propagate_kernel(green_ref, split_ref, effective_ref, spread_ref, out_ref, factor_ref, held_ref, sems):
    history, points, _ = green_ref.shape
    factor_ref[...] = jnp.dot(
        split(effective_ref[...] * time_step), spread_ref[...], preferred_element_type=jnp.float32
    )
    tile = held_ref.shape[2]
    row = lax.broadcasted_iota(jnp.int32, (BANDS, WIDTH), 0)
    same = lax.broadcasted_iota(jnp.int32, (BANDS, WIDTH), 1) % BANDS == row

    def copy(number, slot):
        return pltpu.make_async_copy(
            held_ref.at[slot], out_ref.at[:, pl.ds(number * tile, tile), :], sems.at[slot]
        )

    def matrix(factors, n):
        parts = [
            jnp.where(same, jnp.broadcast_to(factor[n : n + 1], same.shape), 0.0) for factor in factors
        ]
        whole = jnp.concatenate(parts, axis=0)
        high = whole.astype(jnp.bfloat16)
        low = (whole - high.astype(jnp.float32)).astype(jnp.bfloat16)
        return jnp.concatenate([high, high, low], axis=0)

    def advance(number, slot):
        start = number * tile if points == tile else pl.multiple_of(number * tile, TILE)
        factors = [
            factor_ref[pl.ds(start, tile), spot * WIDTH : (spot + 1) * WIDTH] for spot in range(2 * BANDS)
        ]
        for first in range(0, tile, AT_ONCE):
            batch = range(first, min(first + AT_ONCE, tile))
            results = []
            for n in batch:
                k = number * tile + n
                added = jnp.dot(split_ref[k], matrix(factors, n), preferred_element_type=jnp.float32)
                results.append(times_of(green_ref, k) + added)
            for n, result in zip(batch, results):
                if points % TILE:
                    held_ref[slot, :, n, :] = result
                else:
                    rows = held_ref.reshape(2 * history * tile, WIDTH)
                    rows[pl.ds(slot * history * tile + n, history, stride=tile), :] = result
        copy(number, slot).start()

    tiles = points // tile
    if tiles == 1:
        advance(0, 0)
        copy(0, 0).wait()
        return

    def step(number, carry):
        slot = number % 2

        @pl.when(number > 1)
        def _():
            copy(number - 2, slot).wait()

        advance(number, slot)
        return carry

    lax.fori_loop(0, tiles, step, 0)
    for number in (tiles - 2, tiles - 1):
        copy(number, number % 2).wait()


def gather_tables():
    blocks = 2 * BANDS
    pairs = STEPS * STEPS // 2
    table = np.zeros((pairs, 2, blocks, BANDS, 2, BANDS, BANDS), np.float32)
    signs = np.zeros((pairs, blocks, BANDS), np.float32)
    for pair in range(pairs):
        for p in range(blocks):
            i, j = divmod(2 * pair + p // BANDS, STEPS)
            h, a = divmod((p + STEPS * i) % blocks, BANDS)
            g, c = divmod((p + j) % blocks, BANDS)
            table[pair, :, p, :, h ^ g, a, c] = 1 if (h, g) == (0, 1) else -1
            signs[pair, p] = 1 if h == g else -1
    return signs.reshape(pairs, WIDTH), table.reshape(-1, WIDTH).astype(ml_dtypes.bfloat16)


def spread_table():
    table = np.zeros((2, BANDS, BANDS, 2, BANDS, 2, BANDS, BANDS), np.float32)
    for h, g, a, b in np.ndindex(2, 2, BANDS, BANDS):
        table[1 if h == g else 0, a, b, g, b, h, a, :] = -1 if (h, g) == (1, 0) else 1
    return np.tile(table.reshape(WIDTH, -1), (2, 1)).astype(ml_dtypes.bfloat16)


def in_vmem():
    return pl.BlockSpec(memory_space=pltpu.VMEM)


def in_smem():
    return pl.BlockSpec(memory_space=pltpu.SMEM)


def anywhere():
    return pl.BlockSpec(memory_space=pl.ANY)


def params(megabytes):
    return pltpu.CompilerParams(vmem_limit_bytes=megabytes * 1024 * 1024)


def cost(per_element, arrays):
    size = SIDE * SIDE * TILE * WIDTH
    return pl.CostEstimate(flops=per_element * size, bytes_accessed=4 * arrays * size, transcendentals=0)


def held_blocks(count, parts):
    return [
        pltpu.VMEM((count, TILE * SIDE * SIDE // parts, WIDTH), jnp.float32),
        pltpu.SemaphoreType.DMA((count,)),
    ]


def forward(place, greens, steps, parts):
    points = SIDE * SIDE
    return pl.pallas_call(
        functools.partial(forward_kernel, steps, parts),
        out_shape=[
            jax.ShapeDtypeStruct((points, TILE, WIDTH), jnp.float32),
            jax.ShapeDtypeStruct((STEPS, TILE * points, WIDTH), jnp.float32),
        ],
        in_specs=[in_smem()] + [anywhere()] * len(steps),
        out_specs=[in_vmem()] * 2,
        scratch_shapes=[pltpu.VMEM((points, TILE, WIDTH), jnp.float32)] + held_blocks(len(steps), parts),
        compiler_params=params(8),
        cost_estimate=cost(400, 6),
        name="forward",
    )(place, *greens)


def early_lines(place, lattice, weights, screens, steps, parts, work=None):
    points = SIDE * SIDE
    inputs = (place, lattice, weights, *screens) + (() if work is None else (work,))
    return pl.pallas_call(
        functools.partial(early_kernel, steps, parts),
        out_shape=jax.ShapeDtypeStruct((points, TILE, WIDTH), jnp.float32),
        in_specs=[in_smem(), in_vmem(), in_vmem()]
        + [anywhere()] * len(steps)
        + [in_vmem()] * (work is not None),
        out_specs=in_vmem(),
        input_output_aliases={} if work is None else {len(inputs) - 1: 0},
        scratch_shapes=held_blocks(len(steps), parts),
        compiler_params=params(4),
        cost_estimate=cost(25 * len(steps), 3),
        name="early",
    )(*inputs)


def sigma_of(place, lattice, weights, screens, work, steps, parts):
    points = SIDE * SIDE
    inputs = (place, lattice, weights, *screens, work)
    work, sigma = pl.pallas_call(
        functools.partial(sigma_kernel, steps, parts),
        out_shape=[
            jax.ShapeDtypeStruct((points, TILE, WIDTH), jnp.float32),
            jax.ShapeDtypeStruct((TILE * points, WIDTH), jnp.float32),
        ],
        in_specs=[in_smem()] + [in_vmem()] * 2 + [anywhere()] * len(steps) + [in_vmem()],
        out_specs=[in_vmem()] * 2,
        input_output_aliases={len(inputs) - 1: 0},
        scratch_shapes=held_blocks(len(steps), parts) if steps else [],
        compiler_params=params(4),
        cost_estimate=cost(200, 6),
        name="sigma",
    )(*inputs)
    return sigma


def contract(owners, sigma, equal_time, greens, block, share, before=()):
    points = owners.shape[0] * block
    rows = -(-points // 16) * 16
    signs, gather = gather_tables()
    return pl.pallas_call(
        functools.partial(contract_kernel, share),
        out_shape=jax.ShapeDtypeStruct((points, WIDTH), jnp.float32),
        in_specs=[in_smem()] + [in_vmem()] * 5 + [anywhere()] * len(before),
        out_specs=in_vmem(),
        scratch_shapes=[
            pltpu.VMEM((rows, STEPS * STEPS * WIDTH), jnp.float32),
            pltpu.VMEM((rows, STEPS * STEPS * WIDTH), jnp.bfloat16),
        ],
        compiler_params=params(10),
        cost_estimate=cost(70 * owners.shape[0], 6),
        name="contract",
    )(owners, sigma, equal_time, jnp.asarray(signs), jnp.asarray(gather), greens, *before)


def pick(place, whole, steps, parts, before=()):
    rows, width = whole.shape[0] // parts, whole.shape[1]
    return pl.pallas_call(
        functools.partial(pick_kernel, steps, parts),
        out_shape=[jax.ShapeDtypeStruct((rows, width), whole.dtype)] * len(steps),
        in_specs=[in_smem(), anywhere()] + [anywhere()] * len(before),
        out_specs=[in_vmem()] * len(steps),
        scratch_shapes=[pltpu.SemaphoreType.DMA((len(steps),))],
        compiler_params=params(56),
        cost_estimate=cost(0, 2),
        name="pick",
    )(place, whole, *before)


def split_own(greens):
    history, points, width = greens.shape
    return pl.pallas_call(
        split_kernel,
        out_shape=jax.ShapeDtypeStruct((points, history, 3 * width), jnp.bfloat16),
        in_specs=[in_vmem()],
        out_specs=in_vmem(),
        compiler_params=params(4),
        cost_estimate=cost(3, 2),
        name="split_own",
    )(greens)


def propagate(greens, pieces, effective):
    history, points, width = greens.shape
    tile = points if points % TILE else TILE
    spread = spread_table()
    return pl.pallas_call(
        propagate_kernel,
        out_shape=jax.ShapeDtypeStruct(greens.shape, jnp.float32),
        in_specs=[in_vmem()] * 4,
        out_specs=anywhere(),
        scratch_shapes=[
            pltpu.VMEM((points, spread.shape[1]), jnp.float32),
            pltpu.VMEM((2, history, tile, width), jnp.float32),
            pltpu.SemaphoreType.DMA((2,)),
        ],
        compiler_params=params(6),
        cost_estimate=cost(32, 5),
        name="propagate",
    )(greens, pieces, effective, jnp.asarray(spread))


def partner_of(place, step, count):
    if count == 1:
        return 0
    if count & (count - 1) == 0:
        return place ^ step
    return (place + step) % count


def exchange(value, axis, step, count):
    pairs = [(place, partner_of(place, step, count)) for place in range(count)]
    return lax.ppermute(value, axis, pairs)


def exchange_order(count):
    along = {}
    for step in range(1, count):
        along.setdefault(step // 2, []).append(step)
    single = [along[n] for n in along if n and n & (n - 1) == 0]
    mixed = [along[n] for n in along if n & (n - 1)]
    order = [step for steps in zip(*single[::-1]) for step in steps]
    return order + along[0] + [step for steps in mixed for step in steps]


def class_weights(quad_class):
    table = jnp.array(quadrature, jnp.float32)
    match = quad_class[:, None] == jnp.arange(4, dtype=jnp.int32)[None, :]
    return jnp.sum(jnp.where(match, table[None, :], jnp.float32(0.0)), axis=1)


def per_device(parts, blocks, green_row, screened, hamilton, equal_time, quad_class, live_count):
    history, local, width = green_row.shape
    points = local * parts
    times = history // parts
    place = lax.axis_index("ka")
    seat = place.reshape(1)
    position = jnp.arange(history, dtype=jnp.int32)
    weights = jnp.where(
        position < live_count[0], time_step * class_weights(quad_class), jnp.float32(0.0)
    ) * jnp.float32(1.0 / points)
    weights = lax.dynamic_slice_in_dim(weights, place * times, times)

    if times == TILE and local % SIDE == 0:
        groups, sources = 1, parts
        order = exchange_order(parts)
        moved = []
        wholes = [x.reshape(parts * TILE * local, width) for x in (green_row, screened)]
        blocks_of_green = [
            lax.dynamic_slice_in_dim(wholes[0], partner_of(place, step, parts) * (TILE * local), TILE * local)
            for step in order
        ]
        blocks_of_screen = pick(seat, wholes[1], order, parts, blocks_of_green[:1])
        moved = []
        for whole, sent in zip(wholes, (blocks_of_green, blocks_of_screen)):
            found = {step: exchange(block, "ka", step, parts) for step, block in zip(order, sent)}
            moved.append([{0: whole, **found}])
        order = [0] + order
    else:
        groups, sources = -(-times // TILE), 1
        order = [0]
        padding = groups * TILE - times
        moved = []
        for x in (green_row, screened):
            x = lax.all_to_all(x, "ka", split_axis=0, concat_axis=0, tiled=True)
            x = x.reshape(parts, times, local, width).transpose(1, 0, 2, 3).reshape(times, points, width)
            x = jnp.pad(x, ((0, padding), (0, 0), (0, 0))).reshape(groups, TILE * points, width)
            moved.append([{0: x[group]} for group in range(groups)])
        weights = jnp.pad(weights, (0, padding))
    weights = jnp.broadcast_to(weights.reshape(groups, TILE, 1), (groups, TILE, width))

    early = order[: max(1, len(order) - LATE)]
    late = order[len(early) :]
    own_pieces = split_own(green_row)
    share = hubbard / (points * blocks)
    sigmas = []
    for group in range(groups):
        green, screen = moved[0][group], moved[1][group]
        listed = order
        lattice, greens = forward(seat, [green[step] for step in listed], listed, sources)
        listed = early[-1:] + early[:-1]
        work = early_lines(seat, lattice, weights[group], [screen[step] for step in listed], listed, sources)
        for step in late[:-1]:
            work = early_lines(seat, lattice, weights[group], [screen[step]], [step], sources, work)
        last = late[-1:]
        sigma = sigma_of(
            seat, lattice, weights[group], [screen[step] for step in last], work, last, sources
        )
        sigmas.append((sigma, greens))

    if sources == parts and parts % 2 == 0 and parts & (parts - 1) == 0:
        (sigma, greens), = sigmas

        def blocks_of(steps, before=()):
            owners = jnp.stack([partner_of(place, step, parts) for step in steps])
            return contract(owners, sigma, equal_time, greens, local, share, before)

        others = exchange(blocks_of([*range(3, parts, 2), 1]), "ka", 1, parts)
        far = blocks_of(list(range(2, parts, 2))) + others[:-local]
        pieces = [
            exchange(far[(n - 1) * local : n * local], "ka", 2 * n, parts)
            for n in range(parts // 2 - 1, 0, -1)
        ]
        pieces += [blocks_of([0], pieces[:1]), others[-local:]]
        collision = tree_sum(pieces)
    else:
        whole = jnp.zeros((1,), jnp.int32)
        partial_value = tree_sum(
            [
                contract(whole, sigma, equal_time, greens, points, share if group == 0 else 0.0)
                for group, (sigma, greens) in enumerate(sigmas)
            ]
        )
        owners = [partner_of(place, step, parts) for step in range(parts)]
        pieces = [lax.dynamic_slice_in_dim(partial_value, owner * local, local) for owner in owners]
        collision = tree_sum(
            pieces[:1] + [exchange(pieces[step], "ka", step, parts) for step in range(1, parts)]
        )
    collision = tree_sum(
        [collision] + [exchange(collision, "hist", step, blocks) for step in range(blocks - 1, 0, -1)]
    )
    return propagate(green_row, own_pieces, hamilton + collision)


def solution(mesh):
    in_specs = (
        P("hist", "ka", None),
        P("hist", "ka", None),
        P("ka", None),
        P("ka", None),
        P("hist"),
        P("hist"),
    )
    out_specs = P("hist", "ka", None)
    return jax.shard_map(
        functools.partial(per_device, mesh.shape["ka"], mesh.shape["hist"]),
        mesh=mesh,
        in_specs=in_specs,
        out_specs=out_specs,
        check_vma=False,
    )
```

```python
import functools
import math

import jax
import jax.numpy as jnp
import ml_dtypes
import numpy as np
from jax import lax
from jax.experimental import pallas as pl
from jax.experimental.pallas import tpu as pltpu
from jax.sharding import PartitionSpec as P

SIDE = 24
BANDS = 8
ENTRIES = BANDS * BANDS
WIDTH = 2 * ENTRIES
TILE = 8
STEPS = 4

time_step = 0.1
hubbard = 1.0
quadrature = (0.375, 1.1666666, 0.9583333, 1.0)

AT_ONCE = 4
COLUMNS = 3
LATE = 2
AHEAD = 3


def lane_sign(shape):
    lane = lax.broadcasted_iota(jnp.int32, shape, len(shape) - 1)
    return lane < ENTRIES


def swap(x):
    return pltpu.roll(x, ENTRIES, 1)


def roll_blocks(x, blocks):
    return x if blocks == 0 else pltpu.roll(x, WIDTH - BANDS * blocks, x.ndim - 1)


def tree_sum(terms):
    while len(terms) > 1:
        terms = [sum(terms[i : i + 2][1:], terms[i]) for i in range(0, len(terms), 2)]
    return terms[0]


def split(x):
    high = x.astype(jnp.bfloat16)
    return jnp.concatenate([high, (x - high.astype(jnp.float32)).astype(jnp.bfloat16)], axis=1)


def dft24(x, sign, low):
    root3 = jnp.where(low, -1.0, 1.0) * (sign * math.sqrt(3.0) / 2)
    turn = jnp.where(low, -1.0, 1.0) * float(sign)
    half = math.sqrt(0.5)
    turn_half = turn * half
    columns = [[None] * 8 for _ in range(3)]
    for n2 in range(8):
        x0, x1, x2 = (x[(8 * n1 + 3 * n2) % 24] for n1 in range(3))
        total = x1 + x2
        base = x0 - 0.5 * total
        spin = swap(x1 - x2) * root3
        columns[0][n2] = x0 + total
        columns[1][n2] = base + spin
        columns[2][n2] = base - spin
    out = [None] * 24
    for k1 in range(3):
        c = columns[k1]
        a0, a1 = c[0] + c[4], c[0] - c[4]
        a2, a3 = c[2] + c[6], c[2] - c[6]
        a4, a5 = c[1] + c[5], c[1] - c[5]
        a6, a7 = c[3] + c[7], c[3] - c[7]
        b0, b1 = a0 + a2, a0 - a2
        b2, b3 = a4 + a6, a4 - a6
        i_a3 = swap(a3) * turn
        i_b3 = swap(b3) * turn
        c0, c1 = a1 + i_a3, a1 - i_a3
        p = (a5 - a7) * half
        m = swap(a5 + a7) * turn_half
        e, f = p + m, p - m
        values = [b0 + b2, c0 + e, b1 + i_b3, c1 - f, b0 - b2, c0 - e, b1 - i_b3, c1 + f]
        for k2 in range(8):
            out[(16 * k1 + 9 * k2) % 24] = values[k2]
    return out


def load_line(ref, line):
    stride = ref.shape[0] // TILE
    return [ref[pl.ds(line * SIDE + k2, TILE, stride=stride), :] for k2 in range(SIDE)]


def fetch(place, steps, block_refs, held_ref, sems):
    copies = []
    for slot, (step, source) in enumerate(zip(steps, block_refs)):
        rows = held_ref.shape[1]
        if step == 0 and source.shape[0] != rows:
            source = source.at[pl.ds(pl.multiple_of(place * rows, TILE), rows)]
        copies.append(pltpu.make_async_copy(source, held_ref.at[slot], sems.at[slot]))
        copies[-1].start()
    return copies


def along_first(work_ref, sign, low, store):
    def columns(group, carry):
        some = [COLUMNS * group + n for n in range(COLUMNS)]
        rows = [[work_ref[k1 * SIDE + column] for k1 in range(SIDE)] for column in some]
        values = [dft24(row, sign, low) for row in rows]
        for column, value in zip(some, values):
            for r1 in range(SIDE):
                store(r1 * SIDE + column, value[r1])
        return carry

    lax.fori_loop(0, SIDE // COLUMNS, columns, 0)


def pick_kernel(steps, parts, place_ref, whole_ref, *refs):
    block_refs, sems = refs[-1 - len(steps) : -1], refs[-1]
    copies = []
    for n, (step, block_ref) in enumerate(zip(steps, block_refs)):
        rows = block_ref.shape[0]
        start = pl.multiple_of(partner_of(place_ref[0], step, parts) * rows, TILE)
        copies.append(pltpu.make_async_copy(whole_ref.at[pl.ds(start, rows)], block_ref, sems.at[n]))
        copies[-1].start()
    for copy in copies:
        copy.wait()


def times_of(ref, k):
    history, points, width = ref.shape
    if points % TILE:
        return ref[:, k, :]
    return ref.reshape(history * points, width)[pl.ds(k, history, stride=points), :]


def split_kernel(green_ref, split_ref):
    history, points, _ = green_ref.shape

    def write(k):
        green = times_of(green_ref, k)
        high = green.astype(jnp.bfloat16)
        low = (green - high.astype(jnp.float32)).astype(jnp.bfloat16)
        for n, part in enumerate((high, low, high)):
            split_ref[k, :, n * WIDTH : (n + 1) * WIDTH] = part

    if points % TILE:
        for k in range(points):
            write(k)
        return

    def some(n, carry):
        for k in range(4):
            write(4 * n + k)
        return carry

    lax.fori_loop(0, points // 4, some, 0)


def forward_kernel(steps, parts, place_ref, *refs):
    block_refs, (lattice_ref, greens_ref, work_ref, held_ref, sems) = refs[: len(steps)], refs[len(steps) :]
    low = lane_sign((TILE, WIDTH))
    place = place_ref[0]
    copies = fetch(place, steps, block_refs, held_ref, sems)
    rows = held_ref.shape[1]
    lines = rows // (TILE * SIDE)
    for slot, step in enumerate(steps):
        copies[slot].wait()
        green_ref = held_ref.at[slot]
        owner = partner_of(place, step, parts)

        def along_second(i, carry):
            for r2, value in enumerate(dft24(load_line(green_ref, i), -1, low)):
                work_ref[(owner * lines + i) * SIDE + r2] = value
            return carry

        lax.fori_loop(0, lines, along_second, 0, unroll=lines <= 4)
        green = green_ref[...]
        spot = pl.ds(pl.multiple_of(owner * rows, TILE), rows)
        for j in range(STEPS):
            greens_ref[j, spot, :] = roll_blocks(green, j)

    def store(point, value):
        lattice_ref[point] = value

    along_first(work_ref, -1, low, store)


def product_lines(steps, parts, place, lattice_ref, weights, screen_refs, held_ref, sems, work_ref):
    low = lane_sign((TILE, WIDTH))
    turn = jnp.where(low, -1.0, 1.0)
    copies = fetch(place, steps, screen_refs, held_ref, sems)
    lines = held_ref.shape[1] // (TILE * SIDE)
    for slot, step in enumerate(steps):
        copies[slot].wait()
        screen_ref = held_ref.at[slot]
        first = partner_of(place, step, parts) * lines

        def along_second(i, carry):
            rows = []
            for r2, value in enumerate(load_line(screen_ref, i)):
                screen = value * weights
                other = swap(screen)
                lattice = lattice_ref[(first + i) * SIDE + r2]
                rows.append(
                    swap(lattice) * turn * jnp.where(low, screen, other)
                    - lattice * jnp.where(low, other, screen)
                )
            for k2, value in enumerate(dft24(rows, 1, low)):
                work_ref[(first + i) * SIDE + k2] = value
            return carry

        lax.fori_loop(0, lines, along_second, 0, unroll=lines <= 4)


def early_kernel(steps, parts, place_ref, lattice_ref, weight_ref, *refs):
    screen_refs, (*_, work_ref, held_ref, sems) = refs[: len(steps)], refs[len(steps) :]
    product_lines(
        steps, parts, place_ref[0], lattice_ref, weight_ref[...], screen_refs, held_ref, sems, work_ref
    )


def sigma_kernel(steps, parts, place_ref, lattice_ref, weight_ref, *refs):
    screen_refs, refs = refs[: len(steps)], refs[len(steps) :]
    _, work_ref, sigma_ref, *late = refs
    low = lane_sign((TILE, WIDTH))
    if steps:
        held_ref, sems = late
        product_lines(
            steps, parts, place_ref[0], lattice_ref, weight_ref[...], screen_refs, held_ref, sems, work_ref
        )

    def store(point, value):
        sigma_ref[pl.ds(point * TILE, TILE), :] = value

    along_first(work_ref, 1, low, store)


def contract_kernel(share, owner_ref, sigma_ref, equal_ref, sign_ref, gather_ref, greens_ref, *refs):
    partial_ref, sums_ref, pieces_ref = refs[-3:]
    low = lane_sign((TILE, WIDTH))
    points = partial_ref.shape[0]
    block = points // owner_ref.shape[0]
    tiles = block // TILE
    batch = max(n for n in range(1, 10) if tiles % n == 0)

    def contract(group, carry):
        slot, first = group // (tiles // batch), group % (tiles // batch) * batch
        owner = owner_ref[slot]
        units = [(tile, s) for tile in range(batch) for s in range(TILE)]

        def prepare(tile, s):
            point = owner * block + (first + tile) * TILE
            sigma = sigma_ref[pl.ds(point * TILE + s, TILE, stride=TILE), :]
            row = pl.multiple_of((owner * TILE + s) * block + (first + tile) * TILE, TILE)
            return (
                [roll_blocks(sigma, STEPS * i) for i in range(STEPS)],
                [greens_ref[j, pl.ds(row, TILE), :] for j in range(STEPS)],
            )

        ready = [prepare(*unit) for unit in units[:AHEAD]]
        for n, (tile, s) in enumerate(units):
            if n + AHEAD < len(units):
                ready.append(prepare(*units[n + AHEAD]))
            sigmas, greens = ready.pop(0)
            terms = [sigma * green for sigma in sigmas for green in greens]
            sums = terms if s == 0 else [a + b for a, b in zip(sums, terms)]
            if s == TILE - 1:
                row = pl.ds(pl.multiple_of(slot * block + (first + tile) * TILE, TILE), TILE)
                for spot, value in enumerate(sums):
                    sums_ref[row, spot * WIDTH : (spot + 1) * WIDTH] = value
        return carry

    lax.fori_loop(0, points // (TILE * batch), contract, 0)

    lane = lax.broadcasted_iota(jnp.int32, equal_ref.shape, 1)
    inner = lane - ENTRIES
    occupied = jnp.sum(jnp.where((inner >= 0) & (inner % (BANDS + 1) == 0), equal_ref[...], 0.0))
    spots = lax.broadcasted_iota(jnp.int32, (points, WIDTH), 1)
    on_diagonal = (spots < ENTRIES) & (spots % (BANDS + 1) == 0)
    lower = lax.broadcasted_iota(jnp.int32, (sums_ref.shape[0], WIDTH), 1) < ENTRIES
    for pair in range(STEPS * STEPS // 2):
        first_part = sums_ref[:, 2 * pair * WIDTH : (2 * pair + 1) * WIDTH]
        second_part = sums_ref[:, (2 * pair + 1) * WIDTH : (2 * pair + 2) * WIDTH]
        folded = jnp.where(lower, first_part, second_part) + sign_ref[pair : pair + 1, :] * swap(
            jnp.where(lower, second_part, first_part)
        )
        pieces_ref[:, 2 * pair * WIDTH : (2 * pair + 2) * WIDTH] = split(folded)
    total = jnp.dot(pieces_ref[...], gather_ref[...], preferred_element_type=jnp.float32)
    partial_ref[...] = total[:points] + jnp.where(on_diagonal, occupied * share, 0.0)


def propagate_kernel(green_ref, split_ref, effective_ref, spread_ref, out_ref, factor_ref, held_ref, sems):
    history, points, _ = green_ref.shape
    factor_ref[...] = jnp.dot(
        split(effective_ref[...] * time_step), spread_ref[...], preferred_element_type=jnp.float32
    )
    tile = held_ref.shape[2]
    row = lax.broadcasted_iota(jnp.int32, (BANDS, WIDTH), 0)
    same = lax.broadcasted_iota(jnp.int32, (BANDS, WIDTH), 1) % BANDS == row

    def copy(number, slot):
        return pltpu.make_async_copy(
            held_ref.at[slot], out_ref.at[:, pl.ds(number * tile, tile), :], sems.at[slot]
        )

    def matrix(factors, n):
        parts = [
            jnp.where(same, jnp.broadcast_to(factor[n : n + 1], same.shape), 0.0) for factor in factors
        ]
        whole = jnp.concatenate(parts, axis=0)
        high = whole.astype(jnp.bfloat16)
        low = (whole - high.astype(jnp.float32)).astype(jnp.bfloat16)
        return jnp.concatenate([high, high, low], axis=0)

    def advance(number, slot):
        start = number * tile if points == tile else pl.multiple_of(number * tile, TILE)
        factors = [
            factor_ref[pl.ds(start, tile), spot * WIDTH : (spot + 1) * WIDTH] for spot in range(2 * BANDS)
        ]
        for first in range(0, tile, AT_ONCE):
            batch = range(first, min(first + AT_ONCE, tile))
            results = []
            for n in batch:
                k = number * tile + n
                added = jnp.dot(split_ref[k], matrix(factors, n), preferred_element_type=jnp.float32)
                results.append(times_of(green_ref, k) + added)
            for n, result in zip(batch, results):
                if points % TILE:
                    held_ref[slot, :, n, :] = result
                else:
                    rows = held_ref.reshape(2 * history * tile, WIDTH)
                    rows[pl.ds(slot * history * tile + n, history, stride=tile), :] = result
        copy(number, slot).start()

    tiles = points // tile
    if tiles == 1:
        advance(0, 0)
        copy(0, 0).wait()
        return

    def step(number, carry):
        slot = number % 2

        @pl.when(number > 1)
        def _():
            copy(number - 2, slot).wait()

        advance(number, slot)
        return carry

    lax.fori_loop(0, tiles, step, 0)
    for number in (tiles - 2, tiles - 1):
        copy(number, number % 2).wait()


def gather_tables():
    blocks = 2 * BANDS
    pairs = STEPS * STEPS // 2
    table = np.zeros((pairs, 2, blocks, BANDS, 2, BANDS, BANDS), np.float32)
    signs = np.zeros((pairs, blocks, BANDS), np.float32)
    for pair in range(pairs):
        for p in range(blocks):
            i, j = divmod(2 * pair + p // BANDS, STEPS)
            h, a = divmod((p + STEPS * i) % blocks, BANDS)
            g, c = divmod((p + j) % blocks, BANDS)
            table[pair, :, p, :, h ^ g, a, c] = 1 if (h, g) == (0, 1) else -1
            signs[pair, p] = 1 if h == g else -1
    return signs.reshape(pairs, WIDTH), table.reshape(-1, WIDTH).astype(ml_dtypes.bfloat16)


def spread_table():
    table = np.zeros((2, BANDS, BANDS, 2, BANDS, 2, BANDS, BANDS), np.float32)
    for h, g, a, b in np.ndindex(2, 2, BANDS, BANDS):
        table[1 if h == g else 0, a, b, g, b, h, a, :] = -1 if (h, g) == (1, 0) else 1
    return np.tile(table.reshape(WIDTH, -1), (2, 1)).astype(ml_dtypes.bfloat16)


def in_vmem():
    return pl.BlockSpec(memory_space=pltpu.VMEM)


def in_smem():
    return pl.BlockSpec(memory_space=pltpu.SMEM)


def anywhere():
    return pl.BlockSpec(memory_space=pl.ANY)


def params(megabytes):
    return pltpu.CompilerParams(vmem_limit_bytes=megabytes * 1024 * 1024)


def cost(per_element, arrays):
    size = SIDE * SIDE * TILE * WIDTH
    return pl.CostEstimate(flops=per_element * size, bytes_accessed=4 * arrays * size, transcendentals=0)


def held_blocks(count, parts):
    return [
        pltpu.VMEM((count, TILE * SIDE * SIDE // parts, WIDTH), jnp.float32),
        pltpu.SemaphoreType.DMA((count,)),
    ]


def forward(place, greens, steps, parts):
    points = SIDE * SIDE
    return pl.pallas_call(
        functools.partial(forward_kernel, steps, parts),
        out_shape=[
            jax.ShapeDtypeStruct((points, TILE, WIDTH), jnp.float32),
            jax.ShapeDtypeStruct((STEPS, TILE * points, WIDTH), jnp.float32),
        ],
        in_specs=[in_smem()] + [anywhere()] * len(steps),
        out_specs=[in_vmem()] * 2,
        scratch_shapes=[pltpu.VMEM((points, TILE, WIDTH), jnp.float32)] + held_blocks(len(steps), parts),
        compiler_params=params(6),
        cost_estimate=cost(400, 6),
        name="forward",
    )(place, *greens)


def early_lines(place, lattice, weights, screens, steps, parts, work=None):
    points = SIDE * SIDE
    inputs = (place, lattice, weights, *screens) + (() if work is None else (work,))
    return pl.pallas_call(
        functools.partial(early_kernel, steps, parts),
        out_shape=jax.ShapeDtypeStruct((points, TILE, WIDTH), jnp.float32),
        in_specs=[in_smem(), in_vmem(), in_vmem()]
        + [anywhere()] * len(steps)
        + [in_vmem()] * (work is not None),
        out_specs=in_vmem(),
        input_output_aliases={} if work is None else {len(inputs) - 1: 0},
        scratch_shapes=held_blocks(len(steps), parts),
        compiler_params=params(4),
        cost_estimate=cost(25 * len(steps), 3),
        name="early",
    )(*inputs)


def sigma_of(place, lattice, weights, screens, work, steps, parts):
    points = SIDE * SIDE
    inputs = (place, lattice, weights, *screens, work)
    work, sigma = pl.pallas_call(
        functools.partial(sigma_kernel, steps, parts),
        out_shape=[
            jax.ShapeDtypeStruct((points, TILE, WIDTH), jnp.float32),
            jax.ShapeDtypeStruct((TILE * points, WIDTH), jnp.float32),
        ],
        in_specs=[in_smem()] + [in_vmem()] * 2 + [anywhere()] * len(steps) + [in_vmem()],
        out_specs=[in_vmem()] * 2,
        input_output_aliases={len(inputs) - 1: 0},
        scratch_shapes=held_blocks(len(steps), parts) if steps else [],
        compiler_params=params(2),
        cost_estimate=cost(200, 6),
        name="sigma",
    )(*inputs)
    return sigma


def contract(owners, sigma, equal_time, greens, block, share, before=()):
    points = owners.shape[0] * block
    rows = -(-points // 16) * 16
    signs, gather = gather_tables()
    return pl.pallas_call(
        functools.partial(contract_kernel, share),
        out_shape=jax.ShapeDtypeStruct((points, WIDTH), jnp.float32),
        in_specs=[in_smem()] + [in_vmem()] * 5 + [anywhere()] * len(before),
        out_specs=in_vmem(),
        scratch_shapes=[
            pltpu.VMEM((rows, STEPS * STEPS * WIDTH), jnp.float32),
            pltpu.VMEM((rows, STEPS * STEPS * WIDTH), jnp.bfloat16),
        ],
        compiler_params=params(6),
        cost_estimate=cost(70 * owners.shape[0], 6),
        name="contract",
    )(owners, sigma, equal_time, jnp.asarray(signs), jnp.asarray(gather), greens, *before)


def pick(place, whole, steps, parts, before=()):
    rows, width = whole.shape[0] // parts, whole.shape[1]
    return pl.pallas_call(
        functools.partial(pick_kernel, steps, parts),
        out_shape=[jax.ShapeDtypeStruct((rows, width), whole.dtype)] * len(steps),
        in_specs=[in_smem(), anywhere()] + [anywhere()] * len(before),
        out_specs=[in_vmem()] * len(steps),
        scratch_shapes=[pltpu.SemaphoreType.DMA((len(steps),))],
        compiler_params=params(56),
        cost_estimate=cost(0, 2),
        name="pick",
    )(place, whole, *before)


def split_own(greens):
    history, points, width = greens.shape
    return pl.pallas_call(
        split_kernel,
        out_shape=jax.ShapeDtypeStruct((points, history, 3 * width), jnp.bfloat16),
        in_specs=[in_vmem()],
        out_specs=in_vmem(),
        compiler_params=params(4),
        cost_estimate=cost(3, 2),
        name="split_own",
    )(greens)


def propagate(greens, pieces, effective):
    history, points, width = greens.shape
    tile = points if points % TILE else TILE
    spread = spread_table()
    return pl.pallas_call(
        propagate_kernel,
        out_shape=jax.ShapeDtypeStruct(greens.shape, jnp.float32),
        in_specs=[in_vmem()] * 4,
        out_specs=anywhere(),
        scratch_shapes=[
            pltpu.VMEM((points, spread.shape[1]), jnp.float32),
            pltpu.VMEM((2, history, tile, width), jnp.float32),
            pltpu.SemaphoreType.DMA((2,)),
        ],
        compiler_params=params(3),
        cost_estimate=cost(32, 5),
        name="propagate",
    )(greens, pieces, effective, jnp.asarray(spread))


def partner_of(place, step, count):
    if count == 1:
        return 0
    if count & (count - 1) == 0:
        return place ^ step
    return (place + step) % count


def exchange(value, axis, step, count):
    pairs = [(place, partner_of(place, step, count)) for place in range(count)]
    return lax.ppermute(value, axis, pairs)


def exchange_order(count):
    along = {}
    for step in range(1, count):
        along.setdefault(step // 2, []).append(step)
    single = [along[n] for n in along if n and n & (n - 1) == 0]
    mixed = [along[n] for n in along if n & (n - 1)]
    order = [step for steps in zip(*single[::-1]) for step in steps]
    return order + along[0] + [step for steps in mixed for step in steps]


def class_weights(quad_class):
    table = jnp.array(quadrature, jnp.float32)
    match = quad_class[:, None] == jnp.arange(4, dtype=jnp.int32)[None, :]
    return jnp.sum(jnp.where(match, table[None, :], jnp.float32(0.0)), axis=1)


def per_device(parts, blocks, green_row, screened, hamilton, equal_time, quad_class, live_count):
    history, local, width = green_row.shape
    points = local * parts
    times = history // parts
    place = lax.axis_index("ka")
    seat = place.reshape(1)
    position = jnp.arange(history, dtype=jnp.int32)
    weights = jnp.where(
        position < live_count[0], time_step * class_weights(quad_class), jnp.float32(0.0)
    ) * jnp.float32(1.0 / points)
    weights = lax.dynamic_slice_in_dim(weights, place * times, times)

    if times == TILE and local % SIDE == 0:
        groups, sources = 1, parts
        order = exchange_order(parts)
        moved = []
        wholes = [x.reshape(parts * TILE * local, width) for x in (green_row, screened)]
        blocks_of_green = [
            lax.dynamic_slice_in_dim(wholes[0], partner_of(place, step, parts) * (TILE * local), TILE * local)
            for step in order
        ]
        blocks_of_screen = pick(seat, wholes[1], order, parts, blocks_of_green[:1])
        moved = []
        for whole, sent in zip(wholes, (blocks_of_green, blocks_of_screen)):
            found = {step: exchange(block, "ka", step, parts) for step, block in zip(order, sent)}
            moved.append([{0: whole, **found}])
        order = [0] + order
    else:
        groups, sources = -(-times // TILE), 1
        order = [0]
        padding = groups * TILE - times
        moved = []
        for x in (green_row, screened):
            x = lax.all_to_all(x, "ka", split_axis=0, concat_axis=0, tiled=True)
            x = x.reshape(parts, times, local, width).transpose(1, 0, 2, 3).reshape(times, points, width)
            x = jnp.pad(x, ((0, padding), (0, 0), (0, 0))).reshape(groups, TILE * points, width)
            moved.append([{0: x[group]} for group in range(groups)])
        weights = jnp.pad(weights, (0, padding))
    weights = jnp.broadcast_to(weights.reshape(groups, TILE, 1), (groups, TILE, width))

    early = order[: max(1, len(order) - LATE)]
    late = order[len(early) :]
    own_pieces = split_own(green_row)
    share = hubbard / (points * blocks)
    sigmas = []
    for group in range(groups):
        green, screen = moved[0][group], moved[1][group]
        listed = order
        lattice, greens = forward(seat, [green[step] for step in listed], listed, sources)
        listed = early[-1:] + early[:-1]
        work = early_lines(seat, lattice, weights[group], [screen[step] for step in listed], listed, sources)
        for step in late[:-1]:
            work = early_lines(seat, lattice, weights[group], [screen[step]], [step], sources, work)
        last = late[-1:]
        sigma = sigma_of(
            seat, lattice, weights[group], [screen[step] for step in last], work, last, sources
        )
        sigmas.append((sigma, greens))

    if sources == parts and parts % 2 == 0 and parts & (parts - 1) == 0:
        (sigma, greens), = sigmas

        def blocks_of(steps, before=()):
            owners = jnp.stack([partner_of(place, step, parts) for step in steps])
            return contract(owners, sigma, equal_time, greens, local, share, before)

        others = exchange(blocks_of([*range(3, parts, 2), 1]), "ka", 1, parts)
        far = blocks_of(list(range(2, parts, 2))) + others[:-local]
        pieces = [
            exchange(far[(n - 1) * local : n * local], "ka", 2 * n, parts)
            for n in range(parts // 2 - 1, 0, -1)
        ]
        pieces += [blocks_of([0], pieces[:1]), others[-local:]]
        collision = tree_sum(pieces)
    else:
        whole = jnp.zeros((1,), jnp.int32)
        partial_value = tree_sum(
            [
                contract(whole, sigma, equal_time, greens, points, share if group == 0 else 0.0)
                for group, (sigma, greens) in enumerate(sigmas)
            ]
        )
        owners = [partner_of(place, step, parts) for step in range(parts)]
        pieces = [lax.dynamic_slice_in_dim(partial_value, owner * local, local) for owner in owners]
        collision = tree_sum(
            pieces[:1] + [exchange(pieces[step], "ka", step, parts) for step in range(1, parts)]
        )
    collision = tree_sum(
        [collision] + [exchange(collision, "hist", step, blocks) for step in range(blocks - 1, 0, -1)]
    )
    return propagate(green_row, own_pieces, hamilton + collision)


def solution(mesh):
    in_specs = (
        P("hist", "ka", None),
        P("hist", "ka", None),
        P("ka", None),
        P("ka", None),
        P("hist"),
        P("hist"),
    )
    out_specs = P("hist", "ka", None)
    return jax.shard_map(
        functools.partial(per_device, mesh.shape["ka"], mesh.shape["hist"]),
        mesh=mesh,
        in_specs=in_specs,
        out_specs=out_specs,
        check_vma=False,
    )
```

```python
import functools
import math

import jax
import jax.numpy as jnp
import ml_dtypes
import numpy as np
from jax import lax
from jax.experimental import pallas as pl
from jax.experimental.pallas import tpu as pltpu
from jax.sharding import PartitionSpec as P

SIDE = 24
BANDS = 8
ENTRIES = BANDS * BANDS
WIDTH = 2 * ENTRIES
TILE = 8
STEPS = 4

time_step = 0.1
hubbard = 1.0
quadrature = (0.375, 1.1666666, 0.9583333, 1.0)

AT_ONCE = 4
COLUMNS = 4
LATE = 2
AHEAD = 3


def lane_sign(shape):
    lane = lax.broadcasted_iota(jnp.int32, shape, len(shape) - 1)
    return lane < ENTRIES


def swap(x):
    return pltpu.roll(x, ENTRIES, 1)


def roll_blocks(x, blocks):
    return x if blocks == 0 else pltpu.roll(x, WIDTH - BANDS * blocks, x.ndim - 1)


def tree_sum(terms):
    while len(terms) > 1:
        terms = [sum(terms[i : i + 2][1:], terms[i]) for i in range(0, len(terms), 2)]
    return terms[0]


def split(x):
    high = x.astype(jnp.bfloat16)
    return jnp.concatenate([high, (x - high.astype(jnp.float32)).astype(jnp.bfloat16)], axis=1)


def dft24(x, sign, low):
    root3 = jnp.where(low, -1.0, 1.0) * (sign * math.sqrt(3.0) / 2)
    turn = jnp.where(low, -1.0, 1.0) * float(sign)
    half = math.sqrt(0.5)
    turn_half = turn * half
    columns = [[None] * 8 for _ in range(3)]
    for n2 in range(8):
        x0, x1, x2 = (x[(8 * n1 + 3 * n2) % 24] for n1 in range(3))
        total = x1 + x2
        base = x0 - 0.5 * total
        spin = swap(x1 - x2) * root3
        columns[0][n2] = x0 + total
        columns[1][n2] = base + spin
        columns[2][n2] = base - spin
    out = [None] * 24
    for k1 in range(3):
        c = columns[k1]
        a0, a1 = c[0] + c[4], c[0] - c[4]
        a2, a3 = c[2] + c[6], c[2] - c[6]
        a4, a5 = c[1] + c[5], c[1] - c[5]
        a6, a7 = c[3] + c[7], c[3] - c[7]
        b0, b1 = a0 + a2, a0 - a2
        b2, b3 = a4 + a6, a4 - a6
        i_a3 = swap(a3) * turn
        i_b3 = swap(b3) * turn
        c0, c1 = a1 + i_a3, a1 - i_a3
        p = (a5 - a7) * half
        m = swap(a5 + a7) * turn_half
        e, f = p + m, p - m
        values = [b0 + b2, c0 + e, b1 + i_b3, c1 - f, b0 - b2, c0 - e, b1 - i_b3, c1 + f]
        for k2 in range(8):
            out[(16 * k1 + 9 * k2) % 24] = values[k2]
    return out


def load_line(ref, line):
    stride = ref.shape[0] // TILE
    return [ref[pl.ds(line * SIDE + k2, TILE, stride=stride), :] for k2 in range(SIDE)]


def fetch(place, steps, block_refs, held_ref, sems):
    copies = []
    for slot, (step, source) in enumerate(zip(steps, block_refs)):
        rows = held_ref.shape[1]
        if step == 0 and source.shape[0] != rows:
            source = source.at[pl.ds(pl.multiple_of(place * rows, TILE), rows)]
        copies.append(pltpu.make_async_copy(source, held_ref.at[slot], sems.at[slot]))
        copies[-1].start()
    return copies


def along_first(work_ref, sign, low, store):
    def columns(group, carry):
        some = [COLUMNS * group + n for n in range(COLUMNS)]
        rows = [[work_ref[k1 * SIDE + column] for k1 in range(SIDE)] for column in some]
        values = [dft24(row, sign, low) for row in rows]
        for column, value in zip(some, values):
            for r1 in range(SIDE):
                store(r1 * SIDE + column, value[r1])
        return carry

    lax.fori_loop(0, SIDE // COLUMNS, columns, 0)


def pick_kernel(steps, parts, place_ref, whole_ref, *refs):
    block_refs, sems = refs[-1 - len(steps) : -1], refs[-1]
    copies = []
    for n, (step, block_ref) in enumerate(zip(steps, block_refs)):
        rows = block_ref.shape[0]
        start = pl.multiple_of(partner_of(place_ref[0], step, parts) * rows, TILE)
        copies.append(pltpu.make_async_copy(whole_ref.at[pl.ds(start, rows)], block_ref, sems.at[n]))
        copies[-1].start()
    for copy in copies:
        copy.wait()


def times_of(ref, k):
    history, points, width = ref.shape
    if points % TILE:
        return ref[:, k, :]
    return ref.reshape(history * points, width)[pl.ds(k, history, stride=points), :]


def split_kernel(green_ref, split_ref):
    history, points, _ = green_ref.shape

    def write(k):
        green = times_of(green_ref, k)
        high = green.astype(jnp.bfloat16)
        low = (green - high.astype(jnp.float32)).astype(jnp.bfloat16)
        for n, part in enumerate((high, low, high)):
            split_ref[k, :, n * WIDTH : (n + 1) * WIDTH] = part

    if points % TILE:
        for k in range(points):
            write(k)
        return

    def some(n, carry):
        for k in range(4):
            write(4 * n + k)
        return carry

    lax.fori_loop(0, points // 4, some, 0)


def forward_kernel(steps, parts, place_ref, *refs):
    block_refs, (lattice_ref, greens_ref, work_ref, held_ref, sems) = refs[: len(steps)], refs[len(steps) :]
    low = lane_sign((TILE, WIDTH))
    place = place_ref[0]
    copies = fetch(place, steps, block_refs, held_ref, sems)
    rows = held_ref.shape[1]
    lines = rows // (TILE * SIDE)
    for slot, step in enumerate(steps):
        copies[slot].wait()
        green_ref = held_ref.at[slot]
        owner = partner_of(place, step, parts)

        def along_second(i, carry):
            for r2, value in enumerate(dft24(load_line(green_ref, i), -1, low)):
                work_ref[(owner * lines + i) * SIDE + r2] = value
            return carry

        lax.fori_loop(0, lines, along_second, 0, unroll=lines <= 4)
        green = green_ref[...]
        spot = pl.ds(pl.multiple_of(owner * rows, TILE), rows)
        for j in range(STEPS):
            greens_ref[j, spot, :] = roll_blocks(green, j)

    def store(point, value):
        lattice_ref[point] = value

    along_first(work_ref, -1, low, store)


def product_lines(steps, parts, place, lattice_ref, weights, screen_refs, held_ref, sems, work_ref):
    low = lane_sign((TILE, WIDTH))
    turn = jnp.where(low, -1.0, 1.0)
    copies = fetch(place, steps, screen_refs, held_ref, sems)
    lines = held_ref.shape[1] // (TILE * SIDE)
    for slot, step in enumerate(steps):
        copies[slot].wait()
        screen_ref = held_ref.at[slot]
        first = partner_of(place, step, parts) * lines

        def along_second(i, carry):
            rows = []
            for r2, value in enumerate(load_line(screen_ref, i)):
                screen = value * weights
                other = swap(screen)
                lattice = lattice_ref[(first + i) * SIDE + r2]
                rows.append(
                    swap(lattice) * turn * jnp.where(low, screen, other)
                    - lattice * jnp.where(low, other, screen)
                )
            for k2, value in enumerate(dft24(rows, 1, low)):
                work_ref[(first + i) * SIDE + k2] = value
            return carry

        lax.fori_loop(0, lines, along_second, 0, unroll=lines <= 4)


def early_kernel(steps, parts, place_ref, lattice_ref, weight_ref, *refs):
    screen_refs, (*_, work_ref, held_ref, sems) = refs[: len(steps)], refs[len(steps) :]
    product_lines(
        steps, parts, place_ref[0], lattice_ref, weight_ref[...], screen_refs, held_ref, sems, work_ref
    )


def sigma_kernel(steps, parts, place_ref, lattice_ref, weight_ref, *refs):
    screen_refs, refs = refs[: len(steps)], refs[len(steps) :]
    _, work_ref, sigma_ref, *late = refs
    low = lane_sign((TILE, WIDTH))
    if steps:
        held_ref, sems = late
        product_lines(
            steps, parts, place_ref[0], lattice_ref, weight_ref[...], screen_refs, held_ref, sems, work_ref
        )

    def store(point, value):
        sigma_ref[pl.ds(point * TILE, TILE), :] = value

    along_first(work_ref, 1, low, store)


def contract_kernel(share, owner_ref, sigma_ref, equal_ref, sign_ref, gather_ref, greens_ref, *refs):
    partial_ref, sums_ref, pieces_ref = refs[-3:]
    low = lane_sign((TILE, WIDTH))
    points = partial_ref.shape[0]
    block = points // owner_ref.shape[0]
    tiles = block // TILE
    batch = max(n for n in range(1, 10) if tiles % n == 0)

    def contract(group, carry):
        slot, first = group // (tiles // batch), group % (tiles // batch) * batch
        owner = owner_ref[slot]
        units = [(tile, s) for tile in range(batch) for s in range(TILE)]

        def prepare(tile, s):
            point = owner * block + (first + tile) * TILE
            sigma = sigma_ref[pl.ds(point * TILE + s, TILE, stride=TILE), :]
            row = pl.multiple_of((owner * TILE + s) * block + (first + tile) * TILE, TILE)
            return (
                [roll_blocks(sigma, STEPS * i) for i in range(STEPS)],
                [greens_ref[j, pl.ds(row, TILE), :] for j in range(STEPS)],
            )

        ready = [prepare(*unit) for unit in units[:AHEAD]]
        for n, (tile, s) in enumerate(units):
            if n + AHEAD < len(units):
                ready.append(prepare(*units[n + AHEAD]))
            sigmas, greens = ready.pop(0)
            terms = [sigma * green for sigma in sigmas for green in greens]
            sums = terms if s == 0 else [a + b for a, b in zip(sums, terms)]
            if s == TILE - 1:
                row = pl.ds(pl.multiple_of(slot * block + (first + tile) * TILE, TILE), TILE)
                for spot, value in enumerate(sums):
                    sums_ref[row, spot * WIDTH : (spot + 1) * WIDTH] = value
        return carry

    lax.fori_loop(0, points // (TILE * batch), contract, 0)

    lane = lax.broadcasted_iota(jnp.int32, equal_ref.shape, 1)
    inner = lane - ENTRIES
    occupied = jnp.sum(jnp.where((inner >= 0) & (inner % (BANDS + 1) == 0), equal_ref[...], 0.0))
    spots = lax.broadcasted_iota(jnp.int32, (points, WIDTH), 1)
    on_diagonal = (spots < ENTRIES) & (spots % (BANDS + 1) == 0)
    lower = lax.broadcasted_iota(jnp.int32, (sums_ref.shape[0], WIDTH), 1) < ENTRIES
    for pair in range(STEPS * STEPS // 2):
        first_part = sums_ref[:, 2 * pair * WIDTH : (2 * pair + 1) * WIDTH]
        second_part = sums_ref[:, (2 * pair + 1) * WIDTH : (2 * pair + 2) * WIDTH]
        folded = jnp.where(lower, first_part, second_part) + sign_ref[pair : pair + 1, :] * swap(
            jnp.where(lower, second_part, first_part)
        )
        pieces_ref[:, 2 * pair * WIDTH : (2 * pair + 2) * WIDTH] = split(folded)
    total = jnp.dot(pieces_ref[...], gather_ref[...], preferred_element_type=jnp.float32)
    partial_ref[...] = total[:points] + jnp.where(on_diagonal, occupied * share, 0.0)


def propagate_kernel(green_ref, split_ref, effective_ref, spread_ref, out_ref, factor_ref, held_ref, sems):
    history, points, _ = green_ref.shape
    factor_ref[...] = jnp.dot(
        split(effective_ref[...] * time_step), spread_ref[...], preferred_element_type=jnp.float32
    )
    tile = held_ref.shape[2]
    row = lax.broadcasted_iota(jnp.int32, (BANDS, WIDTH), 0)
    same = lax.broadcasted_iota(jnp.int32, (BANDS, WIDTH), 1) % BANDS == row

    def copy(number, slot):
        return pltpu.make_async_copy(
            held_ref.at[slot], out_ref.at[:, pl.ds(number * tile, tile), :], sems.at[slot]
        )

    def matrix(factors, n):
        parts = [
            jnp.where(same, jnp.broadcast_to(factor[n : n + 1], same.shape), 0.0) for factor in factors
        ]
        whole = jnp.concatenate(parts, axis=0)
        high = whole.astype(jnp.bfloat16)
        low = (whole - high.astype(jnp.float32)).astype(jnp.bfloat16)
        return jnp.concatenate([high, high, low], axis=0)

    def advance(number, slot):
        start = number * tile if points == tile else pl.multiple_of(number * tile, TILE)
        factors = [
            factor_ref[pl.ds(start, tile), spot * WIDTH : (spot + 1) * WIDTH] for spot in range(2 * BANDS)
        ]
        for first in range(0, tile, AT_ONCE):
            batch = range(first, min(first + AT_ONCE, tile))
            results = []
            for n in batch:
                k = number * tile + n
                added = jnp.dot(split_ref[k], matrix(factors, n), preferred_element_type=jnp.float32)
                results.append(times_of(green_ref, k) + added)
            for n, result in zip(batch, results):
                if points % TILE:
                    held_ref[slot, :, n, :] = result
                else:
                    rows = held_ref.reshape(2 * history * tile, WIDTH)
                    rows[pl.ds(slot * history * tile + n, history, stride=tile), :] = result
        copy(number, slot).start()

    tiles = points // tile
    if tiles == 1:
        advance(0, 0)
        copy(0, 0).wait()
        return

    def step(number, carry):
        slot = number % 2

        @pl.when(number > 1)
        def _():
            copy(number - 2, slot).wait()

        advance(number, slot)
        return carry

    lax.fori_loop(0, tiles, step, 0)
    for number in (tiles - 2, tiles - 1):
        copy(number, number % 2).wait()


def gather_tables():
    blocks = 2 * BANDS
    pairs = STEPS * STEPS // 2
    table = np.zeros((pairs, 2, blocks, BANDS, 2, BANDS, BANDS), np.float32)
    signs = np.zeros((pairs, blocks, BANDS), np.float32)
    for pair in range(pairs):
        for p in range(blocks):
            i, j = divmod(2 * pair + p // BANDS, STEPS)
            h, a = divmod((p + STEPS * i) % blocks, BANDS)
            g, c = divmod((p + j) % blocks, BANDS)
            table[pair, :, p, :, h ^ g, a, c] = 1 if (h, g) == (0, 1) else -1
            signs[pair, p] = 1 if h == g else -1
    return signs.reshape(pairs, WIDTH), table.reshape(-1, WIDTH).astype(ml_dtypes.bfloat16)


def spread_table():
    table = np.zeros((2, BANDS, BANDS, 2, BANDS, 2, BANDS, BANDS), np.float32)
    for h, g, a, b in np.ndindex(2, 2, BANDS, BANDS):
        table[1 if h == g else 0, a, b, g, b, h, a, :] = -1 if (h, g) == (1, 0) else 1
    return np.tile(table.reshape(WIDTH, -1), (2, 1)).astype(ml_dtypes.bfloat16)


def in_vmem():
    return pl.BlockSpec(memory_space=pltpu.VMEM)


def in_smem():
    return pl.BlockSpec(memory_space=pltpu.SMEM)


def anywhere():
    return pl.BlockSpec(memory_space=pl.ANY)


def params(megabytes):
    return pltpu.CompilerParams(vmem_limit_bytes=megabytes * 1024 * 1024)


def cost(per_element, arrays):
    size = SIDE * SIDE * TILE * WIDTH
    return pl.CostEstimate(flops=per_element * size, bytes_accessed=4 * arrays * size, transcendentals=0)


def held_blocks(count, parts):
    return [
        pltpu.VMEM((count, TILE * SIDE * SIDE // parts, WIDTH), jnp.float32),
        pltpu.SemaphoreType.DMA((count,)),
    ]


def forward(place, greens, steps, parts):
    points = SIDE * SIDE
    return pl.pallas_call(
        functools.partial(forward_kernel, steps, parts),
        out_shape=[
            jax.ShapeDtypeStruct((points, TILE, WIDTH), jnp.float32),
            jax.ShapeDtypeStruct((STEPS, TILE * points, WIDTH), jnp.float32),
        ],
        in_specs=[in_smem()] + [anywhere()] * len(steps),
        out_specs=[in_vmem()] * 2,
        scratch_shapes=[pltpu.VMEM((points, TILE, WIDTH), jnp.float32)] + held_blocks(len(steps), parts),
        compiler_params=params(6),
        cost_estimate=cost(400, 6),
        name="forward",
    )(place, *greens)


def early_lines(place, lattice, weights, screens, steps, parts, work=None):
    points = SIDE * SIDE
    inputs = (place, lattice, weights, *screens) + (() if work is None else (work,))
    return pl.pallas_call(
        functools.partial(early_kernel, steps, parts),
        out_shape=jax.ShapeDtypeStruct((points, TILE, WIDTH), jnp.float32),
        in_specs=[in_smem(), in_vmem(), in_vmem()]
        + [anywhere()] * len(steps)
        + [in_vmem()] * (work is not None),
        out_specs=in_vmem(),
        input_output_aliases={} if work is None else {len(inputs) - 1: 0},
        scratch_shapes=held_blocks(len(steps), parts),
        compiler_params=params(4),
        cost_estimate=cost(25 * len(steps), 3),
        name="early",
    )(*inputs)


def sigma_of(place, lattice, weights, screens, work, steps, parts):
    points = SIDE * SIDE
    inputs = (place, lattice, weights, *screens, work)
    work, sigma = pl.pallas_call(
        functools.partial(sigma_kernel, steps, parts),
        out_shape=[
            jax.ShapeDtypeStruct((points, TILE, WIDTH), jnp.float32),
            jax.ShapeDtypeStruct((TILE * points, WIDTH), jnp.float32),
        ],
        in_specs=[in_smem()] + [in_vmem()] * 2 + [anywhere()] * len(steps) + [in_vmem()],
        out_specs=[in_vmem()] * 2,
        input_output_aliases={len(inputs) - 1: 0},
        scratch_shapes=held_blocks(len(steps), parts) if steps else [],
        compiler_params=params(2),
        cost_estimate=cost(200, 6),
        name="sigma",
    )(*inputs)
    return sigma


def contract(owners, sigma, equal_time, greens, block, share, before=()):
    points = owners.shape[0] * block
    rows = -(-points // 16) * 16
    signs, gather = gather_tables()
    return pl.pallas_call(
        functools.partial(contract_kernel, share),
        out_shape=jax.ShapeDtypeStruct((points, WIDTH), jnp.float32),
        in_specs=[in_smem()] + [in_vmem()] * 5 + [anywhere()] * len(before),
        out_specs=in_vmem(),
        scratch_shapes=[
            pltpu.VMEM((rows, STEPS * STEPS * WIDTH), jnp.float32),
            pltpu.VMEM((rows, STEPS * STEPS * WIDTH), jnp.bfloat16),
        ],
        compiler_params=params(6),
        cost_estimate=cost(70 * owners.shape[0], 6),
        name="contract",
    )(owners, sigma, equal_time, jnp.asarray(signs), jnp.asarray(gather), greens, *before)


def pick(place, whole, steps, parts, before=()):
    rows, width = whole.shape[0] // parts, whole.shape[1]
    return pl.pallas_call(
        functools.partial(pick_kernel, steps, parts),
        out_shape=[jax.ShapeDtypeStruct((rows, width), whole.dtype)] * len(steps),
        in_specs=[in_smem(), anywhere()] + [anywhere()] * len(before),
        out_specs=[in_vmem()] * len(steps),
        scratch_shapes=[pltpu.SemaphoreType.DMA((len(steps),))],
        compiler_params=params(56),
        cost_estimate=cost(0, 2),
        name="pick",
    )(place, whole, *before)


def split_own(greens):
    history, points, width = greens.shape
    return pl.pallas_call(
        split_kernel,
        out_shape=jax.ShapeDtypeStruct((points, history, 3 * width), jnp.bfloat16),
        in_specs=[in_vmem()],
        out_specs=in_vmem(),
        compiler_params=params(4),
        cost_estimate=cost(3, 2),
        name="split_own",
    )(greens)


def propagate(greens, pieces, effective):
    history, points, width = greens.shape
    tile = points if points % TILE else TILE
    spread = spread_table()
    return pl.pallas_call(
        propagate_kernel,
        out_shape=jax.ShapeDtypeStruct(greens.shape, jnp.float32),
        in_specs=[in_vmem()] * 4,
        out_specs=anywhere(),
        scratch_shapes=[
            pltpu.VMEM((points, spread.shape[1]), jnp.float32),
            pltpu.VMEM((2, history, tile, width), jnp.float32),
            pltpu.SemaphoreType.DMA((2,)),
        ],
        compiler_params=params(3),
        cost_estimate=cost(32, 5),
        name="propagate",
    )(greens, pieces, effective, jnp.asarray(spread))


def partner_of(place, step, count):
    if count == 1:
        return 0
    if count & (count - 1) == 0:
        return place ^ step
    return (place + step) % count


def exchange(value, axis, step, count):
    pairs = [(place, partner_of(place, step, count)) for place in range(count)]
    return lax.ppermute(value, axis, pairs)


def exchange_order(count):
    along = {}
    for step in range(1, count):
        along.setdefault(step // 2, []).append(step)
    single = [along[n] for n in along if n and n & (n - 1) == 0]
    mixed = [along[n] for n in along if n & (n - 1)]
    order = [step for steps in zip(*single[::-1]) for step in steps]
    return order + along[0] + [step for steps in mixed for step in steps]


def class_weights(quad_class):
    table = jnp.array(quadrature, jnp.float32)
    match = quad_class[:, None] == jnp.arange(4, dtype=jnp.int32)[None, :]
    return jnp.sum(jnp.where(match, table[None, :], jnp.float32(0.0)), axis=1)


def per_device(parts, blocks, green_row, screened, hamilton, equal_time, quad_class, live_count):
    history, local, width = green_row.shape
    points = local * parts
    times = history // parts
    place = lax.axis_index("ka")
    seat = place.reshape(1)
    position = jnp.arange(history, dtype=jnp.int32)
    weights = jnp.where(
        position < live_count[0], time_step * class_weights(quad_class), jnp.float32(0.0)
    ) * jnp.float32(1.0 / points)
    weights = lax.dynamic_slice_in_dim(weights, place * times, times)

    if times == TILE and local % SIDE == 0:
        groups, sources = 1, parts
        order = exchange_order(parts)
        moved = []
        wholes = [x.reshape(parts * TILE * local, width) for x in (green_row, screened)]
        blocks_of_green = [
            lax.dynamic_slice_in_dim(wholes[0], partner_of(place, step, parts) * (TILE * local), TILE * local)
            for step in order
        ]
        blocks_of_screen = pick(seat, wholes[1], order, parts, blocks_of_green[:1])
        moved = []
        for whole, sent in zip(wholes, (blocks_of_green, blocks_of_screen)):
            found = {step: exchange(block, "ka", step, parts) for step, block in zip(order, sent)}
            moved.append([{0: whole, **found}])
        order = [0] + order
    else:
        groups, sources = -(-times // TILE), 1
        order = [0]
        padding = groups * TILE - times
        moved = []
        for x in (green_row, screened):
            x = lax.all_to_all(x, "ka", split_axis=0, concat_axis=0, tiled=True)
            x = x.reshape(parts, times, local, width).transpose(1, 0, 2, 3).reshape(times, points, width)
            x = jnp.pad(x, ((0, padding), (0, 0), (0, 0))).reshape(groups, TILE * points, width)
            moved.append([{0: x[group]} for group in range(groups)])
        weights = jnp.pad(weights, (0, padding))
    weights = jnp.broadcast_to(weights.reshape(groups, TILE, 1), (groups, TILE, width))

    early = order[: max(1, len(order) - LATE)]
    late = order[len(early) :]
    own_pieces = split_own(green_row)
    share = hubbard / (points * blocks)
    sigmas = []
    for group in range(groups):
        green, screen = moved[0][group], moved[1][group]
        listed = order
        lattice, greens = forward(seat, [green[step] for step in listed], listed, sources)
        listed = early[-1:] + early[:-1]
        work = early_lines(seat, lattice, weights[group], [screen[step] for step in listed], listed, sources)
        for step in late[:-1]:
            work = early_lines(seat, lattice, weights[group], [screen[step]], [step], sources, work)
        last = late[-1:]
        sigma = sigma_of(
            seat, lattice, weights[group], [screen[step] for step in last], work, last, sources
        )
        sigmas.append((sigma, greens))

    if sources == parts and parts % 2 == 0 and parts & (parts - 1) == 0:
        (sigma, greens), = sigmas

        def blocks_of(steps, before=()):
            owners = jnp.stack([partner_of(place, step, parts) for step in steps])
            return contract(owners, sigma, equal_time, greens, local, share, before)

        others = exchange(blocks_of([*range(3, parts, 2), 1]), "ka", 1, parts)
        far = blocks_of(list(range(2, parts, 2))) + others[:-local]
        pieces = [
            exchange(far[(n - 1) * local : n * local], "ka", 2 * n, parts)
            for n in range(parts // 2 - 1, 0, -1)
        ]
        pieces += [blocks_of([0], pieces[:1]), others[-local:]]
        collision = tree_sum(pieces)
    else:
        whole = jnp.zeros((1,), jnp.int32)
        partial_value = tree_sum(
            [
                contract(whole, sigma, equal_time, greens, points, share if group == 0 else 0.0)
                for group, (sigma, greens) in enumerate(sigmas)
            ]
        )
        owners = [partner_of(place, step, parts) for step in range(parts)]
        pieces = [lax.dynamic_slice_in_dim(partial_value, owner * local, local) for owner in owners]
        collision = tree_sum(
            pieces[:1] + [exchange(pieces[step], "ka", step, parts) for step in range(1, parts)]
        )
    collision = tree_sum(
        [collision] + [exchange(collision, "hist", step, blocks) for step in range(blocks - 1, 0, -1)]
    )
    return propagate(green_row, own_pieces, hamilton + collision)


def solution(mesh):
    in_specs = (
        P("hist", "ka", None),
        P("hist", "ka", None),
        P("ka", None),
        P("ka", None),
        P("hist"),
        P("hist"),
    )
    out_specs = P("hist", "ka", None)
    return jax.shard_map(
        functools.partial(per_device, mesh.shape["ka"], mesh.shape["hist"]),
        mesh=mesh,
        in_specs=in_specs,
        out_specs=out_specs,
        check_vma=False,
    )
```

```python
import functools
import math

import jax
import jax.numpy as jnp
import ml_dtypes
import numpy as np
from jax import lax
from jax.experimental import pallas as pl
from jax.experimental.pallas import tpu as pltpu
from jax.sharding import PartitionSpec as P

SIDE = 24
BANDS = 8
ENTRIES = BANDS * BANDS
WIDTH = 2 * ENTRIES
TILE = 8
STEPS = 4

time_step = 0.1
hubbard = 1.0
quadrature = (0.375, 1.1666666, 0.9583333, 1.0)

AT_ONCE = 8
COLUMNS = 6
LATE = 2
AHEAD = 3


def lane_sign(shape):
    lane = lax.broadcasted_iota(jnp.int32, shape, len(shape) - 1)
    return lane < ENTRIES


def swap(x):
    return pltpu.roll(x, ENTRIES, 1)


def roll_blocks(x, blocks):
    return x if blocks == 0 else pltpu.roll(x, WIDTH - BANDS * blocks, x.ndim - 1)


def tree_sum(terms):
    while len(terms) > 1:
        terms = [sum(terms[i : i + 2][1:], terms[i]) for i in range(0, len(terms), 2)]
    return terms[0]


def split(x):
    high = x.astype(jnp.bfloat16)
    return jnp.concatenate([high, (x - high.astype(jnp.float32)).astype(jnp.bfloat16)], axis=1)


def dft24(x, sign, low):
    root3 = jnp.where(low, -1.0, 1.0) * (sign * math.sqrt(3.0) / 2)
    turn = jnp.where(low, -1.0, 1.0) * float(sign)
    half = math.sqrt(0.5)
    turn_half = turn * half
    columns = [[None] * 8 for _ in range(3)]
    for n2 in range(8):
        x0, x1, x2 = (x[(8 * n1 + 3 * n2) % 24] for n1 in range(3))
        total = x1 + x2
        base = x0 - 0.5 * total
        spin = swap(x1 - x2) * root3
        columns[0][n2] = x0 + total
        columns[1][n2] = base + spin
        columns[2][n2] = base - spin
    out = [None] * 24
    for k1 in range(3):
        c = columns[k1]
        a0, a1 = c[0] + c[4], c[0] - c[4]
        a2, a3 = c[2] + c[6], c[2] - c[6]
        a4, a5 = c[1] + c[5], c[1] - c[5]
        a6, a7 = c[3] + c[7], c[3] - c[7]
        b0, b1 = a0 + a2, a0 - a2
        b2, b3 = a4 + a6, a4 - a6
        i_a3 = swap(a3) * turn
        i_b3 = swap(b3) * turn
        c0, c1 = a1 + i_a3, a1 - i_a3
        p = (a5 - a7) * half
        m = swap(a5 + a7) * turn_half
        e, f = p + m, p - m
        values = [b0 + b2, c0 + e, b1 + i_b3, c1 - f, b0 - b2, c0 - e, b1 - i_b3, c1 + f]
        for k2 in range(8):
            out[(16 * k1 + 9 * k2) % 24] = values[k2]
    return out


def load_line(ref, line):
    stride = ref.shape[0] // TILE
    return [ref[pl.ds(line * SIDE + k2, TILE, stride=stride), :] for k2 in range(SIDE)]


def fetch(place, steps, block_refs, held_ref, sems):
    copies = []
    for slot, (step, source) in enumerate(zip(steps, block_refs)):
        rows = held_ref.shape[1]
        if step == 0 and source.shape[0] != rows:
            source = source.at[pl.ds(pl.multiple_of(place * rows, TILE), rows)]
        copies.append(pltpu.make_async_copy(source, held_ref.at[slot], sems.at[slot]))
        copies[-1].start()
    return copies


def along_first(work_ref, sign, low, store):
    def columns(group, carry):
        some = [COLUMNS * group + n for n in range(COLUMNS)]
        rows = [[work_ref[k1 * SIDE + column] for k1 in range(SIDE)] for column in some]
        values = [dft24(row, sign, low) for row in rows]
        for column, value in zip(some, values):
            for r1 in range(SIDE):
                store(r1 * SIDE + column, value[r1])
        return carry

    lax.fori_loop(0, SIDE // COLUMNS, columns, 0)


def pick_kernel(steps, parts, place_ref, whole_ref, *refs):
    block_refs, sems = refs[-1 - len(steps) : -1], refs[-1]
    copies = []
    for n, (step, block_ref) in enumerate(zip(steps, block_refs)):
        rows = block_ref.shape[0]
        start = pl.multiple_of(partner_of(place_ref[0], step, parts) * rows, TILE)
        copies.append(pltpu.make_async_copy(whole_ref.at[pl.ds(start, rows)], block_ref, sems.at[n]))
        copies[-1].start()
    for copy in copies:
        copy.wait()


def times_of(ref, k):
    history, points, width = ref.shape
    if points % TILE:
        return ref[:, k, :]
    return ref.reshape(history * points, width)[pl.ds(k, history, stride=points), :]


def split_kernel(green_ref, split_ref):
    history, points, _ = green_ref.shape

    def write(k):
        green = times_of(green_ref, k)
        high = green.astype(jnp.bfloat16)
        low = (green - high.astype(jnp.float32)).astype(jnp.bfloat16)
        for n, part in enumerate((high, low, high)):
            split_ref[k, :, n * WIDTH : (n + 1) * WIDTH] = part

    if points % TILE:
        for k in range(points):
            write(k)
        return

    def some(n, carry):
        for k in range(4):
            write(4 * n + k)
        return carry

    lax.fori_loop(0, points // 4, some, 0)


def forward_kernel(steps, parts, place_ref, *refs):
    block_refs, (lattice_ref, greens_ref, work_ref, held_ref, sems) = refs[: len(steps)], refs[len(steps) :]
    low = lane_sign((TILE, WIDTH))
    place = place_ref[0]
    copies = fetch(place, steps, block_refs, held_ref, sems)
    rows = held_ref.shape[1]
    lines = rows // (TILE * SIDE)
    for slot, step in enumerate(steps):
        copies[slot].wait()
        green_ref = held_ref.at[slot]
        owner = partner_of(place, step, parts)

        def along_second(i, carry):
            for r2, value in enumerate(dft24(load_line(green_ref, i), -1, low)):
                work_ref[(owner * lines + i) * SIDE + r2] = value
            return carry

        lax.fori_loop(0, lines, along_second, 0, unroll=lines <= 4)
        green = green_ref[...]
        spot = pl.ds(pl.multiple_of(owner * rows, TILE), rows)
        for j in range(STEPS):
            greens_ref[j, spot, :] = roll_blocks(green, j)

    def store(point, value):
        lattice_ref[point] = value

    along_first(work_ref, -1, low, store)


def product_lines(steps, parts, place, lattice_ref, weights, screen_refs, held_ref, sems, work_ref):
    low = lane_sign((TILE, WIDTH))
    turn = jnp.where(low, -1.0, 1.0)
    copies = fetch(place, steps, screen_refs, held_ref, sems)
    lines = held_ref.shape[1] // (TILE * SIDE)
    for slot, step in enumerate(steps):
        copies[slot].wait()
        screen_ref = held_ref.at[slot]
        first = partner_of(place, step, parts) * lines

        def along_second(i, carry):
            rows = []
            for r2, value in enumerate(load_line(screen_ref, i)):
                screen = value * weights
                other = swap(screen)
                lattice = lattice_ref[(first + i) * SIDE + r2]
                rows.append(
                    swap(lattice) * turn * jnp.where(low, screen, other)
                    - lattice * jnp.where(low, other, screen)
                )
            for k2, value in enumerate(dft24(rows, 1, low)):
                work_ref[(first + i) * SIDE + k2] = value
            return carry

        lax.fori_loop(0, lines, along_second, 0, unroll=lines <= 4)


def early_kernel(steps, parts, place_ref, lattice_ref, weight_ref, *refs):
    screen_refs, (*_, work_ref, held_ref, sems) = refs[: len(steps)], refs[len(steps) :]
    product_lines(
        steps, parts, place_ref[0], lattice_ref, weight_ref[...], screen_refs, held_ref, sems, work_ref
    )


def sigma_kernel(steps, parts, place_ref, lattice_ref, weight_ref, *refs):
    screen_refs, refs = refs[: len(steps)], refs[len(steps) :]
    _, work_ref, sigma_ref, *late = refs
    low = lane_sign((TILE, WIDTH))
    if steps:
        held_ref, sems = late
        product_lines(
            steps, parts, place_ref[0], lattice_ref, weight_ref[...], screen_refs, held_ref, sems, work_ref
        )

    def store(point, value):
        sigma_ref[pl.ds(point * TILE, TILE), :] = value

    along_first(work_ref, 1, low, store)


def contract_kernel(share, owner_ref, sigma_ref, equal_ref, sign_ref, gather_ref, greens_ref, *refs):
    partial_ref, sums_ref, pieces_ref = refs[-3:]
    low = lane_sign((TILE, WIDTH))
    points = partial_ref.shape[0]
    block = points // owner_ref.shape[0]
    tiles = block // TILE
    batch = max(n for n in range(1, 10) if tiles % n == 0)

    def contract(group, carry):
        slot, first = group // (tiles // batch), group % (tiles // batch) * batch
        owner = owner_ref[slot]
        units = [(tile, s) for tile in range(batch) for s in range(TILE)]

        def prepare(tile, s):
            point = owner * block + (first + tile) * TILE
            sigma = sigma_ref[pl.ds(point * TILE + s, TILE, stride=TILE), :]
            row = pl.multiple_of((owner * TILE + s) * block + (first + tile) * TILE, TILE)
            return (
                [roll_blocks(sigma, STEPS * i) for i in range(STEPS)],
                [greens_ref[j, pl.ds(row, TILE), :] for j in range(STEPS)],
            )

        ready = [prepare(*unit) for unit in units[:AHEAD]]
        for n, (tile, s) in enumerate(units):
            if n + AHEAD < len(units):
                ready.append(prepare(*units[n + AHEAD]))
            sigmas, greens = ready.pop(0)
            terms = [sigma * green for sigma in sigmas for green in greens]
            sums = terms if s == 0 else [a + b for a, b in zip(sums, terms)]
            if s == TILE - 1:
                row = pl.ds(pl.multiple_of(slot * block + (first + tile) * TILE, TILE), TILE)
                for spot, value in enumerate(sums):
                    sums_ref[row, spot * WIDTH : (spot + 1) * WIDTH] = value
        return carry

    lax.fori_loop(0, points // (TILE * batch), contract, 0)

    lane = lax.broadcasted_iota(jnp.int32, equal_ref.shape, 1)
    inner = lane - ENTRIES
    occupied = jnp.sum(jnp.where((inner >= 0) & (inner % (BANDS + 1) == 0), equal_ref[...], 0.0))
    spots = lax.broadcasted_iota(jnp.int32, (points, WIDTH), 1)
    on_diagonal = (spots < ENTRIES) & (spots % (BANDS + 1) == 0)
    lower = lax.broadcasted_iota(jnp.int32, (sums_ref.shape[0], WIDTH), 1) < ENTRIES
    for pair in range(STEPS * STEPS // 2):
        first_part = sums_ref[:, 2 * pair * WIDTH : (2 * pair + 1) * WIDTH]
        second_part = sums_ref[:, (2 * pair + 1) * WIDTH : (2 * pair + 2) * WIDTH]
        folded = jnp.where(lower, first_part, second_part) + sign_ref[pair : pair + 1, :] * swap(
            jnp.where(lower, second_part, first_part)
        )
        pieces_ref[:, 2 * pair * WIDTH : (2 * pair + 2) * WIDTH] = split(folded)
    total = jnp.dot(pieces_ref[...], gather_ref[...], preferred_element_type=jnp.float32)
    partial_ref[...] = total[:points] + jnp.where(on_diagonal, occupied * share, 0.0)


def propagate_kernel(green_ref, split_ref, effective_ref, spread_ref, out_ref, factor_ref, held_ref, sems):
    history, points, _ = green_ref.shape
    factor_ref[...] = jnp.dot(
        split(effective_ref[...] * time_step), spread_ref[...], preferred_element_type=jnp.float32
    )
    tile = held_ref.shape[2]
    row = lax.broadcasted_iota(jnp.int32, (BANDS, WIDTH), 0)
    same = lax.broadcasted_iota(jnp.int32, (BANDS, WIDTH), 1) % BANDS == row

    def copy(number, slot):
        return pltpu.make_async_copy(
            held_ref.at[slot], out_ref.at[:, pl.ds(number * tile, tile), :], sems.at[slot]
        )

    def matrix(factors, n):
        parts = [
            jnp.where(same, jnp.broadcast_to(factor[n : n + 1], same.shape), 0.0) for factor in factors
        ]
        whole = jnp.concatenate(parts, axis=0)
        high = whole.astype(jnp.bfloat16)
        low = (whole - high.astype(jnp.float32)).astype(jnp.bfloat16)
        return jnp.concatenate([high, high, low], axis=0)

    def advance(number, slot):
        start = number * tile if points == tile else pl.multiple_of(number * tile, TILE)
        factors = [
            factor_ref[pl.ds(start, tile), spot * WIDTH : (spot + 1) * WIDTH] for spot in range(2 * BANDS)
        ]
        for first in range(0, tile, AT_ONCE):
            batch = range(first, min(first + AT_ONCE, tile))
            results = []
            for n in batch:
                k = number * tile + n
                added = jnp.dot(split_ref[k], matrix(factors, n), preferred_element_type=jnp.float32)
                results.append(times_of(green_ref, k) + added)
            for n, result in zip(batch, results):
                if points % TILE:
                    held_ref[slot, :, n, :] = result
                else:
                    rows = held_ref.reshape(2 * history * tile, WIDTH)
                    rows[pl.ds(slot * history * tile + n, history, stride=tile), :] = result
        copy(number, slot).start()

    tiles = points // tile
    if tiles == 1:
        advance(0, 0)
        copy(0, 0).wait()
        return

    def step(number, carry):
        slot = number % 2

        @pl.when(number > 1)
        def _():
            copy(number - 2, slot).wait()

        advance(number, slot)
        return carry

    lax.fori_loop(0, tiles, step, 0)
    for number in (tiles - 2, tiles - 1):
        copy(number, number % 2).wait()


def gather_tables():
    blocks = 2 * BANDS
    pairs = STEPS * STEPS // 2
    table = np.zeros((pairs, 2, blocks, BANDS, 2, BANDS, BANDS), np.float32)
    signs = np.zeros((pairs, blocks, BANDS), np.float32)
    for pair in range(pairs):
        for p in range(blocks):
            i, j = divmod(2 * pair + p // BANDS, STEPS)
            h, a = divmod((p + STEPS * i) % blocks, BANDS)
            g, c = divmod((p + j) % blocks, BANDS)
            table[pair, :, p, :, h ^ g, a, c] = 1 if (h, g) == (0, 1) else -1
            signs[pair, p] = 1 if h == g else -1
    return signs.reshape(pairs, WIDTH), table.reshape(-1, WIDTH).astype(ml_dtypes.bfloat16)


def spread_table():
    table = np.zeros((2, BANDS, BANDS, 2, BANDS, 2, BANDS, BANDS), np.float32)
    for h, g, a, b in np.ndindex(2, 2, BANDS, BANDS):
        table[1 if h == g else 0, a, b, g, b, h, a, :] = -1 if (h, g) == (1, 0) else 1
    return np.tile(table.reshape(WIDTH, -1), (2, 1)).astype(ml_dtypes.bfloat16)


def in_vmem():
    return pl.BlockSpec(memory_space=pltpu.VMEM)


def in_smem():
    return pl.BlockSpec(memory_space=pltpu.SMEM)


def anywhere():
    return pl.BlockSpec(memory_space=pl.ANY)


def params(megabytes):
    return pltpu.CompilerParams(vmem_limit_bytes=megabytes * 1024 * 1024)


def cost(per_element, arrays):
    size = SIDE * SIDE * TILE * WIDTH
    return pl.CostEstimate(flops=per_element * size, bytes_accessed=4 * arrays * size, transcendentals=0)


def held_blocks(count, parts):
    return [
        pltpu.VMEM((count, TILE * SIDE * SIDE // parts, WIDTH), jnp.float32),
        pltpu.SemaphoreType.DMA((count,)),
    ]


def forward(place, greens, steps, parts):
    points = SIDE * SIDE
    return pl.pallas_call(
        functools.partial(forward_kernel, steps, parts),
        out_shape=[
            jax.ShapeDtypeStruct((points, TILE, WIDTH), jnp.float32),
            jax.ShapeDtypeStruct((STEPS, TILE * points, WIDTH), jnp.float32),
        ],
        in_specs=[in_smem()] + [anywhere()] * len(steps),
        out_specs=[in_vmem()] * 2,
        scratch_shapes=[pltpu.VMEM((points, TILE, WIDTH), jnp.float32)] + held_blocks(len(steps), parts),
        compiler_params=params(6),
        cost_estimate=cost(400, 6),
        name="forward",
    )(place, *greens)


def early_lines(place, lattice, weights, screens, steps, parts, work=None):
    points = SIDE * SIDE
    inputs = (place, lattice, weights, *screens) + (() if work is None else (work,))
    return pl.pallas_call(
        functools.partial(early_kernel, steps, parts),
        out_shape=jax.ShapeDtypeStruct((points, TILE, WIDTH), jnp.float32),
        in_specs=[in_smem(), in_vmem(), in_vmem()]
        + [anywhere()] * len(steps)
        + [in_vmem()] * (work is not None),
        out_specs=in_vmem(),
        input_output_aliases={} if work is None else {len(inputs) - 1: 0},
        scratch_shapes=held_blocks(len(steps), parts),
        compiler_params=params(4),
        cost_estimate=cost(25 * len(steps), 3),
        name="early",
    )(*inputs)


def sigma_of(place, lattice, weights, screens, work, steps, parts):
    points = SIDE * SIDE
    inputs = (place, lattice, weights, *screens, work)
    work, sigma = pl.pallas_call(
        functools.partial(sigma_kernel, steps, parts),
        out_shape=[
            jax.ShapeDtypeStruct((points, TILE, WIDTH), jnp.float32),
            jax.ShapeDtypeStruct((TILE * points, WIDTH), jnp.float32),
        ],
        in_specs=[in_smem()] + [in_vmem()] * 2 + [anywhere()] * len(steps) + [in_vmem()],
        out_specs=[in_vmem()] * 2,
        input_output_aliases={len(inputs) - 1: 0},
        scratch_shapes=held_blocks(len(steps), parts) if steps else [],
        compiler_params=params(2),
        cost_estimate=cost(200, 6),
        name="sigma",
    )(*inputs)
    return sigma


def contract(owners, sigma, equal_time, greens, block, share, before=()):
    points = owners.shape[0] * block
    rows = -(-points // 16) * 16
    signs, gather = gather_tables()
    return pl.pallas_call(
        functools.partial(contract_kernel, share),
        out_shape=jax.ShapeDtypeStruct((points, WIDTH), jnp.float32),
        in_specs=[in_smem()] + [in_vmem()] * 5 + [anywhere()] * len(before),
        out_specs=in_vmem(),
        scratch_shapes=[
            pltpu.VMEM((rows, STEPS * STEPS * WIDTH), jnp.float32),
            pltpu.VMEM((rows, STEPS * STEPS * WIDTH), jnp.bfloat16),
        ],
        compiler_params=params(6),
        cost_estimate=cost(70 * owners.shape[0], 6),
        name="contract",
    )(owners, sigma, equal_time, jnp.asarray(signs), jnp.asarray(gather), greens, *before)


def pick(place, whole, steps, parts, before=()):
    rows, width = whole.shape[0] // parts, whole.shape[1]
    return pl.pallas_call(
        functools.partial(pick_kernel, steps, parts),
        out_shape=[jax.ShapeDtypeStruct((rows, width), whole.dtype)] * len(steps),
        in_specs=[in_smem(), anywhere()] + [anywhere()] * len(before),
        out_specs=[in_vmem()] * len(steps),
        scratch_shapes=[pltpu.SemaphoreType.DMA((len(steps),))],
        compiler_params=params(56),
        cost_estimate=cost(0, 2),
        name="pick",
    )(place, whole, *before)


def split_own(greens):
    history, points, width = greens.shape
    return pl.pallas_call(
        split_kernel,
        out_shape=jax.ShapeDtypeStruct((points, history, 3 * width), jnp.bfloat16),
        in_specs=[in_vmem()],
        out_specs=in_vmem(),
        compiler_params=params(4),
        cost_estimate=cost(3, 2),
        name="split_own",
    )(greens)


def propagate(greens, pieces, effective):
    history, points, width = greens.shape
    tile = points if points % TILE else TILE
    spread = spread_table()
    return pl.pallas_call(
        propagate_kernel,
        out_shape=jax.ShapeDtypeStruct(greens.shape, jnp.float32),
        in_specs=[in_vmem()] * 4,
        out_specs=anywhere(),
        scratch_shapes=[
            pltpu.VMEM((points, spread.shape[1]), jnp.float32),
            pltpu.VMEM((2, history, tile, width), jnp.float32),
            pltpu.SemaphoreType.DMA((2,)),
        ],
        compiler_params=params(3),
        cost_estimate=cost(32, 5),
        name="propagate",
    )(greens, pieces, effective, jnp.asarray(spread))


def partner_of(place, step, count):
    if count == 1:
        return 0
    if count & (count - 1) == 0:
        return place ^ step
    return (place + step) % count


def exchange(value, axis, step, count):
    pairs = [(place, partner_of(place, step, count)) for place in range(count)]
    return lax.ppermute(value, axis, pairs)


def exchange_order(count):
    along = {}
    for step in range(1, count):
        along.setdefault(step // 2, []).append(step)
    single = [along[n] for n in along if n and n & (n - 1) == 0]
    mixed = [along[n] for n in along if n & (n - 1)]
    order = [step for steps in zip(*single[::-1]) for step in steps]
    return order + along[0] + [step for steps in mixed for step in steps]


def class_weights(quad_class):
    table = jnp.array(quadrature, jnp.float32)
    match = quad_class[:, None] == jnp.arange(4, dtype=jnp.int32)[None, :]
    return jnp.sum(jnp.where(match, table[None, :], jnp.float32(0.0)), axis=1)


def per_device(parts, blocks, green_row, screened, hamilton, equal_time, quad_class, live_count):
    history, local, width = green_row.shape
    points = local * parts
    times = history // parts
    place = lax.axis_index("ka")
    seat = place.reshape(1)
    position = jnp.arange(history, dtype=jnp.int32)
    weights = jnp.where(
        position < live_count[0], time_step * class_weights(quad_class), jnp.float32(0.0)
    ) * jnp.float32(1.0 / points)
    weights = lax.dynamic_slice_in_dim(weights, place * times, times)

    if times == TILE and local % SIDE == 0:
        groups, sources = 1, parts
        order = exchange_order(parts)
        moved = []
        wholes = [x.reshape(parts * TILE * local, width) for x in (green_row, screened)]
        blocks_of_green = [
            lax.dynamic_slice_in_dim(wholes[0], partner_of(place, step, parts) * (TILE * local), TILE * local)
            for step in order
        ]
        blocks_of_screen = pick(seat, wholes[1], order, parts, blocks_of_green[:1])
        moved = []
        for whole, sent in zip(wholes, (blocks_of_green, blocks_of_screen)):
            found = {step: exchange(block, "ka", step, parts) for step, block in zip(order, sent)}
            moved.append([{0: whole, **found}])
        order = [0] + order
    else:
        groups, sources = -(-times // TILE), 1
        order = [0]
        padding = groups * TILE - times
        moved = []
        for x in (green_row, screened):
            x = lax.all_to_all(x, "ka", split_axis=0, concat_axis=0, tiled=True)
            x = x.reshape(parts, times, local, width).transpose(1, 0, 2, 3).reshape(times, points, width)
            x = jnp.pad(x, ((0, padding), (0, 0), (0, 0))).reshape(groups, TILE * points, width)
            moved.append([{0: x[group]} for group in range(groups)])
        weights = jnp.pad(weights, (0, padding))
    weights = jnp.broadcast_to(weights.reshape(groups, TILE, 1), (groups, TILE, width))

    early = order[: max(1, len(order) - LATE)]
    late = order[len(early) :]
    own_pieces = split_own(green_row)
    share = hubbard / (points * blocks)
    sigmas = []
    for group in range(groups):
        green, screen = moved[0][group], moved[1][group]
        listed = order
        lattice, greens = forward(seat, [green[step] for step in listed], listed, sources)
        listed = early[-1:] + early[:-1]
        work = early_lines(seat, lattice, weights[group], [screen[step] for step in listed], listed, sources)
        for step in late[:-1]:
            work = early_lines(seat, lattice, weights[group], [screen[step]], [step], sources, work)
        last = late[-1:]
        sigma = sigma_of(
            seat, lattice, weights[group], [screen[step] for step in last], work, last, sources
        )
        sigmas.append((sigma, greens))

    if sources == parts and parts % 2 == 0 and parts & (parts - 1) == 0:
        (sigma, greens), = sigmas

        def blocks_of(steps, before=()):
            owners = jnp.stack([partner_of(place, step, parts) for step in steps])
            return contract(owners, sigma, equal_time, greens, local, share, before)

        others = exchange(blocks_of([*range(3, parts, 2), 1]), "ka", 1, parts)
        far = blocks_of(list(range(2, parts, 2))) + others[:-local]
        pieces = [
            exchange(far[(n - 1) * local : n * local], "ka", 2 * n, parts)
            for n in range(parts // 2 - 1, 0, -1)
        ]
        pieces += [blocks_of([0], pieces[:1]), others[-local:]]
        collision = tree_sum(pieces)
    else:
        whole = jnp.zeros((1,), jnp.int32)
        partial_value = tree_sum(
            [
                contract(whole, sigma, equal_time, greens, points, share if group == 0 else 0.0)
                for group, (sigma, greens) in enumerate(sigmas)
            ]
        )
        owners = [partner_of(place, step, parts) for step in range(parts)]
        pieces = [lax.dynamic_slice_in_dim(partial_value, owner * local, local) for owner in owners]
        collision = tree_sum(
            pieces[:1] + [exchange(pieces[step], "ka", step, parts) for step in range(1, parts)]
        )
    collision = tree_sum(
        [collision] + [exchange(collision, "hist", step, blocks) for step in range(blocks - 1, 0, -1)]
    )
    return propagate(green_row, own_pieces, hamilton + collision)


def solution(mesh):
    in_specs = (
        P("hist", "ka", None),
        P("hist", "ka", None),
        P("ka", None),
        P("ka", None),
        P("hist"),
        P("hist"),
    )
    out_specs = P("hist", "ka", None)
    return jax.shard_map(
        functools.partial(per_device, mesh.shape["ka"], mesh.shape["hist"]),
        mesh=mesh,
        in_specs=in_specs,
        out_specs=out_specs,
        check_vma=False,
    )
```
